32 devices in a mesh: dp: 4 (over y, x), ep: 8 (over z, core).
Axes of the slice: x: 2, y: 2, z: 4, core: 2. Of those that a mesh axis runs over, the one named last changes fastest.
Arguments:
- tokens: bfloat16 [4096, 2048], P(('dp', 'ep')), may hold values from -6 to 6
- cotangent: bfloat16 [4096, 2048], P(('dp', 'ep')), may hold values from -6 to 6
- expert_ids: int32 [4096, 8], P(('dp', 'ep')), may hold values from 0 to 31, all different within a row; in each aligned block of 128 rows (0 to 127, 128 to 255, ...) at most 34 rows name the same one
- gate_weights: bfloat16 [4096, 8], P(('dp', 'ep')), may hold values from 0.019897461 to 0.3984375
- w_up: bfloat16 [32, 2048, 384], P('ep'), may hold values from -0.125 to 0.125
- w_down: bfloat16 [32, 2048, 384], P('ep'), may hold values from -0.3125 to 0.3125
Outputs:
- token_grad: bfloat16 [4096, 2048], P(('dp', 'ep'))
- gate_grad: bfloat16 [4096, 8], P(('dp', 'ep'))
- down_grad: float32 [32, 2048, 384], P('ep', 'dp')
The draws below stay inside these ranges and needn't reach their ends.
Inputs may be any that keep to these rules, and one draw needn't show every extreme that they name: `expert_ids`: each token names 8 different experts; among the 128 tokens of one device (aligned blocks of rows) no expert is named more than 34 times, and in some block one expert is named exactly 34 times.
All inputs are finite; a program needn't handle non-finite values.
Results may differ from the reference program's by a relative error of at most 0.008.
Values may be sent and summed in bfloat16 or wider, within the bound.
No kernel may reach another device: no remote copies, remote signals or barrier semaphores. Data moves between devices by JAX's collectives and lax.ppermute only.
A program may use at most 128 MiB of HBM per device.

```python
import math
import jax
import jax.numpy as jnp
import numpy as np
from jax import lax

D = 2048
H = 384
TOPK = 8
TOK_DEV = 128
EXPERTS = 32
CAP = 34
TOKENS = 4096


def strengthened(values, key, source, target, blocks, factor):
    owner, partner = [(jnp.arange(values.shape[position]) // (values.shape[position] // blocks)).reshape([-1 if axis == position else 1 for axis in range(values.ndim)]) for position in (source, target)]
    chosen = jax.random.permutation(key, blocks)[partner]
    strong = (owner == chosen) | (owner == (partner + blocks // 2) % blocks)
    return jnp.where(strong, factor * values, values)


def block_levels(key, dims, shards, least, high):
    level, own = 1.0, jax.random.fold_in(key, 6)
    for dim, blocks in shards:
        steps = jnp.exp(jax.random.uniform(jax.random.fold_in(own, dim), (blocks,), jnp.float32, least / len(shards), high / len(shards)))
        level = level * jnp.repeat(steps, dims[dim] // blocks).reshape([-1 if axis == dim else 1 for axis in range(len(dims))])
    return level


def assign_block(key, own, number, rows, amount, top, limit, skew):
    ranking = jax.random.permutation(key, amount)
    packed, common = load_shares(amount, rows * top, limit, skew, True), load_shares(amount, rows * top, limit, skew, False)
    places = jnp.arange(amount)

    def named(lengths, offset_by):
        used = int((lengths > 0).sum())
        fixed = max(1, used // 4)
        shifted = fixed + (places - fixed + offset_by * (used - fixed)) % max(1, amount - fixed)
        return jnp.zeros((amount,), jnp.int32).at[ranking[jnp.where(places < fixed, places, shifted)]].set(jnp.asarray(lengths, jnp.int32))

    lengths = jnp.where(number % 4 == 0, named(packed, number // 4), named(common, number - number // 4 - 1))
    mixed = jax.random.permutation(jax.random.fold_in(own, 3), amount)
    source_of, sink = mixed[0:amount // 2 * 2:2], mixed[1:amount // 2 * 2:2]
    margin = jnp.minimum(lengths[source_of] - 1, limit - lengths[sink]) // 2
    margin = jnp.where((source_of == ranking[0]) | (sink == ranking[0]) | (lengths[sink] == 0), 0, jnp.maximum(margin, 0))
    shifted = jax.random.randint(jax.random.fold_in(own, 4), (amount // 2,), 0, 1 << 20) % (margin + 1)
    lengths = lengths.at[source_of].add(-shifted).at[sink].add(shifted)
    items = jnp.searchsorted(jnp.cumsum(lengths), jnp.arange(rows * top), side="right").astype(jnp.int32)
    table = items.reshape(top, rows).T
    table = table[jax.random.permutation(jax.random.fold_in(own, 1), rows)]
    offset_by = jax.random.randint(jax.random.fold_in(own, 2), (rows, 1), 0, top)
    return jnp.take_along_axis(table, (jnp.arange(top)[None, :] + offset_by) % top, axis=1)


def load_shares(amount, total, reach, skew, full):
    weights = [(1 << 20) // math.isqrt(rank ** skew) + 1 for rank in range(1, amount + 1)]
    largest = reach if full else min(reach, max(-(-total // amount), total * weights[0] // sum(weights)))
    least = 1 if total - largest >= amount - 1 else 0
    holding, surplus = [largest] + [least] * (amount - 1), total - largest - least * (amount - 1)
    while surplus > 0:
        candidates = [i for i in range(1, amount) if holding[i] < largest] or [i for i in range(1, amount) if holding[i] < reach]
        mass, left = sum([weights[i] for i in candidates]), surplus
        for i in candidates:
            extra = min(reach - holding[i], max(1, left * weights[i] // mass), surplus)
            holding[i] = holding[i] + extra
            surplus = surplus - extra
    return np.array(holding)


def noise(stream_key, extent, scale, reach, split=(), held_as=jnp.bfloat16):
    entries = jax.random.normal(stream_key, extent, jnp.float32) * scale
    if len(split) > 0:
        entries = block_levels(stream_key, extent, split, -0.22, 0.18) * entries
    return jnp.clip(entries, min=-reach, max=reach).astype(held_as)


def gaussian_with(key, extent, deviation, bound, cuts, heavy, held_as=jnp.bfloat16):
    entries = deviation * jax.random.normal(key, extent, jnp.float32)
    if cuts:
        entries = entries * block_levels(key, extent, cuts, -0.22, 0.18)
    return jnp.clip(strengthened(entries, jax.random.fold_in(key, 3), *heavy), -bound, bound).astype(held_as)


def setup_inputs(seed: int = 0) -> dict:
    streams_of = jax.random.split(jax.random.key(seed), 7)
    tokens = noise(streams_of[0], (TOKENS, D), 1.0, 6.0, ((0, 32),))
    cotangent = gaussian_with(streams_of[1], (TOKENS, D), 0.3, 6.0, ((0, 32),), (0, 1, 32, 2.75))
    expert_ids_keys = jax.random.split(jax.random.fold_in(streams_of[2], 1), TOKENS // TOK_DEV)
    expert_ids_turns = jax.random.permutation(jax.random.fold_in(streams_of[2], 3), TOKENS // TOK_DEV)
    expert_ids = jax.vmap(lambda own, number: assign_block(jax.random.fold_in(streams_of[2], 2), own, number, TOK_DEV, EXPERTS, TOPK, CAP, 0))(expert_ids_keys, expert_ids_turns).reshape((TOKENS, TOPK))
    gate_weights = jnp.clip(jnp.exp(math.log(0.3984375) - 2.9969585 * jax.random.uniform(streams_of[3], (TOKENS, TOPK), jnp.float32) ** block_levels(streams_of[3], (TOKENS, TOPK), ((0, 32),), -0.2, 0.2)), 0.019897461, 0.3984375).astype(jnp.bfloat16)
    w_up = noise(streams_of[4], (EXPERTS, D, H), D ** -0.5, 0.125, ((0, 8),))
    w_down = noise(streams_of[5], (EXPERTS, D, H), H ** -0.5, 0.3125, ((0, 8),))
    return dict(tokens=tokens, cotangent=cotangent, expert_ids=expert_ids, gate_weights=gate_weights, w_up=w_up, w_down=w_down)


def reference(tokens, cotangent, expert_ids, gate_weights, w_up, w_down):
    route_total = TOKENS * TOPK
    block_count = TOKENS // TOK_DEV
    block_routes = TOK_DEV * TOPK
    ids = expert_ids.reshape(block_count, block_routes)
    table = (ids[:, :, None] == jnp.arange(EXPERTS, dtype=jnp.int32)[None, None, :]).astype(jnp.int32)
    earlier = jnp.sum(jnp.cumsum(table, axis=1) * table, axis=2) - 1
    block_of = jnp.arange(block_count, dtype=jnp.int32)[:, None]
    global_pos = ((ids * block_count + block_of) * CAP + earlier).astype(jnp.int32)
    region = block_count * CAP
    inverse = jnp.full((EXPERTS * region,), route_total, jnp.int32)
    inverse = inverse.at[global_pos.reshape(route_total)].set(jnp.arange(route_total, dtype=jnp.int32))
    inverse = inverse.reshape(EXPERTS, region)
    flat_gates = gate_weights.reshape(route_total)

    def one_expert(carry, inputs):
        grad_acc, gate_acc = carry
        rows_inv, up_matrix, down_matrix = inputs
        occupied = rows_inv < route_total
        route_of = jnp.minimum(rows_inv, route_total - 1)
        token_of = route_of // TOPK
        x_rows = jnp.where(occupied[:, None], tokens[token_of], jnp.zeros((), tokens.dtype))
        dy_rows = jnp.where(occupied[:, None], cotangent[token_of], jnp.zeros((), cotangent.dtype))
        gate_f = jnp.where(occupied, flat_gates[route_of], jnp.zeros((), flat_gates.dtype)).astype(jnp.float32)
        pre_act = jnp.dot(x_rows, up_matrix, preferred_element_type=jnp.float32)
        hidden = jax.nn.silu(pre_act).astype(jnp.bfloat16)
        back_hidden = jnp.dot(dy_rows, down_matrix, preferred_element_type=jnp.float32)
        gate_rows = jnp.sum(back_hidden * hidden.astype(jnp.float32), axis=1).astype(jnp.bfloat16)
        sig = jax.nn.sigmoid(pre_act)
        slope = sig * (1.0 + pre_act * (1.0 - sig))
        grad_pre = (gate_f[:, None] * back_hidden * slope).astype(jnp.bfloat16)
        route_grad = jnp.dot(grad_pre, up_matrix.T, preferred_element_type=jnp.float32).astype(jnp.bfloat16)
        scaled_cot = (gate_f[:, None] * dy_rows.astype(jnp.float32)).astype(jnp.bfloat16)
        down_part = jnp.dot(scaled_cot.T, hidden, preferred_element_type=jnp.float32)
        grad_acc = grad_acc.at[token_of].add(jnp.where(occupied[:, None], route_grad.astype(jnp.float32), jnp.zeros((), jnp.float32)))
        gate_acc = gate_acc.at[route_of].add(jnp.where(occupied, gate_rows.astype(jnp.float32), jnp.zeros((), jnp.float32)))
        return (grad_acc, gate_acc), down_part

    start_carry = (jnp.zeros((TOKENS, D), jnp.float32), jnp.zeros((route_total,), jnp.float32))
    (grad_acc, gate_acc), down_grad = lax.scan(one_expert, start_carry, (inverse, w_up, w_down))
    token_grad = grad_acc.astype(jnp.bfloat16)
    gate_grad = gate_acc.reshape(TOKENS, TOPK).astype(jnp.bfloat16)
    return (token_grad, gate_grad, down_grad)
```

```python
import jax
import jax.numpy as jnp
from jax import lax
from jax.sharding import PartitionSpec as P


def shards(tokens, cotangent, expert_ids, gate_weights, w_up, w_down):
    tok_rows, width = tokens.shape
    top_count = expert_ids.shape[1]
    ep_count = lax.axis_size("ep")
    local_experts = w_up.shape[0]
    experts_total = local_experts * ep_count
    base_load = tok_rows * top_count // experts_total
    capacity = base_load + max(1, base_load // 16)
    rows = ep_count * capacity
    bf16, f32 = jnp.bfloat16, jnp.float32

    ids_all = lax.all_gather(expert_ids, "ep", axis=0, tiled=True)
    gates_all = lax.all_gather(gate_weights, "ep", axis=0, tiled=True)
    x_all = lax.all_gather(tokens, "ep", axis=0, tiled=True)
    dy_all = lax.all_gather(cotangent, "ep", axis=0, tiled=True)

    first = lax.axis_index("ep") * local_experts
    mine = first + jnp.arange(local_experts, dtype=jnp.int32)
    hits = ids_all[:, :, None] == mine[None, None, :]
    member = jnp.any(hits, axis=1)
    gate_of = jnp.sum(jnp.where(hits, gates_all[:, :, None].astype(f32), 0.0), axis=1)
    place = jnp.cumsum(member.astype(jnp.int32), axis=0) - 1
    place = jnp.where(member, place, rows)
    pick = (place.T[:, None, :] == jnp.arange(rows, dtype=jnp.int32)[None, :, None]).astype(bf16)

    def pick_rows(values):
        return jnp.einsum("brt,td->brd", pick, values, preferred_element_type=f32).astype(bf16)

    x_rows = pick_rows(x_all)
    gate_rows = jnp.einsum("brt,tb->br", pick, gate_of.astype(bf16), preferred_element_type=f32)[..., None]
    pre_act = jnp.einsum("brd,bdh->brh", x_rows, w_up, preferred_element_type=f32)
    sig = jax.nn.sigmoid(pre_act)
    hidden = (pre_act * sig).astype(bf16)
    slope = sig * (1.0 + pre_act * (1.0 - sig))
    dy_rows = pick_rows(dy_all)
    back_hidden = jnp.einsum("brd,bdh->brh", dy_rows, w_down, preferred_element_type=f32)
    gate_slots = jnp.sum(back_hidden * hidden.astype(f32), axis=2).astype(bf16)
    grad_pre = (gate_rows * back_hidden * slope).astype(bf16)
    scaled_cot = (gate_rows * dy_rows.astype(f32)).astype(bf16)
    partial_grad = jnp.einsum("brd,brh->bdh", scaled_cot, hidden, preferred_element_type=f32).astype(bf16)
    down_grad = lax.psum_scatter(partial_grad, "dp", scatter_dimension=1, tiled=True).astype(f32)
    route_grad = jnp.einsum("brh,bdh->brd", grad_pre, w_up, preferred_element_type=f32).astype(bf16)
    token_part = jnp.einsum("brt,brd->td", pick, route_grad, preferred_element_type=f32).astype(bf16)
    token_grad = lax.psum_scatter(token_part, "ep", scatter_dimension=0, tiled=True)
    gate_part = jnp.einsum("brt,br->tb", pick, gate_slots, preferred_element_type=f32)
    gate_part = jnp.sum(jnp.where(hits, gate_part[:, None, :], 0.0), axis=2).astype(bf16)
    gate_grad = lax.psum_scatter(gate_part, "ep", scatter_dimension=0, tiled=True)
    return (token_grad, gate_grad, down_grad)


def solution(mesh):
    return jax.shard_map(
        shards,
        mesh=mesh,
        in_specs=(
            P(("dp", "ep"), None),
            P(("dp", "ep"), None),
            P(("dp", "ep"), None),
            P(("dp", "ep"), None),
            P("ep", None, None),
            P("ep", None, None),
        ),
        out_specs=(P(("dp", "ep"), None), P(("dp", "ep"), None), P("ep", "dp", None)),
        check_vma=False,
    )
```

```python
import functools

import jax
import jax.numpy as jnp
from jax import lax
from jax.experimental import pallas as pl
from jax.experimental.pallas import tpu as pltpu
from jax.sharding import PartitionSpec as P

LANES = 128
SLICES = 2
VMEM_LIMIT = 60 * 1024 * 1024
bf16, f32 = jnp.bfloat16, jnp.float32
ANY = pl.BlockSpec(memory_space=pl.ANY)
VMEM = pl.BlockSpec(memory_space=pltpu.VMEM)
SMEM = pl.BlockSpec(memory_space=pltpu.SMEM)


def pick_block(place, slot, chips, mine, other, act):
    left, even = place[0] >= slot, place[1] == 0
    for is_left in (True, False):
        for is_even in (True, False):
            step = slot if is_left else chips - slot
            ref = (mine if is_left == is_even else other)[step - 1]

            @pl.when((left == is_left) & (even == is_even))
            def _():
                act(ref)


def start_blocks(place, chips, own, mine, other, dst, sem):
    rows = own.shape[0]
    pltpu.make_async_copy(own, dst.at[pl.ds(0, rows), :], sem.at[0]).start()
    for slot in range(1, chips):
        target = dst.at[pl.ds(slot * rows, rows), :]
        pick_block(
            place, slot, chips, mine, other,
            lambda ref: pltpu.make_async_copy(ref, target, sem.at[slot]).start(),
        )


def wait_blocks(chips, own, dst, sem):
    rows = own.shape[0]
    for slot in range(chips):
        pltpu.make_async_copy(own, dst.at[pl.ds(slot * rows, rows), :], sem.at[slot]).wait()


def weight_copies(weights, dst, sem, pieces):
    experts, _, hidden = weights.shape
    copies = []
    for b in range(experts):
        for start, size, to in pieces:
            copies.append(
                pltpu.make_async_copy(
                    weights.at[b, pl.ds(start, size), :],
                    dst.at[pl.ds(to, size), pl.ds(b * hidden, hidden)],
                    sem,
                )
            )
    return copies


def run_all(copies):
    for copy in copies:
        copy.start()
    return copies


def wait_all(copies):
    for copy in copies:
        copy.wait()


def row_tile(total):
    return 512 if total % 512 == 0 else total


def up_kernel(chips, experts, hidden, width, top, place, own, *refs):
    mine, other = refs[: chips - 1], refs[chips - 1 : 2 * chips - 2]
    w_up, hid, scaled, slope_g, meta, rows_v, w_v, sem, w_sem = refs[2 * chips - 2 :]
    loads = run_all(weight_copies(w_up, w_v, w_sem, ((0, width, 0),)))
    start_blocks(place, chips, own, mine, other, rows_v, sem)
    wait_blocks(chips, own, rows_v, sem)
    wait_all(loads)
    total = rows_v.shape[0]
    tile = row_tile(total)
    lane = lax.broadcasted_iota(jnp.int32, (tile, LANES), 1)
    first = place[2] * experts

    def step(i, carry):
        at = pl.ds(pl.multiple_of(i * tile, tile), tile)
        info = rows_v[at, pl.ds(width, LANES)].astype(f32)
        meta[at, :] = info
        ids = jnp.where(lane < top, info, -1.0)
        gates = pltpu.roll(info, LANES - top, 1)
        pair = 2 if experts % 2 == 0 else 1
        for b0 in range(0, experts, pair):
            pre = jnp.dot(
                rows_v[at, pl.ds(0, width)],
                w_v[:, pl.ds(b0 * hidden, pair * hidden)],
                preferred_element_type=f32,
            )
            for b in range(b0, b0 + pair):
                hit = ids == (first + b).astype(f32)
                gate = jnp.sum(jnp.where(hit, gates, 0.0), axis=1, keepdims=True)
                part = pre[:, (b - b0) * hidden : (b - b0 + 1) * hidden]
                sig = 1.0 / (1.0 + jnp.exp(-part))
                act = part * sig
                cols = pl.ds(b * hidden, hidden)
                hid[at, cols] = act.astype(bf16)
                scaled[at, cols] = (gate * act).astype(bf16)
                slope_g[at, cols] = (gate * (sig * (1.0 + part * (1.0 - sig)))).astype(bf16)
        return carry

    lax.fori_loop(0, total // tile, step, 0)


def back_kernel(chips, experts, hidden, top, pieces, last, place, own, *refs):
    mine, other = refs[: chips - 1], refs[chips - 1 : 2 * chips - 2]
    refs = refs[2 * chips - 2 :]
    w_down, refs = refs[0], refs[1:]
    before = None
    if last:
        if last == 2:
            before, refs = refs[0], refs[1:]
        hid, slope_g, meta, grad_pre, gate_back, rows_v, w_v, sem, w_sem = refs
    else:
        if last is None:
            before, refs = refs[0], refs[1:]
        out, rows_v, w_v, sem, w_sem = refs
    loads = run_all(weight_copies(w_down, w_v, w_sem, pieces))
    start_blocks(place, chips, own, mine, other, rows_v, sem)
    wait_blocks(chips, own, rows_v, sem)
    wait_all(loads)
    total = rows_v.shape[0]
    tile = row_tile(total)
    lane = lax.broadcasted_iota(jnp.int32, (tile, LANES), 1)
    first = place[2] * experts

    def step(i, carry):
        at = pl.ds(pl.multiple_of(i * tile, tile), tile)
        if last:
            ids = jnp.where(lane < top, meta[at, :], -1.0)
            picked = jnp.zeros((tile, LANES), f32)
        pair = 2 if experts % 2 == 0 else 1
        for b0 in range(0, experts, pair):
            both = pl.ds(b0 * hidden, pair * hidden)
            back = jnp.dot(rows_v[at, :], w_v[:, both], preferred_element_type=f32)
            if before is not None:
                back = back + before[at, both]
            if not last:
                out[at, both] = back
                continue
            for b in range(b0, b0 + pair):
                cols = pl.ds(b * hidden, hidden)
                part = back[:, (b - b0) * hidden : (b - b0 + 1) * hidden]
                grad_pre[at, cols] = (part * slope_g[at, cols].astype(f32)).astype(bf16)
                gate = jnp.sum(part * hid[at, cols].astype(f32), axis=1, keepdims=True)
                picked = picked + jnp.where(ids == (first + b).astype(f32), gate, 0.0)
        if last:
            gate_back[at, :] = picked.astype(bf16)
        return carry

    lax.fori_loop(0, total // tile, step, 0)


def down_kernel(chips, experts, hidden, place, own, *refs):
    mine, other = refs[: chips - 1], refs[chips - 1 : 2 * chips - 2]
    scaled, out, rows_v, sem = refs[2 * chips - 2 :]
    start_blocks(place, chips, own, mine, other, rows_v, sem)
    wait_blocks(chips, own, rows_v, sem)
    width = rows_v.shape[1]
    tile = 256 if width % 256 == 0 else LANES
    for b in range(experts):

        def step(i, carry):
            at = pl.ds(pl.multiple_of(i * tile, tile), tile)
            out[b, at, :] = lax.dot_general(
                rows_v[:, at], scaled[:, pl.ds(b * hidden, hidden)],
                (((0,), (0,)), ((), ())), preferred_element_type=f32,
            ).astype(bf16)
            return carry

        lax.fori_loop(0, width // tile, step, 0)


def token_kernel(chips, pieces, extra, place, *refs):
    grad_pre, refs = refs[0], refs[1:]
    if extra:
        gate_back, refs = refs[0], refs[1:]
    w_up, own, refs = refs[0], refs[1], refs[2:]
    mine, other = refs[: chips - 1], refs[chips - 1 : 2 * chips - 2]
    w_v, rows_v, sem, w_sem = refs[2 * chips - 2 :]
    loads = run_all(weight_copies(w_up, w_v, w_sem, pieces))
    rows, width = own.shape[0], w_v.shape[0]
    if extra:
        rows_v[:, pl.ds(width, LANES)] = gate_back[...]
    wait_all(loads)
    for slot in reversed(range(chips)):
        at = pl.ds(slot * rows, rows)
        rows_v[at, pl.ds(0, width)] = lax.dot_general(
            grad_pre[at, :], w_v[...], (((1,), (1,)), ((), ())), preferred_element_type=f32
        ).astype(bf16)
        source = rows_v.at[at, :]
        if slot == 0:
            pltpu.make_async_copy(source, own, sem.at[0]).start()
        else:
            pick_block(
                place, slot, chips, mine, other,
                lambda ref: pltpu.make_async_copy(source, ref, sem.at[slot]).start(),
            )
    for slot in range(chips):
        pltpu.make_async_copy(rows_v.at[pl.ds(slot * rows, rows), :], own, sem.at[slot]).wait()


def cost(flops, nbytes):
    return pl.CostEstimate(flops=int(flops), bytes_accessed=int(nbytes), transcendentals=0)


def params():
    return pltpu.CompilerParams(vmem_limit_bytes=VMEM_LIMIT)


def shards(tokens, cotangent, expert_ids, gate_weights, w_up, w_down):
    tok_rows, width = tokens.shape
    top = expert_ids.shape[1]
    ep_count, dp_count = lax.axis_size("ep"), lax.axis_size("dp")
    experts, _, hidden = w_up.shape
    chips = ep_count // 2
    total = ep_count * tok_rows
    inner = experts * hidden
    here = lax.axis_index("ep")
    place = jnp.stack([here // 2, here % 2, here]).astype(jnp.int32)
    swap = [(p, p ^ 1) for p in range(ep_count)]

    def reach(p, step):
        return p + 2 * step if p % 2 == 0 else p - 2 * step

    def inside(p):
        return 0 <= p < ep_count

    def gather(own):
        block = jnp.concatenate([own, lax.ppermute(own, "ep", swap)], axis=0)
        mine, other, held = [], [], block
        for step in range(1, chips):
            pairs = [(p, reach(p, 1)) for p in range(ep_count) if inside(reach(p, 1)) and inside(reach(p, 1 - step))]
            held = lax.ppermute(held, "ep", pairs)
            mine.append(held)
            other.append(lax.ppermute(held, "ep", [(p, p ^ 1) for p in range(ep_count) if inside(reach(p, -step))]))
        return block, mine, other

    def scatter(own, mine, other):
        carry = None
        for step in range(chips - 1, 0, -1):
            swapped = lax.ppermute(other[step - 1], "ep", [(p, p ^ 1) for p in range(ep_count) if inside(reach(p ^ 1, -step))])
            held = mine[step - 1].astype(f32) + swapped.astype(f32)
            if carry is not None:
                held = held + carry.astype(f32)
            carry = lax.ppermute(
                held.astype(bf16), "ep", [(p, reach(p, -1)) for p in range(ep_count) if inside(reach(p, -step))]
            )
        block = own.astype(f32)
        if carry is not None:
            block = block + carry.astype(f32)
        given = lax.ppermute(block[tok_rows:].astype(bf16), "ep", swap)
        return (block[:tok_rows] + given.astype(f32)).astype(bf16)

    info = jnp.concatenate(
        [expert_ids.astype(bf16), gate_weights, jnp.zeros((tok_rows, LANES - 2 * top), bf16)], axis=1
    )
    x_blocks = gather(jnp.concatenate([tokens, info], axis=1))
    share = width // dp_count
    piece = share // SLICES
    cut = cotangent.reshape(tok_rows, dp_count, SLICES, piece)
    dy_blocks = [gather(cut[:, :, s].reshape(tok_rows, dp_count * piece)) for s in range(SLICES)]

    def flat(blocks):
        return (blocks[0], *blocks[1], *blocks[2])

    many = 2 * chips - 1
    full = width + LANES
    hid, scaled, slope_g, meta = pl.pallas_call(
        functools.partial(up_kernel, chips, experts, hidden, width, top),
        in_specs=[SMEM] + [ANY] * (many + 1),
        out_specs=[VMEM] * 4,
        out_shape=[jax.ShapeDtypeStruct((total, inner), bf16)] * 3 + [jax.ShapeDtypeStruct((total, LANES), f32)],
        scratch_shapes=[
            pltpu.VMEM((total, full), bf16),
            pltpu.VMEM((width, inner), bf16),
            pltpu.SemaphoreType.DMA((chips,)),
            pltpu.SemaphoreType.DMA,
        ],
        compiler_params=params(),
        cost_estimate=cost(2 * total * width * inner, 2 * (total * full + width * inner + 3 * total * inner)),
        name="up",
    )(place, *flat(x_blocks), w_up)

    down_parts, before = [], None
    for s in range(SLICES):
        cols = dp_count * piece
        pieces = tuple((i * share + s * piece, piece, i * piece) for i in range(dp_count))
        last = s == SLICES - 1
        mode = (2 if s else 1) if last else (None if s else 0)
        ins = [place, *flat(dy_blocks[s]), w_down]
        specs = [SMEM] + [ANY] * (many + 1)
        if s:
            ins.append(before)
            specs.append(VMEM)
        if last:
            ins += [hid, slope_g, meta]
            specs += [VMEM] * 3
            outs = [jax.ShapeDtypeStruct((total, inner), bf16), jax.ShapeDtypeStruct((total, LANES), bf16)]
        else:
            outs = [jax.ShapeDtypeStruct((total, inner), f32)]
        result = pl.pallas_call(
            functools.partial(back_kernel, chips, experts, hidden, top, pieces, mode),
            in_specs=specs,
            out_specs=[VMEM] * len(outs),
            out_shape=outs,
            scratch_shapes=[
                pltpu.VMEM((total, cols), bf16),
                pltpu.VMEM((cols, inner), bf16),
                pltpu.SemaphoreType.DMA((chips,)),
                pltpu.SemaphoreType.DMA,
            ],
            compiler_params=params(),
            cost_estimate=cost(2 * total * cols * inner, 2 * (total * cols + cols * inner + 4 * total * inner)),
            name="back",
        )(*ins)
        if last:
            grad_pre, gate_back = result
        else:
            (before,) = result
        down_parts.append(
            pl.pallas_call(
                functools.partial(down_kernel, chips, experts, hidden),
                in_specs=[SMEM] + [ANY] * many + [VMEM],
                out_specs=VMEM,
                out_shape=jax.ShapeDtypeStruct((experts, cols, hidden), bf16),
                scratch_shapes=[pltpu.VMEM((total, cols), bf16), pltpu.SemaphoreType.DMA((chips,))],
                compiler_params=params(),
                cost_estimate=cost(2 * total * cols * inner, 2 * (total * cols + total * inner + cols * inner)),
                name="down",
            )(place, *flat(dy_blocks[s]), scaled)
        )

    token_parts = []
    half = width // SLICES
    for s in range(SLICES):
        extra = s == 0
        cols = half + (LANES if extra else 0)
        outs = pl.pallas_call(
            functools.partial(token_kernel, chips, ((s * half, half, 0),), extra),
            in_specs=[SMEM] + [VMEM] * (2 if extra else 1) + [ANY],
            out_specs=[ANY] * many,
            out_shape=[jax.ShapeDtypeStruct((2 * tok_rows, cols), bf16)] * many,
            scratch_shapes=[
                pltpu.VMEM((half, inner), bf16),
                pltpu.VMEM((total, cols), bf16),
                pltpu.SemaphoreType.DMA((chips,)),
                pltpu.SemaphoreType.DMA,
            ],
            compiler_params=params(),
            cost_estimate=cost(2 * total * half * inner, 2 * (total * cols + total * inner + half * inner)),
            name="token",
        )(place, grad_pre, *((gate_back,) if extra else ()), w_up)
        token_parts.append(scatter(outs[0], outs[1:chips], outs[chips:]))

    gate_grad = token_parts[0][:, half : half + top]
    token_grad = jnp.concatenate([token_parts[0][:, :half]] + token_parts[1:], axis=1)
    down_grad = jnp.concatenate(
        [lax.psum_scatter(part, "dp", scatter_dimension=1, tiled=True) for part in down_parts], axis=1
    ).astype(f32)
    return (token_grad, gate_grad, down_grad)


def solution(mesh):
    return jax.shard_map(
        shards,
        mesh=mesh,
        in_specs=(
            P(("dp", "ep"), None),
            P(("dp", "ep"), None),
            P(("dp", "ep"), None),
            P(("dp", "ep"), None),
            P("ep", None, None),
            P("ep", None, None),
        ),
        out_specs=(P(("dp", "ep"), None), P(("dp", "ep"), None), P("ep", "dp", None)),
        check_vma=False,
    )
```

```python
import functools

import jax
import jax.numpy as jnp
from jax import lax
from jax.experimental import pallas as pl
from jax.experimental.pallas import tpu as pltpu
from jax.sharding import PartitionSpec as P

LANES = 128
SLICES = 2
VMEM_LIMIT = 60 * 1024 * 1024
bf16, f32 = jnp.bfloat16, jnp.float32
ANY = pl.BlockSpec(memory_space=pl.ANY)
VMEM = pl.BlockSpec(memory_space=pltpu.VMEM)
SMEM = pl.BlockSpec(memory_space=pltpu.SMEM)


def weight_copies(weights, dst, sem, pieces):
    experts, _, hidden = weights.shape
    return [
        pltpu.make_async_copy(
            weights.at[b, pl.ds(start, size), :],
            dst.at[pl.ds(to, size), pl.ds(b * hidden, hidden)],
            sem.at[b],
        )
        for b in range(experts)
        for start, size, to in pieces
    ]


def load_weights(weights, dst, sem, pieces):
    @pl.when(pl.program_id(0) == 0)
    def _():
        for copy in weight_copies(weights, dst, sem, pieces):
            copy.start()


def wait_weights(weights, dst, sem, pieces, b0, b1):
    @pl.when(pl.program_id(0) == 0)
    def _():
        copies = weight_copies(weights, dst, sem, pieces)
        for copy in copies[b0 * len(pieces) : b1 * len(pieces)]:
            copy.wait()


def pair_of(experts):
    return 2 if experts % 2 == 0 else 1


def up_kernel(width, top, place, rows, w_up, hid, scaled, slope_g, w_v, sem):
    experts, _, hidden = w_up.shape
    pieces = ((0, width, 0),)
    load_weights(w_up, w_v, sem, pieces)
    info = rows[:, pl.ds(width, LANES)].astype(f32)
    lane = lax.broadcasted_iota(jnp.int32, info.shape, 1)
    ids = jnp.where(lane < top, info, -1.0)
    gates = pltpu.roll(info, LANES - top, 1)
    pair = pair_of(experts)
    for b0 in range(0, experts, pair):
        wait_weights(w_up, w_v, sem, pieces, b0, b0 + pair)
        pre = jnp.dot(
            rows[:, pl.ds(0, width)], w_v[:, pl.ds(b0 * hidden, pair * hidden)], preferred_element_type=f32
        )
        for b in range(b0, b0 + pair):
            hit = ids == (place[0] * experts + b).astype(f32)
            gate = jnp.sum(jnp.where(hit, gates, 0.0), axis=1, keepdims=True)
            part = pre[:, (b - b0) * hidden : (b - b0 + 1) * hidden]
            sig = 1.0 / (1.0 + jnp.exp(-part))
            act = part * sig
            cols = pl.ds(b * hidden, hidden)
            hid[:, cols] = act.astype(bf16)
            scaled[:, cols] = (gate * act).astype(bf16)
            slope_g[:, cols] = (gate * (sig * (1.0 + part * (1.0 - sig)))).astype(bf16)


def back_kernel(width, top, pieces, first, last, after, place, rows, w_down, *refs):
    refs = list(refs)[after:]
    before = None if first else refs.pop(0)
    if last:
        hid, slope_g, meta, grad_pre, gate_back, w_v, sem = refs
    else:
        out, w_v, sem = refs
    experts, _, hidden = w_down.shape
    load_weights(w_down, w_v, sem, pieces)
    if last:
        info = meta[...].astype(f32)
        lane = lax.broadcasted_iota(jnp.int32, info.shape, 1)
        ids = jnp.where(lane < top, info, -1.0)
        picked = jnp.zeros(info.shape, f32)
    pair = pair_of(experts)
    for b0 in range(0, experts, pair):
        wait_weights(w_down, w_v, sem, pieces, b0, b0 + pair)
        both = pl.ds(b0 * hidden, pair * hidden)
        back = jnp.dot(rows[...], w_v[:, both], preferred_element_type=f32)
        if before is not None:
            back = back + before[:, both]
        if not last:
            out[:, both] = back
            continue
        for b in range(b0, b0 + pair):
            cols = pl.ds(b * hidden, hidden)
            part = back[:, (b - b0) * hidden : (b - b0 + 1) * hidden]
            grad_pre[:, cols] = (part * slope_g[:, cols].astype(f32)).astype(bf16)
            gate = jnp.sum(part * hid[:, cols].astype(f32), axis=1, keepdims=True)
            picked = picked + jnp.where(ids == (place[0] * experts + b).astype(f32), gate, 0.0)
    if last:
        gate_back[...] = picked.astype(bf16)


def down_kernel(experts, orders, place, rows, scaled, *refs):
    outs, (held, sem) = refs[:-2], refs[-2:]
    groups, parts = len(orders), len(orders[0])
    hidden = scaled.shape[1] // experts
    piece = rows.shape[1] // parts
    cut = piece // groups
    copies = []
    for q in reversed(range(parts)):
        at = pl.multiple_of((place[1] ^ q) * piece, piece)
        full = lax.dot_general(
            rows[:, pl.ds(at, piece)], scaled[...], (((0,), (0,)), ((), ())), preferred_element_type=f32
        ).astype(bf16)
        for g, order in enumerate(orders):
            for b in range(experts):
                held[g, q, b] = full[g * cut : (g + 1) * cut, b * hidden : (b + 1) * hidden]
            p = order.index(q)
            half = parts // 2
            out = outs[2 * g + p // half]
            copy = pltpu.make_async_copy(held.at[g, q], out.at[p % half], sem.at[g, q])
            copy.start()
            copies.append(copy)
    for copy in copies:
        copy.wait()


def token_kernel(pieces, extra, after, *refs):
    grad_pre, refs = refs[after], refs[after + 1 :]
    if extra:
        gate_back, refs = refs[0], refs[1:]
    w_up, out, w_v, sem = refs
    load_weights(w_up, w_v, sem, pieces)
    wait_weights(w_up, w_v, sem, pieces, 0, w_up.shape[0])
    width = w_v.shape[0]
    out[:, pl.ds(0, width)] = lax.dot_general(
        grad_pre[...], w_v[...], (((1,), (1,)), ((), ())), preferred_element_type=f32
    ).astype(bf16)
    if extra:
        out[:, pl.ds(width, LANES)] = gate_back[...]


def cost(flops, nbytes):
    return pl.CostEstimate(flops=int(flops), bytes_accessed=int(nbytes), transcendentals=0)


def params(name=None):
    return pltpu.CompilerParams(vmem_limit_bytes=VMEM_LIMIT)


def shards(tokens, cotangent, expert_ids, gate_weights, w_up, w_down):
    tok_rows, width = tokens.shape
    top = expert_ids.shape[1]
    ep_count, dp_count = lax.axis_size("ep"), lax.axis_size("dp")
    experts, _, hidden = w_up.shape
    total = ep_count * tok_rows
    inner = experts * hidden
    place = jnp.stack([lax.axis_index("ep"), lax.axis_index("dp")]).astype(jnp.int32)
    bits = dp_count.bit_length() - 1
    groups = 2

    info = jnp.concatenate(
        [expert_ids.astype(bf16), gate_weights, jnp.zeros((tok_rows, LANES - 2 * top), bf16)], axis=1
    )
    x_all = lax.all_gather(jnp.concatenate([tokens, info], axis=1), "ep", axis=0, tiled=True)
    share = width // dp_count
    slices = SLICES if share % (SLICES * LANES) == 0 else 1
    piece = share // slices
    cols = dp_count * piece
    cut = cotangent.reshape(tok_rows, dp_count, slices, piece)
    cut = [cut[:, :, s].reshape(tok_rows, cols) for s in range(slices)]
    dy_all = []
    for part in cut:
        x_all, part = lax.optimization_barrier((x_all, part))
        dy_all.append(lax.all_gather(part, "ep", axis=0, tiled=True))

    full = width + LANES
    tile = 512 if total % 512 == 0 else total
    grid = (total // tile,)

    def by_rows(n):
        return pl.BlockSpec((tile, n), lambda i: (i, 0))

    def weights_scratch(rows):
        return [pltpu.VMEM((rows, inner), bf16), pltpu.SemaphoreType.DMA((experts,))]

    def shape(rows, n, dtype=bf16):
        return jax.ShapeDtypeStruct((rows, n), dtype)

    hid, scaled, slope_g = pl.pallas_call(
        functools.partial(up_kernel, width, top),
        grid=grid,
        in_specs=[SMEM, by_rows(full), ANY],
        out_specs=[by_rows(inner)] * 3,
        out_shape=[shape(total, inner)] * 3,
        scratch_shapes=weights_scratch(width),
        compiler_params=params(),
        cost_estimate=cost(2 * total * width * inner, 2 * (total * full + width * inner + 3 * total * inner)),
        name="up",
    )(place, x_all, w_up)

    orders = []
    for g in range(groups):
        turn = [(g + t) % bits for t in range(bits)]
        orders.append(
            tuple(sum(((p >> (bits - 1 - t)) & 1) << turn[t] for t in range(bits)) for p in range(dp_count))
        )

    def down(s):
        half = dp_count // 2
        cut_rows = piece // groups
        return pl.pallas_call(
            functools.partial(down_kernel, experts, tuple(orders)),
            in_specs=[SMEM, VMEM, VMEM],
            out_specs=[ANY] * (2 * groups),
            out_shape=[jax.ShapeDtypeStruct((half, experts, cut_rows, hidden), bf16)] * (2 * groups),
            scratch_shapes=[
                pltpu.VMEM((groups, dp_count, experts, cut_rows, hidden), bf16),
                pltpu.SemaphoreType.DMA((groups, dp_count)),
            ],
            compiler_params=params(),
            cost_estimate=cost(2 * total * cols * inner, 2 * (total * cols + total * inner + cols * inner)),
            name="down",
        )(place, dy_all[s], scaled)

    def exchange(state, t):
        new = []
        for g, (keep, send) in enumerate(state):
            bit = 1 << ((g + t) % bits)
            got = lax.ppermute(send, "dp", [(i, i ^ bit) for i in range(dp_count)])
            both = keep.astype(f32) + got.astype(f32)
            if t < bits - 1:
                both = both.astype(bf16)
            half = both.shape[0] // 2
            new.append((both[:half], both[half:]) if half else both[0])
        return new

    def back(s, before, after):
        first, last = s == 0, s == slices - 1
        pieces = tuple((i * share + s * piece, piece, i * piece) for i in range(dp_count))
        ins, specs = [place, dy_all[s], w_down, *after], [SMEM, by_rows(cols), ANY] + [ANY] * len(after)
        if not first:
            ins.append(before)
            specs.append(by_rows(inner))
        if last:
            ins += [hid, slope_g, x_all]
            specs += [by_rows(inner), by_rows(inner), pl.BlockSpec((tile, LANES), lambda i: (i, width // LANES))]
            outs, out_specs = [shape(total, inner), shape(total, LANES)], [by_rows(inner), by_rows(LANES)]
        else:
            outs, out_specs = shape(total, inner, f32), by_rows(inner)
        return pl.pallas_call(
            functools.partial(back_kernel, cols, top, pieces, first, last, len(after)),
            grid=grid,
            in_specs=specs,
            out_specs=out_specs,
            out_shape=outs,
            scratch_shapes=weights_scratch(cols),
            compiler_params=params(),
            cost_estimate=cost(2 * total * cols * inner, 2 * (total * cols + cols * inner + 4 * total * inner)),
            name="back",
        )(*ins)

    def token(s, grad_pre, gate_back, after):
        half = width // slices
        extra = s == 0
        n = half + (LANES if extra else 0)
        return pl.pallas_call(
            functools.partial(token_kernel, ((s * half, half, 0),), extra, len(after)),
            grid=grid,
            in_specs=[ANY] * len(after) + [by_rows(inner)] + ([by_rows(LANES)] if extra else []) + [ANY],
            out_specs=by_rows(n),
            out_shape=shape(total, n),
            scratch_shapes=weights_scratch(half),
            compiler_params=params(),
            cost_estimate=cost(2 * total * half * inner, 2 * (total * n + total * inner + half * inner)),
            name="token",
        )(*after, grad_pre, *((gate_back,) if extra else ()), w_up)

    states, before = [], None
    for s in range(slices):
        outs = down(s)
        before = back(s, before, outs[:1] if s < slices - 1 else [])
        states.append([(outs[2 * g], outs[2 * g + 1]) for g in range(groups)])
    grad_pre, gate_back = before
    down_parts = []
    for t in range(bits):
        states = [exchange(state, t) for state in states]
        if t == 0:
            first_sums = [pair[0] for pair in states[0]] if slices > 1 and bits > 1 else []
    down_parts = [part for state in states for part in state]
    token_parts = [
        lax.psum_scatter(
            token(s, grad_pre, gate_back, first_sums if s else []), "ep", scatter_dimension=0, tiled=True
        )
        for s in range(slices)
    ]
    half = width // slices
    gate_grad = token_parts[0][:, half : half + top]
    token_grad = jnp.concatenate([token_parts[0][:, :half]] + token_parts[1:], axis=1)
    down_grad = jnp.concatenate(down_parts, axis=1)
    return (token_grad, gate_grad, down_grad)


def solution(mesh):
    return jax.shard_map(
        shards,
        mesh=mesh,
        in_specs=(
            P(("dp", "ep"), None),
            P(("dp", "ep"), None),
            P(("dp", "ep"), None),
            P(("dp", "ep"), None),
            P("ep", None, None),
            P("ep", None, None),
        ),
        out_specs=(P(("dp", "ep"), None), P(("dp", "ep"), None), P("ep", "dp", None)),
        check_vma=False,
    )
```

```python
import functools

import jax
import jax.numpy as jnp
from jax import lax
from jax.experimental import pallas as pl
from jax.experimental.pallas import tpu as pltpu
from jax.sharding import PartitionSpec as P

LANES = 128
PACK = 16
SLICES = 2
GROUP = 2
VMEM_LIMIT = 60 * 1024 * 1024
bf16, f32 = jnp.bfloat16, jnp.float32
ANY = pl.BlockSpec(memory_space=pl.ANY)
SMEM = pl.BlockSpec(memory_space=pltpu.SMEM)
FIRST = (((0,), (0,)), ((), ()))
LAST = (((1,), (1,)), ((), ()))


def dot(a, b, dims=(((1,), (0,)), ((), ()))):
    return lax.dot_general(a, b, dims, preferred_element_type=f32)


def up_kernel(groups, width, top, cap, place, rows, w_up, pick, meta, hid, scaled, slope_g, held, gates):
    experts = held.shape[0]
    i = pl.program_id(0)

    @pl.when(i < groups)
    def _():
        info = rows[:, pl.ds(width, LANES)]
        meta[...] = info
        across = info.astype(f32).T
        count = across.shape[1]
        ids, weights = across[:top], across[top : 2 * top]
        before = lax.broadcasted_iota(jnp.int32, (count, count), 0) < lax.broadcasted_iota(
            jnp.int32, (count, count), 1
        )
        chosen = [ids == (place[0] * experts + b).astype(f32) for b in range(experts)]
        member = [jnp.sum(jnp.where(hit, 1.0, 0.0), axis=0, keepdims=True) for hit in chosen]
        table = jnp.concatenate(member + [jnp.zeros((PACK - experts, count), f32)], axis=0)
        prior = dot(table.astype(bf16), before.astype(bf16))
        spot = lax.broadcasted_iota(jnp.int32, (cap, count), 0).astype(f32)
        for b in range(experts):
            rank = jnp.where(member[b] > 0.0, prior[b : b + 1], -1.0)
            hot = spot == rank
            gate = jnp.sum(jnp.where(chosen[b], weights, 0.0), axis=0, keepdims=True)
            one = jnp.where(hot, 1.0, 0.0)
            pick[0, pl.ds(b * cap, cap), :] = one.astype(bf16)
            at = pl.ds(pl.multiple_of(i * cap, PACK), cap)
            gates[b, at, :] = jnp.broadcast_to(jnp.sum(one * gate, axis=1, keepdims=True), (cap, LANES))
        got = dot(pick[0], rows[:, pl.ds(0, width)]).astype(bf16)
        for b in range(experts):
            held[b, pl.ds(pl.multiple_of(i * cap, PACK), cap), :] = got[b * cap : (b + 1) * cap]

    @pl.when(i >= groups)
    def _():
        b = i - groups
        pre = dot(held[b], w_up[0])
        gate = gates[b][:, :1]
        sig = 0.5 + 0.5 * jnp.tanh(0.5 * pre)
        act = pre * sig
        hid[0] = act.astype(bf16)
        scaled[0] = (gate * act).astype(bf16)
        slope_g[0] = (gate * (sig + act * (1.0 - sig))).astype(bf16)


def gather_rows(i, cap, pick, rows, held):
    experts = held.shape[0]
    got = dot(pick[0], rows[...]).astype(bf16)
    for b in range(experts):
        held[b, pl.ds(pl.multiple_of(i * cap, PACK), cap), :] = got[b * cap : (b + 1) * cap]


def down_copies(orders, b, sent, outs, sem):
    parts = len(orders[0])
    half = parts // 2
    copies = []
    for q in range(parts):
        for g, order in enumerate(orders):
            p = order.index(q)
            copies.append(
                pltpu.make_async_copy(sent.at[g, q, b], outs[2 * g + p // half].at[p % half, b], sem.at[g, q, b])
            )
    return copies


def down_rows(orders, place, b, held, scaled, sent, outs, sem):
    parts = len(orders[0])
    piece = held.shape[1] // parts
    cut = piece // len(orders)
    for q in range(parts):
        at = pl.multiple_of((place[1] ^ q) * piece, LANES)
        full = dot(held[:, pl.ds(at, piece)], scaled, FIRST).astype(bf16)
        for g in range(len(orders)):
            sent[g, q, b] = full[g * cut : (g + 1) * cut]
    for copy in down_copies(orders, b, sent, outs, sem):
        copy.start()


def mid_kernel(groups, cap, orders, place, pick, rows, w_down, scaled, back, *refs):
    outs, (held, sent, sem) = refs[:-3], refs[-3:]
    experts = held.shape[0]
    i = pl.program_id(0)

    @pl.when(i < groups)
    def _():
        gather_rows(i, cap, pick, rows, held)

    @pl.when(i >= groups)
    def _():
        b = i - groups
        down_rows(orders, place, b, held.at[b], scaled[0], sent, outs, sem)
        back[0] = dot(held[b], w_down[...].reshape(held.shape[2], back.shape[2]))

    @pl.when(i == groups + experts - 1)
    def _():
        for b in range(experts):
            for copy in down_copies(orders, b, sent, outs, sem):
                copy.wait()


def down_kernel(orders, place, rows, scaled, *refs):
    outs, (sent, sem) = refs[:-2], refs[-2:]
    experts = sent.shape[2]
    b = pl.program_id(0)
    down_rows(orders, place, b, rows.at[0], scaled[0], sent, outs, sem)

    @pl.when(b == experts - 1)
    def _():
        for e in range(experts):
            for copy in down_copies(orders, e, sent, outs, sem):
                copy.wait()


def tail_kernel(groups, cap, width, top, has_before, after, place, pick, rows, w_down, w_up, hid, slope_g, meta, *refs):
    before = refs[0] if has_before else None
    out, kept, held, grads, sem = refs[has_before + after :]
    experts = held.shape[0]
    i = pl.program_id(0)

    @pl.when(i < groups)
    def _():
        gather_rows(i, cap, pick, rows, held)

    @pl.when((i >= groups) & (i < groups + experts))
    def _():
        b = i - groups
        pltpu.make_async_copy(held.at[b], kept.at[b], sem.at[b]).start()
        back = dot(held[b], w_down[...].reshape(held.shape[2], hid.shape[2]))
        if before is not None:
            back = back + before[0]
        gate = jnp.sum(back * hid[0].astype(f32), axis=1, keepdims=True)
        lane = lax.broadcasted_iota(jnp.int32, (back.shape[0], LANES), 1)
        gate = jnp.where(lane == b, gate, 0.0).astype(bf16)
        grad = (back * slope_g[0].astype(f32)).astype(bf16)
        route = dot(grad, w_up[0], LAST).astype(bf16)
        at = pl.ds(pl.multiple_of(b * cap, PACK), cap)
        for g in range(groups):
            grads[g, at, pl.ds(0, width)] = route[g * cap : (g + 1) * cap]
            grads[g, at, pl.ds(width, LANES)] = gate[g * cap : (g + 1) * cap]

    @pl.when(i >= groups + experts)
    def _():
        g = i - groups - experts
        total = dot(pick[0], grads[g], FIRST)
        out[:, pl.ds(0, width)] = total[:, :width].astype(bf16)
        by_expert = total[:, width:]
        info = meta[...].astype(f32)
        lane = lax.broadcasted_iota(jnp.int32, info.shape, 1)
        ids = jnp.where(lane < top, info, -1.0)
        picked = jnp.zeros(info.shape, f32)
        for b in range(experts):
            hit = ids == (place[0] * experts + b).astype(f32)
            picked = picked + jnp.where(hit, by_expert[:, b : b + 1], 0.0)
        out[:, pl.ds(width, LANES)] = picked.astype(bf16)

    @pl.when(i == 2 * groups + experts - 1)
    def _():
        for b in range(experts):
            pltpu.make_async_copy(held.at[b], kept.at[b], sem.at[b]).wait()


def cost(flops, nbytes):
    return pl.CostEstimate(flops=int(flops), bytes_accessed=int(nbytes), transcendentals=0)


def shards(tokens, cotangent, expert_ids, gate_weights, w_up, w_down):
    tok_rows, width = tokens.shape
    top = expert_ids.shape[1]
    ep_count, dp_count = lax.axis_size("ep"), lax.axis_size("dp")
    experts, _, hidden = w_up.shape
    base_load = tok_rows * top // (experts * ep_count)
    capacity = base_load + max(1, base_load // 16)
    total = ep_count * tok_rows
    groups = ep_count // GROUP
    members = GROUP * tok_rows
    cap = -(-GROUP * capacity // PACK) * PACK
    routes = groups * cap
    full = width + LANES
    place = jnp.stack([lax.axis_index("ep"), lax.axis_index("dp")]).astype(jnp.int32)
    bits = dp_count.bit_length() - 1
    turns = 2
    share = width // dp_count
    slices = SLICES if share % (SLICES * LANES) == 0 else 1
    piece = share // slices
    cols = dp_count * piece

    info = jnp.concatenate(
        [expert_ids.astype(bf16), gate_weights, jnp.zeros((tok_rows, LANES - 2 * top), bf16)], axis=1
    )
    x_all = lax.all_gather(jnp.concatenate([tokens, info], axis=1), "ep", axis=0, tiled=True)
    cut = cotangent.reshape(tok_rows, dp_count, slices, piece)
    cut = [cut[:, :, s].reshape(tok_rows, cols) for s in range(slices)]
    dy_all = []
    for part in cut:
        x_all, part = lax.optimization_barrier((x_all, part))
        dy_all.append(lax.all_gather(part, "ep", axis=0, tiled=True))

    def at_group(i):
        return jnp.minimum(i, groups - 1)

    def at_expert(i):
        return jnp.clip(i - groups, 0, experts - 1)

    def by_group(n):
        return pl.BlockSpec((members, n), lambda i: (at_group(i), 0))

    def by_expert(rows, n):
        return pl.BlockSpec((1, rows, n), lambda i: (at_expert(i), 0, 0))

    def shape(*dims, dtype=bf16):
        return jax.ShapeDtypeStruct(dims, dtype)

    def call(kernel, name, grid, flops, nbytes, **kw):
        return pl.pallas_call(
            kernel,
            grid=(grid,),
            compiler_params=pltpu.CompilerParams(vmem_limit_bytes=VMEM_LIMIT),
            cost_estimate=cost(flops, nbytes),
            name=name,
            **kw,
        )

    act = shape(experts, routes, hidden)
    act_spec = by_expert(routes, hidden)
    pick_spec = pl.BlockSpec((1, experts * cap, members), lambda i: (at_group(i), 0, 0))
    pick_flops = 2 * total * experts * cap * width
    main_flops = 2 * experts * routes * width * hidden
    row_bytes = 2 * experts * hidden * width
    pick, meta, hid, scaled, slope_g = call(
        functools.partial(up_kernel, groups, width, top, cap),
        "up",
        groups + experts,
        pick_flops + main_flops,
        2 * total * full + row_bytes,
        in_specs=[SMEM, by_group(full), by_expert(width, hidden)],
        out_specs=[pick_spec, by_group(LANES), act_spec, act_spec, act_spec],
        out_shape=[shape(groups, experts * cap, members), shape(total, LANES), act, act, act],
        scratch_shapes=[pltpu.VMEM((experts, routes, width), bf16), pltpu.VMEM((experts, routes, LANES), f32)],
    )(place, x_all, w_up)

    orders = []
    for g in range(turns):
        turn = [(g + t) % bits for t in range(bits)]
        orders.append(
            tuple(sum(((p >> (bits - 1 - t)) & 1) << turn[t] for t in range(bits)) for p in range(dp_count))
        )
    orders = tuple(orders)
    cut_rows = piece // turns
    down_outs = [shape(dp_count // 2, experts, cut_rows, hidden)] * (2 * turns)
    down_scratch = [
        pltpu.VMEM((turns, dp_count, experts, cut_rows, hidden), bf16),
        pltpu.SemaphoreType.DMA((turns, dp_count, experts)),
    ]
    w_cut = w_down.reshape(experts, dp_count, slices, piece, hidden)

    def cut_spec(s):
        return pl.BlockSpec((1, dp_count, 1, piece, hidden), lambda i: (at_expert(i), 0, s, 0, 0))

    def exchange(state, t):
        new = []
        for g, (keep, send) in enumerate(state):
            bit = 1 << ((g + t) % bits)
            got = lax.ppermute(send, "dp", [(i, i ^ bit) for i in range(dp_count)])
            both = keep.astype(f32) + got.astype(f32)
            if t < bits - 1:
                both = both.astype(bf16)
            half = both.shape[0] // 2
            new.append((both[:half], both[half:]) if half else both[0])
        return new

    states, before = [], None
    for s in range(slices - 1):
        before, *outs = call(
            functools.partial(mid_kernel, groups, cap, orders),
            "mid",
            groups + experts,
            (pick_flops + 2 * main_flops) // slices,
            2 * total * cols + 2 * row_bytes // slices,
            in_specs=[SMEM, pick_spec, by_group(cols), cut_spec(s), act_spec],
            out_specs=[act_spec] + [ANY] * len(down_outs),
            out_shape=[shape(experts, routes, hidden, dtype=f32)] + down_outs,
            scratch_shapes=[pltpu.VMEM((experts, routes, cols), bf16)] + down_scratch,
        )(place, pick, dy_all[s], w_cut, scaled)
        states.append([(outs[2 * g], outs[2 * g + 1]) for g in range(turns)])

    done, after = 0, []
    if states and bits > 1:
        states = [exchange(state, 0) for state in states]
        done, after = 1, [pair[0] for state in states for pair in state]

    def at_end(i):
        return jnp.clip(i - groups - experts, 0, groups - 1)

    last = slices - 1
    token_part, kept = call(
        functools.partial(tail_kernel, groups, cap, width, top, before is not None, len(after)),
        "tail",
        2 * groups + experts,
        pick_flops * (1 + 1 / slices) + main_flops * (1 + 1 / slices),
        2 * total * (full + cols) + 2 * row_bytes,
        in_specs=[
            SMEM,
            pl.BlockSpec(
                (1, experts * cap, members),
                lambda i: (jnp.where(i < groups, i, at_end(i)), 0, 0),
            ),
            by_group(cols),
            cut_spec(last),
            by_expert(width, hidden),
            act_spec,
            act_spec,
            pl.BlockSpec((members, LANES), lambda i: (at_end(i), 0)),
        ]
        + ([act_spec] if before is not None else [])
        + [ANY] * len(after),
        out_specs=[pl.BlockSpec((members, full), lambda i: (at_end(i), 0)), ANY],
        out_shape=[shape(total, full), shape(experts, routes, cols)],
        scratch_shapes=[
            pltpu.VMEM((experts, routes, cols), bf16),
            pltpu.VMEM((groups, experts * cap, full), bf16),
            pltpu.SemaphoreType.DMA((experts,)),
        ],
    )(place, pick, dy_all[last], w_cut, w_up, hid, slope_g, meta, *([] if before is None else [before]), *after)
    summed = lax.psum_scatter(token_part, "ep", scatter_dimension=0, tiled=True)

    outs = call(
        functools.partial(down_kernel, orders),
        "down",
        experts,
        main_flops // slices,
        2 * experts * routes * cols + row_bytes // slices,
        in_specs=[SMEM]
        + [pl.BlockSpec((1, routes, n), lambda b: (b, 0, 0)) for n in (cols, hidden)],
        out_specs=[ANY] * len(down_outs),
        out_shape=down_outs,
        scratch_shapes=down_scratch,
    )(place, kept, scaled)
    states = [(done, state) for state in states]
    states.append((0, [(outs[2 * g], outs[2 * g + 1]) for g in range(turns)]))
    for t in range(bits):
        states = [(done, state) if t < done else (done, exchange(state, t)) for done, state in states]
    states = [state for _, state in states]
    down_grad = jnp.concatenate([part for state in states for part in state], axis=1)
    return (summed[:, :width], summed[:, width : width + top], down_grad)


def solution(mesh):
    return jax.shard_map(
        shards,
        mesh=mesh,
        in_specs=(
            P(("dp", "ep"), None),
            P(("dp", "ep"), None),
            P(("dp", "ep"), None),
            P(("dp", "ep"), None),
            P("ep", None, None),
            P("ep", None, None),
        ),
        out_specs=(P(("dp", "ep"), None), P(("dp", "ep"), None), P("ep", "dp", None)),
        check_vma=False,
    )
```

```python
import functools

import jax
import jax.numpy as jnp
from jax import lax
from jax.experimental import pallas as pl
from jax.experimental.pallas import tpu as pltpu
from jax.sharding import PartitionSpec as P

LANES = 128
PACK = 16
SLICES = 2
GROUP = 2
VMEM_LIMIT = 60 * 1024 * 1024
bf16, f32 = jnp.bfloat16, jnp.float32
ANY = pl.BlockSpec(memory_space=pl.ANY)
SMEM = pl.BlockSpec(memory_space=pltpu.SMEM)
FIRST = (((0,), (0,)), ((), ()))
LAST = (((1,), (1,)), ((), ()))


def dot(a, b, dims=(((1,), (0,)), ((), ()))):
    return lax.dot_general(a, b, dims, preferred_element_type=f32)


def pack_kernel(top, parts, tokens, cotangent, ids, gates, x_out, *dy_out):
    count, width = tokens.shape
    x_out[:, pl.ds(0, width)] = tokens[...]
    info = jnp.concatenate(
        [ids[...].astype(f32), gates[...].astype(f32), jnp.zeros((LANES - 2 * top, count), f32)], axis=0
    )
    x_out[:, pl.ds(width, LANES)] = info.T.astype(bf16)
    piece = width // parts // len(dy_out)
    for s, out in enumerate(dy_out):
        for i in range(parts):
            out[:, pl.ds(i * piece, piece)] = cotangent[:, pl.ds((i * len(dy_out) + s) * piece, piece)]


def start_blocks(place, chips, own, mine, other, dst, sem):
    half = own.shape[0] // 2
    left_core = place[2] == 0

    def start(ref, slot, flip):
        for part in range(2):
            to = (part ^ flip) * half
            if not isinstance(flip, int):
                to = pl.multiple_of(to, half)
            pltpu.make_async_copy(
                ref.at[pl.ds(part * half, half), :], dst.at[slot, pl.ds(to, half), :], sem.at[slot, part]
            ).start()

    start(own, 0, place[2])
    for slot in range(1, chips):
        left = place[3] >= slot
        for is_left in (True, False):
            for is_core in (True, False):
                step = slot if is_left else chips - slot
                ref = (mine if is_left == is_core else other)[step - 1]

                @pl.when((left == is_left) & (left_core == is_core))
                def _():
                    start(ref, slot, 0 if is_left else 1)


def up_kernel(groups, width, top, cap, place, *refs):
    own, refs = refs[0], refs[1:]
    mine, other = refs[: groups - 1], refs[groups - 1 : 2 * groups - 2]
    w_up, pick, meta, hid, scaled, slope_g, held, gates, all_rows, sem = refs[2 * groups - 2 :]
    experts = held.shape[0]
    i = pl.program_id(0)

    @pl.when(i == 0)
    def _():
        start_blocks(place, groups, own, mine, other, all_rows, sem)

    @pl.when(i < groups)
    def _():
        half = own.shape[0] // 2
        for part in range(2):
            pltpu.make_async_copy(
                own.at[pl.ds(part * half, half), :], all_rows.at[i, pl.ds(part * half, half), :], sem.at[i, part]
            ).wait()
        rows = all_rows.at[i]
        group = lax.rem(place[3] - i + groups, groups)
        first = pl.multiple_of(group * cap, PACK)
        info = rows[:, pl.ds(width, LANES)]
        meta[...] = info
        across = info.astype(f32).T
        count = across.shape[1]
        ids, weights = across[:top], across[top : 2 * top]
        before = lax.broadcasted_iota(jnp.int32, (count, count), 0) < lax.broadcasted_iota(
            jnp.int32, (count, count), 1
        )
        chosen = [ids == (place[0] * experts + b).astype(f32) for b in range(experts)]
        member = [jnp.sum(jnp.where(hit, 1.0, 0.0), axis=0, keepdims=True) for hit in chosen]
        table = jnp.concatenate(member + [jnp.zeros((PACK - experts, count), f32)], axis=0)
        prior = dot(table.astype(bf16), before.astype(bf16))
        spot = lax.broadcasted_iota(jnp.int32, (cap, count), 0).astype(f32)
        for b in range(experts):
            rank = jnp.where(member[b] > 0.0, prior[b : b + 1], -1.0)
            one = jnp.where(spot == rank, 1.0, 0.0)
            gate = jnp.sum(jnp.where(chosen[b], weights, 0.0), axis=0, keepdims=True)
            pick[0, pl.ds(b * cap, cap), :] = one.astype(bf16)
            gates[b, pl.ds(first, cap), :] = jnp.broadcast_to(
                jnp.sum(one * gate, axis=1, keepdims=True), (cap, LANES)
            )
        got = dot(pick[0], rows[:, pl.ds(0, width)]).astype(bf16)
        for b in range(experts):
            held[b, pl.ds(first, cap), :] = got[b * cap : (b + 1) * cap]

    @pl.when(i >= groups)
    def _():
        b = i - groups
        pre = dot(held[b], w_up[0])
        gate = gates[b][:, :1]
        sig = 0.5 + 0.5 * jnp.tanh(0.5 * pre)
        act = pre * sig
        hid[0] = act.astype(bf16)
        scaled[0] = (gate * act).astype(bf16)
        slope_g[0] = (gate * (sig + act * (1.0 - sig))).astype(bf16)


def gather_rows(i, cap, pick, rows, held):
    experts = held.shape[0]
    got = dot(pick[0], rows[...]).astype(bf16)
    for b in range(experts):
        held[b, pl.ds(pl.multiple_of(i * cap, PACK), cap), :] = got[b * cap : (b + 1) * cap]


def down_copies(orders, b, sent, outs, sem):
    parts = len(orders[0])
    half = parts // 2
    copies = []
    for q in range(parts):
        for g, order in enumerate(orders):
            p = order.index(q)
            copies.append(
                pltpu.make_async_copy(sent.at[g, q, b], outs[2 * g + p // half].at[p % half, b], sem.at[g, q, b])
            )
    return copies


def down_rows(orders, place, b, held, scaled, sent, outs, sem):
    parts = len(orders[0])
    piece = held.shape[1] // parts
    cut = piece // len(orders)
    for q in range(parts):
        at = pl.multiple_of((place[1] ^ q) * piece, LANES)
        full = dot(held[:, pl.ds(at, piece)], scaled, FIRST).astype(bf16)
        for g in range(len(orders)):
            sent[g, q, b] = full[g * cut : (g + 1) * cut]
    for copy in down_copies(orders, b, sent, outs, sem):
        copy.start()


def mid_kernel(groups, cap, orders, place, pick, rows, w_down, scaled, back, *refs):
    outs, (held, sent, sem) = refs[:-3], refs[-3:]
    experts = held.shape[0]
    i = pl.program_id(0)

    @pl.when(i < groups)
    def _():
        gather_rows(i, cap, pick, rows, held)

    @pl.when(i >= groups)
    def _():
        b = i - groups
        down_rows(orders, place, b, held.at[b], scaled[0], sent, outs, sem)
        back[0] = dot(held[b], w_down[...].reshape(held.shape[2], back.shape[2]))

    @pl.when(i == groups + experts - 1)
    def _():
        for b in range(experts):
            for copy in down_copies(orders, b, sent, outs, sem):
                copy.wait()


def down_kernel(orders, after, place, rows, scaled, *refs):
    outs, (sent, sem) = refs[after:-2], refs[-2:]
    experts = sent.shape[2]
    b = pl.program_id(0)
    down_rows(orders, place, b, rows.at[0], scaled[0], sent, outs, sem)

    @pl.when(b == experts - 1)
    def _():
        for e in range(experts):
            for copy in down_copies(orders, e, sent, outs, sem):
                copy.wait()


def tail_kernel(groups, cap, width, top, has_before, place, pick, rows, w_down, w_up, hid, slope_g, meta, *refs):
    before = refs[0] if has_before else None
    out, kept, held, grads, sem = refs[has_before:]
    experts = held.shape[0]
    i = pl.program_id(0)

    @pl.when(i < groups)
    def _():
        gather_rows(i, cap, pick, rows, held)

    @pl.when((i >= groups) & (i < groups + experts))
    def _():
        b = i - groups
        pltpu.make_async_copy(held.at[b], kept.at[b], sem.at[b]).start()
        back = dot(held[b], w_down[...].reshape(held.shape[2], hid.shape[2]))
        if before is not None:
            back = back + before[0]
        gate = jnp.sum(back * hid[0].astype(f32), axis=1, keepdims=True)
        lane = lax.broadcasted_iota(jnp.int32, (back.shape[0], LANES), 1)
        gate = jnp.where(lane == b, gate, 0.0).astype(bf16)
        grad = (back * slope_g[0].astype(f32)).astype(bf16)
        route = dot(grad, w_up[0], LAST).astype(bf16)
        at = pl.ds(pl.multiple_of(b * cap, PACK), cap)
        for g in range(groups):
            grads[g, at, pl.ds(0, width)] = route[g * cap : (g + 1) * cap]
            grads[g, at, pl.ds(width, LANES)] = gate[g * cap : (g + 1) * cap]

    @pl.when(i >= groups + experts)
    def _():
        g = i - groups - experts
        total = dot(pick[0], grads[g], FIRST)
        out[:, pl.ds(0, width)] = total[:, :width].astype(bf16)
        by_expert = total[:, width:]
        info = meta[...].astype(f32)
        lane = lax.broadcasted_iota(jnp.int32, info.shape, 1)
        ids = jnp.where(lane < top, info, -1.0)
        picked = jnp.zeros(info.shape, f32)
        for b in range(experts):
            hit = ids == (place[0] * experts + b).astype(f32)
            picked = picked + jnp.where(hit, by_expert[:, b : b + 1], 0.0)
        out[:, pl.ds(width, LANES)] = picked.astype(bf16)

    @pl.when(i == 2 * groups + experts - 1)
    def _():
        for b in range(experts):
            pltpu.make_async_copy(held.at[b], kept.at[b], sem.at[b]).wait()


def cost(flops, nbytes):
    return pl.CostEstimate(flops=int(flops), bytes_accessed=int(nbytes), transcendentals=0)


def shards(tokens, cotangent, expert_ids, gate_weights, w_up, w_down):
    tok_rows, width = tokens.shape
    top = expert_ids.shape[1]
    ep_count, dp_count = lax.axis_size("ep"), lax.axis_size("dp")
    experts, _, hidden = w_up.shape
    base_load = tok_rows * top // (experts * ep_count)
    capacity = base_load + max(1, base_load // 16)
    total = ep_count * tok_rows
    groups = ep_count // GROUP
    members = GROUP * tok_rows
    cap = -(-GROUP * capacity // PACK) * PACK
    routes = groups * cap
    full = width + LANES
    here = lax.axis_index("ep")
    place = jnp.stack([here, lax.axis_index("dp"), here % GROUP, here // GROUP]).astype(jnp.int32)
    bits = dp_count.bit_length() - 1
    turns = 2
    share = width // dp_count
    slices = SLICES if share % (SLICES * LANES) == 0 else 1
    piece = share // slices
    cols = dp_count * piece

    def shape(*dims, dtype=bf16):
        return jax.ShapeDtypeStruct(dims, dtype)

    x_own, *dy_own = pl.pallas_call(
        functools.partial(pack_kernel, top, dp_count),
        out_shape=[shape(tok_rows, full)] + [shape(tok_rows, cols)] * slices,
        compiler_params=pltpu.CompilerParams(vmem_limit_bytes=VMEM_LIMIT),
        cost_estimate=cost(0, 8 * tok_rows * width),
        name="pack",
    )(tokens, cotangent, expert_ids.T, gate_weights.T)
    dy_all = [lax.all_gather(part, "ep", axis=0, tiled=True) for part in dy_own]

    def reach(p, step):
        q = p + GROUP * step if p % GROUP == 0 else p - GROUP * step
        return q if 0 <= q < ep_count else None

    def hop(value, pairs):
        return lax.ppermute(value, "ep", pairs)

    x_own = jnp.concatenate([x_own, hop(x_own, [(p, p ^ 1) for p in range(ep_count)])], axis=0)
    x_mine, x_other, moving = [], [], x_own
    for step in range(1, groups):
        moving = hop(
            moving,
            [(p, reach(p, 1)) for p in range(ep_count) if None not in (reach(p, 1), reach(p, 1 - step))],
        )
        x_mine.append(moving)
        x_other.append(hop(moving, [(p, p ^ 1) for p in range(ep_count) if reach(p, -step) is not None]))

    def at_group(i):
        return jnp.minimum(i, groups - 1)

    def at_expert(i):
        return jnp.clip(i - groups, 0, experts - 1)

    def at_slot(i, place):
        return lax.rem(place[3] - at_group(i) + groups, groups)

    def by_group(n):
        return pl.BlockSpec((members, n), lambda i, *_: (at_group(i), 0))

    def by_expert(rows, n):
        return pl.BlockSpec((1, rows, n), lambda i, *_: (at_expert(i), 0, 0))

    def call(kernel, name, grid, flops, nbytes, in_specs, out_specs, out_shape, scratch_shapes, prefetch=0):
        return pl.pallas_call(
            kernel,
            grid_spec=pltpu.PrefetchScalarGridSpec(
                num_scalar_prefetch=prefetch,
                grid=(grid,),
                in_specs=in_specs,
                out_specs=out_specs,
                scratch_shapes=scratch_shapes,
            ),
            out_shape=out_shape,
            compiler_params=pltpu.CompilerParams(vmem_limit_bytes=VMEM_LIMIT),
            cost_estimate=cost(flops, nbytes),
            name=name,
        )

    act = shape(experts, routes, hidden)
    act_spec = by_expert(routes, hidden)
    pick_spec = pl.BlockSpec((1, experts * cap, members), lambda i, *_: (at_group(i), 0, 0))
    pick_flops = 2 * total * experts * cap * width
    main_flops = 2 * experts * routes * width * hidden
    row_bytes = 2 * experts * hidden * width
    pick, meta, hid, scaled, slope_g = call(
        functools.partial(up_kernel, groups, width, top, cap),
        "up",
        groups + experts,
        pick_flops + main_flops,
        2 * total * full + row_bytes,
        prefetch=1,
        in_specs=[ANY] * (2 * groups - 1) + [by_expert(width, hidden)],
        out_specs=[
            pl.BlockSpec((1, experts * cap, members), lambda i, place: (at_slot(i, place), 0, 0)),
            pl.BlockSpec((members, LANES), lambda i, place: (at_slot(i, place), 0)),
            act_spec,
            act_spec,
            act_spec,
        ],
        out_shape=[shape(groups, experts * cap, members), shape(total, LANES), act, act, act],
        scratch_shapes=[
            pltpu.VMEM((experts, routes, width), bf16),
            pltpu.VMEM((experts, routes, LANES), f32),
            pltpu.VMEM((groups, members, full), bf16),
            pltpu.SemaphoreType.DMA((groups, 2)),
        ],
    )(place, x_own, *x_mine, *x_other, w_up)

    orders = []
    for g in range(turns):
        turn = [(g + t) % bits for t in range(bits)]
        orders.append(
            tuple(sum(((p >> (bits - 1 - t)) & 1) << turn[t] for t in range(bits)) for p in range(dp_count))
        )
    orders = tuple(orders)
    cut_rows = piece // turns
    down_outs = [shape(dp_count // 2, experts, cut_rows, hidden)] * (2 * turns)
    down_scratch = [
        pltpu.VMEM((turns, dp_count, experts, cut_rows, hidden), bf16),
        pltpu.SemaphoreType.DMA((turns, dp_count, experts)),
    ]
    w_cut = w_down.reshape(experts, dp_count, slices, piece, hidden)

    def cut_spec(s):
        return pl.BlockSpec((1, dp_count, 1, piece, hidden), lambda i: (at_expert(i), 0, s, 0, 0))

    def exchange(state, t):
        new = []
        for g, (keep, send) in enumerate(state):
            bit = 1 << ((g + t) % bits)
            got = lax.ppermute(send, "dp", [(i, i ^ bit) for i in range(dp_count)])
            both = keep.astype(f32) + got.astype(f32)
            if t < bits - 1:
                both = both.astype(bf16)
            half = both.shape[0] // 2
            new.append((both[:half], both[half:]) if half else both[0])
        return new

    states, before = [], None
    for s in range(slices - 1):
        before, *outs = call(
            functools.partial(mid_kernel, groups, cap, orders),
            "mid",
            groups + experts,
            (pick_flops + 2 * main_flops) // slices,
            2 * total * cols + 2 * row_bytes // slices,
            in_specs=[SMEM, pick_spec, by_group(cols), cut_spec(s), act_spec],
            out_specs=[act_spec] + [ANY] * len(down_outs),
            out_shape=[shape(experts, routes, hidden, dtype=f32)] + down_outs,
            scratch_shapes=[pltpu.VMEM((experts, routes, cols), bf16)] + down_scratch,
        )(place, pick, dy_all[s], w_cut, scaled)
        states.append([(outs[2 * g], outs[2 * g + 1]) for g in range(turns)])

    done, after = 0, []
    if states and bits > 1:
        states = [exchange(state, 0) for state in states]
        done, after = 1, [pair[0] for state in states for pair in state]

    def at_end(i):
        return jnp.clip(i - groups - experts, 0, groups - 1)

    last = slices - 1
    token_part, kept = call(
        functools.partial(tail_kernel, groups, cap, width, top, before is not None),
        "tail",
        2 * groups + experts,
        8 * main_flops,
        4 * row_bytes,
        in_specs=[
            SMEM,
            pl.BlockSpec(
                (1, experts * cap, members),
                lambda i: (jnp.where(i < groups, i, at_end(i)), 0, 0),
            ),
            by_group(cols),
            cut_spec(last),
            by_expert(width, hidden),
            act_spec,
            act_spec,
            pl.BlockSpec((members, LANES), lambda i: (at_end(i), 0)),
        ]
        + ([act_spec] if before is not None else []),
        out_specs=[pl.BlockSpec((members, full), lambda i: (at_end(i), 0)), ANY],
        out_shape=[shape(total, full), shape(experts, routes, cols)],
        scratch_shapes=[
            pltpu.VMEM((experts, routes, cols), bf16),
            pltpu.VMEM((groups, experts * cap, full), bf16),
            pltpu.SemaphoreType.DMA((experts,)),
        ],
    )(place, pick, dy_all[last], w_cut, w_up, hid, slope_g, meta, *([] if before is None else [before]))
    summed = lax.psum_scatter(token_part, "ep", scatter_dimension=0, tiled=True)

    outs = call(
        functools.partial(down_kernel, orders, len(after)),
        "down",
        experts,
        16 * main_flops,
        8 * row_bytes,
        in_specs=[SMEM]
        + [pl.BlockSpec((1, routes, n), lambda b: (b, 0, 0)) for n in (cols, hidden)]
        + [ANY] * len(after),
        out_specs=[ANY] * len(down_outs),
        out_shape=down_outs,
        scratch_shapes=down_scratch,
    )(place, kept, scaled, *after)
    states = [(done, state) for state in states]
    states.append((0, [(outs[2 * g], outs[2 * g + 1]) for g in range(turns)]))
    for t in range(bits):
        states = [(done, state) if t < done else (done, exchange(state, t)) for done, state in states]
    states = [state for _, state in states]
    down_grad = jnp.concatenate([part for state in states for part in state], axis=1)
    return (summed[:, :width], summed[:, width : width + top], down_grad)


def solution(mesh):
    return jax.shard_map(
        shards,
        mesh=mesh,
        in_specs=(
            P(("dp", "ep"), None),
            P(("dp", "ep"), None),
            P(("dp", "ep"), None),
            P(("dp", "ep"), None),
            P("ep", None, None),
            P("ep", None, None),
        ),
        out_specs=(P(("dp", "ep"), None), P(("dp", "ep"), None), P("ep", "dp", None)),
        check_vma=False,
    )
```

```python
import functools

import jax
import jax.numpy as jnp
from jax import lax
from jax.experimental import pallas as pl
from jax.experimental.pallas import tpu as pltpu
from jax.sharding import PartitionSpec as P

LANES = 128
PACK = 16
SLICES = 2
GROUP = 2
VMEM_LIMIT = 60 * 1024 * 1024
bf16, f32 = jnp.bfloat16, jnp.float32
ANY = pl.BlockSpec(memory_space=pl.ANY)
SMEM = pl.BlockSpec(memory_space=pltpu.SMEM)
FIRST = (((0,), (0,)), ((), ()))
LAST = (((1,), (1,)), ((), ()))


def dot(a, b, dims=(((1,), (0,)), ((), ()))):
    return lax.dot_general(a, b, dims, preferred_element_type=f32)


def pack_kernel(top, parts, tokens, cotangent, ids, gates, x_out, *dy_out):
    count, width = tokens.shape
    x_out[:, pl.ds(0, width)] = tokens[...]
    info = jnp.concatenate(
        [ids[...].astype(f32), gates[...].astype(f32), jnp.zeros((LANES - 2 * top, count), f32)], axis=0
    )
    x_out[:, pl.ds(width, LANES)] = info.T.astype(bf16)
    piece = width // parts // len(dy_out)
    for s, out in enumerate(dy_out):
        for i in range(parts):
            out[:, pl.ds(i * piece, piece)] = cotangent[:, pl.ds((i * len(dy_out) + s) * piece, piece)]


def start_blocks(place, chips, own, mine, other, dst, sem):
    half = own.shape[0] // 2
    left_core = place[2] == 0

    def start(ref, slot, flip):
        for part in range(2):
            to = (part ^ flip) * half
            if not isinstance(flip, int):
                to = pl.multiple_of(to, half)
            pltpu.make_async_copy(
                ref.at[pl.ds(part * half, half), :], dst.at[slot, pl.ds(to, half), :], sem.at[slot, part]
            ).start()

    start(own, 0, place[2])
    for slot in range(1, chips):
        left = place[3] >= slot
        for is_left in (True, False):
            for is_core in (True, False):
                step = slot if is_left else chips - slot
                ref = (mine if is_left == is_core else other)[step - 1]

                @pl.when((left == is_left) & (left_core == is_core))
                def _():
                    start(ref, slot, 0 if is_left else 1)


def up_kernel(groups, width, top, cap, after, place, rows, w_up, *refs):
    pick, meta, hid, scaled, slope_g, held, gates = refs[after:]
    experts = held.shape[0]
    i = pl.program_id(0)

    @pl.when(i < groups)
    def _():
        info = rows[:, pl.ds(width, LANES)]
        meta[...] = info
        across = info.astype(f32).T
        count = across.shape[1]
        ids, weights = across[:top], across[top : 2 * top]
        before = lax.broadcasted_iota(jnp.int32, (count, count), 0) < lax.broadcasted_iota(
            jnp.int32, (count, count), 1
        )
        chosen = [ids == (place[0] * experts + b).astype(f32) for b in range(experts)]
        member = [jnp.sum(jnp.where(hit, 1.0, 0.0), axis=0, keepdims=True) for hit in chosen]
        table = jnp.concatenate(member + [jnp.zeros((PACK - experts, count), f32)], axis=0)
        prior = dot(table.astype(bf16), before.astype(bf16))
        spot = lax.broadcasted_iota(jnp.int32, (cap, count), 0).astype(f32)
        for b in range(experts):
            rank = jnp.where(member[b] > 0.0, prior[b : b + 1], -1.0)
            hot = spot == rank
            gate = jnp.sum(jnp.where(chosen[b], weights, 0.0), axis=0, keepdims=True)
            one = jnp.where(hot, 1.0, 0.0)
            pick[0, pl.ds(b * cap, cap), :] = one.astype(bf16)
            at = pl.ds(pl.multiple_of(i * cap, PACK), cap)
            gates[b, at, :] = jnp.broadcast_to(jnp.sum(one * gate, axis=1, keepdims=True), (cap, LANES))
        got = dot(pick[0], rows[:, pl.ds(0, width)]).astype(bf16)
        for b in range(experts):
            held[b, pl.ds(pl.multiple_of(i * cap, PACK), cap), :] = got[b * cap : (b + 1) * cap]

    @pl.when(i >= groups)
    def _():
        b = i - groups
        pre = dot(held[b], w_up[0])
        gate = gates[b][:, :1]
        sig = 0.5 + 0.5 * jnp.tanh(0.5 * pre)
        act = pre * sig
        hid[0] = act.astype(bf16)
        scaled[0] = (gate * act).astype(bf16)
        slope_g[0] = (gate * (sig + act * (1.0 - sig))).astype(bf16)


def gather_rows(place, i, cap, pick, blocks, moved, held, sem):
    experts, groups = held.shape[0], moved.shape[0]
    own, mine, other = blocks[0], blocks[1:groups], blocks[groups:]

    @pl.when(i == 0)
    def _():
        start_blocks(place, groups, own, mine, other, moved, sem)

    half = own.shape[0] // 2
    for part in range(2):
        at = pl.ds(part * half, half)
        pltpu.make_async_copy(own.at[at, :], moved.at[i, at, :], sem.at[i, part]).wait()
    first = pl.multiple_of(lax.rem(place[3] - i + groups, groups) * cap, PACK)
    got = dot(pick[0], moved[i]).astype(bf16)
    for b in range(experts):
        held[b, pl.ds(first, cap), :] = got[b * cap : (b + 1) * cap]


def down_copies(orders, b, sent, outs, sem):
    parts = len(orders[0])
    half = parts // 2
    copies = []
    for q in range(parts):
        for g, order in enumerate(orders):
            p = order.index(q)
            copies.append(
                pltpu.make_async_copy(sent.at[g, q, b], outs[2 * g + p // half].at[p % half, b], sem.at[g, q, b])
            )
    return copies


def down_rows(orders, place, b, held, scaled, sent, outs, sem):
    parts = len(orders[0])
    piece = held.shape[1] // parts
    cut = piece // len(orders)
    for q in range(parts):
        at = pl.multiple_of((place[1] ^ q) * piece, LANES)
        full = dot(held[:, pl.ds(at, piece)], scaled, FIRST).astype(bf16)
        for g in range(len(orders)):
            sent[g, q, b] = full[g * cut : (g + 1) * cut]
    for copy in down_copies(orders, b, sent, outs, sem):
        copy.start()


def mid_kernel(groups, cap, orders, after, place, pick, *refs):
    blocks, refs = refs[: 2 * groups - 1], refs[2 * groups - 1 :]
    w_down, scaled, refs = refs[0], refs[1], refs[2 + after :]
    back, outs, (held, moved, block_sem, sent, sem) = refs[0], refs[1:-5], refs[-5:]
    experts = held.shape[0]
    i = pl.program_id(0)

    @pl.when(i < groups)
    def _():
        gather_rows(place, i, cap, pick, blocks, moved, held, block_sem)

    @pl.when(i >= groups)
    def _():
        b = i - groups
        down_rows(orders, place, b, held.at[b], scaled[0], sent, outs, sem)
        back[0] = dot(held[b], w_down[...].reshape(held.shape[2], back.shape[2]))

    @pl.when(i == groups + experts - 1)
    def _():
        for b in range(experts):
            for copy in down_copies(orders, b, sent, outs, sem):
                copy.wait()


def down_kernel(orders, after, place, rows, scaled, *refs):
    outs, (sent, sem) = refs[after:-2], refs[-2:]
    experts = sent.shape[2]
    b = pl.program_id(0)
    down_rows(orders, place, b, rows.at[0], scaled[0], sent, outs, sem)

    @pl.when(b == experts - 1)
    def _():
        for e in range(experts):
            for copy in down_copies(orders, e, sent, outs, sem):
                copy.wait()


def tail_kernel(groups, cap, width, top, has_before, place, pick, *refs):
    blocks, refs = refs[: 2 * groups - 1], refs[2 * groups - 1 :]
    w_down, w_up, hid, slope_g, meta = refs[:5]
    before = refs[5] if has_before else None
    out, kept, held, moved, block_sem, grads, sem = refs[5 + has_before :]
    experts = held.shape[0]
    i = pl.program_id(0)

    @pl.when(i < groups)
    def _():
        gather_rows(place, i, cap, pick, blocks, moved, held, block_sem)

    @pl.when((i >= groups) & (i < groups + experts))
    def _():
        b = i - groups
        pltpu.make_async_copy(held.at[b], kept.at[b], sem.at[b]).start()
        back = dot(held[b], w_down[...].reshape(held.shape[2], hid.shape[2]))
        if before is not None:
            back = back + before[0]
        gate = jnp.sum(back * hid[0].astype(f32), axis=1, keepdims=True)
        lane = lax.broadcasted_iota(jnp.int32, (back.shape[0], LANES), 1)
        gate = jnp.where(lane == b, gate, 0.0).astype(bf16)
        grad = (back * slope_g[0].astype(f32)).astype(bf16)
        route = dot(grad, w_up[0], LAST).astype(bf16)
        at = pl.ds(pl.multiple_of(b * cap, PACK), cap)
        for g in range(groups):
            grads[g, at, pl.ds(0, width)] = route[g * cap : (g + 1) * cap]
            grads[g, at, pl.ds(width, LANES)] = gate[g * cap : (g + 1) * cap]

    @pl.when(i >= groups + experts)
    def _():
        g = i - groups - experts
        total = dot(pick[0], grads[g], FIRST)
        out[:, pl.ds(0, width)] = total[:, :width].astype(bf16)
        by_expert = total[:, width:]
        info = meta[...].astype(f32)
        lane = lax.broadcasted_iota(jnp.int32, info.shape, 1)
        ids = jnp.where(lane < top, info, -1.0)
        picked = jnp.zeros(info.shape, f32)
        for b in range(experts):
            hit = ids == (place[0] * experts + b).astype(f32)
            picked = picked + jnp.where(hit, by_expert[:, b : b + 1], 0.0)
        out[:, pl.ds(width, LANES)] = picked.astype(bf16)

    @pl.when(i == 2 * groups + experts - 1)
    def _():
        for b in range(experts):
            pltpu.make_async_copy(held.at[b], kept.at[b], sem.at[b]).wait()


def cost(flops, nbytes):
    return pl.CostEstimate(flops=int(flops), bytes_accessed=int(nbytes), transcendentals=0)


def shards(tokens, cotangent, expert_ids, gate_weights, w_up, w_down):
    tok_rows, width = tokens.shape
    top = expert_ids.shape[1]
    ep_count, dp_count = lax.axis_size("ep"), lax.axis_size("dp")
    experts, _, hidden = w_up.shape
    base_load = tok_rows * top // (experts * ep_count)
    capacity = base_load + max(1, base_load // 16)
    total = ep_count * tok_rows
    groups = ep_count // GROUP
    members = GROUP * tok_rows
    cap = -(-GROUP * capacity // PACK) * PACK
    routes = groups * cap
    full = width + LANES
    here = lax.axis_index("ep")
    place = jnp.stack([here, lax.axis_index("dp"), here % GROUP, here // GROUP]).astype(jnp.int32)
    bits = dp_count.bit_length() - 1
    turns = 2
    share = width // dp_count
    slices = SLICES if share % (SLICES * LANES) == 0 else 1
    piece = share // slices
    cols = dp_count * piece

    def shape(*dims, dtype=bf16):
        return jax.ShapeDtypeStruct(dims, dtype)

    x_own, *dy_own = pl.pallas_call(
        functools.partial(pack_kernel, top, dp_count),
        out_shape=[shape(tok_rows, full)] + [shape(tok_rows, cols)] * slices,
        compiler_params=pltpu.CompilerParams(vmem_limit_bytes=VMEM_LIMIT),
        cost_estimate=cost(0, 8 * tok_rows * width),
        name="pack",
    )(tokens, cotangent, expert_ids.T, gate_weights.T)
    x_all = lax.all_gather(x_own, "ep", axis=0, tiled=True)

    def reach(p, step):
        q = p + GROUP * step if p % GROUP == 0 else p - GROUP * step
        return q if 0 <= q < ep_count else None

    def hop(value, pairs):
        return lax.ppermute(value, "ep", pairs)

    dy_own = [jnp.concatenate([part, hop(part, [(p, p ^ 1) for p in range(ep_count)])], axis=0) for part in dy_own]
    moving, dy_mine, dy_other = dy_own, [], []
    for step in range(1, groups):
        line = [(p, reach(p, 1)) for p in range(ep_count) if None not in (reach(p, 1), reach(p, 1 - step))]
        swap = [(p, p ^ 1) for p in range(ep_count) if reach(p, -step) is not None]
        moving = [hop(part, line) for part in moving]
        dy_mine.append(moving)
        dy_other.append([hop(part, swap) for part in moving])
    dy_blocks = [
        [dy_own[s]] + [part[s] for part in dy_mine] + [part[s] for part in dy_other] for s in range(slices)
    ]
    up_after = dy_mine[-2][-1:] if groups > 2 else []
    mid_after = dy_mine[-1][-1:]

    def at_group(i):
        return jnp.minimum(i, groups - 1)

    def at_expert(i):
        return jnp.clip(i - groups, 0, experts - 1)

    def at_slot(i, place):
        return lax.rem(place[3] - at_group(i) + groups, groups)

    def by_group(n):
        return pl.BlockSpec((members, n), lambda i, *_: (at_group(i), 0))

    def by_expert(rows, n):
        return pl.BlockSpec((1, rows, n), lambda i, *_: (at_expert(i), 0, 0))

    def call(kernel, name, grid, flops, nbytes, in_specs, out_specs, out_shape, scratch_shapes, prefetch=0):
        return pl.pallas_call(
            kernel,
            grid_spec=pltpu.PrefetchScalarGridSpec(
                num_scalar_prefetch=prefetch,
                grid=(grid,),
                in_specs=in_specs,
                out_specs=out_specs,
                scratch_shapes=scratch_shapes,
            ),
            out_shape=out_shape,
            compiler_params=pltpu.CompilerParams(vmem_limit_bytes=VMEM_LIMIT),
            cost_estimate=cost(flops, nbytes),
            name=name,
        )

    act = shape(experts, routes, hidden)
    act_spec = by_expert(routes, hidden)
    pick_spec = pl.BlockSpec((1, experts * cap, members), lambda i, *_: (at_group(i), 0, 0))
    pick_flops = 2 * total * experts * cap * width
    main_flops = 2 * experts * routes * width * hidden
    row_bytes = 2 * experts * hidden * width
    pick, meta, hid, scaled, slope_g = call(
        functools.partial(up_kernel, groups, width, top, cap, len(up_after)),
        "up",
        groups + experts,
        pick_flops + main_flops,
        2 * total * full + row_bytes,
        in_specs=[SMEM, by_group(full), by_expert(width, hidden)] + [ANY] * len(up_after),
        out_specs=[pick_spec, by_group(LANES), act_spec, act_spec, act_spec],
        out_shape=[shape(groups, experts * cap, members), shape(total, LANES), act, act, act],
        scratch_shapes=[pltpu.VMEM((experts, routes, width), bf16), pltpu.VMEM((experts, routes, LANES), f32)],
    )(place, x_all, w_up, *up_after)

    orders = []
    for g in range(turns):
        turn = [(g + t) % bits for t in range(bits)]
        orders.append(
            tuple(sum(((p >> (bits - 1 - t)) & 1) << turn[t] for t in range(bits)) for p in range(dp_count))
        )
    orders = tuple(orders)
    cut_rows = piece // turns
    down_outs = [shape(dp_count // 2, experts, cut_rows, hidden)] * (2 * turns)
    down_scratch = [
        pltpu.VMEM((turns, dp_count, experts, cut_rows, hidden), bf16),
        pltpu.SemaphoreType.DMA((turns, dp_count, experts)),
    ]
    w_cut = w_down.reshape(experts, dp_count, slices, piece, hidden)

    def cut_spec(s):
        return pl.BlockSpec((1, dp_count, 1, piece, hidden), lambda i, *_: (at_expert(i), 0, s, 0, 0))

    def exchange(state, t):
        new = []
        for g, (keep, send) in enumerate(state):
            bit = 1 << ((g + t) % bits)
            got = lax.ppermute(send, "dp", [(i, i ^ bit) for i in range(dp_count)])
            both = keep.astype(f32) + got.astype(f32)
            if t < bits - 1:
                both = both.astype(bf16)
            half = both.shape[0] // 2
            new.append((both[:half], both[half:]) if half else both[0])
        return new

    slot_spec = pl.BlockSpec((1, experts * cap, members), lambda i, place: (at_slot(i, place), 0, 0))
    block_scratch = [pltpu.VMEM((groups, members, cols), bf16), pltpu.SemaphoreType.DMA((groups, 2))]
    states, before = [], None
    for s in range(slices - 1):
        before, *outs = call(
            functools.partial(mid_kernel, groups, cap, orders, len(mid_after)),
            "mid",
            groups + experts,
            (pick_flops + 2 * main_flops) // slices,
            2 * total * cols + 2 * row_bytes // slices,
            prefetch=1,
            in_specs=[slot_spec] + [ANY] * (2 * groups - 1) + [cut_spec(s), act_spec] + [ANY] * len(mid_after),
            out_specs=[act_spec] + [ANY] * len(down_outs),
            out_shape=[shape(experts, routes, hidden, dtype=f32)] + down_outs,
            scratch_shapes=[pltpu.VMEM((experts, routes, cols), bf16)] + block_scratch + down_scratch,
        )(place, pick, *dy_blocks[s], w_cut, scaled, *mid_after)
        states.append([(outs[2 * g], outs[2 * g + 1]) for g in range(turns)])

    done, after = 0, []
    if states and bits > 1:
        states = [exchange(state, 0) for state in states]
        done, after = 1, [pair[0] for state in states for pair in state]

    def at_end(i):
        return jnp.clip(i - groups - experts, 0, groups - 1)

    last = slices - 1
    token_part, kept = call(
        functools.partial(tail_kernel, groups, cap, width, top, before is not None),
        "tail",
        2 * groups + experts,
        8 * main_flops,
        4 * row_bytes,
        prefetch=1,
        in_specs=[
            pl.BlockSpec(
                (1, experts * cap, members),
                lambda i, place: (jnp.where(i < groups, at_slot(i, place), at_end(i)), 0, 0),
            ),
        ]
        + [ANY] * (2 * groups - 1)
        + [
            cut_spec(last),
            by_expert(width, hidden),
            act_spec,
            act_spec,
            pl.BlockSpec((members, LANES), lambda i, *_: (at_end(i), 0)),
        ]
        + ([act_spec] if before is not None else []),
        out_specs=[pl.BlockSpec((members, full), lambda i, *_: (at_end(i), 0)), ANY],
        out_shape=[shape(total, full), shape(experts, routes, cols)],
        scratch_shapes=[
            pltpu.VMEM((experts, routes, cols), bf16),
            *block_scratch,
            pltpu.VMEM((groups, experts * cap, full), bf16),
            pltpu.SemaphoreType.DMA((experts,)),
        ],
    )(place, pick, *dy_blocks[last], w_cut, w_up, hid, slope_g, meta, *([] if before is None else [before]))
    summed = lax.psum_scatter(token_part, "ep", scatter_dimension=0, tiled=True)

    outs = call(
        functools.partial(down_kernel, orders, len(after)),
        "down",
        experts,
        16 * main_flops,
        8 * row_bytes,
        in_specs=[SMEM]
        + [pl.BlockSpec((1, routes, n), lambda b: (b, 0, 0)) for n in (cols, hidden)]
        + [ANY] * len(after),
        out_specs=[ANY] * len(down_outs),
        out_shape=down_outs,
        scratch_shapes=down_scratch,
    )(place, kept, scaled, *after)
    states = [(done, state) for state in states]
    states.append((0, [(outs[2 * g], outs[2 * g + 1]) for g in range(turns)]))
    for t in range(bits):
        states = [(done, state) if t < done else (done, exchange(state, t)) for done, state in states]
    states = [state for _, state in states]
    down_grad = jnp.concatenate([part for state in states for part in state], axis=1)
    return (summed[:, :width], summed[:, width : width + top], down_grad)


def solution(mesh):
    return jax.shard_map(
        shards,
        mesh=mesh,
        in_specs=(
            P(("dp", "ep"), None),
            P(("dp", "ep"), None),
            P(("dp", "ep"), None),
            P(("dp", "ep"), None),
            P("ep", None, None),
            P("ep", None, None),
        ),
        out_specs=(P(("dp", "ep"), None), P(("dp", "ep"), None), P("ep", "dp", None)),
        check_vma=False,
    )
```

```python
import functools

import jax
import jax.numpy as jnp
from jax import lax
from jax.experimental import pallas as pl
from jax.experimental.pallas import tpu as pltpu
from jax.sharding import PartitionSpec as P

LANES = 128
PACK = 16
SLICES = 2
GROUP = 2
VMEM_LIMIT = 60 * 1024 * 1024
bf16, f32 = jnp.bfloat16, jnp.float32
ANY = pl.BlockSpec(memory_space=pl.ANY)
SMEM = pl.BlockSpec(memory_space=pltpu.SMEM)
FIRST = (((0,), (0,)), ((), ()))
LAST = (((1,), (1,)), ((), ()))


def dot(a, b, dims=(((1,), (0,)), ((), ()))):
    return lax.dot_general(a, b, dims, preferred_element_type=f32)


def pack_kernel(top, tokens, ids, gates, x_out):
    count, width = tokens.shape
    x_out[:, pl.ds(0, width)] = tokens[...]
    info = jnp.concatenate(
        [ids[...].astype(f32), gates[...].astype(f32), jnp.zeros((LANES - 2 * top, count), f32)], axis=0
    )
    x_out[:, pl.ds(width, LANES)] = info.T.astype(bf16)


def flip_kernel(w, out):
    out[0] = w[0].T


def start_blocks(place, chips, own, mine, other, dst, sem):
    half = own.shape[0] // 2
    left_core = place[2] == 0

    def start(ref, slot, flip):
        for part in range(2):
            to = (part ^ flip) * half
            if not isinstance(flip, int):
                to = pl.multiple_of(to, half)
            pltpu.make_async_copy(
                ref.at[pl.ds(part * half, half), :], dst.at[slot, pl.ds(to, half), :], sem.at[slot, part]
            ).start()

    start(own, 0, place[2])
    for slot in range(1, chips):
        left = place[3] >= slot
        for is_left in (True, False):
            for is_core in (True, False):
                step = slot if is_left else chips - slot
                ref = (mine if is_left == is_core else other)[step - 1]

                @pl.when((left == is_left) & (left_core == is_core))
                def _():
                    start(ref, slot, 0 if is_left else 1)


def up_kernel(groups, width, top, cap, after, place, rows, w_up, *refs):
    pick, meta, hid, scaled, slope_g, held, gates = refs[after:]
    experts = held.shape[0]
    i = pl.program_id(0)

    @pl.when(i < groups)
    def _():
        info = rows[:, pl.ds(width, LANES)]
        meta[...] = info
        across = info.astype(f32).T
        count = across.shape[1]
        ids, weights = across[:top], across[top : 2 * top]
        before = lax.broadcasted_iota(jnp.int32, (count, count), 0) < lax.broadcasted_iota(
            jnp.int32, (count, count), 1
        )
        chosen = [ids == (place[0] * experts + b).astype(f32) for b in range(experts)]
        member = [jnp.sum(jnp.where(hit, 1.0, 0.0), axis=0, keepdims=True) for hit in chosen]
        table = jnp.concatenate(member + [jnp.zeros((PACK - experts, count), f32)], axis=0)
        prior = dot(table.astype(bf16), before.astype(bf16))
        spot = lax.broadcasted_iota(jnp.int32, (cap, count), 0).astype(f32)
        for b in range(experts):
            rank = jnp.where(member[b] > 0.0, prior[b : b + 1], -1.0)
            hot = spot == rank
            gate = jnp.sum(jnp.where(chosen[b], weights, 0.0), axis=0, keepdims=True)
            one = jnp.where(hot, 1.0, 0.0)
            pick[0, pl.ds(b * cap, cap), :] = one.astype(bf16)
            at = pl.ds(pl.multiple_of(i * cap, PACK), cap)
            gates[b, at, :] = jnp.broadcast_to(jnp.sum(one * gate, axis=1, keepdims=True), (cap, LANES))
        got = dot(pick[0], rows[:, pl.ds(0, width)]).astype(bf16)
        for b in range(experts):
            held[b, pl.ds(pl.multiple_of(i * cap, PACK), cap), :] = got[b * cap : (b + 1) * cap]

    @pl.when(i >= groups)
    def _():
        b = i - groups
        pre = dot(held[b], w_up[0])
        gate = gates[b][:, :1]
        sig = 0.5 + 0.5 * jnp.tanh(0.5 * pre)
        act = pre * sig
        hid[0] = act.astype(bf16)
        scaled[0] = (gate * act).astype(bf16)
        slope_g[0] = (gate * (sig + act * (1.0 - sig))).astype(bf16)


def gather_rows(place, i, cap, pick, blocks, moved, held, sem):
    experts, groups = held.shape[0], moved.shape[0]
    own, mine, other = blocks[0], blocks[1:groups], blocks[groups:]

    @pl.when(i == 0)
    def _():
        start_blocks(place, groups, own, mine, other, moved, sem)

    half = own.shape[0] // 2
    for part in range(2):
        at = pl.ds(part * half, half)
        pltpu.make_async_copy(own.at[at, :], moved.at[i, at, :], sem.at[i, part]).wait()
    first = pl.multiple_of(lax.rem(place[3] - i + groups, groups) * cap, PACK)
    got = dot(pick[0], moved[i]).astype(bf16)
    for b in range(experts):
        held[b, pl.ds(first, cap), :] = got[b * cap : (b + 1) * cap]


def down_copies(orders, b, sent, outs, sem):
    parts = len(orders[0])
    half = parts // 2
    copies = []
    for q in range(parts):
        for g, order in enumerate(orders):
            p = order.index(q)
            copies.append(
                pltpu.make_async_copy(sent.at[g, q, b], outs[2 * g + p // half].at[p % half, b], sem.at[g, q, b])
            )
    return copies


def down_rows(orders, place, b, s, slices, held, scaled, sent, outs, sem):
    parts = len(orders[0])
    share = held.shape[1] // parts
    piece = share // slices
    cut = piece // len(orders)
    for q in range(parts):
        at = pl.multiple_of((place[1] ^ q) * share + s * piece, LANES)
        full = dot(held[:, pl.ds(at, piece)], scaled, FIRST).astype(bf16)
        for g in range(len(orders)):
            sent[g, q, b] = full[g * cut : (g + 1) * cut]
    for copy in down_copies(orders, b, sent, outs, sem):
        copy.start()


def down_kernel(orders, s, slices, after, place, rows, scaled, *refs):
    outs, (sent, sem) = refs[after:-2], refs[-2:]
    experts = sent.shape[2]
    b = pl.program_id(0)
    down_rows(orders, place, b, s, slices, rows.at[0], scaled[0], sent, outs, sem)

    @pl.when(b == experts - 1)
    def _():
        for e in range(experts):
            for copy in down_copies(orders, e, sent, outs, sem):
                copy.wait()


def tail_kernel(groups, cap, width, top, place, pick, *refs):
    blocks, refs = refs[: 2 * groups - 1], refs[2 * groups - 1 :]
    w_down, w_flip, hid, slope_g, meta, out, kept, held, moved, block_sem, grads, sem = refs
    experts = held.shape[0]
    i = pl.program_id(0)

    @pl.when(i < groups)
    def _():
        gather_rows(place, i, cap, pick, blocks, moved, held, block_sem)

    @pl.when((i >= groups) & (i < groups + experts))
    def _():
        b = i - groups
        pltpu.make_async_copy(held.at[b], kept.at[b], sem.at[b]).start()
        back = dot(held[b], w_down[0])
        gate = jnp.sum(back * hid[0].astype(f32), axis=1, keepdims=True)
        lane = lax.broadcasted_iota(jnp.int32, (back.shape[0], LANES), 1)
        gate = jnp.where(lane == b, gate, 0.0).astype(bf16)
        grad = (back * slope_g[0].astype(f32)).astype(bf16)
        route = dot(grad, w_flip[0]).astype(bf16)
        at = pl.ds(pl.multiple_of(b * cap, PACK), cap)
        for g in range(groups):
            grads[g, at, pl.ds(0, width)] = route[g * cap : (g + 1) * cap]
            grads[g, at, pl.ds(width, LANES)] = gate[g * cap : (g + 1) * cap]

    @pl.when(i >= groups + experts)
    def _():
        g = i - groups - experts
        total = dot(pick[0], grads[g], FIRST)
        out[:, pl.ds(0, width)] = total[:, :width].astype(bf16)
        by_expert = total[:, width:]
        info = meta[...].astype(f32)
        lane = lax.broadcasted_iota(jnp.int32, info.shape, 1)
        ids = jnp.where(lane < top, info, -1.0)
        picked = jnp.zeros(info.shape, f32)
        for b in range(experts):
            hit = ids == (place[0] * experts + b).astype(f32)
            picked = picked + jnp.where(hit, by_expert[:, b : b + 1], 0.0)
        out[:, pl.ds(width, LANES)] = picked.astype(bf16)

    @pl.when(i == 2 * groups + experts - 1)
    def _():
        for b in range(experts):
            pltpu.make_async_copy(held.at[b], kept.at[b], sem.at[b]).wait()


def cost(flops, nbytes):
    return pl.CostEstimate(flops=int(flops), bytes_accessed=int(nbytes), transcendentals=0)


def shards(tokens, cotangent, expert_ids, gate_weights, w_up, w_down):
    tok_rows, width = tokens.shape
    top = expert_ids.shape[1]
    ep_count, dp_count = lax.axis_size("ep"), lax.axis_size("dp")
    experts, _, hidden = w_up.shape
    base_load = tok_rows * top // (experts * ep_count)
    capacity = base_load + max(1, base_load // 16)
    total = ep_count * tok_rows
    groups = ep_count // GROUP
    members = GROUP * tok_rows
    cap = -(-GROUP * capacity // PACK) * PACK
    routes = groups * cap
    full = width + LANES
    here = lax.axis_index("ep")
    place = jnp.stack([here, lax.axis_index("dp"), here % GROUP, here // GROUP]).astype(jnp.int32)
    bits = dp_count.bit_length() - 1
    turns = 2
    share = width // dp_count
    slices = SLICES if share % (SLICES * LANES) == 0 else 1
    piece = share // slices

    def shape(*dims, dtype=bf16):
        return jax.ShapeDtypeStruct(dims, dtype)

    x_own = pl.pallas_call(
        functools.partial(pack_kernel, top),
        out_shape=shape(tok_rows, full),
        compiler_params=pltpu.CompilerParams(vmem_limit_bytes=VMEM_LIMIT),
        cost_estimate=cost(0, 4 * tok_rows * width),
        name="pack",
    )(tokens, expert_ids.T, gate_weights.T)
    x_all = lax.all_gather(x_own, "ep", axis=0, tiled=True)

    def reach(p, step):
        q = p + GROUP * step if p % GROUP == 0 else p - GROUP * step
        return q if 0 <= q < ep_count else None

    def hop(value, pairs):
        return lax.ppermute(value, "ep", pairs)

    def at_group(i):
        return jnp.minimum(i, groups - 1)

    def at_expert(i):
        return jnp.clip(i - groups, 0, experts - 1)

    def at_slot(i, place):
        return lax.rem(place[3] - at_group(i) + groups, groups)

    def by_group(n):
        return pl.BlockSpec((members, n), lambda i, *_: (at_group(i), 0))

    def by_expert(rows, n):
        return pl.BlockSpec((1, rows, n), lambda i, *_: (at_expert(i), 0, 0))

    def call(kernel, name, grid, flops, nbytes, in_specs, out_specs, out_shape, scratch_shapes, prefetch=0):
        return pl.pallas_call(
            kernel,
            grid_spec=pltpu.PrefetchScalarGridSpec(
                num_scalar_prefetch=prefetch,
                grid=(grid,),
                in_specs=in_specs,
                out_specs=out_specs,
                scratch_shapes=scratch_shapes,
            ),
            out_shape=out_shape,
            compiler_params=pltpu.CompilerParams(vmem_limit_bytes=VMEM_LIMIT),
            cost_estimate=cost(flops, nbytes),
            name=name,
        )

    row_bytes = 2 * experts * hidden * width
    w_flip = call(
        flip_kernel,
        "flip",
        experts,
        0,
        2 * row_bytes,
        in_specs=[pl.BlockSpec((1, width, hidden), lambda b: (b, 0, 0))],
        out_specs=pl.BlockSpec((1, hidden, width), lambda b: (b, 0, 0)),
        out_shape=shape(experts, hidden, width),
        scratch_shapes=[],
    )(w_up)
    dy_own = jnp.concatenate([cotangent, hop(cotangent, [(p, p ^ 1) for p in range(ep_count)])], axis=0)
    moving, dy_mine, dy_other = dy_own, [], []
    for step in range(1, groups):
        line = [(p, reach(p, 1)) for p in range(ep_count) if None not in (reach(p, 1), reach(p, 1 - step))]
        swap = [(p, p ^ 1) for p in range(ep_count) if reach(p, -step) is not None]
        moving = hop(moving, line)
        dy_mine.append(moving)
        dy_other.append(swap)
        if step == 1:
            moving, w_flip = lax.optimization_barrier((moving, w_flip))
    dy_other = [hop(part, swap) for part, swap in zip(dy_mine[:-1], dy_other[:-1])] + dy_other[-1:]

    act = shape(experts, routes, hidden)
    act_spec = by_expert(routes, hidden)
    pick_spec = pl.BlockSpec((1, experts * cap, members), lambda i, *_: (at_group(i), 0, 0))
    pick_flops = 2 * total * experts * cap * width
    main_flops = 2 * experts * routes * width * hidden
    up_after = dy_mine[-2:-1]
    pick, meta, hid, scaled, slope_g = call(
        functools.partial(up_kernel, groups, width, top, cap, len(up_after)),
        "up",
        groups + experts,
        pick_flops + main_flops,
        2 * total * full + row_bytes,
        in_specs=[SMEM, by_group(full), by_expert(width, hidden)] + [ANY] * len(up_after),
        out_specs=[pick_spec, by_group(LANES), act_spec, act_spec, act_spec],
        out_shape=[shape(groups, experts * cap, members), shape(total, LANES), act, act, act],
        scratch_shapes=[pltpu.VMEM((experts, routes, width), bf16), pltpu.VMEM((experts, routes, LANES), f32)],
    )(place, x_all, w_up, *up_after)

    last_block, hid = lax.optimization_barrier((dy_mine[-1], hid))
    dy_other[-1] = hop(last_block, dy_other[-1])

    orders = []
    for g in range(turns):
        turn = [(g + t) % bits for t in range(bits)]
        orders.append(
            tuple(sum(((p >> (bits - 1 - t)) & 1) << turn[t] for t in range(bits)) for p in range(dp_count))
        )
    orders = tuple(orders)
    cut_rows = piece // turns
    down_outs = [shape(dp_count // 2, experts, cut_rows, hidden)] * (2 * turns)
    down_scratch = [
        pltpu.VMEM((turns, dp_count, experts, cut_rows, hidden), bf16),
        pltpu.SemaphoreType.DMA((turns, dp_count, experts)),
    ]
    def exchange(state, t):
        new = []
        for g, (keep, send) in enumerate(state):
            bit = 1 << ((g + t) % bits)
            got = lax.ppermute(send, "dp", [(i, i ^ bit) for i in range(dp_count)])
            both = keep.astype(f32) + got.astype(f32)
            if t < bits - 1:
                both = both.astype(bf16)
            half = both.shape[0] // 2
            new.append((both[:half], both[half:]) if half else both[0])
        return new

    def at_end(i):
        return jnp.clip(i - groups - experts, 0, groups - 1)

    token_part, kept = call(
        functools.partial(tail_kernel, groups, cap, width, top),
        "tail",
        2 * groups + experts,
        8 * main_flops,
        4 * row_bytes,
        prefetch=1,
        in_specs=[
            pl.BlockSpec(
                (1, experts * cap, members),
                lambda i, place: (jnp.where(i < groups, at_slot(i, place), at_end(i)), 0, 0),
            ),
        ]
        + [ANY] * (2 * groups - 1)
        + [
            by_expert(width, hidden),
            by_expert(hidden, width),
            act_spec,
            act_spec,
            pl.BlockSpec((members, LANES), lambda i, *_: (at_end(i), 0)),
        ],
        out_specs=[pl.BlockSpec((members, full), lambda i, *_: (at_end(i), 0)), ANY],
        out_shape=[shape(total, full), shape(experts, routes, width)],
        scratch_shapes=[
            pltpu.VMEM((experts, routes, width), bf16),
            pltpu.VMEM((groups, members, width), bf16),
            pltpu.SemaphoreType.DMA((groups, 2)),
            pltpu.VMEM((groups, experts * cap, full), bf16),
            pltpu.SemaphoreType.DMA((experts,)),
        ],
    )(place, pick, dy_own, *dy_mine, *dy_other, w_down, w_flip, hid, slope_g, meta)
    summed = lax.psum_scatter(token_part, "ep", scatter_dimension=0, tiled=True)

    states = []
    for s in range(slices):
        outs = call(
            functools.partial(down_kernel, orders, s, slices, 0),
            "down",
            experts,
            16 * main_flops,
            8 * row_bytes,
            in_specs=[SMEM] + [pl.BlockSpec((1, routes, n), lambda b: (b, 0, 0)) for n in (width, hidden)],
            out_specs=[ANY] * len(down_outs),
            out_shape=down_outs,
            scratch_shapes=down_scratch,
        )(place, kept, scaled)
        states.append([(outs[2 * g], outs[2 * g + 1]) for g in range(turns)])
    for t in range(bits):
        states = [exchange(state, t) for state in states]
    down_grad = jnp.concatenate([part for state in states for part in state], axis=1)
    return (summed[:, :width], summed[:, width : width + top], down_grad)


def solution(mesh):
    return jax.shard_map(
        shards,
        mesh=mesh,
        in_specs=(
            P(("dp", "ep"), None),
            P(("dp", "ep"), None),
            P(("dp", "ep"), None),
            P(("dp", "ep"), None),
            P("ep", None, None),
            P("ep", None, None),
        ),
        out_specs=(P(("dp", "ep"), None), P(("dp", "ep"), None), P("ep", "dp", None)),
        check_vma=False,
    )
```

```python
import functools

import jax
import jax.numpy as jnp
from jax import lax
from jax.experimental import pallas as pl
from jax.experimental.pallas import tpu as pltpu
from jax.sharding import PartitionSpec as P

LANES = 128
PACK = 16
GROUP = 2
VMEM_LIMIT = 60 * 1024 * 1024
bf16, f32 = jnp.bfloat16, jnp.float32
ANY = pl.BlockSpec(memory_space=pl.ANY)
SMEM = pl.BlockSpec(memory_space=pltpu.SMEM)
FIRST = (((0,), (0,)), ((), ()))


def dot(a, b, dims=(((1,), (0,)), ((), ()))):
    return lax.dot_general(a, b, dims, preferred_element_type=f32)


def pack_kernel(top, tokens, ids, gates, x_out):
    count, width = tokens.shape
    x_out[:, pl.ds(0, width)] = tokens[...]
    info = jnp.concatenate(
        [ids[...].astype(f32), gates[...].astype(f32), jnp.zeros((LANES - 2 * top, count), f32)], axis=0
    )
    x_out[:, pl.ds(width, LANES)] = info.T.astype(bf16)


def flip_kernel(w, out):
    out[0] = w[0].T


def block_copies(place, ref, dst, sem, flip):
    half = ref.shape[0] // 2
    copies = []
    for part in range(2):
        to = (part ^ flip) * half
        if not isinstance(flip, int):
            to = pl.multiple_of(to, half)
        copies.append(
            pltpu.make_async_copy(ref.at[pl.ds(part * half, half), :], dst.at[pl.ds(to, half), :], sem.at[part])
        )
    return copies


def by_side(place, is_left, mine, other, act):
    for left in (True, False):
        for core in (True, False):
            ref = (mine if left == core else other)(left)
            if ref is not None:

                @pl.when((is_left == left) & ((place[2] == 0) == core))
                def _():
                    act(ref, 0 if left else 1)


def start_blocks(place, chips, own, mine, other, dst, sem):
    for copy in block_copies(place, own, dst.at[0], sem.at[0], place[2]):
        copy.start()
    for slot in range(1, chips):

        def pick(blocks, left):
            step = slot if left else chips - slot
            return blocks[step - 1] if step <= len(blocks) else None

        def start(ref, flip):
            for copy in block_copies(place, ref, dst.at[slot], sem.at[slot], flip):
                copy.start()

        by_side(place, place[3] >= slot, functools.partial(pick, mine), functools.partial(pick, other), start)


def up_kernel(groups, width, top, cap, after, place, rows, w_up, *refs):
    pick, meta, hid, scaled, slope_g, held, gates = refs[after:]
    experts = held.shape[0]
    i = pl.program_id(0)

    @pl.when(i < groups)
    def _():
        info = rows[:, pl.ds(width, LANES)]
        meta[...] = info
        across = info.astype(f32).T
        count = across.shape[1]
        ids, weights = across[:top], across[top : 2 * top]
        before = lax.broadcasted_iota(jnp.int32, (count, count), 0) < lax.broadcasted_iota(
            jnp.int32, (count, count), 1
        )
        chosen = [ids == (place[0] * experts + b).astype(f32) for b in range(experts)]
        member = [jnp.sum(jnp.where(hit, 1.0, 0.0), axis=0, keepdims=True) for hit in chosen]
        table = jnp.concatenate(member + [jnp.zeros((PACK - experts, count), f32)], axis=0)
        prior = dot(table.astype(bf16), before.astype(bf16))
        spot = lax.broadcasted_iota(jnp.int32, (cap, count), 0).astype(f32)
        for b in range(experts):
            rank = jnp.where(member[b] > 0.0, prior[b : b + 1], -1.0)
            hot = spot == rank
            gate = jnp.sum(jnp.where(chosen[b], weights, 0.0), axis=0, keepdims=True)
            one = jnp.where(hot, 1.0, 0.0)
            pick[0, pl.ds(b * cap, cap), :] = one.astype(bf16)
            at = pl.ds(pl.multiple_of(i * cap, PACK), cap)
            gates[b, at, :] = jnp.broadcast_to(jnp.sum(one * gate, axis=1, keepdims=True), (cap, LANES))
        got = dot(pick[0], rows[:, pl.ds(0, width)]).astype(bf16)
        for b in range(experts):
            held[b, pl.ds(pl.multiple_of(i * cap, PACK), cap), :] = got[b * cap : (b + 1) * cap]

    @pl.when(i >= groups)
    def _():
        b = i - groups
        pre = dot(held[b], w_up[0])
        gate = gates[b][:, :1]
        sig = 0.5 + 0.5 * jnp.tanh(0.5 * pre)
        act = pre * sig
        hid[0] = act.astype(bf16)
        scaled[0] = (gate * act).astype(bf16)
        slope_g[0] = (gate * (sig + act * (1.0 - sig))).astype(bf16)


def early_kernel(groups, cap, place, pick, *refs):
    steps = groups - 2
    own, mine, other, refs = refs[0], refs[1 : 1 + steps], refs[1 + steps : 1 + 2 * steps], refs[1 + 2 * steps :]
    w_down, back, kept, held, moved, block_sem, sem = refs
    experts = held.shape[0]
    i = pl.program_id(0)

    @pl.when(i == 0)
    def _():
        start_blocks(place, groups, own, mine, other, moved, block_sem)

    here = (i == 0) | (jnp.where(place[3] >= i, i, groups - i) <= steps)
    first = pl.multiple_of(lax.rem(place[3] - i + 2 * groups, groups) * cap, PACK)

    @pl.when((i < groups) & here)
    def _():
        half = own.shape[0] // 2
        for part in range(2):
            at = pl.ds(part * half, half)
            pltpu.make_async_copy(own.at[at, :], moved.at[i, at, :], block_sem.at[i, part]).wait()
        got = dot(pick[0], moved[i]).astype(bf16)
        for b in range(experts):
            held[b, pl.ds(first, cap), :] = got[b * cap : (b + 1) * cap]

    @pl.when((i < groups) & jnp.logical_not(here))
    def _():
        for b in range(experts):
            held[b, pl.ds(first, cap), :] = jnp.zeros((cap, held.shape[2]), bf16)

    @pl.when(i >= groups)
    def _():
        b = i - groups
        pltpu.make_async_copy(held.at[b], kept.at[b], sem.at[b]).start()
        back[0] = dot(held[b], w_down[0])

    @pl.when(i == groups + experts - 1)
    def _():
        for b in range(experts):
            pltpu.make_async_copy(held.at[b], kept.at[b], sem.at[b]).wait()


def last_group(place, groups):
    chip = place[3]
    return (chip == 0) | (chip == groups - 1), jnp.where(chip == 0, groups - 1, 0)


def fill_kernel(groups, cap, place, pick, mine, other, early, kept, late, rows, table, sem, table_sem, out_sem):
    del early
    experts = late.shape[0]
    has, group = last_group(place, groups)

    @pl.when(has)
    def _():
        fetch = pltpu.make_async_copy(pick.at[group], table, table_sem)
        fetch.start()

        def start(ref, flip):
            for copy in block_copies(place, ref, rows, sem, flip):
                copy.start()

        by_side(place, place[3] != 0, lambda left: mine, lambda left: other, start)
        fetch.wait()
        for copy in block_copies(place, mine, rows, sem, 0):
            copy.wait()
        got = dot(table[...], rows[...]).astype(bf16)
        for b in range(experts):
            late[b] = got[b * cap : (b + 1) * cap]
        at = pl.ds(pl.multiple_of(group * cap, PACK), cap)
        copies = [pltpu.make_async_copy(late.at[b], kept.at[b, at, :], out_sem.at[b]) for b in range(experts)]
        for copy in copies:
            copy.start()
        for copy in copies:
            copy.wait()

    @pl.when(jnp.logical_not(has))
    def _():
        late[...] = jnp.zeros(late.shape, bf16)


def down_copies(orders, b, sent, outs, sem):
    parts = len(orders[0])
    half = parts // 2
    copies = []
    for q in range(parts):
        for g, order in enumerate(orders):
            p = order.index(q)
            copies.append(
                pltpu.make_async_copy(sent.at[g, q, b], outs[2 * g + p // half].at[p % half, b], sem.at[g, q, b])
            )
    return copies


def down_kernel(orders, after, place, rows, scaled, *refs):
    outs, (sent, sem) = refs[after:-2], refs[-2:]
    experts = sent.shape[2]
    b = pl.program_id(0)
    parts = len(orders[0])
    share = rows.shape[2] // parts
    cut = share // len(orders)
    for q in reversed(range(parts)):
        at = pl.multiple_of((place[1] ^ q) * share, LANES)
        full = dot(rows[0, :, pl.ds(at, share)], scaled[0], FIRST).astype(bf16)
        for g in range(len(orders)):
            sent[g, q, b] = full[g * cut : (g + 1) * cut]
    for copy in down_copies(orders, b, sent, outs, sem):
        copy.start()

    @pl.when(b == experts - 1)
    def _():
        for e in range(experts):
            for copy in down_copies(orders, e, sent, outs, sem):
                copy.wait()


def tail_kernel(groups, cap, width, top, after, place, pick, late, early, w_down, w_flip, hid, slope_g, meta, *refs):
    out, total, grads = refs[after:]
    experts = grads.shape[1] // cap
    i = pl.program_id(0)

    @pl.when(i < experts)
    def _():
        has, group = last_group(place, groups)
        total[...] = early[0]

        @pl.when(has)
        def _():
            at = pl.ds(pl.multiple_of(group * cap, PACK), cap)
            total[at, :] = dot(late[0], w_down[0])

        back = total[...]
        gate = jnp.sum(back * hid[0].astype(f32), axis=1, keepdims=True)
        lane = lax.broadcasted_iota(jnp.int32, (back.shape[0], LANES), 1)
        gate = jnp.where(lane == i, gate, 0.0).astype(bf16)
        grad = (back * slope_g[0].astype(f32)).astype(bf16)
        route = dot(grad, w_flip[0]).astype(bf16)
        at = pl.ds(pl.multiple_of(i * cap, PACK), cap)
        for g in range(groups):
            grads[g, at, pl.ds(0, width)] = route[g * cap : (g + 1) * cap]
            grads[g, at, pl.ds(width, LANES)] = gate[g * cap : (g + 1) * cap]

    @pl.when(i >= experts)
    def _():
        g = i - experts
        summed = dot(pick[0], grads[g], FIRST)
        out[:, pl.ds(0, width)] = summed[:, :width].astype(bf16)
        by_expert = summed[:, width:]
        info = meta[...].astype(f32)
        lane = lax.broadcasted_iota(jnp.int32, info.shape, 1)
        ids = jnp.where(lane < top, info, -1.0)
        picked = jnp.zeros(info.shape, f32)
        for b in range(experts):
            hit = ids == (place[0] * experts + b).astype(f32)
            picked = picked + jnp.where(hit, by_expert[:, b : b + 1], 0.0)
        out[:, pl.ds(width, LANES)] = picked.astype(bf16)


def finish_kernel(width, top, rows, token, gate):
    token[...] = rows[:, pl.ds(0, width)]
    gate[...] = rows[:, pl.ds(width, LANES)].astype(f32).T[:top].astype(bf16)


def cost(flops, nbytes):
    return pl.CostEstimate(flops=int(flops), bytes_accessed=int(nbytes), transcendentals=0)


def shards(tokens, cotangent, expert_ids, gate_weights, w_up, w_down):
    tok_rows, width = tokens.shape
    top = expert_ids.shape[1]
    ep_count, dp_count = lax.axis_size("ep"), lax.axis_size("dp")
    experts, _, hidden = w_up.shape
    base_load = tok_rows * top // (experts * ep_count)
    capacity = base_load + max(1, base_load // 16)
    total = ep_count * tok_rows
    groups = ep_count // GROUP
    members = GROUP * tok_rows
    cap = -(-GROUP * capacity // PACK) * PACK
    routes = groups * cap
    full = width + LANES
    here = lax.axis_index("ep")
    place = jnp.stack([here, lax.axis_index("dp"), here % GROUP, here // GROUP]).astype(jnp.int32)
    bits = dp_count.bit_length() - 1
    turns = 2
    share = width // dp_count

    def shape(*dims, dtype=bf16):
        return jax.ShapeDtypeStruct(dims, dtype)

    x_own = pl.pallas_call(
        functools.partial(pack_kernel, top),
        out_shape=shape(tok_rows, full),
        compiler_params=pltpu.CompilerParams(vmem_limit_bytes=VMEM_LIMIT),
        cost_estimate=cost(0, 4 * tok_rows * width),
        name="pack",
    )(tokens, expert_ids.T, gate_weights.T)
    x_all = lax.all_gather(x_own, "ep", axis=0, tiled=True)

    def reach(p, step):
        q = p + GROUP * step if p % GROUP == 0 else p - GROUP * step
        return q if 0 <= q < ep_count else None

    def hop(value, pairs):
        return lax.ppermute(value, "ep", pairs)

    def at_group(i):
        return jnp.minimum(i, groups - 1)

    def at_expert(i):
        return jnp.clip(i - groups, 0, experts - 1)

    def at_slot(i, place):
        return lax.rem(place[3] - at_group(i) + groups, groups)

    def by_group(n):
        return pl.BlockSpec((members, n), lambda i, *_: (at_group(i), 0))

    def by_expert(rows, n):
        return pl.BlockSpec((1, rows, n), lambda i, *_: (at_expert(i), 0, 0))

    def call(kernel, name, grid, flops, nbytes, in_specs, out_specs, out_shape, scratch_shapes, prefetch=0):
        return pl.pallas_call(
            kernel,
            grid_spec=pltpu.PrefetchScalarGridSpec(
                num_scalar_prefetch=prefetch,
                grid=(grid,),
                in_specs=in_specs,
                out_specs=out_specs,
                scratch_shapes=scratch_shapes,
            ),
            out_shape=out_shape,
            compiler_params=pltpu.CompilerParams(vmem_limit_bytes=VMEM_LIMIT),
            cost_estimate=cost(flops, nbytes),
            name=name,
        )

    row_bytes = 2 * experts * hidden * width
    w_flip = call(
        flip_kernel,
        "flip",
        experts,
        0,
        2 * row_bytes,
        in_specs=[pl.BlockSpec((1, width, hidden), lambda b: (b, 0, 0))],
        out_specs=pl.BlockSpec((1, hidden, width), lambda b: (b, 0, 0)),
        out_shape=shape(experts, hidden, width),
        scratch_shapes=[],
    )(w_up)
    dy_own = jnp.concatenate([cotangent, hop(cotangent, [(p, p ^ 1) for p in range(ep_count)])], axis=0)
    moving, dy_mine, dy_other = dy_own, [], []
    lines = [None] + [
        [(p, reach(p, 1)) for p in range(ep_count) if None not in (reach(p, 1), reach(p, 1 - step))]
        for step in range(1, groups)
    ]
    swaps = [None] + [
        [(p, p ^ 1) for p in range(ep_count) if reach(p, -step) is not None] for step in range(1, groups)
    ]
    for step in range(1, groups - 1):
        moving = hop(moving, lines[step])
        if step == 1:
            moving, w_flip = lax.optimization_barrier((moving, w_flip))
        dy_mine.append(moving)
        dy_other.append(hop(moving, swaps[step]))

    act = shape(experts, routes, hidden)
    act_spec = by_expert(routes, hidden)
    pick_spec = pl.BlockSpec((1, experts * cap, members), lambda i, *_: (at_group(i), 0, 0))
    pick_flops = 2 * total * experts * cap * width
    main_flops = 2 * experts * routes * width * hidden
    up_after = dy_other[:1]
    pick, meta, hid, scaled, slope_g = call(
        functools.partial(up_kernel, groups, width, top, cap, len(up_after)),
        "up",
        groups + experts,
        pick_flops + main_flops,
        2 * total * full + row_bytes,
        in_specs=[SMEM, by_group(full), by_expert(width, hidden)] + [ANY] * len(up_after),
        out_specs=[pick_spec, by_group(LANES), act_spec, act_spec, act_spec],
        out_shape=[shape(groups, experts * cap, members), shape(total, LANES), act, act, act],
        scratch_shapes=[pltpu.VMEM((experts, routes, width), bf16), pltpu.VMEM((experts, routes, LANES), f32)],
    )(place, x_all, w_up, *up_after)

    moving, hid = lax.optimization_barrier((moving, hid))
    moving = hop(moving, lines[-1])
    slot_spec = pl.BlockSpec((1, experts * cap, members), lambda i, place: (at_slot(i, place), 0, 0))
    back, kept = call(
        functools.partial(early_kernel, groups, cap),
        "early",
        groups + experts,
        8 * main_flops,
        4 * row_bytes,
        prefetch=1,
        in_specs=[slot_spec] + [ANY] * (2 * groups - 3) + [by_expert(width, hidden)],
        out_specs=[act_spec, ANY],
        out_shape=[shape(experts, routes, hidden, dtype=f32), shape(experts, routes, width)],
        scratch_shapes=[
            pltpu.VMEM((experts, routes, width), bf16),
            pltpu.VMEM((groups, members, width), bf16),
            pltpu.SemaphoreType.DMA((groups, 2)),
            pltpu.SemaphoreType.DMA((experts,)),
        ],
    )(place, pick, dy_own, *dy_mine, *dy_other, w_down)
    last_mine, kept = lax.optimization_barrier((moving, kept))
    last_other = hop(last_mine, swaps[-1])
    kept, late = pl.pallas_call(
        functools.partial(fill_kernel, groups, cap),
        in_specs=[SMEM] + [ANY] * 4,
        out_specs=[ANY, pl.BlockSpec(memory_space=pltpu.VMEM)],
        out_shape=[shape(experts, routes, width), shape(experts, cap, width)],
        input_output_aliases={4: 0},
        scratch_shapes=[
            pltpu.VMEM((members, width), bf16),
            pltpu.VMEM((experts * cap, members), bf16),
            pltpu.SemaphoreType.DMA((2,)),
            pltpu.SemaphoreType.DMA,
            pltpu.SemaphoreType.DMA((experts,)),
        ],
        compiler_params=pltpu.CompilerParams(vmem_limit_bytes=VMEM_LIMIT),
        cost_estimate=cost(pick_flops // groups, 2 * total * width),
        name="fill",
    )(place, pick, last_mine, last_other, kept)

    orders = []
    for g in range(turns):
        turn = [(g + t) % bits for t in range(bits)]
        orders.append(
            tuple(sum(((p >> (bits - 1 - t)) & 1) << turn[t] for t in range(bits)) for p in range(dp_count))
        )
    orders = tuple(orders)
    cut_rows = share // turns

    def down(start, count, after):
        outs = call(
            functools.partial(down_kernel, orders, len(after)),
            "down",
            count,
            (400 if after else 1) * main_flops,
            row_bytes,
            in_specs=[SMEM]
            + [pl.BlockSpec((1, routes, n), lambda b: (b + start, 0, 0)) for n in (width, hidden)]
            + [ANY] * len(after),
            out_specs=[ANY] * (2 * turns),
            out_shape=[shape(dp_count // 2, count, cut_rows, hidden)] * (2 * turns),
            scratch_shapes=[
                pltpu.VMEM((turns, dp_count, count, cut_rows, hidden), bf16),
                pltpu.SemaphoreType.DMA((turns, dp_count, count)),
            ],
        )(place, kept, scaled, *after)
        return [(outs[2 * g], outs[2 * g + 1]) for g in range(turns)]

    def exchange(state, t):
        new = []
        for g, (keep, send) in enumerate(state):
            bit = 1 << ((g + t) % bits)
            got = lax.ppermute(send, "dp", [(i, i ^ bit) for i in range(dp_count)])
            both = keep.astype(f32) + got.astype(f32)
            if t < bits - 1:
                both = both.astype(bf16)
            half = both.shape[0] // 2
            new.append((both[:half], both[half:]) if half else both[0])
        return new

    counts = [1, experts - 1] if experts > 1 else [experts]
    states = [down(0, counts[0], [])]
    ahead = [pair[0] for pair in states[0]][:1]
    states[0] = exchange(states[0], 0)

    def at_end(i):
        return jnp.clip(i - experts, 0, groups - 1)

    def at_first(rows, n):
        return pl.BlockSpec((1, rows, n), lambda i, *_: (jnp.minimum(i, experts - 1), 0, 0))

    token_part = call(
        functools.partial(tail_kernel, groups, cap, width, top, len(ahead)),
        "tail",
        groups + experts,
        100 * main_flops,
        4 * row_bytes,
        prefetch=1,
        in_specs=[
            pl.BlockSpec((1, experts * cap, members), lambda i, *_: (at_end(i), 0, 0)),
            at_first(cap, width),
            at_first(routes, hidden),
            at_first(width, hidden),
            at_first(hidden, width),
            at_first(routes, hidden),
            at_first(routes, hidden),
            pl.BlockSpec((members, LANES), lambda i, *_: (at_end(i), 0)),
        ]
        + [ANY] * len(ahead),
        out_specs=pl.BlockSpec((members, full), lambda i, *_: (at_end(i), 0)),
        out_shape=shape(total, full),
        scratch_shapes=[
            pltpu.VMEM((routes, hidden), f32),
            pltpu.VMEM((groups, experts * cap, full), bf16),
        ],
    )(place, pick, late, back, w_down, w_flip, hid, slope_g, meta, *ahead)
    summed = lax.psum_scatter(token_part, "ep", scatter_dimension=0, tiled=True)

    done = [1]
    if len(counts) > 1:
        sums = [pair[0] if isinstance(pair, tuple) else pair for pair in states[0]]
        states.append(down(counts[0], counts[1], sums))
        done.append(0)
    for t in range(bits):
        states = [state if t < first else exchange(state, t) for state, first in zip(states, done)]
    down_grad = jnp.zeros((experts, share, hidden), f32)
    start = 0
    for count, state in zip(counts, states):
        for g, part in enumerate(state):
            down_grad = lax.dynamic_update_slice(down_grad, part, (start, g * cut_rows, 0))
        start += count
    token_grad, gate_grad = pl.pallas_call(
        functools.partial(finish_kernel, width, top),
        out_shape=[shape(tok_rows, width), shape(top, tok_rows)],
        compiler_params=pltpu.CompilerParams(vmem_limit_bytes=VMEM_LIMIT),
        cost_estimate=cost(0, 4 * tok_rows * width),
        name="finish",
    )(summed)
    return (token_grad, gate_grad.T, down_grad)


def solution(mesh):
    return jax.shard_map(
        shards,
        mesh=mesh,
        in_specs=(
            P(("dp", "ep"), None),
            P(("dp", "ep"), None),
            P(("dp", "ep"), None),
            P(("dp", "ep"), None),
            P("ep", None, None),
            P("ep", None, None),
        ),
        out_specs=(P(("dp", "ep"), None), P(("dp", "ep"), None), P("ep", "dp", None)),
        check_vma=False,
    )
```

```python
import functools

import jax
import jax.numpy as jnp
from jax import lax
from jax.experimental import pallas as pl
from jax.experimental.pallas import tpu as pltpu
from jax.sharding import PartitionSpec as P

LANES = 128
PACK = 16
GROUP = 2
VMEM_LIMIT = 60 * 1024 * 1024
bf16, f32 = jnp.bfloat16, jnp.float32
ANY = pl.BlockSpec(memory_space=pl.ANY)
SMEM = pl.BlockSpec(memory_space=pltpu.SMEM)
FIRST = (((0,), (0,)), ((), ()))


def dot(a, b, dims=(((1,), (0,)), ((), ()))):
    return lax.dot_general(a, b, dims, preferred_element_type=f32)


def pack_kernel(top, tokens, ids, gates, x_out):
    count, width = tokens.shape
    x_out[:, pl.ds(0, width)] = tokens[...]
    info = jnp.concatenate(
        [ids[...].astype(f32), gates[...].astype(f32), jnp.zeros((LANES - 2 * top, count), f32)], axis=0
    )
    x_out[:, pl.ds(width, LANES)] = info.T.astype(bf16)


def flip_kernel(w, out):
    out[0] = w[0].T


def block_copies(place, ref, dst, sem, flip):
    half = ref.shape[0] // 2
    copies = []
    for part in range(2):
        to = (part ^ flip) * half
        if not isinstance(flip, int):
            to = pl.multiple_of(to, half)
        copies.append(
            pltpu.make_async_copy(ref.at[pl.ds(part * half, half), :], dst.at[pl.ds(to, half), :], sem.at[part])
        )
    return copies


def by_side(place, is_left, mine, other, act):
    for left in (True, False):
        for core in (True, False):
            ref = (mine if left == core else other)(left)
            if ref is not None:

                @pl.when((is_left == left) & ((place[2] == 0) == core))
                def _():
                    act(ref, 0 if left else 1)


def start_blocks(place, chips, own, mine, other, dst, sem):
    for copy in block_copies(place, own, dst.at[0], sem.at[0], place[2]):
        copy.start()
    for slot in range(1, chips):

        def pick(blocks, left):
            step = slot if left else chips - slot
            return blocks[step - 1] if step <= len(blocks) else None

        def start(ref, flip):
            for copy in block_copies(place, ref, dst.at[slot], sem.at[slot], flip):
                copy.start()

        by_side(place, place[3] >= slot, functools.partial(pick, mine), functools.partial(pick, other), start)


def copy_all(pairs, sem):
    copies = [pltpu.make_async_copy(src, dst, sem.at[n]) for n, (src, dst) in enumerate(pairs)]
    for copy in copies:
        copy.start()
    return copies


def up_kernel(groups, width, top, cap, after, place, x_all, w_up, *refs):
    refs = refs[after:]
    pick_out, meta, hid_out, scaled_out, slope_out, rows, w_v, held, gates, pick, hid, scaled, slope, sems, out_sem = refs
    experts, members = held.shape[0], rows.shape[1]
    arrive = copy_all([(x_all.at[pl.ds(g * members, members), :], rows.at[g]) for g in range(groups)], sems.at[0])
    weights = copy_all([(w_up.at[b], w_v.at[b]) for b in range(experts)], sems.at[1])
    before = lax.broadcasted_iota(jnp.int32, (members, members), 0) < lax.broadcasted_iota(
        jnp.int32, (members, members), 1
    )
    before = before.astype(bf16)
    spot = lax.broadcasted_iota(jnp.int32, (cap, members), 0).astype(f32)
    for g in range(groups):
        arrive[g].wait()
        info = rows[g, :, pl.ds(width, LANES)]
        meta[pl.ds(g * members, members), :] = info
        across = info.astype(f32).T
        ids, parts = across[:top], across[top : 2 * top]
        chosen = [ids == (place[0] * experts + b).astype(f32) for b in range(experts)]
        member = [jnp.sum(jnp.where(hit, 1.0, 0.0), axis=0, keepdims=True) for hit in chosen]
        table = jnp.concatenate(member + [jnp.zeros((PACK - experts, members), f32)], axis=0)
        prior = dot(table.astype(bf16), before)
        for b in range(experts):
            rank = jnp.where(member[b] > 0.0, prior[b : b + 1], -1.0)
            one = jnp.where(spot == rank, 1.0, 0.0)
            gate = jnp.sum(jnp.where(chosen[b], parts, 0.0), axis=0, keepdims=True)
            pick[g, pl.ds(b * cap, cap), :] = one.astype(bf16)
            gates[b, pl.ds(g * cap, cap), :] = jnp.broadcast_to(
                jnp.sum(one * gate, axis=1, keepdims=True), (cap, LANES)
            )
        got = dot(pick[g], rows[g, :, pl.ds(0, width)]).astype(bf16)
        for b in range(experts):
            held[b, pl.ds(g * cap, cap), :] = got[b * cap : (b + 1) * cap]
    outs = copy_all([(pick, pick_out)], out_sem.at[3])
    for b in range(experts):
        weights[b].wait()
        pre = dot(held[b], w_v[b])
        gate = gates[b][:, :1]
        sig = 0.5 + 0.5 * jnp.tanh(0.5 * pre)
        act = pre * sig
        hid[b] = act.astype(bf16)
        scaled[b] = (gate * act).astype(bf16)
        slope[b] = (gate * (sig + act * (1.0 - sig))).astype(bf16)
        for n, (src, dst) in enumerate(((hid, hid_out), (scaled, scaled_out), (slope, slope_out))):
            copy = pltpu.make_async_copy(src.at[b], dst.at[b], out_sem.at[n, b])
            copy.start()
            outs.append(copy)
    for copy in outs:
        copy.wait()


def down_kernel(orders, start, place, kept, scaled_in, *refs):
    outs, (rows, scaled, sent, in_sem, sem) = refs[:-5], refs[-5:]
    experts = sent.shape[2]
    arrive = copy_all([(kept.at[start + b], rows.at[b]) for b in range(experts)], in_sem.at[0])
    others = copy_all([(scaled_in.at[start + b], scaled.at[b]) for b in range(experts)], in_sem.at[1])
    parts = len(orders[0])
    half = parts // 2
    share = rows.shape[2] // parts
    cut = share // len(orders)
    copies = []
    for b in range(experts):
        arrive[b].wait()
        others[b].wait()
        for q in range(parts):
            at = pl.multiple_of((place[1] ^ q) * share, LANES)
            full = dot(rows[b, :, pl.ds(at, share)], scaled[b], FIRST).astype(bf16)
            for g, order in enumerate(orders):
                sent[g, q, b] = full[g * cut : (g + 1) * cut]
                p = order.index(q)
                copy = pltpu.make_async_copy(
                    sent.at[g, q, b], outs[2 * g + p // half].at[p % half, b], sem.at[g, q, b]
                )
                copy.start()
                copies.append(copy)
    for copy in copies:
        copy.wait()


def tail_kernel(groups, cap, width, top, place, *refs):
    steps = groups - 1
    own, mine, other, refs = refs[0], refs[1 : 1 + steps], refs[1 + steps : 1 + 2 * steps], refs[1 + 2 * steps :]
    pick_in, w_down, w_flip, hid_in, slope_in, meta, out_all, kept = refs[:8]
    pick, moved, held, grads, out, down_v, flip_v, hid, slope, block_sem, sems, keep_sem, out_sem = refs[8:]
    experts, members = held.shape[0], moved.shape[1]
    half = members // 2
    first_pick = copy_all([(pick_in, pick)], sems.at[0])
    start_blocks(place, groups, own, mine, other, moved, block_sem)
    loads = [
        copy_all([(src.at[b], dst.at[b]) for b in range(experts)], sems.at[n])
        for n, (src, dst) in enumerate(((w_down, down_v), (hid_in, hid), (slope_in, slope), (w_flip, flip_v)), 1)
    ]
    first_pick[0].wait()
    for slot in range(groups):
        for part in range(2):
            at = pl.ds(part * half, half)
            pltpu.make_async_copy(own.at[at, :], moved.at[slot, at, :], block_sem.at[slot, part]).wait()
        group = lax.rem(place[3] - slot + groups, groups)
        first = pl.multiple_of(group * cap, PACK)
        got = dot(pick[group], moved[slot]).astype(bf16)
        for b in range(experts):
            held[b, pl.ds(first, cap), :] = got[b * cap : (b + 1) * cap]
    keep = copy_all([(held.at[b], kept.at[b]) for b in range(experts)], keep_sem)
    lane = lax.broadcasted_iota(jnp.int32, (groups * cap, LANES), 1)
    for b in range(experts):
        for load in loads[:3]:
            load[b].wait()
        back = dot(held[b], down_v[b])
        gate = jnp.sum(back * hid[b].astype(f32), axis=1, keepdims=True)
        gate = jnp.where(lane == b, gate, 0.0).astype(bf16)
        grad = (back * slope[b].astype(f32)).astype(bf16)
        loads[3][b].wait()
        route = dot(grad, flip_v[b]).astype(bf16)
        for g in range(groups):
            grads[g, pl.ds(b * cap, cap), pl.ds(0, width)] = route[g * cap : (g + 1) * cap]
            grads[g, pl.ds(b * cap, cap), pl.ds(width, LANES)] = gate[g * cap : (g + 1) * cap]
    lane = lax.broadcasted_iota(jnp.int32, (members, LANES), 1)
    for g in range(groups):
        total = dot(pick[g], grads[g], FIRST)
        out[g, :, pl.ds(0, width)] = total[:, :width].astype(bf16)
        by_expert = total[:, width:]
        ids = jnp.where(lane < top, meta[pl.ds(g * members, members), :].astype(f32), -1.0)
        picked = jnp.zeros(ids.shape, f32)
        for b in range(experts):
            hit = ids == (place[0] * experts + b).astype(f32)
            picked = picked + jnp.where(hit, by_expert[:, b : b + 1], 0.0)
        out[g, :, pl.ds(width, LANES)] = picked.astype(bf16)
        copy = pltpu.make_async_copy(out.at[g], out_all.at[pl.ds(g * members, members), :], out_sem.at[g])
        copy.start()
        keep.append(copy)
    for copy in keep:
        copy.wait()


def finish_kernel(width, top, rows, token, gate):
    token[...] = rows[:, pl.ds(0, width)]
    gate[...] = rows[:, pl.ds(width, LANES)].astype(f32).T[:top].astype(bf16)


def cost(flops, nbytes):
    return pl.CostEstimate(flops=int(flops), bytes_accessed=int(nbytes), transcendentals=0)


def shards(tokens, cotangent, expert_ids, gate_weights, w_up, w_down):
    tok_rows, width = tokens.shape
    top = expert_ids.shape[1]
    ep_count, dp_count = lax.axis_size("ep"), lax.axis_size("dp")
    experts, _, hidden = w_up.shape
    base_load = tok_rows * top // (experts * ep_count)
    capacity = base_load + max(1, base_load // 16)
    total = ep_count * tok_rows
    groups = ep_count // GROUP
    members = GROUP * tok_rows
    cap = -(-GROUP * capacity // PACK) * PACK
    routes = groups * cap
    full = width + LANES
    here = lax.axis_index("ep")
    place = jnp.stack([here, lax.axis_index("dp"), here % GROUP, here // GROUP]).astype(jnp.int32)
    bits = dp_count.bit_length() - 1
    turns = 2
    share = width // dp_count

    def shape(*dims, dtype=bf16):
        return jax.ShapeDtypeStruct(dims, dtype)

    x_own = pl.pallas_call(
        functools.partial(pack_kernel, top),
        out_shape=shape(tok_rows, full),
        compiler_params=pltpu.CompilerParams(vmem_limit_bytes=VMEM_LIMIT),
        cost_estimate=cost(0, 4 * tok_rows * width),
        name="pack",
    )(tokens, expert_ids.T, gate_weights.T)
    x_all = lax.all_gather(x_own, "ep", axis=0, tiled=True)

    def reach(p, step):
        q = p + GROUP * step if p % GROUP == 0 else p - GROUP * step
        return q if 0 <= q < ep_count else None

    def hop(value, pairs):
        return lax.ppermute(value, "ep", pairs)

    def at_group(i):
        return jnp.minimum(i, groups - 1)

    def at_expert(i):
        return jnp.clip(i - groups, 0, experts - 1)

    def at_slot(i, place):
        return lax.rem(place[3] - at_group(i) + groups, groups)

    def by_group(n):
        return pl.BlockSpec((members, n), lambda i, *_: (at_group(i), 0))

    def by_expert(rows, n):
        return pl.BlockSpec((1, rows, n), lambda i, *_: (at_expert(i), 0, 0))

    def call(kernel, name, grid, flops, nbytes, in_specs, out_specs, out_shape, scratch_shapes, prefetch=0):
        return pl.pallas_call(
            kernel,
            grid_spec=pltpu.PrefetchScalarGridSpec(
                num_scalar_prefetch=prefetch,
                grid=(grid,),
                in_specs=in_specs,
                out_specs=out_specs,
                scratch_shapes=scratch_shapes,
            ),
            out_shape=out_shape,
            compiler_params=pltpu.CompilerParams(vmem_limit_bytes=VMEM_LIMIT),
            cost_estimate=cost(flops, nbytes),
            name=name,
        )

    row_bytes = 2 * experts * hidden * width
    w_flip = call(
        flip_kernel,
        "flip",
        experts,
        0,
        2 * row_bytes,
        in_specs=[pl.BlockSpec((1, width, hidden), lambda b: (b, 0, 0))],
        out_specs=pl.BlockSpec((1, hidden, width), lambda b: (b, 0, 0)),
        out_shape=shape(experts, hidden, width),
        scratch_shapes=[],
    )(w_up)
    dy_own = jnp.concatenate([cotangent, hop(cotangent, [(p, p ^ 1) for p in range(ep_count)])], axis=0)
    lines = [None] + [
        [(p, reach(p, 1)) for p in range(ep_count) if None not in (reach(p, 1), reach(p, 1 - step))]
        for step in range(1, groups)
    ]
    swaps = [None] + [
        [(p, p ^ 1) for p in range(ep_count) if reach(p, -step) is not None] for step in range(1, groups)
    ]
    moving, dy_mine, dy_other = dy_own, [], []
    for step in range(1, groups - 1):
        moving = hop(moving, lines[step])
        if step == 1:
            moving, w_flip = lax.optimization_barrier((moving, w_flip))
        dy_mine.append(moving)

    act = shape(experts, routes, hidden)
    act_spec = by_expert(routes, hidden)
    pick_spec = pl.BlockSpec((1, experts * cap, members), lambda i, *_: (at_group(i), 0, 0))
    pick_flops = 2 * total * experts * cap * width
    main_flops = 2 * experts * routes * width * hidden
    act3 = pltpu.VMEM((experts, routes, hidden), bf16)
    pick_v = pltpu.VMEM((groups, experts * cap, members), bf16)
    most = max(experts, groups)

    def one(kernel, name, flops, nbytes, in_specs, out_specs, out_shape, scratch_shapes):
        return pl.pallas_call(
            kernel,
            in_specs=in_specs,
            out_specs=out_specs,
            out_shape=out_shape,
            scratch_shapes=scratch_shapes,
            compiler_params=pltpu.CompilerParams(vmem_limit_bytes=VMEM_LIMIT),
            cost_estimate=cost(flops, nbytes),
            name=name,
        )

    pick, meta, hid, scaled, slope_g = one(
        functools.partial(up_kernel, groups, width, top, cap, 0),
        "up",
        pick_flops + main_flops,
        2 * total * full + row_bytes,
        [SMEM, ANY, ANY],
        [ANY, pl.BlockSpec(memory_space=pltpu.VMEM), ANY, ANY, ANY],
        [shape(groups, experts * cap, members), shape(total, LANES), act, act, act],
        [
            pltpu.VMEM((groups, members, full), bf16),
            pltpu.VMEM((experts, width, hidden), bf16),
            pltpu.VMEM((experts, routes, width), bf16),
            pltpu.VMEM((experts, routes, LANES), f32),
            pick_v,
            act3,
            act3,
            act3,
            pltpu.SemaphoreType.DMA((2, most)),
            pltpu.SemaphoreType.DMA((4, experts)),
        ],
    )(place, x_all, w_up)
    *dy_mine, hid = lax.optimization_barrier((*dy_mine, hid))
    dy_mine.append(hop(dy_mine[-1], lines[-1]))
    dy_other = [hop(part, swap) for part, swap in zip(dy_mine, swaps[1:])]

    orders = []
    for g in range(turns):
        turn = [(g + t) % bits for t in range(bits)]
        orders.append(
            tuple(sum(((p >> (bits - 1 - t)) & 1) << turn[t] for t in range(bits)) for p in range(dp_count))
        )
    orders = tuple(orders)
    cut_rows = share // turns

    def down(start, count):
        outs = one(
            functools.partial(down_kernel, orders, start),
            "down",
            16 * main_flops,
            8 * row_bytes,
            [SMEM, ANY, ANY],
            [ANY] * (2 * turns),
            [shape(dp_count // 2, count, cut_rows, hidden)] * (2 * turns),
            [
                pltpu.VMEM((count, routes, width), bf16),
                pltpu.VMEM((count, routes, hidden), bf16),
                pltpu.VMEM((turns, dp_count, count, cut_rows, hidden), bf16),
                pltpu.SemaphoreType.DMA((2, count)),
                pltpu.SemaphoreType.DMA((turns, dp_count, count)),
            ],
        )(place, kept, scaled)
        return [(outs[2 * g], outs[2 * g + 1]) for g in range(turns)]

    def exchange(state, t):
        new = []
        for g, (keep, send) in enumerate(state):
            bit = 1 << ((g + t) % bits)
            got = lax.ppermute(send, "dp", [(i, i ^ bit) for i in range(dp_count)])
            both = keep.astype(f32) + got.astype(f32)
            if t < bits - 1:
                both = both.astype(bf16)
            half = both.shape[0] // 2
            new.append((both[:half], both[half:]) if half else both[0])
        return new

    token_part, kept = one(
        functools.partial(tail_kernel, groups, cap, width, top),
        "tail",
        8 * main_flops,
        4 * row_bytes,
        [SMEM] + [ANY] * (2 * groups - 1) + [ANY] * 5 + [pl.BlockSpec(memory_space=pltpu.VMEM)],
        [ANY, ANY],
        [shape(total, full), shape(experts, routes, width)],
        [
            pick_v,
            pltpu.VMEM((groups, members, width), bf16),
            pltpu.VMEM((experts, routes, width), bf16),
            pltpu.VMEM((groups, experts * cap, full), bf16),
            pltpu.VMEM((groups, members, full), bf16),
            pltpu.VMEM((experts, width, hidden), bf16),
            pltpu.VMEM((experts, hidden, width), bf16),
            act3,
            act3,
            pltpu.SemaphoreType.DMA((groups, 2)),
            pltpu.SemaphoreType.DMA((5, experts)),
            pltpu.SemaphoreType.DMA((experts,)),
            pltpu.SemaphoreType.DMA((groups,)),
        ],
    )(place, dy_own, *dy_mine, *dy_other, pick, w_down, w_flip, hid, slope_g, meta)
    summed = lax.psum_scatter(token_part, "ep", scatter_dimension=0, tiled=True)
    token_grad, gate_grad = pl.pallas_call(
        functools.partial(finish_kernel, width, top),
        out_shape=[shape(tok_rows, width), shape(top, tok_rows)],
        compiler_params=pltpu.CompilerParams(vmem_limit_bytes=VMEM_LIMIT),
        cost_estimate=cost(0, 4 * tok_rows * width),
        name="finish",
    )(summed)

    counts = [experts // 2, experts - experts // 2] if experts > 1 else [experts]
    states = [down(start, count) for start, count in zip((0, counts[0]), counts)]
    for t in range(bits):
        states = [exchange(state, t) for state in states]
    token_grad, states = lax.optimization_barrier((token_grad, states))
    down_grad = jnp.concatenate([jnp.concatenate(state, axis=1) for state in states], axis=0)
    return (token_grad, gate_grad.T, down_grad)


def solution(mesh):
    return jax.shard_map(
        shards,
        mesh=mesh,
        in_specs=(
            P(("dp", "ep"), None),
            P(("dp", "ep"), None),
            P(("dp", "ep"), None),
            P(("dp", "ep"), None),
            P("ep", None, None),
            P("ep", None, None),
        ),
        out_specs=(P(("dp", "ep"), None), P(("dp", "ep"), None), P("ep", "dp", None)),
        check_vma=False,
    )
```

```python
import functools

import jax
import jax.numpy as jnp
from jax import lax
from jax.experimental import pallas as pl
from jax.experimental.pallas import tpu as pltpu
from jax.sharding import PartitionSpec as P

LANES = 128
PACK = 16
GROUP = 2
VMEM_LIMIT = 60 * 1024 * 1024
bf16, f32 = jnp.bfloat16, jnp.float32
ANY = pl.BlockSpec(memory_space=pl.ANY)
SMEM = pl.BlockSpec(memory_space=pltpu.SMEM)
FIRST = (((0,), (0,)), ((), ()))


def dot(a, b, dims=(((1,), (0,)), ((), ()))):
    return lax.dot_general(a, b, dims, preferred_element_type=f32)


def pack_kernel(top, tokens, ids, gates, x_out):
    count, width = tokens.shape
    x_out[:, pl.ds(0, width)] = tokens[...]
    info = jnp.concatenate(
        [ids[...].astype(f32), gates[...].astype(f32), jnp.zeros((LANES - 2 * top, count), f32)], axis=0
    )
    x_out[:, pl.ds(width, LANES)] = info.T.astype(bf16)


def flip_kernel(w, out):
    out[0] = w[0].T


def block_copies(place, ref, dst, sem, flip):
    half = ref.shape[0] // 2
    copies = []
    for part in range(2):
        to = (part ^ flip) * half
        if not isinstance(flip, int):
            to = pl.multiple_of(to, half)
        copies.append(
            pltpu.make_async_copy(ref.at[pl.ds(part * half, half), :], dst.at[pl.ds(to, half), :], sem.at[part])
        )
    return copies


def by_side(place, is_left, mine, other, act):
    for left in (True, False):
        for core in (True, False):
            ref = (mine if left == core else other)(left)
            if ref is not None:

                @pl.when((is_left == left) & ((place[2] == 0) == core))
                def _():
                    act(ref, 0 if left else 1)


def start_blocks(place, chips, own, mine, other, dst, sem):
    for copy in block_copies(place, own, dst.at[0], sem.at[0], place[2]):
        copy.start()
    for slot in range(1, chips):

        def pick(blocks, left):
            step = slot if left else chips - slot
            return blocks[step - 1] if step <= len(blocks) else None

        def start(ref, flip):
            for copy in block_copies(place, ref, dst.at[slot], sem.at[slot], flip):
                copy.start()

        by_side(place, place[3] >= slot, functools.partial(pick, mine), functools.partial(pick, other), start)


def copy_all(pairs, sem):
    copies = [pltpu.make_async_copy(src, dst, sem.at[n]) for n, (src, dst) in enumerate(pairs)]
    for copy in copies:
        copy.start()
    return copies


def up_kernel(groups, width, top, cap, after, place, x_all, w_up, *refs):
    refs = refs[after:]
    pick_out, meta, hid_out, scaled_out, slope_out, rows, w_v, held, gates, pick, hid, scaled, slope, sems, out_sem = refs
    experts, members = held.shape[0], rows.shape[1]
    arrive = copy_all([(x_all.at[pl.ds(g * members, members), :], rows.at[g]) for g in range(groups)], sems.at[0])
    weights = copy_all([(w_up.at[b], w_v.at[b]) for b in range(experts)], sems.at[1])
    before = lax.broadcasted_iota(jnp.int32, (members, members), 0) < lax.broadcasted_iota(
        jnp.int32, (members, members), 1
    )
    before = before.astype(bf16)
    spot = lax.broadcasted_iota(jnp.int32, (cap, members), 0).astype(f32)
    for g in range(groups):
        arrive[g].wait()
        info = rows[g, :, pl.ds(width, LANES)]
        meta[pl.ds(g * members, members), :] = info
        across = info.astype(f32).T
        ids, parts = across[:top], across[top : 2 * top]
        chosen = [ids == (place[0] * experts + b).astype(f32) for b in range(experts)]
        member = [jnp.sum(jnp.where(hit, 1.0, 0.0), axis=0, keepdims=True) for hit in chosen]
        table = jnp.concatenate(member + [jnp.zeros((PACK - experts, members), f32)], axis=0)
        prior = dot(table.astype(bf16), before)
        for b in range(experts):
            rank = jnp.where(member[b] > 0.0, prior[b : b + 1], -1.0)
            one = jnp.where(spot == rank, 1.0, 0.0)
            gate = jnp.sum(jnp.where(chosen[b], parts, 0.0), axis=0, keepdims=True)
            pick[g, pl.ds(b * cap, cap), :] = one.astype(bf16)
            gates[b, pl.ds(g * cap, cap), :] = jnp.broadcast_to(
                jnp.sum(one * gate, axis=1, keepdims=True), (cap, LANES)
            )
        got = dot(pick[g], rows[g, :, pl.ds(0, width)]).astype(bf16)
        for b in range(experts):
            held[b, pl.ds(g * cap, cap), :] = got[b * cap : (b + 1) * cap]
    outs = copy_all([(pick, pick_out)], out_sem.at[3])
    for b in range(experts):
        weights[b].wait()
        pre = dot(held[b], w_v[b])
        gate = gates[b][:, :1]
        sig = 0.5 + 0.5 * jnp.tanh(0.5 * pre)
        act = pre * sig
        hid[b] = act.astype(bf16)
        scaled[b] = (gate * act).astype(bf16)
        slope[b] = (gate * (sig + act * (1.0 - sig))).astype(bf16)
        for n, (src, dst) in enumerate(((hid, hid_out), (scaled, scaled_out), (slope, slope_out))):
            copy = pltpu.make_async_copy(src.at[b], dst.at[b], out_sem.at[n, b])
            copy.start()
            outs.append(copy)
    for copy in outs:
        copy.wait()


def down_kernel(orders, start, place, kept, scaled_in, *refs):
    outs, (rows, scaled, sent, in_sem, sem) = refs[:-5], refs[-5:]
    experts = sent.shape[2]
    arrive = copy_all([(kept.at[start + b], rows.at[b]) for b in range(experts)], in_sem.at[0])
    others = copy_all([(scaled_in.at[start + b], scaled.at[b]) for b in range(experts)], in_sem.at[1])
    parts = len(orders[0])
    half = parts // 2
    share = rows.shape[2] // parts
    cut = share // len(orders)
    copies = []
    for b in range(experts):
        arrive[b].wait()
        others[b].wait()
        for q in range(parts):
            at = pl.multiple_of((place[1] ^ q) * share, LANES)
            full = dot(rows[b, :, pl.ds(at, share)], scaled[b], FIRST).astype(bf16)
            for g, order in enumerate(orders):
                sent[g, q, b] = full[g * cut : (g + 1) * cut]
                p = order.index(q)
                copy = pltpu.make_async_copy(
                    sent.at[g, q, b], outs[2 * g + p // half].at[p % half, b], sem.at[g, q, b]
                )
                copy.start()
                copies.append(copy)
    for copy in copies:
        copy.wait()


def last_group(place, groups):
    return (place[3] == 0) | (place[3] == groups - 1), jnp.where(place[3] == 0, groups - 1, 0)


def gate_columns(place, top, experts, by_expert, info):
    lane = lax.broadcasted_iota(jnp.int32, info.shape, 1)
    ids = jnp.where(lane < top, info, -1.0)
    picked = jnp.zeros(info.shape, f32)
    for b in range(experts):
        hit = ids == (place[0] * experts + b).astype(f32)
        picked = picked + jnp.where(hit, by_expert[:, b : b + 1], 0.0)
    return picked


def gate_terms(back, hid, b):
    lane = lax.broadcasted_iota(jnp.int32, (back.shape[0], LANES), 1)
    gate = jnp.sum(back * hid.astype(f32), axis=1, keepdims=True)
    return jnp.where(lane == b, gate, 0.0).astype(bf16)


def early_kernel(groups, cap, width, top, place, *refs):
    steps = groups - 2
    own, mine, other, refs = refs[0], refs[1 : 1 + steps], refs[1 + steps : 1 + 2 * steps], refs[1 + 2 * steps :]
    pick_in, w_down, w_flip, hid_in, slope_in, meta, out_all, kept = refs[:8]
    pick, moved, held, grads, out, down_v, flip_v, hid, slope, block_sem, sems, keep_sem, out_sem = refs[8:]
    experts, members = held.shape[0], moved.shape[1]
    half = members // 2
    first_pick = copy_all([(pick_in, pick)], sems.at[0])
    start_blocks(place, groups, own, mine, other, moved, block_sem)
    loads = [
        copy_all([(src.at[b], dst.at[b]) for b in range(experts)], sems.at[n])
        for n, (src, dst) in enumerate(((w_down, down_v), (hid_in, hid), (slope_in, slope), (w_flip, flip_v)), 1)
    ]
    first_pick[0].wait()
    for slot in range(groups):
        group = lax.rem(place[3] - slot + groups, groups)
        first = pl.multiple_of(group * cap, PACK)
        here = True if slot == 0 else jnp.where(place[3] >= slot, slot, groups - slot) <= steps

        @pl.when(here)
        def _():
            for part in range(2):
                at = pl.ds(part * half, half)
                pltpu.make_async_copy(own.at[at, :], moved.at[slot, at, :], block_sem.at[slot, part]).wait()
            got = dot(pick[group], moved[slot]).astype(bf16)
            for b in range(experts):
                held[b, pl.ds(first, cap), :] = got[b * cap : (b + 1) * cap]

        @pl.when(jnp.logical_not(here))
        def _():
            for b in range(experts):
                held[b, pl.ds(first, cap), :] = jnp.zeros((cap, width), bf16)

    keep = copy_all([(held.at[b], kept.at[b]) for b in range(experts)], keep_sem)
    for b in range(experts):
        for load in loads[:3]:
            load[b].wait()
        back = dot(held[b], down_v[b])
        gate = gate_terms(back, hid[b], b)
        grad = (back * slope[b].astype(f32)).astype(bf16)
        loads[3][b].wait()
        route = dot(grad, flip_v[b]).astype(bf16)
        for g in range(groups):
            grads[g, pl.ds(b * cap, cap), pl.ds(0, width)] = route[g * cap : (g + 1) * cap]
            grads[g, pl.ds(b * cap, cap), pl.ds(width, LANES)] = gate[g * cap : (g + 1) * cap]
    for g in range(groups):
        total = dot(pick[g], grads[g], FIRST)
        out[g, :, pl.ds(0, width)] = total[:, :width].astype(bf16)
        info = meta[pl.ds(g * members, members), :].astype(f32)
        out[g, :, pl.ds(width, LANES)] = gate_columns(place, top, experts, total[:, width:], info).astype(bf16)
        copy = pltpu.make_async_copy(out.at[g], out_all.at[pl.ds(g * members, members), :], out_sem.at[g])
        copy.start()
        keep.append(copy)
    for copy in keep:
        copy.wait()


def late_kernel(groups, cap, width, top, place, pick_in, mine, other, w_down, w_flip, hid_in, slope_in, *refs):
    meta, _, _, out_all, kept, pick, moved, held, grads, out, down_v, flip_v, hid, slope, info, block_sem, sems = refs
    experts, members = held.shape[0], moved.shape[0]
    has, group = last_group(place, groups)
    at = pl.ds(pl.multiple_of(group * cap, PACK), cap)
    tokens = pl.ds(pl.multiple_of(group * members, members), members)

    @pl.when(has)
    def _():
        def start(ref, flip):
            for copy in block_copies(place, ref, moved, block_sem, flip):
                copy.start()

        by_side(place, place[3] != 0, lambda left: mine, lambda left: other, start)
        small = copy_all([(pick_in.at[group], pick), (meta.at[tokens, :], info)], sems.at[0])
        loads = [
            copy_all([(src.at[b], dst.at[b]) for b in range(experts)], sems.at[n])
            for n, (src, dst) in enumerate(((w_down, down_v), (w_flip, flip_v)), 1)
        ]
        loads += [
            copy_all([(src.at[b, at, :], dst.at[b]) for b in range(experts)], sems.at[n])
            for n, (src, dst) in enumerate(((hid_in, hid), (slope_in, slope)), 3)
        ]
        for copy in small + block_copies(place, mine, moved, block_sem, 0):
            copy.wait()
        got = dot(pick[...], moved[...]).astype(bf16)
        for b in range(experts):
            held[b] = got[b * cap : (b + 1) * cap]
        ends = copy_all([(held.at[b], kept.at[b, at, :]) for b in range(experts)], sems.at[5])
        for b in range(experts):
            for load in loads:
                load[b].wait()
            back = dot(held[b], down_v[b])
            grad = (back * slope[b].astype(f32)).astype(bf16)
            grads[pl.ds(b * cap, cap), pl.ds(0, width)] = dot(grad, flip_v[b]).astype(bf16)
            grads[pl.ds(b * cap, cap), pl.ds(width, LANES)] = gate_terms(back, hid[b], b)
        total = dot(pick[...], grads[...], FIRST)
        out[:, pl.ds(0, width)] = total[:, :width].astype(bf16)
        columns = gate_columns(place, top, experts, total[:, width:], info[...].astype(f32))
        out[:, pl.ds(width, LANES)] = columns.astype(bf16)
        ends += copy_all([(out, out_all.at[tokens, :])], sems.at[6])
        for copy in ends:
            copy.wait()


def finish_kernel(width, top, rows, token, gate):
    token[...] = rows[:, pl.ds(0, width)]
    gate[...] = rows[:, pl.ds(width, LANES)].astype(f32).T[:top].astype(bf16)


def cost(flops, nbytes):
    return pl.CostEstimate(flops=int(flops), bytes_accessed=int(nbytes), transcendentals=0)


def shards(tokens, cotangent, expert_ids, gate_weights, w_up, w_down):
    tok_rows, width = tokens.shape
    top = expert_ids.shape[1]
    ep_count, dp_count = lax.axis_size("ep"), lax.axis_size("dp")
    experts, _, hidden = w_up.shape
    base_load = tok_rows * top // (experts * ep_count)
    capacity = base_load + max(1, base_load // 16)
    total = ep_count * tok_rows
    groups = ep_count // GROUP
    members = GROUP * tok_rows
    cap = -(-GROUP * capacity // PACK) * PACK
    routes = groups * cap
    full = width + LANES
    here = lax.axis_index("ep")
    place = jnp.stack([here, lax.axis_index("dp"), here % GROUP, here // GROUP]).astype(jnp.int32)
    bits = dp_count.bit_length() - 1
    turns = 2
    share = width // dp_count

    def shape(*dims, dtype=bf16):
        return jax.ShapeDtypeStruct(dims, dtype)

    x_own = pl.pallas_call(
        functools.partial(pack_kernel, top),
        out_shape=shape(tok_rows, full),
        compiler_params=pltpu.CompilerParams(vmem_limit_bytes=VMEM_LIMIT),
        cost_estimate=cost(0, 4 * tok_rows * width),
        name="pack",
    )(tokens, expert_ids.T, gate_weights.T)
    x_all = lax.all_gather(x_own, "ep", axis=0, tiled=True)

    def reach(p, step):
        q = p + GROUP * step if p % GROUP == 0 else p - GROUP * step
        return q if 0 <= q < ep_count else None

    def hop(value, pairs):
        return lax.ppermute(value, "ep", pairs)

    def at_group(i):
        return jnp.minimum(i, groups - 1)

    def at_expert(i):
        return jnp.clip(i - groups, 0, experts - 1)

    def at_slot(i, place):
        return lax.rem(place[3] - at_group(i) + groups, groups)

    def by_group(n):
        return pl.BlockSpec((members, n), lambda i, *_: (at_group(i), 0))

    def by_expert(rows, n):
        return pl.BlockSpec((1, rows, n), lambda i, *_: (at_expert(i), 0, 0))

    def call(kernel, name, grid, flops, nbytes, in_specs, out_specs, out_shape, scratch_shapes, prefetch=0):
        return pl.pallas_call(
            kernel,
            grid_spec=pltpu.PrefetchScalarGridSpec(
                num_scalar_prefetch=prefetch,
                grid=(grid,),
                in_specs=in_specs,
                out_specs=out_specs,
                scratch_shapes=scratch_shapes,
            ),
            out_shape=out_shape,
            compiler_params=pltpu.CompilerParams(vmem_limit_bytes=VMEM_LIMIT),
            cost_estimate=cost(flops, nbytes),
            name=name,
        )

    row_bytes = 2 * experts * hidden * width
    w_flip = call(
        flip_kernel,
        "flip",
        experts,
        0,
        2 * row_bytes,
        in_specs=[pl.BlockSpec((1, width, hidden), lambda b: (b, 0, 0))],
        out_specs=pl.BlockSpec((1, hidden, width), lambda b: (b, 0, 0)),
        out_shape=shape(experts, hidden, width),
        scratch_shapes=[],
    )(w_up)
    dy_own = jnp.concatenate([cotangent, hop(cotangent, [(p, p ^ 1) for p in range(ep_count)])], axis=0)
    lines = [None] + [
        [(p, reach(p, 1)) for p in range(ep_count) if None not in (reach(p, 1), reach(p, 1 - step))]
        for step in range(1, groups)
    ]
    swaps = [None] + [
        [(p, p ^ 1) for p in range(ep_count) if reach(p, -step) is not None] for step in range(1, groups)
    ]
    moving, dy_mine, dy_other = dy_own, [], []
    for step in range(1, groups - 1):
        moving = hop(moving, lines[step])
        if step == 1:
            moving, w_flip = lax.optimization_barrier((moving, w_flip))
        dy_mine.append(moving)

    act = shape(experts, routes, hidden)
    act_spec = by_expert(routes, hidden)
    pick_spec = pl.BlockSpec((1, experts * cap, members), lambda i, *_: (at_group(i), 0, 0))
    pick_flops = 2 * total * experts * cap * width
    main_flops = 2 * experts * routes * width * hidden
    act3 = pltpu.VMEM((experts, routes, hidden), bf16)
    pick_v = pltpu.VMEM((groups, experts * cap, members), bf16)
    most = max(experts, groups)

    def one(kernel, name, flops, nbytes, in_specs, out_specs, out_shape, scratch_shapes):
        return pl.pallas_call(
            kernel,
            in_specs=in_specs,
            out_specs=out_specs,
            out_shape=out_shape,
            scratch_shapes=scratch_shapes,
            compiler_params=pltpu.CompilerParams(vmem_limit_bytes=VMEM_LIMIT),
            cost_estimate=cost(flops, nbytes),
            name=name,
        )

    pick, meta, hid, scaled, slope_g = one(
        functools.partial(up_kernel, groups, width, top, cap, 0),
        "up",
        pick_flops + main_flops,
        2 * total * full + row_bytes,
        [SMEM, ANY, ANY],
        [ANY, pl.BlockSpec(memory_space=pltpu.VMEM), ANY, ANY, ANY],
        [shape(groups, experts * cap, members), shape(total, LANES), act, act, act],
        [
            pltpu.VMEM((groups, members, full), bf16),
            pltpu.VMEM((experts, width, hidden), bf16),
            pltpu.VMEM((experts, routes, width), bf16),
            pltpu.VMEM((experts, routes, LANES), f32),
            pick_v,
            act3,
            act3,
            act3,
            pltpu.SemaphoreType.DMA((2, most)),
            pltpu.SemaphoreType.DMA((4, experts)),
        ],
    )(place, x_all, w_up)
    *dy_mine, hid = lax.optimization_barrier((*dy_mine, hid))
    moving = hop(dy_mine[-1], lines[-1])
    dy_other = [hop(part, swap) for part, swap in zip(dy_mine, swaps[1:])]

    orders = []
    for g in range(turns):
        turn = [(g + t) % bits for t in range(bits)]
        orders.append(
            tuple(sum(((p >> (bits - 1 - t)) & 1) << turn[t] for t in range(bits)) for p in range(dp_count))
        )
    orders = tuple(orders)
    cut_rows = share // turns

    def down(start, count):
        outs = one(
            functools.partial(down_kernel, orders, start),
            "down",
            16 * main_flops,
            8 * row_bytes,
            [SMEM, ANY, ANY],
            [ANY] * (2 * turns),
            [shape(dp_count // 2, count, cut_rows, hidden)] * (2 * turns),
            [
                pltpu.VMEM((count, routes, width), bf16),
                pltpu.VMEM((count, routes, hidden), bf16),
                pltpu.VMEM((turns, dp_count, count, cut_rows, hidden), bf16),
                pltpu.SemaphoreType.DMA((2, count)),
                pltpu.SemaphoreType.DMA((turns, dp_count, count)),
            ],
        )(place, kept, scaled)
        return [(outs[2 * g], outs[2 * g + 1]) for g in range(turns)]

    def exchange(state, t):
        new = []
        for g, (keep, send) in enumerate(state):
            bit = 1 << ((g + t) % bits)
            got = lax.ppermute(send, "dp", [(i, i ^ bit) for i in range(dp_count)])
            both = keep.astype(f32) + got.astype(f32)
            if t < bits - 1:
                both = both.astype(bf16)
            half = both.shape[0] // 2
            new.append((both[:half], both[half:]) if half else both[0])
        return new

    weights_v = [pltpu.VMEM((experts, width, hidden), bf16), pltpu.VMEM((experts, hidden, width), bf16)]
    parts_shape = [shape(total, full), shape(experts, routes, width)]
    token_part, kept = one(
        functools.partial(early_kernel, groups, cap, width, top),
        "early",
        8 * main_flops,
        4 * row_bytes,
        [SMEM] + [ANY] * (2 * groups - 3) + [ANY] * 5 + [pl.BlockSpec(memory_space=pltpu.VMEM)],
        [ANY, ANY],
        parts_shape,
        [
            pick_v,
            pltpu.VMEM((groups, members, width), bf16),
            pltpu.VMEM((experts, routes, width), bf16),
            pltpu.VMEM((groups, experts * cap, full), bf16),
            pltpu.VMEM((groups, members, full), bf16),
            *weights_v,
            act3,
            act3,
            pltpu.SemaphoreType.DMA((groups, 2)),
            pltpu.SemaphoreType.DMA((5, experts)),
            pltpu.SemaphoreType.DMA((experts,)),
            pltpu.SemaphoreType.DMA((groups,)),
        ],
    )(place, dy_own, *dy_mine, *dy_other, pick, w_down, w_flip, hid, slope_g, meta)
    moving, kept = lax.optimization_barrier((moving, kept))
    act_v = pltpu.VMEM((experts, cap, hidden), bf16)
    token_part, kept = pl.pallas_call(
        functools.partial(late_kernel, groups, cap, width, top),
        in_specs=[SMEM] + [ANY] * 10,
        out_specs=[ANY, ANY],
        out_shape=parts_shape,
        input_output_aliases={9: 0, 10: 1},
        scratch_shapes=[
            pltpu.VMEM((experts * cap, members), bf16),
            pltpu.VMEM((members, width), bf16),
            pltpu.VMEM((experts, cap, width), bf16),
            pltpu.VMEM((experts * cap, full), bf16),
            pltpu.VMEM((members, full), bf16),
            *weights_v,
            act_v,
            act_v,
            pltpu.VMEM((members, LANES), bf16),
            pltpu.SemaphoreType.DMA((2,)),
            pltpu.SemaphoreType.DMA((7, most)),
        ],
        compiler_params=pltpu.CompilerParams(vmem_limit_bytes=VMEM_LIMIT),
        cost_estimate=cost(main_flops, 2 * row_bytes),
        name="late",
    )(place, pick, moving, hop(moving, swaps[-1]), w_down, w_flip, hid, slope_g, meta, token_part, kept)
    summed = lax.psum_scatter(token_part, "ep", scatter_dimension=0, tiled=True)
    token_grad, gate_grad = pl.pallas_call(
        functools.partial(finish_kernel, width, top),
        out_shape=[shape(tok_rows, width), shape(top, tok_rows)],
        compiler_params=pltpu.CompilerParams(vmem_limit_bytes=VMEM_LIMIT),
        cost_estimate=cost(0, 4 * tok_rows * width),
        name="finish",
    )(summed)

    counts = [experts // 2, experts - experts // 2] if experts > 1 else [experts]
    states = [down(start, count) for start, count in zip((0, counts[0]), counts)]
    for t in range(bits):
        if t == bits - 1:
            keeps = [[pair[0] for pair in state] for state in states]
            token_grad, keeps[-1] = lax.optimization_barrier((token_grad, keeps[-1]))
            states = [
                [(keep, pair[1]) for keep, pair in zip(kept_back, state)] for kept_back, state in zip(keeps, states)
            ]
        states = [exchange(state, t) for state in states]
    down_grad = jnp.concatenate([jnp.concatenate(state, axis=1) for state in states], axis=0)
    return (token_grad, gate_grad.T, down_grad)


def solution(mesh):
    return jax.shard_map(
        shards,
        mesh=mesh,
        in_specs=(
            P(("dp", "ep"), None),
            P(("dp", "ep"), None),
            P(("dp", "ep"), None),
            P(("dp", "ep"), None),
            P("ep", None, None),
            P("ep", None, None),
        ),
        out_specs=(P(("dp", "ep"), None), P(("dp", "ep"), None), P("ep", "dp", None)),
        check_vma=False,
    )
```

```python
import functools
import math

import jax
import jax.numpy as jnp
from jax import lax
from jax.experimental import pallas as pl
from jax.experimental.pallas import tpu as pltpu
from jax.sharding import PartitionSpec as P

LANES = 128
PACK = 16
GROUP = 2
SLACK = 6 * 1024 * 1024
bf16, f32 = jnp.bfloat16, jnp.float32
ANY = pl.BlockSpec(memory_space=pl.ANY)
SMEM = pl.BlockSpec(memory_space=pltpu.SMEM)
VMEM = pl.BlockSpec(memory_space=pltpu.VMEM)
FIRST = (((0,), (0,)), ((), ()))


def dot(a, b, dims=(((1,), (0,)), ((), ()))):
    return lax.dot_general(a, b, dims, preferred_element_type=f32)


def pack_kernel(top, tokens, ids, gates, x_out):
    count, width = tokens.shape
    x_out[:, pl.ds(0, width)] = tokens[...]
    info = jnp.concatenate(
        [ids[...].astype(f32), gates[...].astype(f32), jnp.zeros((LANES - 2 * top, count), f32)], axis=0
    )
    x_out[:, pl.ds(width, LANES)] = info.T.astype(bf16)


def flip_kernel(w, out):
    out[0] = w[0].T


def block_copies(place, ref, dst, sem, flip):
    half = ref.shape[0] // 2
    copies = []
    for part in range(2):
        to = (part ^ flip) * half
        if not isinstance(flip, int):
            to = pl.multiple_of(to, half)
        copies.append(
            pltpu.make_async_copy(ref.at[pl.ds(part * half, half), :], dst.at[pl.ds(to, half), :], sem.at[part])
        )
    return copies


def by_side(place, is_left, mine, other, act):
    for left in (True, False):
        for core in (True, False):
            ref = (mine if left == core else other)(left)
            if ref is not None:

                @pl.when((is_left == left) & ((place[2] == 0) == core))
                def _():
                    act(ref, 0 if left else 1)


def start_blocks(place, chips, own, mine, other, dst, sem):
    for copy in block_copies(place, own, dst.at[0], sem.at[0], place[2]):
        copy.start()
    for slot in range(1, chips):

        def pick(blocks, left):
            step = slot if left else chips - slot
            return blocks[step - 1] if step <= len(blocks) else None

        def start(ref, flip):
            for copy in block_copies(place, ref, dst.at[slot], sem.at[slot], flip):
                copy.start()

        by_side(place, place[3] >= slot, functools.partial(pick, mine), functools.partial(pick, other), start)


def copy_all(pairs, sem):
    copies = [pltpu.make_async_copy(src, dst, sem.at[n]) for n, (src, dst) in enumerate(pairs)]
    for copy in copies:
        copy.start()
    return copies


def up_kernel(groups, width, top, cap, after, place, x_all, w_up, *refs):
    refs = refs[after:]
    pick_out, meta, hid_out, scaled_out, slope_out, rows, held, gates, pick, hid, scaled, slope, sems, out_sem = refs
    experts, members = held.shape[0], rows.shape[1]
    arrive = copy_all([(x_all.at[pl.ds(g * members, members), :], rows.at[g]) for g in range(groups)], sems.at[0])
    before = lax.broadcasted_iota(jnp.int32, (members, members), 0) < lax.broadcasted_iota(
        jnp.int32, (members, members), 1
    )
    before = before.astype(bf16)
    spot = lax.broadcasted_iota(jnp.int32, (cap, members), 0).astype(f32)
    for g in range(groups):
        arrive[g].wait()
        info = rows[g, :, pl.ds(width, LANES)]
        meta[pl.ds(g * members, members), :] = info
        across = info.astype(f32).T
        ids, parts = across[:top], across[top : 2 * top]
        chosen = [ids == (place[0] * experts + b).astype(f32) for b in range(experts)]
        member = [jnp.sum(jnp.where(hit, 1.0, 0.0), axis=0, keepdims=True) for hit in chosen]
        table = jnp.concatenate(member + [jnp.zeros((PACK - experts, members), f32)], axis=0)
        prior = dot(table.astype(bf16), before)
        for b in range(experts):
            rank = jnp.where(member[b] > 0.0, prior[b : b + 1], -1.0)
            one = jnp.where(spot == rank, 1.0, 0.0)
            gate = jnp.sum(jnp.where(chosen[b], parts, 0.0), axis=0, keepdims=True)
            pick[g, pl.ds(b * cap, cap), :] = one.astype(bf16)
            gates[b, pl.ds(g * cap, cap), :] = jnp.broadcast_to(
                jnp.sum(one * gate, axis=1, keepdims=True), (cap, LANES)
            )
        got = dot(pick[g], rows[g, :, pl.ds(0, width)]).astype(bf16)
        for b in range(experts):
            held[b, pl.ds(g * cap, cap), :] = got[b * cap : (b + 1) * cap]
    outs = copy_all([(pick, pick_out)], out_sem.at[3])
    for b in range(experts):
        pre = dot(held[b], w_up[b])
        gate = gates[b][:, :1]
        sig = 0.5 + 0.5 * jnp.tanh(0.5 * pre)
        act = pre * sig
        hid[b] = act.astype(bf16)
        scaled[b] = (gate * act).astype(bf16)
        slope[b] = (gate * (sig + act * (1.0 - sig))).astype(bf16)
        for n, (src, dst) in enumerate(((hid, hid_out), (scaled, scaled_out), (slope, slope_out))):
            copy = pltpu.make_async_copy(src.at[b], dst.at[b], out_sem.at[n, b])
            copy.start()
            outs.append(copy)
    for copy in outs:
        copy.wait()


def down_kernel(orders, start, place, kept, scaled_in, *refs):
    outs, (rows, scaled, sent, in_sem, sem) = refs[:-5], refs[-5:]
    experts = sent.shape[2]
    arrive = copy_all([(kept.at[start + b], rows.at[b]) for b in range(experts)], in_sem.at[0])
    others = copy_all([(scaled_in.at[start + b], scaled.at[b]) for b in range(experts)], in_sem.at[1])
    parts = len(orders[0])
    half = parts // 2
    share = rows.shape[2] // parts
    cut = share // len(orders)
    copies = []
    for b in range(experts):
        arrive[b].wait()
        others[b].wait()
        for q in range(parts):
            at = pl.multiple_of((place[1] ^ q) * share, LANES)
            full = dot(rows[b, :, pl.ds(at, share)], scaled[b], FIRST).astype(bf16)
            for g, order in enumerate(orders):
                sent[g, q, b] = full[g * cut : (g + 1) * cut]
                p = order.index(q)
                copy = pltpu.make_async_copy(
                    sent.at[g, q, b], outs[2 * g + p // half].at[p % half, b], sem.at[g, q, b]
                )
                copy.start()
                copies.append(copy)
    for copy in copies:
        copy.wait()


def tail_kernel(groups, cap, width, top, place, *refs):
    steps = groups - 1
    own, mine, other, refs = refs[0], refs[1 : 1 + steps], refs[1 + steps : 1 + 2 * steps], refs[1 + 2 * steps :]
    pick, w_down, w_flip, hid, slope, meta, out_all, kept = refs[:8]
    moved, held, grads, out, block_sem, keep_sem, out_sem = refs[8:]
    experts, members = held.shape[0], moved.shape[1]
    half = members // 2
    start_blocks(place, groups, own, mine, other, moved, block_sem)
    for slot in range(groups):
        for part in range(2):
            at = pl.ds(part * half, half)
            pltpu.make_async_copy(own.at[at, :], moved.at[slot, at, :], block_sem.at[slot, part]).wait()
        group = lax.rem(place[3] - slot + groups, groups)
        first = pl.multiple_of(group * cap, PACK)
        got = dot(pick[group], moved[slot]).astype(bf16)
        for b in range(experts):
            held[b, pl.ds(first, cap), :] = got[b * cap : (b + 1) * cap]
    keep = copy_all([(held.at[b], kept.at[b]) for b in range(experts)], keep_sem)
    lane = lax.broadcasted_iota(jnp.int32, (groups * cap, LANES), 1)
    for b in range(experts):
        back = dot(held[b], w_down[b])
        gate = jnp.sum(back * hid[b].astype(f32), axis=1, keepdims=True)
        gate = jnp.where(lane == b, gate, 0.0).astype(bf16)
        grad = (back * slope[b].astype(f32)).astype(bf16)
        route = dot(grad, w_flip[b]).astype(bf16)
        for g in range(groups):
            grads[g, pl.ds(b * cap, cap), pl.ds(0, width)] = route[g * cap : (g + 1) * cap]
            grads[g, pl.ds(b * cap, cap), pl.ds(width, LANES)] = gate[g * cap : (g + 1) * cap]
    lane = lax.broadcasted_iota(jnp.int32, (members, LANES), 1)
    for g in range(groups):
        total = dot(pick[g], grads[g], FIRST)
        out[g, :, pl.ds(0, width)] = total[:, :width].astype(bf16)
        by_expert = total[:, width:]
        ids = jnp.where(lane < top, meta[pl.ds(g * members, members), :].astype(f32), -1.0)
        picked = jnp.zeros(ids.shape, f32)
        for b in range(experts):
            hit = ids == (place[0] * experts + b).astype(f32)
            picked = picked + jnp.where(hit, by_expert[:, b : b + 1], 0.0)
        out[g, :, pl.ds(width, LANES)] = picked.astype(bf16)
        copy = pltpu.make_async_copy(out.at[g], out_all.at[pl.ds(g * members, members), :], out_sem.at[g])
        copy.start()
        keep.append(copy)
    for copy in keep:
        copy.wait()


def finish_kernel(width, top, rows, token, gate):
    token[...] = rows[:, pl.ds(0, width)]
    gate[...] = rows[:, pl.ds(width, LANES)].astype(f32).T[:top].astype(bf16)


def cost(flops, nbytes):
    return pl.CostEstimate(flops=int(flops), bytes_accessed=int(nbytes), transcendentals=0)


def shards(tokens, cotangent, expert_ids, gate_weights, w_up, w_down):
    tok_rows, width = tokens.shape
    top = expert_ids.shape[1]
    ep_count, dp_count = lax.axis_size("ep"), lax.axis_size("dp")
    experts, _, hidden = w_up.shape
    base_load = tok_rows * top // (experts * ep_count)
    capacity = base_load + max(1, base_load // 16)
    total = ep_count * tok_rows
    groups = ep_count // GROUP
    members = GROUP * tok_rows
    cap = -(-GROUP * capacity // PACK) * PACK
    routes = groups * cap
    full = width + LANES
    here = lax.axis_index("ep")
    place = jnp.stack([here, lax.axis_index("dp"), here % GROUP, here // GROUP]).astype(jnp.int32)
    bits = dp_count.bit_length() - 1
    turns = 2
    share = width // dp_count

    def shape(*dims, dtype=bf16):
        return jax.ShapeDtypeStruct(dims, dtype)

    x_own = pl.pallas_call(
        functools.partial(pack_kernel, top),
        out_shape=shape(tok_rows, full),
        compiler_params=pltpu.CompilerParams(vmem_limit_bytes=SLACK * 4),
        cost_estimate=cost(0, 4 * tok_rows * width),
        name="pack",
    )(tokens, expert_ids.T, gate_weights.T)
    x_all = lax.all_gather(x_own, "ep", axis=0, tiled=True)

    def reach(p, step):
        q = p + GROUP * step if p % GROUP == 0 else p - GROUP * step
        return q if 0 <= q < ep_count else None

    def hop(value, pairs):
        return lax.ppermute(value, "ep", pairs)

    def at_group(i):
        return jnp.minimum(i, groups - 1)

    def at_expert(i):
        return jnp.clip(i - groups, 0, experts - 1)

    def at_slot(i, place):
        return lax.rem(place[3] - at_group(i) + groups, groups)

    def by_group(n):
        return pl.BlockSpec((members, n), lambda i, *_: (at_group(i), 0))

    def by_expert(rows, n):
        return pl.BlockSpec((1, rows, n), lambda i, *_: (at_expert(i), 0, 0))

    def one(kernel, name, flops, nbytes, in_specs, out_specs, out_shape, scratch_shapes):
        def run(*args):
            held = [x.inner_aval if hasattr(x, "inner_aval") else x for x in scratch_shapes]
            held += [x for x, spec in zip((*args, *out_shape), (*in_specs, *out_specs)) if spec is VMEM]
            room = sum(math.prod(x.shape) * jnp.dtype(x.dtype).itemsize for x in held if hasattr(x, "dtype") and jnp.issubdtype(x.dtype, jnp.floating))
            return pl.pallas_call(
                kernel,
                in_specs=in_specs,
                out_specs=out_specs,
                out_shape=out_shape,
                scratch_shapes=scratch_shapes,
                compiler_params=pltpu.CompilerParams(vmem_limit_bytes=room + SLACK),
                cost_estimate=cost(flops, nbytes),
                name=name,
            )(*args)

        return run

    def call(kernel, name, grid, flops, nbytes, in_specs, out_specs, out_shape, scratch_shapes, prefetch=0):
        return pl.pallas_call(
            kernel,
            grid_spec=pltpu.PrefetchScalarGridSpec(
                num_scalar_prefetch=prefetch,
                grid=(grid,),
                in_specs=in_specs,
                out_specs=out_specs,
                scratch_shapes=scratch_shapes,
            ),
            out_shape=out_shape,
            compiler_params=pltpu.CompilerParams(vmem_limit_bytes=SLACK * 4),
            cost_estimate=cost(flops, nbytes),
            name=name,
        )

    row_bytes = 2 * experts * hidden * width
    w_flip = call(
        flip_kernel,
        "flip",
        experts,
        0,
        2 * row_bytes,
        in_specs=[pl.BlockSpec((1, width, hidden), lambda b: (b, 0, 0))],
        out_specs=pl.BlockSpec((1, hidden, width), lambda b: (b, 0, 0)),
        out_shape=shape(experts, hidden, width),
        scratch_shapes=[],
    )(w_up)
    dy_own = jnp.concatenate([cotangent, hop(cotangent, [(p, p ^ 1) for p in range(ep_count)])], axis=0)
    lines = [None] + [
        [(p, reach(p, 1)) for p in range(ep_count) if None not in (reach(p, 1), reach(p, 1 - step))]
        for step in range(1, groups)
    ]
    swaps = [None] + [
        [(p, p ^ 1) for p in range(ep_count) if reach(p, -step) is not None] for step in range(1, groups)
    ]
    moving, dy_mine, dy_other = dy_own, [], []
    for step in range(1, groups - 1):
        moving = hop(moving, lines[step])
        if step == 1:
            moving, w_flip = lax.optimization_barrier((moving, w_flip))
        dy_mine.append(moving)

    act = shape(experts, routes, hidden)
    act_spec = by_expert(routes, hidden)
    pick_spec = pl.BlockSpec((1, experts * cap, members), lambda i, *_: (at_group(i), 0, 0))
    pick_flops = 2 * total * experts * cap * width
    main_flops = 2 * experts * routes * width * hidden
    act3 = pltpu.VMEM((experts, routes, hidden), bf16)
    pick_v = pltpu.VMEM((groups, experts * cap, members), bf16)
    most = max(experts, groups)

    pick, meta, hid, scaled, slope_g = one(
        functools.partial(up_kernel, groups, width, top, cap, 0),
        "up",
        pick_flops + main_flops,
        2 * total * full + row_bytes,
        [SMEM, ANY, VMEM],
        [ANY, VMEM, ANY, ANY, ANY],
        [shape(groups, experts * cap, members), shape(total, LANES), act, act, act],
        [
            pltpu.VMEM((groups, members, full), bf16),
            pltpu.VMEM((experts, routes, width), bf16),
            pltpu.VMEM((experts, routes, LANES), f32),
            pick_v,
            act3,
            act3,
            act3,
            pltpu.SemaphoreType.DMA((2, most)),
            pltpu.SemaphoreType.DMA((4, experts)),
        ],
    )(place, x_all, w_up)
    *dy_mine, hid = lax.optimization_barrier((*dy_mine, hid))
    dy_mine.append(hop(dy_mine[-1], lines[-1]))
    dy_other = [hop(part, swap) for part, swap in zip(dy_mine, swaps[1:])]

    orders = []
    for g in range(turns):
        turn = [(g + t) % bits for t in range(bits)]
        orders.append(
            tuple(sum(((p >> (bits - 1 - t)) & 1) << turn[t] for t in range(bits)) for p in range(dp_count))
        )
    orders = tuple(orders)
    cut_rows = share // turns

    def down(start, count):
        outs = one(
            functools.partial(down_kernel, orders, start),
            "down",
            16 * main_flops,
            8 * row_bytes,
            [SMEM, ANY, ANY],
            [ANY] * (2 * turns),
            [shape(dp_count // 2, count, cut_rows, hidden)] * (2 * turns),
            [
                pltpu.VMEM((count, routes, width), bf16),
                pltpu.VMEM((count, routes, hidden), bf16),
                pltpu.VMEM((turns, dp_count, count, cut_rows, hidden), bf16),
                pltpu.SemaphoreType.DMA((2, count)),
                pltpu.SemaphoreType.DMA((turns, dp_count, count)),
            ],
        )(place, kept, scaled)
        return [(outs[2 * g], outs[2 * g + 1]) for g in range(turns)]

    def exchange(state, t):
        new = []
        for g, (keep, send) in enumerate(state):
            bit = 1 << ((g + t) % bits)
            got = lax.ppermute(send, "dp", [(i, i ^ bit) for i in range(dp_count)])
            both = keep.astype(f32) + got.astype(f32)
            if t < bits - 1:
                both = both.astype(bf16)
            half = both.shape[0] // 2
            new.append((both[:half], both[half:]) if half else both[0])
        return new

    token_part, kept = one(
        functools.partial(tail_kernel, groups, cap, width, top),
        "tail",
        8 * main_flops,
        4 * row_bytes,
        [SMEM] + [ANY] * (2 * groups - 1) + [VMEM] * 6,
        [ANY, ANY],
        [shape(total, full), shape(experts, routes, width)],
        [
            pltpu.VMEM((groups, members, width), bf16),
            pltpu.VMEM((experts, routes, width), bf16),
            pltpu.VMEM((groups, experts * cap, full), bf16),
            pltpu.VMEM((groups, members, full), bf16),
            pltpu.SemaphoreType.DMA((groups, 2)),
            pltpu.SemaphoreType.DMA((experts,)),
            pltpu.SemaphoreType.DMA((groups,)),
        ],
    )(place, dy_own, *dy_mine, *dy_other, pick, w_down, w_flip, hid, slope_g, meta)
    summed = lax.psum_scatter(token_part, "ep", scatter_dimension=0, tiled=True)
    token_grad, gate_grad = pl.pallas_call(
        functools.partial(finish_kernel, width, top),
        out_shape=[shape(tok_rows, width), shape(top, tok_rows)],
        compiler_params=pltpu.CompilerParams(vmem_limit_bytes=SLACK * 4),
        cost_estimate=cost(0, 4 * tok_rows * width),
        name="finish",
    )(summed)

    counts = [experts // 2, experts - experts // 2] if experts > 1 else [experts]
    states = [down(start, count) for start, count in zip((0, counts[0]), counts)]
    for t in range(bits):
        states = [exchange(state, t) for state in states]
    token_grad, states = lax.optimization_barrier((token_grad, states))
    down_grad = jnp.concatenate([jnp.concatenate(state, axis=1) for state in states], axis=0)
    return (token_grad, gate_grad.T, down_grad)


def solution(mesh):
    return jax.shard_map(
        shards,
        mesh=mesh,
        in_specs=(
            P(("dp", "ep"), None),
            P(("dp", "ep"), None),
            P(("dp", "ep"), None),
            P(("dp", "ep"), None),
            P("ep", None, None),
            P("ep", None, None),
        ),
        out_specs=(P(("dp", "ep"), None), P(("dp", "ep"), None), P("ep", "dp", None)),
        check_vma=False,
    )
```

```python
import functools

import jax
import jax.numpy as jnp
from jax import lax
from jax.experimental import pallas as pl
from jax.experimental.pallas import tpu as pltpu
from jax.sharding import PartitionSpec as P

LANES = 128
PACK = 16
SLICES = 2
GROUP = 2
VMEM_LIMIT = 60 * 1024 * 1024
bf16, f32 = jnp.bfloat16, jnp.float32
ANY = pl.BlockSpec(memory_space=pl.ANY)
SMEM = pl.BlockSpec(memory_space=pltpu.SMEM)
VMEM = pl.BlockSpec(memory_space=pltpu.VMEM)
FIRST = (((0,), (0,)), ((), ()))


def dot(a, b, dims=(((1,), (0,)), ((), ()))):
    return lax.dot_general(a, b, dims, preferred_element_type=f32)


def pack_kernel(top, parts, tokens, cotangent, ids, gates, x_out, *dy_out):
    count, width = tokens.shape
    x_out[:, pl.ds(0, width)] = tokens[...]
    info = jnp.concatenate(
        [ids[...].astype(f32), gates[...].astype(f32), jnp.zeros((LANES - 2 * top, count), f32)], axis=0
    )
    x_out[:, pl.ds(width, LANES)] = info.T.astype(bf16)
    piece = width // parts // len(dy_out)
    for s, out in enumerate(dy_out):
        for i in range(parts):
            out[:, pl.ds(i * piece, piece)] = cotangent[:, pl.ds((i * len(dy_out) + s) * piece, piece)]


def flip_kernel(w, out):
    out[0] = w[0].T


def block_copies(place, ref, dst, sem, flip):
    half = ref.shape[0] // 2
    copies = []
    for part in range(2):
        to = (part ^ flip) * half
        if not isinstance(flip, int):
            to = pl.multiple_of(to, half)
        copies.append(
            pltpu.make_async_copy(ref.at[pl.ds(part * half, half), :], dst.at[pl.ds(to, half), :], sem.at[part])
        )
    return copies


def by_side(place, is_left, mine, other, act):
    for left in (True, False):
        for core in (True, False):
            ref = (mine if left == core else other)(left)
            if ref is not None:

                @pl.when((is_left == left) & ((place[2] == 0) == core))
                def _():
                    act(ref, 0 if left else 1)


def start_blocks(place, chips, own, mine, other, dst, sem):
    for copy in block_copies(place, own, dst.at[0], sem.at[0], place[2]):
        copy.start()
    for slot in range(1, chips):

        def pick(blocks, left):
            step = slot if left else chips - slot
            return blocks[step - 1] if step <= len(blocks) else None

        def start(ref, flip):
            for copy in block_copies(place, ref, dst.at[slot], sem.at[slot], flip):
                copy.start()

        by_side(place, place[3] >= slot, functools.partial(pick, mine), functools.partial(pick, other), start)


def copy_all(pairs, sem):
    copies = [pltpu.make_async_copy(src, dst, sem.at[n]) for n, (src, dst) in enumerate(pairs)]
    for copy in copies:
        copy.start()
    return copies


def up_kernel(groups, width, top, cap, after, place, x_all, w_up, *refs):
    refs = refs[after:]
    pick_out, meta, hid_out, scaled_out, slope_out, rows, w_v, held, gates, pick, hid, scaled, slope, sems, out_sem = refs
    experts, members = held.shape[0], rows.shape[1]
    arrive = copy_all([(x_all.at[pl.ds(g * members, members), :], rows.at[g]) for g in range(groups)], sems.at[0])
    weights = copy_all([(w_up.at[b], w_v.at[b]) for b in range(experts)], sems.at[1])
    before = lax.broadcasted_iota(jnp.int32, (members, members), 0) < lax.broadcasted_iota(
        jnp.int32, (members, members), 1
    )
    before = before.astype(bf16)
    spot = lax.broadcasted_iota(jnp.int32, (cap, members), 0).astype(f32)
    for g in range(groups):
        arrive[g].wait()
        info = rows[g, :, pl.ds(width, LANES)]
        meta[pl.ds(g * members, members), :] = info
        across = info.astype(f32).T
        ids, parts = across[:top], across[top : 2 * top]
        chosen = [ids == (place[0] * experts + b).astype(f32) for b in range(experts)]
        member = [jnp.sum(jnp.where(hit, 1.0, 0.0), axis=0, keepdims=True) for hit in chosen]
        table = jnp.concatenate(member + [jnp.zeros((PACK - experts, members), f32)], axis=0)
        prior = dot(table.astype(bf16), before)
        for b in range(experts):
            rank = jnp.where(member[b] > 0.0, prior[b : b + 1], -1.0)
            one = jnp.where(spot == rank, 1.0, 0.0)
            gate = jnp.sum(jnp.where(chosen[b], parts, 0.0), axis=0, keepdims=True)
            pick[g, pl.ds(b * cap, cap), :] = one.astype(bf16)
            gates[b, pl.ds(g * cap, cap), :] = jnp.broadcast_to(
                jnp.sum(one * gate, axis=1, keepdims=True), (cap, LANES)
            )
        got = dot(pick[g], rows[g, :, pl.ds(0, width)]).astype(bf16)
        for b in range(experts):
            held[b, pl.ds(g * cap, cap), :] = got[b * cap : (b + 1) * cap]
    outs = copy_all([(pick, pick_out)], out_sem.at[3])
    for b in range(experts):
        weights[b].wait()
        pre = dot(held[b], w_v[b])
        gate = gates[b][:, :1]
        sig = 0.5 + 0.5 * jnp.tanh(0.5 * pre)
        act = pre * sig
        hid[b] = act.astype(bf16)
        scaled[b] = (gate * act).astype(bf16)
        slope[b] = (gate * (sig + act * (1.0 - sig))).astype(bf16)
        for n, (src, dst) in enumerate(((hid, hid_out), (scaled, scaled_out), (slope, slope_out))):
            copy = pltpu.make_async_copy(src.at[b], dst.at[b], out_sem.at[n, b])
            copy.start()
            outs.append(copy)
    for copy in outs:
        copy.wait()


def slice_copies(weights, dst, pieces, sem):
    return [
        copy_all([(weights.at[b, pl.ds(at, size), :], dst.at[b, pl.ds(to, size), :]) for at, size, to in pieces], sem.at[b])
        for b in range(weights.shape[0])
    ]


def pick_blocks(place, cap, blocks, pick, moved, held, sem):
    groups, members = moved.shape[0], moved.shape[1]
    half = members // 2
    own = blocks[0]
    for slot in range(groups):
        for part in range(2):
            at = pl.ds(part * half, half)
            pltpu.make_async_copy(own.at[at, :], moved.at[slot, at, :], sem.at[slot, part]).wait()
        group = lax.rem(place[3] - slot + groups, groups)
        first = pl.multiple_of(group * cap, PACK)
        got = dot(pick[group], moved[slot]).astype(bf16)
        for b in range(held.shape[0]):
            held[b, pl.ds(first, cap), :] = got[b * cap : (b + 1) * cap]


def down_rows(orders, place, b, rows, scaled, made, outs, sem):
    made[b] = dot(rows, scaled, FIRST).astype(bf16)
    parts = len(orders[0])
    half = parts // 2
    piece = made.shape[1] // parts
    cut = piece // len(orders)
    copies = []
    for g, order in enumerate(orders):
        for p, q in enumerate(order):
            at = pl.multiple_of((place[1] ^ q) * piece + g * cut, PACK)
            out = outs[2 * g + p // half].at[p % half, b]
            copies.append(pltpu.make_async_copy(made.at[b, pl.ds(at, cut), :], out, sem.at[g, q, b]))
            copies[-1].start()
    return copies


def mid_kernel(groups, cap, orders, pieces, place, *refs):
    count = 2 * groups - 1
    blocks, refs = refs[:count], refs[count:]
    pick_in, w_down, scaled_in, back_out = refs[:4]
    outs, refs = refs[4 : 4 + 2 * len(orders)], refs[4 + 2 * len(orders) :]
    pick, moved, held, down_v, scaled, back, made, block_sem, w_sem, sems, sem = refs
    experts = held.shape[0]
    first_pick = copy_all([(pick_in, pick)], sems.at[0])
    start_blocks(place, groups, blocks[0], blocks[1:groups], blocks[groups:], moved, block_sem)
    weights = slice_copies(w_down, down_v, pieces, w_sem)
    others = copy_all([(scaled_in.at[b], scaled.at[b]) for b in range(experts)], sems.at[1])
    first_pick[0].wait()
    pick_blocks(place, cap, blocks, pick, moved, held, block_sem)
    copies = []
    for b in range(experts):
        others[b].wait()
        copies += down_rows(orders, place, b, held[b], scaled[b], made, outs, sem)
    for b in range(experts):
        for copy in weights[b]:
            copy.wait()
        back[b] = dot(held[b], down_v[b])
        copies.append(pltpu.make_async_copy(back.at[b], back_out.at[b], sems.at[2, b]))
        copies[-1].start()
    for copy in copies:
        copy.wait()


def down_kernel(orders, after, place, kept, scaled_in, *refs):
    outs, (rows, scaled, made, in_sem, sem) = refs[after:-5], refs[-5:]
    experts = made.shape[0]
    arrive = copy_all([(kept.at[b], rows.at[b]) for b in range(experts)], in_sem.at[0])
    others = copy_all([(scaled_in.at[b], scaled.at[b]) for b in range(experts)], in_sem.at[1])
    copies = []
    for b in range(experts):
        arrive[b].wait()
        others[b].wait()
        copies += down_rows(orders, place, b, rows[b], scaled[b], made, outs, sem)
    for copy in copies:
        copy.wait()


def tail_kernel(groups, cap, width, top, pieces, has_before, place, *refs):
    count = 2 * groups - 1
    blocks, refs = refs[:count], refs[count:]
    pick_in, w_down, w_flip, hid_in, slope_in, meta = refs[:6]
    before_in = refs[6] if has_before else None
    out_all, kept = refs[6 + has_before : 8 + has_before]
    refs = refs[8 + has_before :]
    pick, moved, held, grads, out, down_v, flip_v, hid, slope, before, block_sem, w_sem, sems, keep_sem, out_sem = refs
    experts, members = held.shape[0], moved.shape[1]
    first_pick = copy_all([(pick_in, pick)], sems.at[0])
    start_blocks(place, groups, blocks[0], blocks[1:groups], blocks[groups:], moved, block_sem)
    weights = slice_copies(w_down, down_v, pieces, w_sem)
    sources = [(hid_in, hid), (slope_in, slope), (w_flip, flip_v)] + ([(before_in, before)] if has_before else [])
    loads = [
        copy_all([(src.at[b], dst.at[b]) for b in range(experts)], sems.at[n]) for n, (src, dst) in enumerate(sources, 1)
    ]
    first_pick[0].wait()
    pick_blocks(place, cap, blocks, pick, moved, held, block_sem)
    keep = copy_all([(held.at[b], kept.at[b]) for b in range(experts)], keep_sem)
    lane = lax.broadcasted_iota(jnp.int32, (groups * cap, LANES), 1)
    for b in range(experts):
        for copy in weights[b] + [load[b] for load in loads]:
            copy.wait()
        back = dot(held[b], down_v[b])
        if has_before:
            back = back + before[b]
        gate = jnp.sum(back * hid[b].astype(f32), axis=1, keepdims=True)
        gate = jnp.where(lane == b, gate, 0.0).astype(bf16)
        grad = (back * slope[b].astype(f32)).astype(bf16)
        route = dot(grad, flip_v[b]).astype(bf16)
        for g in range(groups):
            grads[g, pl.ds(b * cap, cap), pl.ds(0, width)] = route[g * cap : (g + 1) * cap]
            grads[g, pl.ds(b * cap, cap), pl.ds(width, LANES)] = gate[g * cap : (g + 1) * cap]
    lane = lax.broadcasted_iota(jnp.int32, (members, LANES), 1)
    for g in range(groups):
        total = dot(pick[g], grads[g], FIRST)
        out[g, :, pl.ds(0, width)] = total[:, :width].astype(bf16)
        by_expert = total[:, width:]
        ids = jnp.where(lane < top, meta[pl.ds(g * members, members), :].astype(f32), -1.0)
        picked = jnp.zeros(ids.shape, f32)
        for b in range(experts):
            hit = ids == (place[0] * experts + b).astype(f32)
            picked = picked + jnp.where(hit, by_expert[:, b : b + 1], 0.0)
        out[g, :, pl.ds(width, LANES)] = picked.astype(bf16)
        copy = pltpu.make_async_copy(out.at[g], out_all.at[pl.ds(g * members, members), :], out_sem.at[g])
        copy.start()
        keep.append(copy)
    for copy in keep:
        copy.wait()


def add_kernel(*refs):
    count = len(refs) // 4
    for n in range(count):
        total = (refs[2 * n][...].astype(f32) + refs[2 * n + 1][...].astype(f32)).astype(bf16)
        half = total.shape[0] // 2
        refs[2 * count + 2 * n][...] = total[:half]
        refs[2 * count + 2 * n + 1][...] = total[half:]


def finish_kernel(width, top, rows, token, gate):
    token[...] = rows[:, pl.ds(0, width)]
    gate[...] = rows[:, pl.ds(width, LANES)].astype(f32).T[:top].astype(bf16)


def cost(flops, nbytes):
    return pl.CostEstimate(flops=int(flops), bytes_accessed=int(nbytes), transcendentals=0)


def shards(tokens, cotangent, expert_ids, gate_weights, w_up, w_down):
    tok_rows, width = tokens.shape
    top = expert_ids.shape[1]
    ep_count, dp_count = lax.axis_size("ep"), lax.axis_size("dp")
    experts, _, hidden = w_up.shape
    base_load = tok_rows * top // (experts * ep_count)
    capacity = base_load + max(1, base_load // 16)
    total = ep_count * tok_rows
    groups = ep_count // GROUP
    members = GROUP * tok_rows
    cap = -(-GROUP * capacity // PACK) * PACK
    routes = groups * cap
    full = width + LANES
    here = lax.axis_index("ep")
    place = jnp.stack([here, lax.axis_index("dp"), here % GROUP, here // GROUP]).astype(jnp.int32)
    bits = dp_count.bit_length() - 1
    turns = 2
    share = width // dp_count
    slices = SLICES if share % (SLICES * LANES) == 0 else 1
    piece = share // slices
    cols = dp_count * piece

    def shape(*dims, dtype=bf16):
        return jax.ShapeDtypeStruct(dims, dtype)

    x_own, *dy_own = pl.pallas_call(
        functools.partial(pack_kernel, top, dp_count),
        out_shape=[shape(tok_rows, full)] + [shape(tok_rows, cols)] * slices,
        compiler_params=pltpu.CompilerParams(vmem_limit_bytes=VMEM_LIMIT),
        cost_estimate=cost(0, 8 * tok_rows * width),
        name="pack",
    )(tokens, cotangent, expert_ids.T, gate_weights.T)
    x_all = lax.all_gather(x_own, "ep", axis=0, tiled=True)

    def reach(p, step):
        q = p + GROUP * step if p % GROUP == 0 else p - GROUP * step
        return q if 0 <= q < ep_count else None

    def hop(value, pairs):
        return lax.ppermute(value, "ep", pairs)

    def at_group(i):
        return jnp.minimum(i, groups - 1)

    def at_expert(i):
        return jnp.clip(i - groups, 0, experts - 1)

    def at_slot(i, place):
        return lax.rem(place[3] - at_group(i) + groups, groups)

    def by_group(n):
        return pl.BlockSpec((members, n), lambda i, *_: (at_group(i), 0))

    def by_expert(rows, n):
        return pl.BlockSpec((1, rows, n), lambda i, *_: (at_expert(i), 0, 0))

    def call(kernel, name, grid, flops, nbytes, in_specs, out_specs, out_shape, scratch_shapes, prefetch=0):
        return pl.pallas_call(
            kernel,
            grid_spec=pltpu.PrefetchScalarGridSpec(
                num_scalar_prefetch=prefetch,
                grid=(grid,),
                in_specs=in_specs,
                out_specs=out_specs,
                scratch_shapes=scratch_shapes,
            ),
            out_shape=out_shape,
            compiler_params=pltpu.CompilerParams(vmem_limit_bytes=VMEM_LIMIT),
            cost_estimate=cost(flops, nbytes),
            name=name,
        )

    row_bytes = 2 * experts * hidden * width
    w_flip = call(
        flip_kernel,
        "flip",
        experts,
        0,
        2 * row_bytes,
        in_specs=[pl.BlockSpec((1, width, hidden), lambda b: (b, 0, 0))],
        out_specs=pl.BlockSpec((1, hidden, width), lambda b: (b, 0, 0)),
        out_shape=shape(experts, hidden, width),
        scratch_shapes=[],
    )(w_up)
    dy_own = [jnp.concatenate([part, hop(part, [(p, p ^ 1) for p in range(ep_count)])], axis=0) for part in dy_own]
    lines = [None] + [
        [(p, reach(p, 1)) for p in range(ep_count) if None not in (reach(p, 1), reach(p, 1 - step))]
        for step in range(1, groups)
    ]
    swaps = [None] + [
        [(p, p ^ 1) for p in range(ep_count) if reach(p, -step) is not None] for step in range(1, groups)
    ]
    moving, dy_mine, dy_other = dy_own, [], []
    for step in range(1, groups - 1):
        moving = [hop(part, lines[step]) for part in moving]
        if step == 1:
            moving[0], w_flip = lax.optimization_barrier((moving[0], w_flip))
        dy_mine.append(moving)

    act = shape(experts, routes, hidden)
    act_spec = by_expert(routes, hidden)
    pick_spec = pl.BlockSpec((1, experts * cap, members), lambda i, *_: (at_group(i), 0, 0))
    pick_flops = 2 * total * experts * cap * width
    main_flops = 2 * experts * routes * width * hidden
    act3 = pltpu.VMEM((experts, routes, hidden), bf16)
    pick_v = pltpu.VMEM((groups, experts * cap, members), bf16)
    most = max(experts, groups)

    def one(kernel, name, flops, nbytes, in_specs, out_specs, out_shape, scratch_shapes):
        return pl.pallas_call(
            kernel,
            in_specs=in_specs,
            out_specs=out_specs,
            out_shape=out_shape,
            scratch_shapes=scratch_shapes,
            compiler_params=pltpu.CompilerParams(vmem_limit_bytes=VMEM_LIMIT),
            cost_estimate=cost(flops, nbytes),
            name=name,
        )

    pick, meta, hid, scaled, slope_g = one(
        functools.partial(up_kernel, groups, width, top, cap, 0),
        "up",
        pick_flops + main_flops,
        2 * total * full + row_bytes,
        [SMEM, ANY, ANY],
        [ANY, pl.BlockSpec(memory_space=pltpu.VMEM), ANY, ANY, ANY],
        [shape(groups, experts * cap, members), shape(total, LANES), act, act, act],
        [
            pltpu.VMEM((groups, members, full), bf16),
            pltpu.VMEM((experts, width, hidden), bf16),
            pltpu.VMEM((experts, routes, width), bf16),
            pltpu.VMEM((experts, routes, LANES), f32),
            pick_v,
            act3,
            act3,
            act3,
            pltpu.SemaphoreType.DMA((2, most)),
            pltpu.SemaphoreType.DMA((4, experts)),
        ],
    )(place, x_all, w_up)
    dy_mine, hid = lax.optimization_barrier((dy_mine, hid))
    dy_mine.append([hop(part, lines[-1]) for part in dy_mine[-1]])
    dy_other = [[hop(part, swap) for part in row] for row, swap in zip(dy_mine, swaps[1:])]
    blocks = [[dy_own[s]] + [row[s] for row in dy_mine] + [row[s] for row in dy_other] for s in range(slices)]

    orders = []
    for g in range(turns):
        turn = [(g + t) % bits for t in range(bits)]
        orders.append(
            tuple(sum(((p >> (bits - 1 - t)) & 1) << turn[t] for t in range(bits)) for p in range(dp_count))
        )
    orders = tuple(orders)
    cut_rows = piece // turns

    down_outs = [shape(dp_count // 2, experts, cut_rows, hidden)] * (2 * turns)
    made = pltpu.VMEM((experts, cols, hidden), bf16)
    made_sem = pltpu.SemaphoreType.DMA((turns, dp_count, experts))
    held = pltpu.VMEM((experts, routes, cols), bf16)
    moved = pltpu.VMEM((groups, members, cols), bf16)
    down_v = pltpu.VMEM((experts, cols, hidden), bf16)
    back_v = pltpu.VMEM((experts, routes, hidden), f32)
    block_sem = pltpu.SemaphoreType.DMA((groups, 2))
    w_sem = pltpu.SemaphoreType.DMA((experts, dp_count))

    def pieces(s):
        return tuple((i * share + s * piece, piece, i * piece) for i in range(dp_count))

    def pairs(outs):
        return [(outs[2 * g], outs[2 * g + 1]) for g in range(turns)]

    def exchange(state, t):
        got = [
            lax.ppermute(send, "dp", [(i, i ^ (1 << ((g + t) % bits))) for i in range(dp_count)])
            for g, (_, send) in enumerate(state)
        ]
        if t == bits - 1:
            return [keep.astype(f32)[0] + more.astype(f32)[0] for (keep, _), more in zip(state, got)]
        operands = [x for (keep, _), more in zip(state, got) for x in (keep, more)]
        half = shape(operands[0].shape[0] // 2, *operands[0].shape[1:])
        return pairs(
            one(
                add_kernel,
                "add",
                0,
                sum(4 * x.size for x in operands),
                [VMEM] * len(operands),
                [VMEM] * len(operands),
                [half] * len(operands),
                [],
            )(*operands)
        )

    states, before = [], []
    for s in range(slices - 1):
        back, *outs = one(
            functools.partial(mid_kernel, groups, cap, orders, pieces(s)),
            "mid",
            main_flops,
            row_bytes,
            [SMEM] + [ANY] * (2 * groups + 2),
            [ANY] * (1 + 2 * turns),
            [shape(experts, routes, hidden, dtype=f32)] + down_outs,
            [pick_v, moved, held, down_v, act3, back_v, made, block_sem, w_sem, pltpu.SemaphoreType.DMA((3, most)), made_sem],
        )(place, *blocks[s], pick, w_down, scaled)
        before = [back]
        states.append(exchange(pairs(outs), 0) if bits > 1 else pairs(outs))
    token_part, kept = one(
        functools.partial(tail_kernel, groups, cap, width, top, pieces(slices - 1), len(before)),
        "tail",
        100 * main_flops,
        4 * row_bytes,
        [SMEM] + [ANY] * (2 * groups - 1) + [ANY] * 5 + [VMEM] + [ANY] * len(before),
        [ANY, ANY],
        [shape(total, full), shape(experts, routes, cols)],
        [
            pick_v,
            moved,
            held,
            pltpu.VMEM((groups, experts * cap, full), bf16),
            pltpu.VMEM((groups, members, full), bf16),
            down_v,
            pltpu.VMEM((experts, hidden, width), bf16),
            act3,
            act3,
            back_v,
            block_sem,
            w_sem,
            pltpu.SemaphoreType.DMA((5, experts)),
            pltpu.SemaphoreType.DMA((experts,)),
            pltpu.SemaphoreType.DMA((groups,)),
        ],
    )(place, *blocks[-1], pick, w_down, w_flip, hid, slope_g, meta, *before)
    summed = lax.psum_scatter(token_part, "ep", scatter_dimension=0, tiled=True)
    token_grad, gate_grad = pl.pallas_call(
        functools.partial(finish_kernel, width, top),
        out_shape=[shape(tok_rows, width), shape(top, tok_rows)],
        compiler_params=pltpu.CompilerParams(vmem_limit_bytes=VMEM_LIMIT),
        cost_estimate=cost(0, 4 * tok_rows * width),
        name="finish",
    )(summed)

    after = [pair[0] for state in states for pair in state] if bits > 1 else []
    outs = one(
        functools.partial(down_kernel, orders, len(after)),
        "down",
        400 * main_flops,
        row_bytes,
        [SMEM] + [ANY] * (2 + len(after)),
        [ANY] * (2 * turns),
        down_outs,
        [held, act3, made, pltpu.SemaphoreType.DMA((2, experts)), made_sem],
    )(place, kept, scaled, *after)
    if bits > 1:
        states.append(exchange(pairs(outs), 0))
        keeps = [pair[0] for pair in states[-1]]
        token_grad, keeps = lax.optimization_barrier((token_grad, keeps))
        states[-1] = [(keep, pair[1]) for keep, pair in zip(keeps, states[-1])]
    else:
        states.append(pairs(outs))
    for t in range(1 if bits > 1 else 0, bits):
        states = [exchange(state, t) for state in states]
    down_grad = jnp.concatenate([part for state in states for part in state], axis=1)
    return (token_grad, gate_grad.T, down_grad)


def solution(mesh):
    return jax.shard_map(
        shards,
        mesh=mesh,
        in_specs=(
            P(("dp", "ep"), None),
            P(("dp", "ep"), None),
            P(("dp", "ep"), None),
            P(("dp", "ep"), None),
            P("ep", None, None),
            P("ep", None, None),
        ),
        out_specs=(P(("dp", "ep"), None), P(("dp", "ep"), None), P("ep", "dp", None)),
        check_vma=False,
    )
```

```python
import functools

import jax
import jax.numpy as jnp
from jax import lax
from jax.experimental import pallas as pl
from jax.experimental.pallas import tpu as pltpu
from jax.sharding import PartitionSpec as P

LANES = 128
PACK = 16
GROUP = 2
VMEM_LIMIT = 60 * 1024 * 1024
bf16, f32 = jnp.bfloat16, jnp.float32
ANY = pl.BlockSpec(memory_space=pl.ANY)
SMEM = pl.BlockSpec(memory_space=pltpu.SMEM)
VMEM = pl.BlockSpec(memory_space=pltpu.VMEM)
FIRST = (((0,), (0,)), ((), ()))


def dot(a, b, dims=(((1,), (0,)), ((), ()))):
    return lax.dot_general(a, b, dims, preferred_element_type=f32)


def pack_kernel(top, tokens, ids, gates, x_out):
    count, width = tokens.shape
    x_out[:, pl.ds(0, width)] = tokens[...]
    info = jnp.concatenate(
        [ids[...].astype(f32), gates[...].astype(f32), jnp.zeros((LANES - 2 * top, count), f32)], axis=0
    )
    x_out[:, pl.ds(width, LANES)] = info.T.astype(bf16)


def flip_kernel(w, out):
    out[0] = w[0].T


def block_copies(place, ref, dst, sem, flip):
    half = ref.shape[0] // 2
    copies = []
    for part in range(2):
        to = (part ^ flip) * half
        if not isinstance(flip, int):
            to = pl.multiple_of(to, half)
        copies.append(
            pltpu.make_async_copy(ref.at[pl.ds(part * half, half), :], dst.at[pl.ds(to, half), :], sem.at[part])
        )
    return copies


def by_side(place, is_left, mine, other, act):
    for left in (True, False):
        for core in (True, False):
            ref = (mine if left == core else other)(left)
            if ref is not None:

                @pl.when((is_left == left) & ((place[2] == 0) == core))
                def _():
                    act(ref, 0 if left else 1)


def start_blocks(place, chips, own, mine, other, dst, sem):
    for copy in block_copies(place, own, dst.at[0], sem.at[0], place[2]):
        copy.start()
    for slot in range(1, chips):

        def pick(blocks, left):
            step = slot if left else chips - slot
            return blocks[step - 1] if step <= len(blocks) else None

        def start(ref, flip):
            for copy in block_copies(place, ref, dst.at[slot], sem.at[slot], flip):
                copy.start()

        by_side(place, place[3] >= slot, functools.partial(pick, mine), functools.partial(pick, other), start)


def copy_all(pairs, sem):
    copies = [pltpu.make_async_copy(src, dst, sem.at[n]) for n, (src, dst) in enumerate(pairs)]
    for copy in copies:
        copy.start()
    return copies


def up_kernel(groups, width, top, cap, after, place, x_all, w_up, *refs):
    refs = refs[after:]
    pick_out, meta, hid_out, scaled_out, slope_out, rows, w_v, held, gates, pick, hid, scaled, slope, sems, out_sem = refs
    experts, members = held.shape[0], rows.shape[1]
    arrive = copy_all([(x_all.at[pl.ds(g * members, members), :], rows.at[g]) for g in range(groups)], sems.at[0])
    weights = copy_all([(w_up.at[b], w_v.at[b]) for b in range(experts)], sems.at[1])
    before = lax.broadcasted_iota(jnp.int32, (members, members), 0) < lax.broadcasted_iota(
        jnp.int32, (members, members), 1
    )
    before = before.astype(bf16)
    spot = lax.broadcasted_iota(jnp.int32, (cap, members), 0).astype(f32)
    for g in range(groups):
        arrive[g].wait()
        info = rows[g, :, pl.ds(width, LANES)]
        meta[pl.ds(g * members, members), :] = info
        across = info.astype(f32).T
        ids, parts = across[:top], across[top : 2 * top]
        chosen = [ids == (place[0] * experts + b).astype(f32) for b in range(experts)]
        member = [jnp.sum(jnp.where(hit, 1.0, 0.0), axis=0, keepdims=True) for hit in chosen]
        table = jnp.concatenate(member + [jnp.zeros((PACK - experts, members), f32)], axis=0)
        prior = dot(table.astype(bf16), before)
        for b in range(experts):
            rank = jnp.where(member[b] > 0.0, prior[b : b + 1], -1.0)
            one = jnp.where(spot == rank, 1.0, 0.0)
            gate = jnp.sum(jnp.where(chosen[b], parts, 0.0), axis=0, keepdims=True)
            pick[g, pl.ds(b * cap, cap), :] = one.astype(bf16)
            gates[b, pl.ds(g * cap, cap), :] = jnp.broadcast_to(
                jnp.sum(one * gate, axis=1, keepdims=True), (cap, LANES)
            )
        got = dot(pick[g], rows[g, :, pl.ds(0, width)]).astype(bf16)
        for b in range(experts):
            held[b, pl.ds(g * cap, cap), :] = got[b * cap : (b + 1) * cap]
    outs = copy_all([(pick, pick_out)], out_sem.at[3])
    for b in range(experts):
        weights[b].wait()
        pre = dot(held[b], w_v[b])
        gate = gates[b][:, :1]
        sig = 0.5 + 0.5 * jnp.tanh(0.5 * pre)
        act = pre * sig
        hid[b] = act.astype(bf16)
        scaled[b] = (gate * act).astype(bf16)
        slope[b] = (gate * (sig + act * (1.0 - sig))).astype(bf16)
        for n, (src, dst) in enumerate(((hid, hid_out), (scaled, scaled_out), (slope, slope_out))):
            copy = pltpu.make_async_copy(src.at[b], dst.at[b], out_sem.at[n, b])
            copy.start()
            outs.append(copy)
    for copy in outs:
        copy.wait()


def down_kernel(orders, start, place, kept, scaled_in, *refs):
    outs, (rows, scaled, sent, in_sem, sem) = refs[:-5], refs[-5:]
    experts = sent.shape[2]
    arrive = copy_all([(kept.at[start + b], rows.at[b]) for b in range(experts)], in_sem.at[0])
    others = copy_all([(scaled_in.at[start + b], scaled.at[b]) for b in range(experts)], in_sem.at[1])
    parts = len(orders[0])
    half = parts // 2
    share = rows.shape[2] // parts
    cut = share // len(orders)
    copies = []
    for b in range(experts):
        arrive[b].wait()
        others[b].wait()
        for q in range(parts):
            at = pl.multiple_of((place[1] ^ q) * share, LANES)
            full = dot(rows[b, :, pl.ds(at, share)], scaled[b], FIRST).astype(bf16)
            for g, order in enumerate(orders):
                sent[g, q, b] = full[g * cut : (g + 1) * cut]
                p = order.index(q)
                copy = pltpu.make_async_copy(
                    sent.at[g, q, b], outs[2 * g + p // half].at[p % half, b], sem.at[g, q, b]
                )
                copy.start()
                copies.append(copy)
    for copy in copies:
        copy.wait()


def tail_kernel(groups, cap, width, top, place, *refs):
    steps = groups - 1
    own, mine, other, refs = refs[0], refs[1 : 1 + steps], refs[1 + steps : 1 + 2 * steps], refs[1 + 2 * steps :]
    pick_in, w_down, w_flip, hid_in, slope_in, meta, out_all, kept = refs[:8]
    pick, moved, held, grads, out, down_v, flip_v, hid, slope, block_sem, sems, keep_sem, out_sem = refs[8:]
    experts, members = held.shape[0], moved.shape[1]
    half = members // 2
    first_pick = copy_all([(pick_in, pick)], sems.at[0])
    start_blocks(place, groups, own, mine, other, moved, block_sem)
    loads = [
        copy_all([(src.at[b], dst.at[b]) for b in range(experts)], sems.at[n])
        for n, (src, dst) in enumerate(((w_down, down_v), (hid_in, hid), (slope_in, slope), (w_flip, flip_v)), 1)
    ]
    first_pick[0].wait()
    for slot in range(groups):
        for part in range(2):
            at = pl.ds(part * half, half)
            pltpu.make_async_copy(own.at[at, :], moved.at[slot, at, :], block_sem.at[slot, part]).wait()
        group = lax.rem(place[3] - slot + groups, groups)
        first = pl.multiple_of(group * cap, PACK)
        got = dot(pick[group], moved[slot]).astype(bf16)
        for b in range(experts):
            held[b, pl.ds(first, cap), :] = got[b * cap : (b + 1) * cap]
    keep = copy_all([(held.at[b], kept.at[b]) for b in range(experts)], keep_sem)
    lane = lax.broadcasted_iota(jnp.int32, (groups * cap, LANES), 1)
    for b in range(experts):
        for load in loads[:3]:
            load[b].wait()
        back = dot(held[b], down_v[b])
        gate = jnp.sum(back * hid[b].astype(f32), axis=1, keepdims=True)
        gate = jnp.where(lane == b, gate, 0.0).astype(bf16)
        grad = (back * slope[b].astype(f32)).astype(bf16)
        loads[3][b].wait()
        route = dot(grad, flip_v[b]).astype(bf16)
        for g in range(groups):
            grads[g, pl.ds(b * cap, cap), pl.ds(0, width)] = route[g * cap : (g + 1) * cap]
            grads[g, pl.ds(b * cap, cap), pl.ds(width, LANES)] = gate[g * cap : (g + 1) * cap]
    lane = lax.broadcasted_iota(jnp.int32, (members, LANES), 1)
    for g in range(groups):
        total = dot(pick[g], grads[g], FIRST)
        out[g, :, pl.ds(0, width)] = total[:, :width].astype(bf16)
        by_expert = total[:, width:]
        ids = jnp.where(lane < top, meta[pl.ds(g * members, members), :].astype(f32), -1.0)
        picked = jnp.zeros(ids.shape, f32)
        for b in range(experts):
            hit = ids == (place[0] * experts + b).astype(f32)
            picked = picked + jnp.where(hit, by_expert[:, b : b + 1], 0.0)
        out[g, :, pl.ds(width, LANES)] = picked.astype(bf16)
        copy = pltpu.make_async_copy(out.at[g], out_all.at[pl.ds(g * members, members), :], out_sem.at[g])
        copy.start()
        keep.append(copy)
    for copy in keep:
        copy.wait()


def put_kernel(start, *refs):
    *pairs, out, total, sem = refs
    count = total.shape[1]
    cut = total.shape[2]
    copies = []
    for g in range(total.shape[0]):
        keep, got = pairs[2 * g], pairs[2 * g + 1]
        total[g] = keep[0].astype(f32) + got[0].astype(f32)
        copies.append(
            pltpu.make_async_copy(
                total.at[g], out.at[pl.ds(start, count), pl.ds(g * cut, cut), :], sem.at[g]
            )
        )
        copies[-1].start()
    for copy in copies:
        copy.wait()


def finish_kernel(width, top, rows, token, gate):
    token[...] = rows[:, pl.ds(0, width)]
    gate[...] = rows[:, pl.ds(width, LANES)].astype(f32).T[:top].astype(bf16)


def cost(flops, nbytes):
    return pl.CostEstimate(flops=int(flops), bytes_accessed=int(nbytes), transcendentals=0)


def shards(tokens, cotangent, expert_ids, gate_weights, w_up, w_down):
    tok_rows, width = tokens.shape
    top = expert_ids.shape[1]
    ep_count, dp_count = lax.axis_size("ep"), lax.axis_size("dp")
    experts, _, hidden = w_up.shape
    base_load = tok_rows * top // (experts * ep_count)
    capacity = base_load + max(1, base_load // 16)
    total = ep_count * tok_rows
    groups = ep_count // GROUP
    members = GROUP * tok_rows
    cap = -(-GROUP * capacity // PACK) * PACK
    routes = groups * cap
    full = width + LANES
    here = lax.axis_index("ep")
    place = jnp.stack([here, lax.axis_index("dp"), here % GROUP, here // GROUP]).astype(jnp.int32)
    bits = dp_count.bit_length() - 1
    turns = 2
    share = width // dp_count

    def shape(*dims, dtype=bf16):
        return jax.ShapeDtypeStruct(dims, dtype)

    x_own = pl.pallas_call(
        functools.partial(pack_kernel, top),
        out_shape=shape(tok_rows, full),
        compiler_params=pltpu.CompilerParams(vmem_limit_bytes=VMEM_LIMIT),
        cost_estimate=cost(0, 4 * tok_rows * width),
        name="pack",
    )(tokens, expert_ids.T, gate_weights.T)
    x_all = lax.all_gather(x_own, "ep", axis=0, tiled=True)

    def reach(p, step):
        q = p + GROUP * step if p % GROUP == 0 else p - GROUP * step
        return q if 0 <= q < ep_count else None

    def hop(value, pairs):
        return lax.ppermute(value, "ep", pairs)

    def at_group(i):
        return jnp.minimum(i, groups - 1)

    def at_expert(i):
        return jnp.clip(i - groups, 0, experts - 1)

    def at_slot(i, place):
        return lax.rem(place[3] - at_group(i) + groups, groups)

    def by_group(n):
        return pl.BlockSpec((members, n), lambda i, *_: (at_group(i), 0))

    def by_expert(rows, n):
        return pl.BlockSpec((1, rows, n), lambda i, *_: (at_expert(i), 0, 0))

    def call(kernel, name, grid, flops, nbytes, in_specs, out_specs, out_shape, scratch_shapes, prefetch=0):
        return pl.pallas_call(
            kernel,
            grid_spec=pltpu.PrefetchScalarGridSpec(
                num_scalar_prefetch=prefetch,
                grid=(grid,),
                in_specs=in_specs,
                out_specs=out_specs,
                scratch_shapes=scratch_shapes,
            ),
            out_shape=out_shape,
            compiler_params=pltpu.CompilerParams(vmem_limit_bytes=VMEM_LIMIT),
            cost_estimate=cost(flops, nbytes),
            name=name,
        )

    row_bytes = 2 * experts * hidden * width
    w_flip = call(
        flip_kernel,
        "flip",
        experts,
        0,
        2 * row_bytes,
        in_specs=[pl.BlockSpec((1, width, hidden), lambda b: (b, 0, 0))],
        out_specs=pl.BlockSpec((1, hidden, width), lambda b: (b, 0, 0)),
        out_shape=shape(experts, hidden, width),
        scratch_shapes=[],
    )(w_up)
    dy_own = jnp.concatenate([cotangent, hop(cotangent, [(p, p ^ 1) for p in range(ep_count)])], axis=0)
    lines = [None] + [
        [(p, reach(p, 1)) for p in range(ep_count) if None not in (reach(p, 1), reach(p, 1 - step))]
        for step in range(1, groups)
    ]
    swaps = [None] + [
        [(p, p ^ 1) for p in range(ep_count) if reach(p, -step) is not None] for step in range(1, groups)
    ]
    far = [(p, reach(p, 2)) for p in range(ep_count) if reach(p, 2) is not None]
    dy_mine = [hop(dy_own, lines[1])]
    far_own, w_flip = lax.optimization_barrier((dy_own, w_flip))
    if groups > 2:
        dy_mine.append(hop(far_own, far))
    for step in range(3, groups - 1):
        dy_mine.append(hop(dy_mine[-1], lines[step]))

    act = shape(experts, routes, hidden)
    act_spec = by_expert(routes, hidden)
    pick_spec = pl.BlockSpec((1, experts * cap, members), lambda i, *_: (at_group(i), 0, 0))
    pick_flops = 2 * total * experts * cap * width
    main_flops = 2 * experts * routes * width * hidden
    act3 = pltpu.VMEM((experts, routes, hidden), bf16)
    pick_v = pltpu.VMEM((groups, experts * cap, members), bf16)
    most = max(experts, groups)

    def one(kernel, name, flops, nbytes, in_specs, out_specs, out_shape, scratch_shapes):
        return pl.pallas_call(
            kernel,
            in_specs=in_specs,
            out_specs=out_specs,
            out_shape=out_shape,
            scratch_shapes=scratch_shapes,
            compiler_params=pltpu.CompilerParams(vmem_limit_bytes=VMEM_LIMIT),
            cost_estimate=cost(flops, nbytes),
            name=name,
        )

    pick, meta, hid, scaled, slope_g = one(
        functools.partial(up_kernel, groups, width, top, cap, 0),
        "up",
        pick_flops + main_flops,
        2 * total * full + row_bytes,
        [SMEM, ANY, ANY],
        [ANY, pl.BlockSpec(memory_space=pltpu.VMEM), ANY, ANY, ANY],
        [shape(groups, experts * cap, members), shape(total, LANES), act, act, act],
        [
            pltpu.VMEM((groups, members, full), bf16),
            pltpu.VMEM((experts, width, hidden), bf16),
            pltpu.VMEM((experts, routes, width), bf16),
            pltpu.VMEM((experts, routes, LANES), f32),
            pick_v,
            act3,
            act3,
            act3,
            pltpu.SemaphoreType.DMA((2, most)),
            pltpu.SemaphoreType.DMA((4, experts)),
        ],
    )(place, x_all, w_up)
    *dy_mine, hid = lax.optimization_barrier((*dy_mine, hid))
    if groups > 3:
        dy_mine.append(hop(dy_mine[-1], lines[-1]))
    dy_other = [hop(part, swap) for part, swap in zip(dy_mine, swaps[1:])]

    orders = []
    for g in range(turns):
        turn = [(g + t) % bits for t in range(bits)]
        orders.append(
            tuple(sum(((p >> (bits - 1 - t)) & 1) << turn[t] for t in range(bits)) for p in range(dp_count))
        )
    orders = tuple(orders)
    cut_rows = share // turns

    def down(start, count):
        outs = one(
            functools.partial(down_kernel, orders, start),
            "down",
            16 * main_flops,
            8 * row_bytes,
            [SMEM, ANY, ANY],
            [ANY] * (2 * turns),
            [shape(dp_count // 2, count, cut_rows, hidden)] * (2 * turns),
            [
                pltpu.VMEM((count, routes, width), bf16),
                pltpu.VMEM((count, routes, hidden), bf16),
                pltpu.VMEM((turns, dp_count, count, cut_rows, hidden), bf16),
                pltpu.SemaphoreType.DMA((2, count)),
                pltpu.SemaphoreType.DMA((turns, dp_count, count)),
            ],
        )(place, kept, scaled)
        return [(outs[2 * g], outs[2 * g + 1]) for g in range(turns)]

    def exchange(state, t):
        new = []
        for g, (keep, send) in enumerate(state):
            bit = 1 << ((g + t) % bits)
            got = lax.ppermute(send, "dp", [(i, i ^ bit) for i in range(dp_count)])
            both = keep.astype(f32) + got.astype(f32)
            if t < bits - 1:
                both = both.astype(bf16)
            half = both.shape[0] // 2
            new.append((both[:half], both[half:]) if half else both[0])
        return new

    token_part, kept = one(
        functools.partial(tail_kernel, groups, cap, width, top),
        "tail",
        8 * main_flops,
        4 * row_bytes,
        [SMEM] + [ANY] * (2 * groups - 1) + [ANY] * 5 + [pl.BlockSpec(memory_space=pltpu.VMEM)],
        [ANY, ANY],
        [shape(total, full), shape(experts, routes, width)],
        [
            pick_v,
            pltpu.VMEM((groups, members, width), bf16),
            pltpu.VMEM((experts, routes, width), bf16),
            pltpu.VMEM((groups, experts * cap, full), bf16),
            pltpu.VMEM((groups, members, full), bf16),
            pltpu.VMEM((experts, width, hidden), bf16),
            pltpu.VMEM((experts, hidden, width), bf16),
            act3,
            act3,
            pltpu.SemaphoreType.DMA((groups, 2)),
            pltpu.SemaphoreType.DMA((5, experts)),
            pltpu.SemaphoreType.DMA((experts,)),
            pltpu.SemaphoreType.DMA((groups,)),
        ],
    )(place, dy_own, *dy_mine, *dy_other, pick, w_down, w_flip, hid, slope_g, meta)
    summed = lax.psum_scatter(token_part, "ep", scatter_dimension=0, tiled=True)
    token_grad, gate_grad = pl.pallas_call(
        functools.partial(finish_kernel, width, top),
        out_shape=[shape(tok_rows, width), shape(top, tok_rows)],
        compiler_params=pltpu.CompilerParams(vmem_limit_bytes=VMEM_LIMIT),
        cost_estimate=cost(0, 4 * tok_rows * width),
        name="finish",
    )(summed)

    counts = [experts // 2, experts - experts // 2] if experts > 1 else [experts]
    states = [down(start, count) for start, count in zip((0, counts[0]), counts)]
    for t in range(bits - 1):
        states = [exchange(state, t) for state in states]
    last = bits - 1
    states = [
        [
            (keep, lax.ppermute(send, "dp", [(i, i ^ (1 << ((g + last) % bits))) for i in range(dp_count)]))
            for g, (keep, send) in enumerate(state)
        ]
        for state in states
    ]
    keeps = [keep for keep, _ in states[-1]]
    token_grad, keeps = lax.optimization_barrier((token_grad, keeps))
    states[-1] = [(keep, got) for keep, (_, got) in zip(keeps, states[-1])]
    down_grad, start = None, 0
    for count, state in zip(counts, states):
        operands = [x for pair in state for x in pair]
        dest = [] if down_grad is None else [down_grad]

        def put(*refs, start=start, skip=len(dest), used=len(operands)):
            put_kernel(start, *refs[:used], *refs[used + skip :])

        down_grad = pl.pallas_call(
            put,
            in_specs=[VMEM] * len(operands) + [ANY] * len(dest),
            out_specs=ANY,
            out_shape=shape(experts, share, hidden, dtype=f32),
            input_output_aliases={len(operands): 0} if dest else {},
            scratch_shapes=[
                pltpu.VMEM((turns, count, cut_rows, hidden), f32),
                pltpu.SemaphoreType.DMA((turns,)),
            ],
            compiler_params=pltpu.CompilerParams(vmem_limit_bytes=VMEM_LIMIT // 2),
            cost_estimate=cost(0, 4 * experts * share * hidden),
            name="put",
        )(*operands, *dest)
        start += count
    return (token_grad, gate_grad.T, down_grad)


def solution(mesh):
    return jax.shard_map(
        shards,
        mesh=mesh,
        in_specs=(
            P(("dp", "ep"), None),
            P(("dp", "ep"), None),
            P(("dp", "ep"), None),
            P(("dp", "ep"), None),
            P("ep", None, None),
            P("ep", None, None),
        ),
        out_specs=(P(("dp", "ep"), None), P(("dp", "ep"), None), P("ep", "dp", None)),
        check_vma=False,
    )
```

```python
import functools

import jax
import jax.numpy as jnp
from jax import lax
from jax.experimental import pallas as pl
from jax.experimental.pallas import tpu as pltpu
from jax.sharding import PartitionSpec as P

LANES = 128
PACK = 16
GROUP = 2
VMEM_LIMIT = 60 * 1024 * 1024
bf16, f32 = jnp.bfloat16, jnp.float32
ANY = pl.BlockSpec(memory_space=pl.ANY)
SMEM = pl.BlockSpec(memory_space=pltpu.SMEM)
VMEM = pl.BlockSpec(memory_space=pltpu.VMEM)
FIRST = (((0,), (0,)), ((), ()))


def dot(a, b, dims=(((1,), (0,)), ((), ()))):
    return lax.dot_general(a, b, dims, preferred_element_type=f32)


def pack_kernel(top, tokens, ids, gates, x_out):
    count, width = tokens.shape
    x_out[:, pl.ds(0, width)] = tokens[...]
    info = jnp.concatenate(
        [ids[...].astype(f32), gates[...].astype(f32), jnp.zeros((LANES - 2 * top, count), f32)], axis=0
    )
    x_out[:, pl.ds(width, LANES)] = info.T.astype(bf16)


def flip_kernel(w, out):
    out[0] = w[0].T


def start_blocks(place, chips, own, mine, other, dst, sem):
    half = dst.shape[1] // 2

    def start(pair, slot, flip):
        for part in range(2):
            to = (part ^ flip) * half
            if not isinstance(flip, int):
                to = pl.multiple_of(to, half)
            pltpu.make_async_copy(pair[part], dst.at[slot, pl.ds(to, half), :], sem.at[slot, part]).start()

    start(own, 0, place[2])
    for slot in range(1, chips):
        for left in (True, False):
            for core in (True, False):
                pair = (mine if left == core else other)[(slot if left else chips - slot) - 1]

                @pl.when(((place[3] >= slot) == left) & ((place[2] == 0) == core))
                def _():
                    start(pair, slot, 0 if left else 1)


def copy_all(pairs, sem):
    copies = [pltpu.make_async_copy(src, dst, sem.at[n]) for n, (src, dst) in enumerate(pairs)]
    for copy in copies:
        copy.start()
    return copies


def up_kernel(groups, width, top, cap, after, place, x_all, w_up, *refs):
    refs = refs[after:]
    pick_out, meta, hid_out, scaled_out, slope_out, rows, w_v, held, gates, pick, hid, scaled, slope, sems, out_sem = refs
    experts, members = held.shape[0], rows.shape[1]
    arrive = copy_all([(x_all.at[pl.ds(g * members, members), :], rows.at[g]) for g in range(groups)], sems.at[0])
    weights = copy_all([(w_up.at[b], w_v.at[b]) for b in range(experts)], sems.at[1])
    before = lax.broadcasted_iota(jnp.int32, (members, members), 0) < lax.broadcasted_iota(
        jnp.int32, (members, members), 1
    )
    before = before.astype(bf16)
    spot = lax.broadcasted_iota(jnp.int32, (cap, members), 0).astype(f32)
    for g in range(groups):
        arrive[g].wait()
        info = rows[g, :, pl.ds(width, LANES)]
        meta[pl.ds(g * members, members), :] = info
        across = info.astype(f32).T
        ids, parts = across[:top], across[top : 2 * top]
        chosen = [ids == (place[0] * experts + b).astype(f32) for b in range(experts)]
        member = [jnp.sum(jnp.where(hit, 1.0, 0.0), axis=0, keepdims=True) for hit in chosen]
        table = jnp.concatenate(member + [jnp.zeros((PACK - experts, members), f32)], axis=0)
        prior = dot(table.astype(bf16), before)
        for b in range(experts):
            rank = jnp.where(member[b] > 0.0, prior[b : b + 1], -1.0)
            one = jnp.where(spot == rank, 1.0, 0.0)
            gate = jnp.sum(jnp.where(chosen[b], parts, 0.0), axis=0, keepdims=True)
            pick[g, pl.ds(b * cap, cap), :] = one.astype(bf16)
            gates[b, pl.ds(g * cap, cap), :] = jnp.broadcast_to(
                jnp.sum(one * gate, axis=1, keepdims=True), (cap, LANES)
            )
        got = dot(pick[g], rows[g, :, pl.ds(0, width)]).astype(bf16)
        for b in range(experts):
            held[b, pl.ds(g * cap, cap), :] = got[b * cap : (b + 1) * cap]
    outs = copy_all([(pick, pick_out)], out_sem.at[3])
    for b in range(experts):
        weights[b].wait()
        pre = dot(held[b], w_v[b])
        gate = gates[b][:, :1]
        sig = 0.5 + 0.5 * jnp.tanh(0.5 * pre)
        act = pre * sig
        hid[b] = act.astype(bf16)
        scaled[b] = (gate * act).astype(bf16)
        slope[b] = (gate * (sig + act * (1.0 - sig))).astype(bf16)
        for n, (src, dst) in enumerate(((hid, hid_out), (scaled, scaled_out), (slope, slope_out))):
            copy = pltpu.make_async_copy(src.at[b], dst.at[b], out_sem.at[n, b])
            copy.start()
            outs.append(copy)
    for copy in outs:
        copy.wait()


def down_kernel(orders, start, place, kept, scaled_in, *refs):
    outs, (rows, scaled, sent, in_sem, sem) = refs[:-5], refs[-5:]
    experts = sent.shape[2]
    arrive = copy_all([(kept.at[start + b], rows.at[b]) for b in range(experts)], in_sem.at[0])
    others = copy_all([(scaled_in.at[start + b], scaled.at[b]) for b in range(experts)], in_sem.at[1])
    parts = len(orders[0])
    half = parts // 2
    share = rows.shape[2] // parts
    cut = share // len(orders)
    copies = []
    for b in range(experts):
        arrive[b].wait()
        others[b].wait()
        for q in range(parts):
            at = pl.multiple_of((place[1] ^ q) * share, LANES)
            full = dot(rows[b, :, pl.ds(at, share)], scaled[b], FIRST).astype(bf16)
            for g, order in enumerate(orders):
                sent[g, q, b] = full[g * cut : (g + 1) * cut]
                p = order.index(q)
                copy = pltpu.make_async_copy(
                    sent.at[g, q, b], outs[2 * g + p // half].at[p % half, b], sem.at[g, q, b]
                )
                copy.start()
                copies.append(copy)
    for copy in copies:
        copy.wait()


def tail_kernel(groups, cap, width, top, place, *refs):
    count = 2 * groups - 1
    halves = [(refs[2 * n], refs[2 * n + 1]) for n in range(count)]
    own, mine, other, refs = halves[0], halves[1:groups], halves[groups:], refs[2 * count :]
    pick_in, w_down, w_flip, hid_in, slope_in, meta, out_all, kept = refs[:8]
    pick, moved, held, grads, out, down_v, flip_v, hid, slope, block_sem, sems, keep_sem, out_sem = refs[8:]
    experts, members = held.shape[0], moved.shape[1]
    half = members // 2
    first_pick = copy_all([(pick_in, pick)], sems.at[0])
    start_blocks(place, groups, own, mine, other, moved, block_sem)
    loads = [
        copy_all([(src.at[b], dst.at[b]) for b in range(experts)], sems.at[n])
        for n, (src, dst) in enumerate(((w_down, down_v), (hid_in, hid), (slope_in, slope), (w_flip, flip_v)), 1)
    ]
    first_pick[0].wait()
    for slot in range(groups):
        for part in range(2):
            at = pl.ds(part * half, half)
            pltpu.make_async_copy(own[0], moved.at[slot, at, :], block_sem.at[slot, part]).wait()
        group = lax.rem(place[3] - slot + groups, groups)
        first = pl.multiple_of(group * cap, PACK)
        got = dot(pick[group], moved[slot]).astype(bf16)
        for b in range(experts):
            held[b, pl.ds(first, cap), :] = got[b * cap : (b + 1) * cap]
    keep = copy_all([(held.at[b], kept.at[b]) for b in range(experts)], keep_sem)
    lane = lax.broadcasted_iota(jnp.int32, (groups * cap, LANES), 1)
    for b in range(experts):
        for load in loads[:3]:
            load[b].wait()
        back = dot(held[b], down_v[b])
        gate = jnp.sum(back * hid[b].astype(f32), axis=1, keepdims=True)
        gate = jnp.where(lane == b, gate, 0.0).astype(bf16)
        grad = (back * slope[b].astype(f32)).astype(bf16)
        loads[3][b].wait()
        route = dot(grad, flip_v[b]).astype(bf16)
        for g in range(groups):
            grads[g, pl.ds(b * cap, cap), pl.ds(0, width)] = route[g * cap : (g + 1) * cap]
            grads[g, pl.ds(b * cap, cap), pl.ds(width, LANES)] = gate[g * cap : (g + 1) * cap]
    lane = lax.broadcasted_iota(jnp.int32, (members, LANES), 1)
    for g in range(groups):
        total = dot(pick[g], grads[g], FIRST)
        out[g, :, pl.ds(0, width)] = total[:, :width].astype(bf16)
        by_expert = total[:, width:]
        ids = jnp.where(lane < top, meta[pl.ds(g * members, members), :].astype(f32), -1.0)
        picked = jnp.zeros(ids.shape, f32)
        for b in range(experts):
            hit = ids == (place[0] * experts + b).astype(f32)
            picked = picked + jnp.where(hit, by_expert[:, b : b + 1], 0.0)
        out[g, :, pl.ds(width, LANES)] = picked.astype(bf16)
        copy = pltpu.make_async_copy(out.at[g], out_all.at[pl.ds(g * members, members), :], out_sem.at[g])
        copy.start()
        keep.append(copy)
    for copy in keep:
        copy.wait()


def put_kernel(start, *refs):
    *pairs, out, total, sem = refs
    count = total.shape[1]
    cut = total.shape[2]
    copies = []
    for g in range(total.shape[0]):
        keep, got = pairs[2 * g], pairs[2 * g + 1]
        total[g] = keep[0].astype(f32) + got[0].astype(f32)
        copies.append(
            pltpu.make_async_copy(
                total.at[g], out.at[pl.ds(start, count), pl.ds(g * cut, cut), :], sem.at[g]
            )
        )
        copies[-1].start()
    for copy in copies:
        copy.wait()


def finish_kernel(width, top, rows, token, gate):
    token[...] = rows[:, pl.ds(0, width)]
    gate[...] = rows[:, pl.ds(width, LANES)].astype(f32).T[:top].astype(bf16)


def cost(flops, nbytes):
    return pl.CostEstimate(flops=int(flops), bytes_accessed=int(nbytes), transcendentals=0)


def shards(tokens, cotangent, expert_ids, gate_weights, w_up, w_down):
    tok_rows, width = tokens.shape
    top = expert_ids.shape[1]
    ep_count, dp_count = lax.axis_size("ep"), lax.axis_size("dp")
    experts, _, hidden = w_up.shape
    base_load = tok_rows * top // (experts * ep_count)
    capacity = base_load + max(1, base_load // 16)
    total = ep_count * tok_rows
    groups = ep_count // GROUP
    members = GROUP * tok_rows
    cap = -(-GROUP * capacity // PACK) * PACK
    routes = groups * cap
    full = width + LANES
    here = lax.axis_index("ep")
    place = jnp.stack([here, lax.axis_index("dp"), here % GROUP, here // GROUP]).astype(jnp.int32)
    bits = dp_count.bit_length() - 1
    turns = 2
    share = width // dp_count

    def shape(*dims, dtype=bf16):
        return jax.ShapeDtypeStruct(dims, dtype)

    x_own = pl.pallas_call(
        functools.partial(pack_kernel, top),
        out_shape=shape(tok_rows, full),
        compiler_params=pltpu.CompilerParams(vmem_limit_bytes=VMEM_LIMIT),
        cost_estimate=cost(0, 4 * tok_rows * width),
        name="pack",
    )(tokens, expert_ids.T, gate_weights.T)
    x_all = lax.all_gather(x_own, "ep", axis=0, tiled=True)

    def reach(p, step):
        q = p + GROUP * step if p % GROUP == 0 else p - GROUP * step
        return q if 0 <= q < ep_count else None

    def hop(value, pairs):
        return lax.ppermute(value, "ep", pairs)

    def at_group(i):
        return jnp.minimum(i, groups - 1)

    def at_expert(i):
        return jnp.clip(i - groups, 0, experts - 1)

    def at_slot(i, place):
        return lax.rem(place[3] - at_group(i) + groups, groups)

    def by_group(n):
        return pl.BlockSpec((members, n), lambda i, *_: (at_group(i), 0))

    def by_expert(rows, n):
        return pl.BlockSpec((1, rows, n), lambda i, *_: (at_expert(i), 0, 0))

    def call(kernel, name, grid, flops, nbytes, in_specs, out_specs, out_shape, scratch_shapes, prefetch=0):
        return pl.pallas_call(
            kernel,
            grid_spec=pltpu.PrefetchScalarGridSpec(
                num_scalar_prefetch=prefetch,
                grid=(grid,),
                in_specs=in_specs,
                out_specs=out_specs,
                scratch_shapes=scratch_shapes,
            ),
            out_shape=out_shape,
            compiler_params=pltpu.CompilerParams(vmem_limit_bytes=VMEM_LIMIT),
            cost_estimate=cost(flops, nbytes),
            name=name,
        )

    row_bytes = 2 * experts * hidden * width
    w_flip = call(
        flip_kernel,
        "flip",
        experts,
        0,
        2 * row_bytes,
        in_specs=[pl.BlockSpec((1, width, hidden), lambda b: (b, 0, 0))],
        out_specs=pl.BlockSpec((1, hidden, width), lambda b: (b, 0, 0)),
        out_shape=shape(experts, hidden, width),
        scratch_shapes=[],
    )(w_up)
    def at_group(i):
        return jnp.minimum(i, groups - 1)

    def at_expert(i):
        return jnp.clip(i - groups, 0, experts - 1)

    def at_slot(i, place):
        return lax.rem(place[3] - at_group(i) + groups, groups)

    def by_group(n):
        return pl.BlockSpec((members, n), lambda i, *_: (at_group(i), 0))

    def by_expert(rows, n):
        return pl.BlockSpec((1, rows, n), lambda i, *_: (at_expert(i), 0, 0))

    def call(kernel, name, grid, flops, nbytes, in_specs, out_specs, out_shape, scratch_shapes, prefetch=0):
        return pl.pallas_call(
            kernel,
            grid_spec=pltpu.PrefetchScalarGridSpec(
                num_scalar_prefetch=prefetch,
                grid=(grid,),
                in_specs=in_specs,
                out_specs=out_specs,
                scratch_shapes=scratch_shapes,
            ),
            out_shape=out_shape,
            compiler_params=pltpu.CompilerParams(vmem_limit_bytes=VMEM_LIMIT),
            cost_estimate=cost(flops, nbytes),
            name=name,
        )

    row_bytes = 2 * experts * hidden * width
    w_flip = call(
        flip_kernel,
        "flip",
        experts,
        0,
        2 * row_bytes,
        in_specs=[pl.BlockSpec((1, width, hidden), lambda b: (b, 0, 0))],
        out_specs=pl.BlockSpec((1, hidden, width), lambda b: (b, 0, 0)),
        out_shape=shape(experts, hidden, width),
        scratch_shapes=[],
    )(w_up)
    dy_own = jnp.concatenate([cotangent, hop(cotangent, [(p, p ^ 1) for p in range(ep_count)])], axis=0)
    lines = [None] + [
        [(p, reach(p, 1)) for p in range(ep_count) if None not in (reach(p, 1), reach(p, 1 - step))]
        for step in range(1, groups)
    ]
    swaps = [None] + [
        [(p, p ^ 1) for p in range(ep_count) if reach(p, -step) is not None] for step in range(1, groups)
    ]
    dy_own = [cotangent, hop(cotangent, [(p, p ^ 1) for p in range(ep_count)])]
    dy_mine = [[hop(part, lines[1]) for part in dy_own]]
    dy_mine[0][0], w_flip = lax.optimization_barrier((dy_mine[0][0], w_flip))
    for step in range(2, groups - 1):
        dy_mine.append([hop(part, lines[step]) for part in dy_mine[-1]])
    last_own = hop(dy_mine[-1][0], lines[-1])
    dy_other = [[hop(part, swaps[1]) for part in dy_mine[0]]]

    act = shape(experts, routes, hidden)
    act_spec = by_expert(routes, hidden)
    pick_spec = pl.BlockSpec((1, experts * cap, members), lambda i, *_: (at_group(i), 0, 0))
    pick_flops = 2 * total * experts * cap * width
    main_flops = 2 * experts * routes * width * hidden
    act3 = pltpu.VMEM((experts, routes, hidden), bf16)
    pick_v = pltpu.VMEM((groups, experts * cap, members), bf16)
    most = max(experts, groups)

    def one(kernel, name, flops, nbytes, in_specs, out_specs, out_shape, scratch_shapes):
        return pl.pallas_call(
            kernel,
            in_specs=in_specs,
            out_specs=out_specs,
            out_shape=out_shape,
            scratch_shapes=scratch_shapes,
            compiler_params=pltpu.CompilerParams(vmem_limit_bytes=VMEM_LIMIT),
            cost_estimate=cost(flops, nbytes),
            name=name,
        )

    up_after = dy_other[0] + dy_mine[-1][:1]
    pick, meta, hid, scaled, slope_g = one(
        functools.partial(up_kernel, groups, width, top, cap, len(up_after)),
        "up",
        pick_flops + main_flops,
        2 * total * full + row_bytes,
        [SMEM, ANY, ANY] + [ANY] * len(up_after),
        [ANY, pl.BlockSpec(memory_space=pltpu.VMEM), ANY, ANY, ANY],
        [shape(groups, experts * cap, members), shape(total, LANES), act, act, act],
        [
            pltpu.VMEM((groups, members, full), bf16),
            pltpu.VMEM((experts, width, hidden), bf16),
            pltpu.VMEM((experts, routes, width), bf16),
            pltpu.VMEM((experts, routes, LANES), f32),
            pick_v,
            act3,
            act3,
            act3,
            pltpu.SemaphoreType.DMA((2, most)),
            pltpu.SemaphoreType.DMA((4, experts)),
        ],
    )(place, x_all, w_up, *up_after)
    dy_mine, hid = lax.optimization_barrier((dy_mine, hid))
    dy_mine.append([last_own, hop(dy_mine[-1][1], lines[-1])])
    dy_other += [[hop(part, swap) for part in row] for row, swap in zip(dy_mine[1:], swaps[2:])]
    blocks = [part for row in [dy_own] + dy_mine + dy_other for part in row]

    orders = []
    for g in range(turns):
        turn = [(g + t) % bits for t in range(bits)]
        orders.append(
            tuple(sum(((p >> (bits - 1 - t)) & 1) << turn[t] for t in range(bits)) for p in range(dp_count))
        )
    orders = tuple(orders)
    cut_rows = share // turns

    def down(start, count):
        outs = one(
            functools.partial(down_kernel, orders, start),
            "down",
            16 * main_flops,
            8 * row_bytes,
            [SMEM, ANY, ANY],
            [ANY] * (2 * turns),
            [shape(dp_count // 2, count, cut_rows, hidden)] * (2 * turns),
            [
                pltpu.VMEM((count, routes, width), bf16),
                pltpu.VMEM((count, routes, hidden), bf16),
                pltpu.VMEM((turns, dp_count, count, cut_rows, hidden), bf16),
                pltpu.SemaphoreType.DMA((2, count)),
                pltpu.SemaphoreType.DMA((turns, dp_count, count)),
            ],
        )(place, kept, scaled)
        return [(outs[2 * g], outs[2 * g + 1]) for g in range(turns)]

    def exchange(state, t):
        new = []
        for g, (keep, send) in enumerate(state):
            bit = 1 << ((g + t) % bits)
            got = lax.ppermute(send, "dp", [(i, i ^ bit) for i in range(dp_count)])
            both = keep.astype(f32) + got.astype(f32)
            if t < bits - 1:
                both = both.astype(bf16)
            half = both.shape[0] // 2
            new.append((both[:half], both[half:]) if half else both[0])
        return new

    token_part, kept = one(
        functools.partial(tail_kernel, groups, cap, width, top),
        "tail",
        8 * main_flops,
        4 * row_bytes,
        [SMEM] + [ANY] * (4 * groups - 2) + [ANY] * 5 + [pl.BlockSpec(memory_space=pltpu.VMEM)],
        [ANY, ANY],
        [shape(total, full), shape(experts, routes, width)],
        [
            pick_v,
            pltpu.VMEM((groups, members, width), bf16),
            pltpu.VMEM((experts, routes, width), bf16),
            pltpu.VMEM((groups, experts * cap, full), bf16),
            pltpu.VMEM((groups, members, full), bf16),
            pltpu.VMEM((experts, width, hidden), bf16),
            pltpu.VMEM((experts, hidden, width), bf16),
            act3,
            act3,
            pltpu.SemaphoreType.DMA((groups, 2)),
            pltpu.SemaphoreType.DMA((5, experts)),
            pltpu.SemaphoreType.DMA((experts,)),
            pltpu.SemaphoreType.DMA((groups,)),
        ],
    )(place, *blocks, pick, w_down, w_flip, hid, slope_g, meta)
    summed = lax.psum_scatter(token_part, "ep", scatter_dimension=0, tiled=True)
    token_grad, gate_grad = pl.pallas_call(
        functools.partial(finish_kernel, width, top),
        out_shape=[shape(tok_rows, width), shape(top, tok_rows)],
        compiler_params=pltpu.CompilerParams(vmem_limit_bytes=VMEM_LIMIT),
        cost_estimate=cost(0, 4 * tok_rows * width),
        name="finish",
    )(summed)

    counts = [experts // 2, experts - experts // 2] if experts > 1 else [experts]
    states = [down(start, count) for start, count in zip((0, counts[0]), counts)]
    for t in range(bits - 1):
        states = [exchange(state, t) for state in states]
    last = bits - 1
    states = [
        [
            (keep, lax.ppermute(send, "dp", [(i, i ^ (1 << ((g + last) % bits))) for i in range(dp_count)]))
            for g, (keep, send) in enumerate(state)
        ]
        for state in states
    ]
    keeps = [keep for keep, _ in states[-1]]
    token_grad, keeps = lax.optimization_barrier((token_grad, keeps))
    states[-1] = [(keep, got) for keep, (_, got) in zip(keeps, states[-1])]
    down_grad, start = None, 0
    for count, state in zip(counts, states):
        operands = [x for pair in state for x in pair]
        dest = [] if down_grad is None else [down_grad]

        def put(*refs, start=start, skip=len(dest), used=len(operands)):
            put_kernel(start, *refs[:used], *refs[used + skip :])

        down_grad = pl.pallas_call(
            put,
            in_specs=[VMEM] * len(operands) + [ANY] * len(dest),
            out_specs=ANY,
            out_shape=shape(experts, share, hidden, dtype=f32),
            input_output_aliases={len(operands): 0} if dest else {},
            scratch_shapes=[
                pltpu.VMEM((turns, count, cut_rows, hidden), f32),
                pltpu.SemaphoreType.DMA((turns,)),
            ],
            compiler_params=pltpu.CompilerParams(vmem_limit_bytes=VMEM_LIMIT // 2),
            cost_estimate=cost(0, 4 * experts * share * hidden),
            name="put",
        )(*operands, *dest)
        start += count
    return (token_grad, gate_grad.T, down_grad)


def solution(mesh):
    return jax.shard_map(
        shards,
        mesh=mesh,
        in_specs=(
            P(("dp", "ep"), None),
            P(("dp", "ep"), None),
            P(("dp", "ep"), None),
            P(("dp", "ep"), None),
            P("ep", None, None),
            P("ep", None, None),
        ),
        out_specs=(P(("dp", "ep"), None), P(("dp", "ep"), None), P("ep", "dp", None)),
        check_vma=False,
    )
```

```python
import functools

import jax
import jax.numpy as jnp
from jax import lax
from jax.experimental import pallas as pl
from jax.experimental.pallas import tpu as pltpu
from jax.sharding import PartitionSpec as P

LANES = 128
PACK = 16
GROUP = 2
VMEM_LIMIT = 60 * 1024 * 1024
bf16, f32 = jnp.bfloat16, jnp.float32
ANY = pl.BlockSpec(memory_space=pl.ANY)
SMEM = pl.BlockSpec(memory_space=pltpu.SMEM)
VMEM = pl.BlockSpec(memory_space=pltpu.VMEM)
FIRST = (((0,), (0,)), ((), ()))


def dot(a, b, dims=(((1,), (0,)), ((), ()))):
    return lax.dot_general(a, b, dims, preferred_element_type=f32)


def pack_kernel(top, tokens, ids, gates, x_out):
    count, width = tokens.shape
    x_out[:, pl.ds(0, width)] = tokens[...]
    info = jnp.concatenate(
        [ids[...].astype(f32), gates[...].astype(f32), jnp.zeros((LANES - 2 * top, count), f32)], axis=0
    )
    x_out[:, pl.ds(width, LANES)] = info.T.astype(bf16)


def flip_kernel(w, out):
    out[0] = w[0].T


def start_blocks(place, chips, own, mine, other, dst, sem):
    half = dst.shape[1] // 2

    def start(pair, slot, flip):
        for part in range(2):
            to = (part ^ flip) * half
            if not isinstance(flip, int):
                to = pl.multiple_of(to, half)
            pltpu.make_async_copy(pair[part], dst.at[slot, pl.ds(to, half), :], sem.at[slot, part]).start()

    start(own, 0, place[2])
    for slot in range(1, chips):
        for left in (True, False):
            for core in (True, False):
                pair = (mine if left == core else other)[(slot if left else chips - slot) - 1]

                @pl.when(((place[3] >= slot) == left) & ((place[2] == 0) == core))
                def _():
                    start(pair, slot, 0 if left else 1)


def copy_all(pairs, sem):
    copies = [pltpu.make_async_copy(src, dst, sem.at[n]) for n, (src, dst) in enumerate(pairs)]
    for copy in copies:
        copy.start()
    return copies


def up_kernel(groups, width, top, cap, after, place, x_all, w_up, *refs):
    refs = refs[after:]
    pick_out, meta, hid_out, scaled_out, slope_out, rows, w_v, held, gates, pick, hid, scaled, slope, sems, out_sem = refs
    experts, members = held.shape[0], rows.shape[1]
    arrive = copy_all([(x_all.at[pl.ds(g * members, members), :], rows.at[g]) for g in range(groups)], sems.at[0])
    weights = copy_all([(w_up.at[b], w_v.at[b]) for b in range(experts)], sems.at[1])
    before = lax.broadcasted_iota(jnp.int32, (members, members), 0) < lax.broadcasted_iota(
        jnp.int32, (members, members), 1
    )
    before = before.astype(bf16)
    spot = lax.broadcasted_iota(jnp.int32, (cap, members), 0).astype(f32)
    for g in range(groups):
        arrive[g].wait()
        info = rows[g, :, pl.ds(width, LANES)]
        meta[pl.ds(g * members, members), :] = info
        across = info.astype(f32).T
        ids, parts = across[:top], across[top : 2 * top]
        chosen = [ids == (place[0] * experts + b).astype(f32) for b in range(experts)]
        member = [jnp.sum(jnp.where(hit, 1.0, 0.0), axis=0, keepdims=True) for hit in chosen]
        table = jnp.concatenate(member + [jnp.zeros((PACK - experts, members), f32)], axis=0)
        prior = dot(table.astype(bf16), before)
        for b in range(experts):
            rank = jnp.where(member[b] > 0.0, prior[b : b + 1], -1.0)
            one = jnp.where(spot == rank, 1.0, 0.0)
            gate = jnp.sum(jnp.where(chosen[b], parts, 0.0), axis=0, keepdims=True)
            pick[g, pl.ds(b * cap, cap), :] = one.astype(bf16)
            gates[b, pl.ds(g * cap, cap), :] = jnp.broadcast_to(
                jnp.sum(one * gate, axis=1, keepdims=True), (cap, LANES)
            )
        got = dot(pick[g], rows[g, :, pl.ds(0, width)]).astype(bf16)
        for b in range(experts):
            held[b, pl.ds(g * cap, cap), :] = got[b * cap : (b + 1) * cap]
    outs = copy_all([(pick, pick_out)], out_sem.at[3])
    for b in range(experts):
        weights[b].wait()
        pre = dot(held[b], w_v[b])
        gate = gates[b][:, :1]
        sig = 0.5 + 0.5 * jnp.tanh(0.5 * pre)
        act = pre * sig
        hid[b] = act.astype(bf16)
        scaled[b] = (gate * act).astype(bf16)
        slope[b] = (gate * (sig + act * (1.0 - sig))).astype(bf16)
        for n, (src, dst) in enumerate(((hid, hid_out), (scaled, scaled_out), (slope, slope_out))):
            copy = pltpu.make_async_copy(src.at[b], dst.at[b], out_sem.at[n, b])
            copy.start()
            outs.append(copy)
    for copy in outs:
        copy.wait()


def down_kernel(orders, start, after, place, kept, scaled_in, *refs):
    outs, (rows, scaled, sent, in_sem, sem) = refs[after:-5], refs[-5:]
    experts = sent.shape[2]
    arrive = copy_all([(kept.at[start + b], rows.at[b]) for b in range(experts)], in_sem.at[0])
    others = copy_all([(scaled_in.at[start + b], scaled.at[b]) for b in range(experts)], in_sem.at[1])
    parts = len(orders[0])
    half = parts // 2
    share = rows.shape[2] // parts
    cut = share // len(orders)
    copies = []
    for b in range(experts):
        arrive[b].wait()
        others[b].wait()
        for q in range(parts):
            at = pl.multiple_of((place[1] ^ q) * share, LANES)
            full = dot(rows[b, :, pl.ds(at, share)], scaled[b], FIRST).astype(bf16)
            for g, order in enumerate(orders):
                sent[g, q, b] = full[g * cut : (g + 1) * cut]
                p = order.index(q)
                copy = pltpu.make_async_copy(
                    sent.at[g, q, b], outs[2 * g + p // half].at[p % half, b], sem.at[g, q, b]
                )
                copy.start()
                copies.append(copy)
    for copy in copies:
        copy.wait()


def tail_kernel(groups, cap, width, top, place, *refs):
    count = 2 * groups - 1
    halves = [(refs[2 * n], refs[2 * n + 1]) for n in range(count)]
    own, mine, other, refs = halves[0], halves[1:groups], halves[groups:], refs[2 * count :]
    pick_in, w_down, w_flip, hid_in, slope_in, meta, out_all, kept = refs[:8]
    pick, moved, held, grads, out, down_v, flip_v, hid, slope, block_sem, sems, keep_sem, out_sem = refs[8:]
    experts, members = held.shape[0], moved.shape[1]
    half = members // 2
    first_pick = copy_all([(pick_in, pick)], sems.at[0])
    start_blocks(place, groups, own, mine, other, moved, block_sem)
    loads = [
        copy_all([(src.at[b], dst.at[b]) for b in range(experts)], sems.at[n])
        for n, (src, dst) in enumerate(((w_down, down_v), (hid_in, hid), (slope_in, slope), (w_flip, flip_v)), 1)
    ]
    first_pick[0].wait()
    for slot in range(groups):
        for part in range(2):
            at = pl.ds(part * half, half)
            pltpu.make_async_copy(own[0], moved.at[slot, at, :], block_sem.at[slot, part]).wait()
        group = lax.rem(place[3] - slot + groups, groups)
        first = pl.multiple_of(group * cap, PACK)
        got = dot(pick[group], moved[slot]).astype(bf16)
        for b in range(experts):
            held[b, pl.ds(first, cap), :] = got[b * cap : (b + 1) * cap]
    keep = copy_all([(held.at[b], kept.at[b]) for b in range(experts)], keep_sem)
    lane = lax.broadcasted_iota(jnp.int32, (groups * cap, LANES), 1)
    for b in range(experts):
        for load in loads[:3]:
            load[b].wait()
        back = dot(held[b], down_v[b])
        gate = jnp.sum(back * hid[b].astype(f32), axis=1, keepdims=True)
        gate = jnp.where(lane == b, gate, 0.0).astype(bf16)
        grad = (back * slope[b].astype(f32)).astype(bf16)
        loads[3][b].wait()
        route = dot(grad, flip_v[b]).astype(bf16)
        for g in range(groups):
            grads[g, pl.ds(b * cap, cap), pl.ds(0, width)] = route[g * cap : (g + 1) * cap]
            grads[g, pl.ds(b * cap, cap), pl.ds(width, LANES)] = gate[g * cap : (g + 1) * cap]
    lane = lax.broadcasted_iota(jnp.int32, (members, LANES), 1)
    for g in range(groups):
        total = dot(pick[g], grads[g], FIRST)
        out[g, :, pl.ds(0, width)] = total[:, :width].astype(bf16)
        by_expert = total[:, width:]
        ids = jnp.where(lane < top, meta[pl.ds(g * members, members), :].astype(f32), -1.0)
        picked = jnp.zeros(ids.shape, f32)
        for b in range(experts):
            hit = ids == (place[0] * experts + b).astype(f32)
            picked = picked + jnp.where(hit, by_expert[:, b : b + 1], 0.0)
        out[g, :, pl.ds(width, LANES)] = picked.astype(bf16)
        copy = pltpu.make_async_copy(out.at[g], out_all.at[pl.ds(g * members, members), :], out_sem.at[g])
        copy.start()
        keep.append(copy)
    for copy in keep:
        copy.wait()


def put_kernel(start, *refs):
    *pairs, out, total, sem = refs
    count = total.shape[1]
    cut = total.shape[2]
    copies = []
    for g in range(total.shape[0]):
        keep, got = pairs[2 * g], pairs[2 * g + 1]
        total[g] = keep[0].astype(f32) + got[0].astype(f32)
        copies.append(
            pltpu.make_async_copy(
                total.at[g], out.at[pl.ds(start, count), pl.ds(g * cut, cut), :], sem.at[g]
            )
        )
        copies[-1].start()
    for copy in copies:
        copy.wait()


def finish_kernel(width, top, rows, token, gate):
    token[...] = rows[:, pl.ds(0, width)]
    gate[...] = rows[:, pl.ds(width, LANES)].astype(f32).T[:top].astype(bf16)


def cost(flops, nbytes):
    return pl.CostEstimate(flops=int(flops), bytes_accessed=int(nbytes), transcendentals=0)


def shards(tokens, cotangent, expert_ids, gate_weights, w_up, w_down):
    tok_rows, width = tokens.shape
    top = expert_ids.shape[1]
    ep_count, dp_count = lax.axis_size("ep"), lax.axis_size("dp")
    experts, _, hidden = w_up.shape
    base_load = tok_rows * top // (experts * ep_count)
    capacity = base_load + max(1, base_load // 16)
    total = ep_count * tok_rows
    groups = ep_count // GROUP
    members = GROUP * tok_rows
    cap = -(-GROUP * capacity // PACK) * PACK
    routes = groups * cap
    full = width + LANES
    here = lax.axis_index("ep")
    place = jnp.stack([here, lax.axis_index("dp"), here % GROUP, here // GROUP]).astype(jnp.int32)
    bits = dp_count.bit_length() - 1
    turns = 2
    share = width // dp_count

    def shape(*dims, dtype=bf16):
        return jax.ShapeDtypeStruct(dims, dtype)

    x_own = pl.pallas_call(
        functools.partial(pack_kernel, top),
        out_shape=shape(tok_rows, full),
        compiler_params=pltpu.CompilerParams(vmem_limit_bytes=VMEM_LIMIT),
        cost_estimate=cost(0, 4 * tok_rows * width),
        name="pack",
    )(tokens, expert_ids.T, gate_weights.T)
    x_all = lax.all_gather(x_own, "ep", axis=0, tiled=True)

    def reach(p, step):
        q = p + GROUP * step if p % GROUP == 0 else p - GROUP * step
        return q if 0 <= q < ep_count else None

    def hop(value, pairs):
        return lax.ppermute(value, "ep", pairs)

    def at_group(i):
        return jnp.minimum(i, groups - 1)

    def at_expert(i):
        return jnp.clip(i - groups, 0, experts - 1)

    def at_slot(i, place):
        return lax.rem(place[3] - at_group(i) + groups, groups)

    def by_group(n):
        return pl.BlockSpec((members, n), lambda i, *_: (at_group(i), 0))

    def by_expert(rows, n):
        return pl.BlockSpec((1, rows, n), lambda i, *_: (at_expert(i), 0, 0))

    def call(kernel, name, grid, flops, nbytes, in_specs, out_specs, out_shape, scratch_shapes, prefetch=0):
        return pl.pallas_call(
            kernel,
            grid_spec=pltpu.PrefetchScalarGridSpec(
                num_scalar_prefetch=prefetch,
                grid=(grid,),
                in_specs=in_specs,
                out_specs=out_specs,
                scratch_shapes=scratch_shapes,
            ),
            out_shape=out_shape,
            compiler_params=pltpu.CompilerParams(vmem_limit_bytes=VMEM_LIMIT),
            cost_estimate=cost(flops, nbytes),
            name=name,
        )

    row_bytes = 2 * experts * hidden * width
    w_flip = call(
        flip_kernel,
        "flip",
        experts,
        0,
        2 * row_bytes,
        in_specs=[pl.BlockSpec((1, width, hidden), lambda b: (b, 0, 0))],
        out_specs=pl.BlockSpec((1, hidden, width), lambda b: (b, 0, 0)),
        out_shape=shape(experts, hidden, width),
        scratch_shapes=[],
    )(w_up)
    def at_group(i):
        return jnp.minimum(i, groups - 1)

    def at_expert(i):
        return jnp.clip(i - groups, 0, experts - 1)

    def at_slot(i, place):
        return lax.rem(place[3] - at_group(i) + groups, groups)

    def by_group(n):
        return pl.BlockSpec((members, n), lambda i, *_: (at_group(i), 0))

    def by_expert(rows, n):
        return pl.BlockSpec((1, rows, n), lambda i, *_: (at_expert(i), 0, 0))

    def call(kernel, name, grid, flops, nbytes, in_specs, out_specs, out_shape, scratch_shapes, prefetch=0):
        return pl.pallas_call(
            kernel,
            grid_spec=pltpu.PrefetchScalarGridSpec(
                num_scalar_prefetch=prefetch,
                grid=(grid,),
                in_specs=in_specs,
                out_specs=out_specs,
                scratch_shapes=scratch_shapes,
            ),
            out_shape=out_shape,
            compiler_params=pltpu.CompilerParams(vmem_limit_bytes=VMEM_LIMIT),
            cost_estimate=cost(flops, nbytes),
            name=name,
        )

    row_bytes = 2 * experts * hidden * width
    w_flip = call(
        flip_kernel,
        "flip",
        experts,
        0,
        2 * row_bytes,
        in_specs=[pl.BlockSpec((1, width, hidden), lambda b: (b, 0, 0))],
        out_specs=pl.BlockSpec((1, hidden, width), lambda b: (b, 0, 0)),
        out_shape=shape(experts, hidden, width),
        scratch_shapes=[],
    )(w_up)
    dy_own = jnp.concatenate([cotangent, hop(cotangent, [(p, p ^ 1) for p in range(ep_count)])], axis=0)
    lines = [None] + [
        [(p, reach(p, 1)) for p in range(ep_count) if None not in (reach(p, 1), reach(p, 1 - step))]
        for step in range(1, groups)
    ]
    swaps = [None] + [
        [(p, p ^ 1) for p in range(ep_count) if reach(p, -step) is not None] for step in range(1, groups)
    ]
    dy_own = [cotangent, hop(cotangent, [(p, p ^ 1) for p in range(ep_count)])]
    dy_mine = [[hop(part, lines[1]) for part in dy_own]]
    dy_mine[0][0], w_flip = lax.optimization_barrier((dy_mine[0][0], w_flip))
    for step in range(2, groups - 1):
        dy_mine.append([hop(part, lines[step]) for part in dy_mine[-1]])
    dy_mine.append([hop(part, lines[-1]) for part in dy_mine[-1]])
    dy_other = [[hop(part, swaps[1]) for part in dy_mine[0]]]
    early_swap = hop(dy_mine[1][0], swaps[2])

    act = shape(experts, routes, hidden)
    act_spec = by_expert(routes, hidden)
    pick_spec = pl.BlockSpec((1, experts * cap, members), lambda i, *_: (at_group(i), 0, 0))
    pick_flops = 2 * total * experts * cap * width
    main_flops = 2 * experts * routes * width * hidden
    act3 = pltpu.VMEM((experts, routes, hidden), bf16)
    pick_v = pltpu.VMEM((groups, experts * cap, members), bf16)
    most = max(experts, groups)

    def one(kernel, name, flops, nbytes, in_specs, out_specs, out_shape, scratch_shapes):
        return pl.pallas_call(
            kernel,
            in_specs=in_specs,
            out_specs=out_specs,
            out_shape=out_shape,
            scratch_shapes=scratch_shapes,
            compiler_params=pltpu.CompilerParams(vmem_limit_bytes=VMEM_LIMIT),
            cost_estimate=cost(flops, nbytes),
            name=name,
        )

    up_after = dy_other[0] + [early_swap] + dy_mine[-2][1:]
    pick, meta, hid, scaled, slope_g = one(
        functools.partial(up_kernel, groups, width, top, cap, len(up_after)),
        "up",
        pick_flops + main_flops,
        2 * total * full + row_bytes,
        [SMEM, ANY, ANY] + [ANY] * len(up_after),
        [ANY, pl.BlockSpec(memory_space=pltpu.VMEM), ANY, ANY, ANY],
        [shape(groups, experts * cap, members), shape(total, LANES), act, act, act],
        [
            pltpu.VMEM((groups, members, full), bf16),
            pltpu.VMEM((experts, width, hidden), bf16),
            pltpu.VMEM((experts, routes, width), bf16),
            pltpu.VMEM((experts, routes, LANES), f32),
            pick_v,
            act3,
            act3,
            act3,
            pltpu.SemaphoreType.DMA((2, most)),
            pltpu.SemaphoreType.DMA((4, experts)),
        ],
    )(place, x_all, w_up, *up_after)
    for row, swap in zip(dy_mine[1:], swaps[2:]):
        dy_other.append([])
        for n, part in enumerate(row):
            if len(dy_other) == 2 and n == 0:
                dy_other[-1].append(early_swap)
                continue
            part, hid = lax.optimization_barrier((part, hid))
            dy_other[-1].append(hop(part, swap))
    blocks = [part for row in [dy_own] + dy_mine + dy_other for part in row]

    orders = []
    for g in range(turns):
        turn = [(g + t) % bits for t in range(bits)]
        orders.append(
            tuple(sum(((p >> (bits - 1 - t)) & 1) << turn[t] for t in range(bits)) for p in range(dp_count))
        )
    orders = tuple(orders)
    cut_rows = share // turns

    def down(start, count, after):
        outs = one(
            functools.partial(down_kernel, orders, start, len(after)),
            "down",
            16 * main_flops,
            8 * row_bytes,
            [SMEM, ANY, ANY] + [ANY] * len(after),
            [ANY] * (2 * turns),
            [shape(dp_count // 2, count, cut_rows, hidden)] * (2 * turns),
            [
                pltpu.VMEM((count, routes, width), bf16),
                pltpu.VMEM((count, routes, hidden), bf16),
                pltpu.VMEM((turns, dp_count, count, cut_rows, hidden), bf16),
                pltpu.SemaphoreType.DMA((2, count)),
                pltpu.SemaphoreType.DMA((turns, dp_count, count)),
            ],
        )(place, kept, scaled, *after)
        return [(outs[2 * g], outs[2 * g + 1]) for g in range(turns)]

    def exchange(state, t):
        new = []
        for g, (keep, send) in enumerate(state):
            bit = 1 << ((g + t) % bits)
            got = lax.ppermute(send, "dp", [(i, i ^ bit) for i in range(dp_count)])
            both = keep.astype(f32) + got.astype(f32)
            if t < bits - 1:
                both = both.astype(bf16)
            half = both.shape[0] // 2
            new.append((both[:half], both[half:]) if half else both[0])
        return new

    token_part, kept = one(
        functools.partial(tail_kernel, groups, cap, width, top),
        "tail",
        8 * main_flops,
        4 * row_bytes,
        [SMEM] + [ANY] * (4 * groups - 2) + [ANY] * 5 + [pl.BlockSpec(memory_space=pltpu.VMEM)],
        [ANY, ANY],
        [shape(total, full), shape(experts, routes, width)],
        [
            pick_v,
            pltpu.VMEM((groups, members, width), bf16),
            pltpu.VMEM((experts, routes, width), bf16),
            pltpu.VMEM((groups, experts * cap, full), bf16),
            pltpu.VMEM((groups, members, full), bf16),
            pltpu.VMEM((experts, width, hidden), bf16),
            pltpu.VMEM((experts, hidden, width), bf16),
            act3,
            act3,
            pltpu.SemaphoreType.DMA((groups, 2)),
            pltpu.SemaphoreType.DMA((5, experts)),
            pltpu.SemaphoreType.DMA((experts,)),
            pltpu.SemaphoreType.DMA((groups,)),
        ],
    )(place, *blocks, pick, w_down, w_flip, hid, slope_g, meta)
    summed = lax.psum_scatter(token_part, "ep", scatter_dimension=0, tiled=True)
    token_grad, gate_grad = pl.pallas_call(
        functools.partial(finish_kernel, width, top),
        out_shape=[shape(tok_rows, width), shape(top, tok_rows)],
        compiler_params=pltpu.CompilerParams(vmem_limit_bytes=VMEM_LIMIT),
        cost_estimate=cost(0, 4 * tok_rows * width),
        name="finish",
    )(summed)

    counts = [1, experts - 1] if experts > 1 else [experts]
    states = [down(0, counts[0], [])]
    if len(counts) > 1:
        states.append(down(counts[0], counts[1], [states[0][0][0]]))
    for t in range(bits - 1):
        states = [exchange(state, t) for state in states]
    last = bits - 1
    states = [
        [
            (keep, lax.ppermute(send, "dp", [(i, i ^ (1 << ((g + last) % bits))) for i in range(dp_count)]))
            for g, (keep, send) in enumerate(state)
        ]
        for state in states
    ]
    keeps = [keep for keep, _ in states[-1]]
    token_grad, keeps = lax.optimization_barrier((token_grad, keeps))
    states[-1] = [(keep, got) for keep, (_, got) in zip(keeps, states[-1])]
    down_grad, start = None, 0
    for count, state in zip(counts, states):
        operands = [x for pair in state for x in pair]
        dest = [] if down_grad is None else [down_grad]

        def put(*refs, start=start, skip=len(dest), used=len(operands)):
            put_kernel(start, *refs[:used], *refs[used + skip :])

        down_grad = pl.pallas_call(
            put,
            in_specs=[VMEM] * len(operands) + [ANY] * len(dest),
            out_specs=ANY,
            out_shape=shape(experts, share, hidden, dtype=f32),
            input_output_aliases={len(operands): 0} if dest else {},
            scratch_shapes=[
                pltpu.VMEM((turns, count, cut_rows, hidden), f32),
                pltpu.SemaphoreType.DMA((turns,)),
            ],
            compiler_params=pltpu.CompilerParams(vmem_limit_bytes=VMEM_LIMIT // 2),
            cost_estimate=cost(0, 4 * experts * share * hidden),
            name="put",
        )(*operands, *dest)
        start += count
    return (token_grad, gate_grad.T, down_grad)


def solution(mesh):
    return jax.shard_map(
        shards,
        mesh=mesh,
        in_specs=(
            P(("dp", "ep"), None),
            P(("dp", "ep"), None),
            P(("dp", "ep"), None),
            P(("dp", "ep"), None),
            P("ep", None, None),
            P("ep", None, None),
        ),
        out_specs=(P(("dp", "ep"), None), P(("dp", "ep"), None), P("ep", "dp", None)),
        check_vma=False,
    )
```

```python
import functools

import jax
import jax.numpy as jnp
from jax import lax
from jax.experimental import pallas as pl
from jax.experimental.pallas import tpu as pltpu
from jax.sharding import PartitionSpec as P

LANES = 128
PACK = 16
GROUP = 2
VMEM_LIMIT = 60 * 1024 * 1024
bf16, f32 = jnp.bfloat16, jnp.float32
ANY = pl.BlockSpec(memory_space=pl.ANY)
SMEM = pl.BlockSpec(memory_space=pltpu.SMEM)
VMEM = pl.BlockSpec(memory_space=pltpu.VMEM)
FIRST = (((0,), (0,)), ((), ()))


def dot(a, b, dims=(((1,), (0,)), ((), ()))):
    return lax.dot_general(a, b, dims, preferred_element_type=f32)


def pack_kernel(top, tokens, ids, gates, x_out):
    count, width = tokens.shape
    x_out[:, pl.ds(0, width)] = tokens[...]
    info = jnp.concatenate(
        [ids[...].astype(f32), gates[...].astype(f32), jnp.zeros((LANES - 2 * top, count), f32)], axis=0
    )
    x_out[:, pl.ds(width, LANES)] = info.T.astype(bf16)


def flip_kernel(w, out):
    out[0] = w[0].T


def start_blocks(place, chips, own, mine, other, dst, sem):
    half = dst.shape[1] // 2

    def start(pair, slot, flip):
        for part in range(2):
            to = (part ^ flip) * half
            if not isinstance(flip, int):
                to = pl.multiple_of(to, half)
            pltpu.make_async_copy(pair[part], dst.at[slot, pl.ds(to, half), :], sem.at[slot, part]).start()

    start(own, 0, place[2])
    for slot in range(1, chips):
        for left in (True, False):
            for core in (True, False):
                pair = (mine if left == core else other)[(slot if left else chips - slot) - 1]

                @pl.when(((place[3] >= slot) == left) & ((place[2] == 0) == core))
                def _():
                    start(pair, slot, 0 if left else 1)


def copy_all(pairs, sem):
    copies = [pltpu.make_async_copy(src, dst, sem.at[n]) for n, (src, dst) in enumerate(pairs)]
    for copy in copies:
        copy.start()
    return copies


def up_kernel(groups, width, top, cap, after, place, x_all, w_up, *refs):
    refs = refs[after:]
    pick_out, meta, hid_out, scaled_out, slope_out, rows, w_v, held, gates, pick, hid, scaled, slope, sems, out_sem = refs
    experts, members = held.shape[0], rows.shape[1]
    arrive = copy_all([(x_all.at[pl.ds(g * members, members), :], rows.at[g]) for g in range(groups)], sems.at[0])
    weights = copy_all([(w_up.at[b], w_v.at[b]) for b in range(experts)], sems.at[1])
    before = lax.broadcasted_iota(jnp.int32, (members, members), 0) < lax.broadcasted_iota(
        jnp.int32, (members, members), 1
    )
    before = before.astype(bf16)
    spot = lax.broadcasted_iota(jnp.int32, (cap, members), 0).astype(f32)
    for g in range(groups):
        arrive[g].wait()
        info = rows[g, :, pl.ds(width, LANES)]
        meta[pl.ds(g * members, members), :] = info
        across = info.astype(f32).T
        ids, parts = across[:top], across[top : 2 * top]
        chosen = [ids == (place[0] * experts + b).astype(f32) for b in range(experts)]
        member = [jnp.sum(jnp.where(hit, 1.0, 0.0), axis=0, keepdims=True) for hit in chosen]
        table = jnp.concatenate(member + [jnp.zeros((PACK - experts, members), f32)], axis=0)
        prior = dot(table.astype(bf16), before)
        for b in range(experts):
            rank = jnp.where(member[b] > 0.0, prior[b : b + 1], -1.0)
            one = jnp.where(spot == rank, 1.0, 0.0)
            gate = jnp.sum(jnp.where(chosen[b], parts, 0.0), axis=0, keepdims=True)
            pick[g, pl.ds(b * cap, cap), :] = one.astype(bf16)
            gates[b, pl.ds(g * cap, cap), :] = jnp.broadcast_to(
                jnp.sum(one * gate, axis=1, keepdims=True), (cap, LANES)
            )
        got = dot(pick[g], rows[g, :, pl.ds(0, width)]).astype(bf16)
        for b in range(experts):
            held[b, pl.ds(g * cap, cap), :] = got[b * cap : (b + 1) * cap]
    outs = copy_all([(pick, pick_out)], out_sem.at[3])
    for b in range(experts):
        weights[b].wait()
        pre = dot(held[b], w_v[b])
        gate = gates[b][:, :1]
        sig = 0.5 + 0.5 * jnp.tanh(0.5 * pre)
        act = pre * sig
        hid[b] = act.astype(bf16)
        scaled[b] = (gate * act).astype(bf16)
        slope[b] = (gate * (sig + act * (1.0 - sig))).astype(bf16)
        for n, (src, dst) in enumerate(((hid, hid_out), (scaled, scaled_out), (slope, slope_out))):
            copy = pltpu.make_async_copy(src.at[b], dst.at[b], out_sem.at[n, b])
            copy.start()
            outs.append(copy)
    for copy in outs:
        copy.wait()


def down_kernel(orders, start, place, kept, scaled_in, *refs):
    outs, (rows, scaled, sent, in_sem, sem) = refs[:-5], refs[-5:]
    experts = sent.shape[2]
    arrive = copy_all([(kept.at[start + b], rows.at[b]) for b in range(experts)], in_sem.at[0])
    others = copy_all([(scaled_in.at[start + b], scaled.at[b]) for b in range(experts)], in_sem.at[1])
    parts = len(orders[0])
    half = parts // 2
    share = rows.shape[2] // parts
    cut = share // len(orders)
    copies = []
    for b in range(experts):
        arrive[b].wait()
        others[b].wait()
        for q in range(parts):
            at = pl.multiple_of((place[1] ^ q) * share, LANES)
            full = dot(rows[b, :, pl.ds(at, share)], scaled[b], FIRST).astype(bf16)
            for g, order in enumerate(orders):
                sent[g, q, b] = full[g * cut : (g + 1) * cut]
                p = order.index(q)
                copy = pltpu.make_async_copy(
                    sent.at[g, q, b], outs[2 * g + p // half].at[p % half, b], sem.at[g, q, b]
                )
                copy.start()
                copies.append(copy)
    for copy in copies:
        copy.wait()


def tail_kernel(groups, cap, width, top, place, *refs):
    count = 2 * groups - 1
    halves = [(refs[2 * n], refs[2 * n + 1]) for n in range(count)]
    own, mine, other, refs = halves[0], halves[1:groups], halves[groups:], refs[2 * count :]
    pick_in, w_down, w_flip, hid_in, slope_in, meta, out_all, kept = refs[:8]
    pick, moved, held, grads, out, down_v, flip_v, hid, slope, block_sem, sems, keep_sem, out_sem = refs[8:]
    experts, members = held.shape[0], moved.shape[1]
    half = members // 2
    first_pick = copy_all([(pick_in, pick)], sems.at[0])
    start_blocks(place, groups, own, mine, other, moved, block_sem)
    loads = [
        copy_all([(src.at[b], dst.at[b]) for b in range(experts)], sems.at[n])
        for n, (src, dst) in enumerate(((w_down, down_v), (hid_in, hid), (slope_in, slope), (w_flip, flip_v)), 1)
    ]
    first_pick[0].wait()
    for slot in range(groups):
        for part in range(2):
            at = pl.ds(part * half, half)
            pltpu.make_async_copy(own[0], moved.at[slot, at, :], block_sem.at[slot, part]).wait()
        group = lax.rem(place[3] - slot + groups, groups)
        first = pl.multiple_of(group * cap, PACK)
        got = dot(pick[group], moved[slot]).astype(bf16)
        for b in range(experts):
            held[b, pl.ds(first, cap), :] = got[b * cap : (b + 1) * cap]
    keep = copy_all([(held.at[b], kept.at[b]) for b in range(experts)], keep_sem)
    lane = lax.broadcasted_iota(jnp.int32, (groups * cap, LANES), 1)
    for b in range(experts):
        for load in loads[:3]:
            load[b].wait()
        back = dot(held[b], down_v[b])
        gate = jnp.sum(back * hid[b].astype(f32), axis=1, keepdims=True)
        gate = jnp.where(lane == b, gate, 0.0).astype(bf16)
        grad = (back * slope[b].astype(f32)).astype(bf16)
        loads[3][b].wait()
        route = dot(grad, flip_v[b]).astype(bf16)
        for g in range(groups):
            grads[g, pl.ds(b * cap, cap), pl.ds(0, width)] = route[g * cap : (g + 1) * cap]
            grads[g, pl.ds(b * cap, cap), pl.ds(width, LANES)] = gate[g * cap : (g + 1) * cap]
    lane = lax.broadcasted_iota(jnp.int32, (members, LANES), 1)
    for g in range(groups):
        total = dot(pick[g], grads[g], FIRST)
        out[g, :, pl.ds(0, width)] = total[:, :width].astype(bf16)
        by_expert = total[:, width:]
        ids = jnp.where(lane < top, meta[pl.ds(g * members, members), :].astype(f32), -1.0)
        picked = jnp.zeros(ids.shape, f32)
        for b in range(experts):
            hit = ids == (place[0] * experts + b).astype(f32)
            picked = picked + jnp.where(hit, by_expert[:, b : b + 1], 0.0)
        out[g, :, pl.ds(width, LANES)] = picked.astype(bf16)
        copy = pltpu.make_async_copy(out.at[g], out_all.at[pl.ds(g * members, members), :], out_sem.at[g])
        copy.start()
        keep.append(copy)
    for copy in keep:
        copy.wait()


def put_kernel(start, *refs):
    *pairs, out, total, sem = refs
    count = total.shape[1]
    cut = total.shape[2]
    copies = []
    for g in range(total.shape[0]):
        keep, got = pairs[2 * g], pairs[2 * g + 1]
        total[g] = keep[0].astype(f32) + got[0].astype(f32)
        copies.append(
            pltpu.make_async_copy(
                total.at[g], out.at[pl.ds(start, count), pl.ds(g * cut, cut), :], sem.at[g]
            )
        )
        copies[-1].start()
    for copy in copies:
        copy.wait()


def finish_kernel(width, top, rows, token, gate):
    token[...] = rows[:, pl.ds(0, width)]
    gate[...] = rows[:, pl.ds(width, LANES)].astype(f32).T[:top].astype(bf16)


def cost(flops, nbytes):
    return pl.CostEstimate(flops=int(flops), bytes_accessed=int(nbytes), transcendentals=0)


def shards(tokens, cotangent, expert_ids, gate_weights, w_up, w_down):
    tok_rows, width = tokens.shape
    top = expert_ids.shape[1]
    ep_count, dp_count = lax.axis_size("ep"), lax.axis_size("dp")
    experts, _, hidden = w_up.shape
    base_load = tok_rows * top // (experts * ep_count)
    capacity = base_load + max(1, base_load // 16)
    total = ep_count * tok_rows
    groups = ep_count // GROUP
    members = GROUP * tok_rows
    cap = -(-GROUP * capacity // PACK) * PACK
    routes = groups * cap
    full = width + LANES
    here = lax.axis_index("ep")
    place = jnp.stack([here, lax.axis_index("dp"), here % GROUP, here // GROUP]).astype(jnp.int32)
    bits = dp_count.bit_length() - 1
    turns = 2
    share = width // dp_count

    def shape(*dims, dtype=bf16):
        return jax.ShapeDtypeStruct(dims, dtype)

    x_own = pl.pallas_call(
        functools.partial(pack_kernel, top),
        out_shape=shape(tok_rows, full),
        compiler_params=pltpu.CompilerParams(vmem_limit_bytes=VMEM_LIMIT),
        cost_estimate=cost(0, 4 * tok_rows * width),
        name="pack",
    )(tokens, expert_ids.T, gate_weights.T)
    x_all = lax.all_gather(x_own, "ep", axis=0, tiled=True)

    def reach(p, step):
        q = p + GROUP * step if p % GROUP == 0 else p - GROUP * step
        return q if 0 <= q < ep_count else None

    def hop(value, pairs):
        return lax.ppermute(value, "ep", pairs)

    def at_group(i):
        return jnp.minimum(i, groups - 1)

    def at_expert(i):
        return jnp.clip(i - groups, 0, experts - 1)

    def at_slot(i, place):
        return lax.rem(place[3] - at_group(i) + groups, groups)

    def by_group(n):
        return pl.BlockSpec((members, n), lambda i, *_: (at_group(i), 0))

    def by_expert(rows, n):
        return pl.BlockSpec((1, rows, n), lambda i, *_: (at_expert(i), 0, 0))

    def call(kernel, name, grid, flops, nbytes, in_specs, out_specs, out_shape, scratch_shapes, prefetch=0):
        return pl.pallas_call(
            kernel,
            grid_spec=pltpu.PrefetchScalarGridSpec(
                num_scalar_prefetch=prefetch,
                grid=(grid,),
                in_specs=in_specs,
                out_specs=out_specs,
                scratch_shapes=scratch_shapes,
            ),
            out_shape=out_shape,
            compiler_params=pltpu.CompilerParams(vmem_limit_bytes=VMEM_LIMIT),
            cost_estimate=cost(flops, nbytes),
            name=name,
        )

    row_bytes = 2 * experts * hidden * width
    w_flip = call(
        flip_kernel,
        "flip",
        experts,
        0,
        2 * row_bytes,
        in_specs=[pl.BlockSpec((1, width, hidden), lambda b: (b, 0, 0))],
        out_specs=pl.BlockSpec((1, hidden, width), lambda b: (b, 0, 0)),
        out_shape=shape(experts, hidden, width),
        scratch_shapes=[],
    )(w_up)
    def at_group(i):
        return jnp.minimum(i, groups - 1)

    def at_expert(i):
        return jnp.clip(i - groups, 0, experts - 1)

    def at_slot(i, place):
        return lax.rem(place[3] - at_group(i) + groups, groups)

    def by_group(n):
        return pl.BlockSpec((members, n), lambda i, *_: (at_group(i), 0))

    def by_expert(rows, n):
        return pl.BlockSpec((1, rows, n), lambda i, *_: (at_expert(i), 0, 0))

    def call(kernel, name, grid, flops, nbytes, in_specs, out_specs, out_shape, scratch_shapes, prefetch=0):
        return pl.pallas_call(
            kernel,
            grid_spec=pltpu.PrefetchScalarGridSpec(
                num_scalar_prefetch=prefetch,
                grid=(grid,),
                in_specs=in_specs,
                out_specs=out_specs,
                scratch_shapes=scratch_shapes,
            ),
            out_shape=out_shape,
            compiler_params=pltpu.CompilerParams(vmem_limit_bytes=VMEM_LIMIT),
            cost_estimate=cost(flops, nbytes),
            name=name,
        )

    row_bytes = 2 * experts * hidden * width
    w_flip = call(
        flip_kernel,
        "flip",
        experts,
        0,
        2 * row_bytes,
        in_specs=[pl.BlockSpec((1, width, hidden), lambda b: (b, 0, 0))],
        out_specs=pl.BlockSpec((1, hidden, width), lambda b: (b, 0, 0)),
        out_shape=shape(experts, hidden, width),
        scratch_shapes=[],
    )(w_up)
    dy_own = jnp.concatenate([cotangent, hop(cotangent, [(p, p ^ 1) for p in range(ep_count)])], axis=0)
    lines = [None] + [
        [(p, reach(p, 1)) for p in range(ep_count) if None not in (reach(p, 1), reach(p, 1 - step))]
        for step in range(1, groups)
    ]
    swaps = [None] + [
        [(p, p ^ 1) for p in range(ep_count) if reach(p, -step) is not None] for step in range(1, groups)
    ]
    dy_own = [cotangent, hop(cotangent, [(p, p ^ 1) for p in range(ep_count)])]
    dy_mine = [[hop(part, lines[1]) for part in dy_own]]
    dy_mine[0][0], w_flip = lax.optimization_barrier((dy_mine[0][0], w_flip))
    for step in range(2, groups - 1):
        dy_mine.append([hop(part, lines[step]) for part in dy_mine[-1]])
    dy_mine.append([hop(part, lines[-1]) for part in dy_mine[-1]])
    dy_other = [[hop(part, swaps[1]) for part in dy_mine[0]]]
    early_swap = hop(dy_mine[1][0], swaps[2])

    act = shape(experts, routes, hidden)
    act_spec = by_expert(routes, hidden)
    pick_spec = pl.BlockSpec((1, experts * cap, members), lambda i, *_: (at_group(i), 0, 0))
    pick_flops = 2 * total * experts * cap * width
    main_flops = 2 * experts * routes * width * hidden
    act3 = pltpu.VMEM((experts, routes, hidden), bf16)
    pick_v = pltpu.VMEM((groups, experts * cap, members), bf16)
    most = max(experts, groups)

    def one(kernel, name, flops, nbytes, in_specs, out_specs, out_shape, scratch_shapes):
        return pl.pallas_call(
            kernel,
            in_specs=in_specs,
            out_specs=out_specs,
            out_shape=out_shape,
            scratch_shapes=scratch_shapes,
            compiler_params=pltpu.CompilerParams(vmem_limit_bytes=VMEM_LIMIT),
            cost_estimate=cost(flops, nbytes),
            name=name,
        )

    up_after = dy_other[0] + [early_swap] + dy_mine[-2][1:]
    pick, meta, hid, scaled, slope_g = one(
        functools.partial(up_kernel, groups, width, top, cap, len(up_after)),
        "up",
        pick_flops + main_flops,
        2 * total * full + row_bytes,
        [SMEM, ANY, ANY] + [ANY] * len(up_after),
        [ANY, pl.BlockSpec(memory_space=pltpu.VMEM), ANY, ANY, ANY],
        [shape(groups, experts * cap, members), shape(total, LANES), act, act, act],
        [
            pltpu.VMEM((groups, members, full), bf16),
            pltpu.VMEM((experts, width, hidden), bf16),
            pltpu.VMEM((experts, routes, width), bf16),
            pltpu.VMEM((experts, routes, LANES), f32),
            pick_v,
            act3,
            act3,
            act3,
            pltpu.SemaphoreType.DMA((2, most)),
            pltpu.SemaphoreType.DMA((4, experts)),
        ],
    )(place, x_all, w_up, *up_after)
    for row, swap in zip(dy_mine[1:], swaps[2:]):
        dy_other.append([])
        for n, part in enumerate(row):
            if len(dy_other) == 2 and n == 0:
                dy_other[-1].append(early_swap)
                continue
            part, hid = lax.optimization_barrier((part, hid))
            dy_other[-1].append(hop(part, swap))
    blocks = [part for row in [dy_own] + dy_mine + dy_other for part in row]

    orders = []
    for g in range(turns):
        turn = [(g + t) % bits for t in range(bits)]
        orders.append(
            tuple(sum(((p >> (bits - 1 - t)) & 1) << turn[t] for t in range(bits)) for p in range(dp_count))
        )
    orders = tuple(orders)
    cut_rows = share // turns

    def down(start, count):
        outs = one(
            functools.partial(down_kernel, orders, start),
            "down",
            16 * main_flops,
            8 * row_bytes,
            [SMEM, ANY, ANY],
            [ANY] * (2 * turns),
            [shape(dp_count // 2, count, cut_rows, hidden)] * (2 * turns),
            [
                pltpu.VMEM((count, routes, width), bf16),
                pltpu.VMEM((count, routes, hidden), bf16),
                pltpu.VMEM((turns, dp_count, count, cut_rows, hidden), bf16),
                pltpu.SemaphoreType.DMA((2, count)),
                pltpu.SemaphoreType.DMA((turns, dp_count, count)),
            ],
        )(place, kept, scaled)
        return [(outs[2 * g], outs[2 * g + 1]) for g in range(turns)]

    def exchange(state, t):
        new = []
        for g, (keep, send) in enumerate(state):
            bit = 1 << ((g + t) % bits)
            got = lax.ppermute(send, "dp", [(i, i ^ bit) for i in range(dp_count)])
            both = keep.astype(f32) + got.astype(f32)
            if t < bits - 1:
                both = both.astype(bf16)
            half = both.shape[0] // 2
            new.append((both[:half], both[half:]) if half else both[0])
        return new

    token_part, kept = one(
        functools.partial(tail_kernel, groups, cap, width, top),
        "tail",
        8 * main_flops,
        4 * row_bytes,
        [SMEM] + [ANY] * (4 * groups - 2) + [ANY] * 5 + [pl.BlockSpec(memory_space=pltpu.VMEM)],
        [ANY, ANY],
        [shape(total, full), shape(experts, routes, width)],
        [
            pick_v,
            pltpu.VMEM((groups, members, width), bf16),
            pltpu.VMEM((experts, routes, width), bf16),
            pltpu.VMEM((groups, experts * cap, full), bf16),
            pltpu.VMEM((groups, members, full), bf16),
            pltpu.VMEM((experts, width, hidden), bf16),
            pltpu.VMEM((experts, hidden, width), bf16),
            act3,
            act3,
            pltpu.SemaphoreType.DMA((groups, 2)),
            pltpu.SemaphoreType.DMA((5, experts)),
            pltpu.SemaphoreType.DMA((experts,)),
            pltpu.SemaphoreType.DMA((groups,)),
        ],
    )(place, *blocks, pick, w_down, w_flip, hid, slope_g, meta)
    summed = lax.psum_scatter(token_part, "ep", scatter_dimension=0, tiled=True)
    token_grad, gate_grad = pl.pallas_call(
        functools.partial(finish_kernel, width, top),
        out_shape=[shape(tok_rows, width), shape(top, tok_rows)],
        compiler_params=pltpu.CompilerParams(vmem_limit_bytes=VMEM_LIMIT),
        cost_estimate=cost(0, 4 * tok_rows * width),
        name="finish",
    )(summed)

    counts = [experts // 2, experts - experts // 2] if experts > 1 else [experts]
    states = [down(start, count) for start, count in zip((0, counts[0]), counts)]
    for t in range(bits - 1):
        states = [exchange(state, t) for state in states]
    last = bits - 1
    states = [
        [
            (keep, lax.ppermute(send, "dp", [(i, i ^ (1 << ((g + last) % bits))) for i in range(dp_count)]))
            for g, (keep, send) in enumerate(state)
        ]
        for state in states
    ]
    keeps = [keep for keep, _ in states[-1]]
    token_grad, keeps = lax.optimization_barrier((token_grad, keeps))
    states[-1] = [(keep, got) for keep, (_, got) in zip(keeps, states[-1])]
    down_grad, start = None, 0
    for count, state in zip(counts, states):
        operands = [x for pair in state for x in pair]
        dest = [] if down_grad is None else [down_grad]

        def put(*refs, start=start, skip=len(dest), used=len(operands)):
            put_kernel(start, *refs[:used], *refs[used + skip :])

        down_grad = pl.pallas_call(
            put,
            in_specs=[VMEM] * len(operands) + [ANY] * len(dest),
            out_specs=ANY,
            out_shape=shape(experts, share, hidden, dtype=f32),
            input_output_aliases={len(operands): 0} if dest else {},
            scratch_shapes=[
                pltpu.VMEM((turns, count, cut_rows, hidden), f32),
                pltpu.SemaphoreType.DMA((turns,)),
            ],
            compiler_params=pltpu.CompilerParams(vmem_limit_bytes=VMEM_LIMIT // 2),
            cost_estimate=cost(0, 4 * experts * share * hidden),
            name="put",
        )(*operands, *dest)
        start += count
    return (token_grad, gate_grad.T, down_grad)


def solution(mesh):
    return jax.shard_map(
        shards,
        mesh=mesh,
        in_specs=(
            P(("dp", "ep"), None),
            P(("dp", "ep"), None),
            P(("dp", "ep"), None),
            P(("dp", "ep"), None),
            P("ep", None, None),
            P("ep", None, None),
        ),
        out_specs=(P(("dp", "ep"), None), P(("dp", "ep"), None), P("ep", "dp", None)),
        check_vma=False,
    )
```

```python
import functools

import jax
import jax.numpy as jnp
from jax import lax
from jax.experimental import pallas as pl
from jax.experimental.pallas import tpu as pltpu
from jax.sharding import PartitionSpec as P

LANES = 128
PACK = 16
GROUP = 2
VMEM_LIMIT = 60 * 1024 * 1024
bf16, f32 = jnp.bfloat16, jnp.float32
ANY = pl.BlockSpec(memory_space=pl.ANY)
SMEM = pl.BlockSpec(memory_space=pltpu.SMEM)
VMEM = pl.BlockSpec(memory_space=pltpu.VMEM)
FIRST = (((0,), (0,)), ((), ()))


def dot(a, b, dims=(((1,), (0,)), ((), ()))):
    return lax.dot_general(a, b, dims, preferred_element_type=f32)


def pack_kernel(top, tokens, ids, gates, x_out):
    count, width = tokens.shape
    x_out[:, pl.ds(0, width)] = tokens[...]
    info = jnp.concatenate(
        [ids[...].astype(f32), gates[...].astype(f32), jnp.zeros((LANES - 2 * top, count), f32)], axis=0
    )
    x_out[:, pl.ds(width, LANES)] = info.T.astype(bf16)


def flip_kernel(place, w, out):
    del place
    out[0] = w[0].T


def start_blocks(place, chips, own, mine, other, dst, sem):
    half = dst.shape[1] // 2

    def start(pair, slot, flip):
        for part in range(2):
            to = (part ^ flip) * half
            if not isinstance(flip, int):
                to = pl.multiple_of(to, half)
            pltpu.make_async_copy(pair[part], dst.at[slot, pl.ds(to, half), :], sem.at[slot, part]).start()

    start(own, 0, place[2])
    for slot in range(1, chips):
        for left in (True, False):
            for core in (True, False):
                pair = (mine if left == core else other)[(slot if left else chips - slot) - 1]

                @pl.when(((place[3] >= slot) == left) & ((place[2] == 0) == core))
                def _():
                    start(pair, slot, 0 if left else 1)


def copies_of(pairs, sem):
    return [pltpu.make_async_copy(src, dst, sem.at[n]) for n, (src, dst) in enumerate(pairs)]


def staged(steps, later):
    return [later[len(later) * n // steps : len(later) * (n + 1) // steps] for n in range(steps)]


def copy_all(pairs, sem):
    copies = copies_of(pairs, sem)
    for copy in copies:
        copy.start()
    return copies


def up_kernel(groups, width, top, cap, after, place, x_all, w_up, *refs):
    refs = refs[after:]
    pick_out, meta, hid_out, scaled_out, slope_out, rows, w_v, held, gates, pick, hid, scaled, slope, sems, out_sem = refs
    experts, members = held.shape[0], rows.shape[1]
    arrive = copy_all([(x_all.at[pl.ds(g * members, members), :], rows.at[g]) for g in range(groups)], sems.at[0])
    weights = copies_of([(w_up.at[b], w_v.at[b]) for b in range(experts)], sems.at[1])
    stages = staged(groups, weights)
    before = lax.broadcasted_iota(jnp.int32, (members, members), 0) < lax.broadcasted_iota(
        jnp.int32, (members, members), 1
    )
    before = before.astype(bf16)
    spot = lax.broadcasted_iota(jnp.int32, (cap, members), 0).astype(f32)
    for g in range(groups):
        arrive[g].wait()
        for copy in stages[g]:
            copy.start()
        info = rows[g, :, pl.ds(width, LANES)]
        meta[pl.ds(g * members, members), :] = info
        across = info.astype(f32).T
        ids, parts = across[:top], across[top : 2 * top]
        chosen = [ids == (place[0] * experts + b).astype(f32) for b in range(experts)]
        member = [jnp.sum(jnp.where(hit, 1.0, 0.0), axis=0, keepdims=True) for hit in chosen]
        table = jnp.concatenate(member + [jnp.zeros((PACK - experts, members), f32)], axis=0)
        prior = dot(table.astype(bf16), before)
        for b in range(experts):
            rank = jnp.where(member[b] > 0.0, prior[b : b + 1], -1.0)
            one = jnp.where(spot == rank, 1.0, 0.0)
            gate = jnp.sum(jnp.where(chosen[b], parts, 0.0), axis=0, keepdims=True)
            pick[g, pl.ds(b * cap, cap), :] = one.astype(bf16)
            gates[b, pl.ds(g * cap, cap), :] = jnp.broadcast_to(
                jnp.sum(one * gate, axis=1, keepdims=True), (cap, LANES)
            )
        got = dot(pick[g], rows[g, :, pl.ds(0, width)]).astype(bf16)
        for b in range(experts):
            held[b, pl.ds(g * cap, cap), :] = got[b * cap : (b + 1) * cap]
    outs = copy_all([(pick, pick_out)], out_sem.at[3])
    for b in range(experts):
        weights[b].wait()
        pre = dot(held[b], w_v[b])
        gate = gates[b][:, :1]
        sig = 0.5 + 0.5 * jnp.tanh(0.5 * pre)
        act = pre * sig
        hid[b] = act.astype(bf16)
        scaled[b] = (gate * act).astype(bf16)
        slope[b] = (gate * (sig + act * (1.0 - sig))).astype(bf16)
        for n, (src, dst) in enumerate(((hid, hid_out), (scaled, scaled_out), (slope, slope_out))):
            copy = pltpu.make_async_copy(src.at[b], dst.at[b], out_sem.at[n, b])
            copy.start()
            outs.append(copy)
    for copy in outs:
        copy.wait()


def down_kernel(orders, start, place, kept, scaled_in, *refs):
    outs, (rows, scaled, sent, in_sem, sem) = refs[:-5], refs[-5:]
    experts = sent.shape[2]
    arrive = copy_all([(kept.at[start + b], rows.at[b]) for b in range(experts)], in_sem.at[0])
    others = copy_all([(scaled_in.at[start + b], scaled.at[b]) for b in range(experts)], in_sem.at[1])
    parts = len(orders[0])
    half = parts // 2
    share = rows.shape[2] // parts
    cut = share // len(orders)
    copies = []
    for b in range(experts):
        arrive[b].wait()
        others[b].wait()
        for q in range(parts):
            at = pl.multiple_of((place[1] ^ q) * share, LANES)
            full = dot(rows[b, :, pl.ds(at, share)], scaled[b], FIRST).astype(bf16)
            for g, order in enumerate(orders):
                sent[g, q, b] = full[g * cut : (g + 1) * cut]
                p = order.index(q)
                copy = pltpu.make_async_copy(
                    sent.at[g, q, b], outs[2 * g + p // half].at[p % half, b], sem.at[g, q, b]
                )
                copy.start()
                copies.append(copy)
    for copy in copies:
        copy.wait()


def tail_kernel(groups, cap, width, top, place, *refs):
    count = 2 * groups - 1
    halves = [(refs[2 * n], refs[2 * n + 1]) for n in range(count)]
    own, mine, other, refs = halves[0], halves[1:groups], halves[groups:], refs[2 * count :]
    pick_in, w_down, w_flip, hid_in, slope_in, meta, out_all, kept = refs[:8]
    pick, moved, held, grads, out, down_v, flip_v, hid, slope, block_sem, sems, keep_sem, out_sem = refs[8:]
    experts, members = held.shape[0], moved.shape[1]
    half = members // 2
    first_pick = copy_all([(pick_in, pick)], sems.at[0])
    start_blocks(place, groups, own, mine, other, moved, block_sem)
    loads = [
        copies_of([(src.at[b], dst.at[b]) for b in range(experts)], sems.at[n])
        for n, (src, dst) in enumerate(((w_down, down_v), (hid_in, hid), (slope_in, slope), (w_flip, flip_v)), 1)
    ]
    stages = staged(groups, [load[b] for b in range(experts) for load in loads])
    first_pick[0].wait()
    for slot in range(groups):
        for part in range(2):
            at = pl.ds(part * half, half)
            pltpu.make_async_copy(own[0], moved.at[slot, at, :], block_sem.at[slot, part]).wait()
        for copy in stages[slot]:
            copy.start()
        group = lax.rem(place[3] - slot + groups, groups)
        first = pl.multiple_of(group * cap, PACK)
        got = dot(pick[group], moved[slot]).astype(bf16)
        for b in range(experts):
            held[b, pl.ds(first, cap), :] = got[b * cap : (b + 1) * cap]
    keep = copy_all([(held.at[b], kept.at[b]) for b in range(experts)], keep_sem)
    lane = lax.broadcasted_iota(jnp.int32, (groups * cap, LANES), 1)
    for b in range(experts):
        for load in loads[:3]:
            load[b].wait()
        back = dot(held[b], down_v[b])
        gate = jnp.sum(back * hid[b].astype(f32), axis=1, keepdims=True)
        gate = jnp.where(lane == b, gate, 0.0).astype(bf16)
        grad = (back * slope[b].astype(f32)).astype(bf16)
        loads[3][b].wait()
        route = dot(grad, flip_v[b]).astype(bf16)
        for g in range(groups):
            grads[g, pl.ds(b * cap, cap), pl.ds(0, width)] = route[g * cap : (g + 1) * cap]
            grads[g, pl.ds(b * cap, cap), pl.ds(width, LANES)] = gate[g * cap : (g + 1) * cap]
    lane = lax.broadcasted_iota(jnp.int32, (members, LANES), 1)
    for g in range(groups):
        total = dot(pick[g], grads[g], FIRST)
        out[g, :, pl.ds(0, width)] = total[:, :width].astype(bf16)
        by_expert = total[:, width:]
        ids = jnp.where(lane < top, meta[pl.ds(g * members, members), :].astype(f32), -1.0)
        picked = jnp.zeros(ids.shape, f32)
        for b in range(experts):
            hit = ids == (place[0] * experts + b).astype(f32)
            picked = picked + jnp.where(hit, by_expert[:, b : b + 1], 0.0)
        out[g, :, pl.ds(width, LANES)] = picked.astype(bf16)
        copy = pltpu.make_async_copy(out.at[g], out_all.at[pl.ds(g * members, members), :], out_sem.at[g])
        copy.start()
        keep.append(copy)
    for copy in keep:
        copy.wait()


def put_kernel(start, *refs):
    *pairs, out, total, sem = refs
    count = total.shape[1]
    cut = total.shape[2]
    copies = []
    for g in range(total.shape[0]):
        keep, got = pairs[2 * g], pairs[2 * g + 1]
        total[g] = keep[0].astype(f32) + got[0].astype(f32)
        copies.append(
            pltpu.make_async_copy(
                total.at[g], out.at[pl.ds(start, count), pl.ds(g * cut, cut), :], sem.at[g]
            )
        )
        copies[-1].start()
    for copy in copies:
        copy.wait()


def finish_kernel(width, top, rows, token, gate):
    token[...] = rows[:, pl.ds(0, width)]
    gate[...] = rows[:, pl.ds(width, LANES)].astype(f32).T[:top].astype(bf16)


def cost(flops, nbytes):
    return pl.CostEstimate(flops=int(flops), bytes_accessed=int(nbytes), transcendentals=0)


def shards(tokens, cotangent, expert_ids, gate_weights, w_up, w_down):
    tok_rows, width = tokens.shape
    top = expert_ids.shape[1]
    ep_count, dp_count = lax.axis_size("ep"), lax.axis_size("dp")
    experts, _, hidden = w_up.shape
    base_load = tok_rows * top // (experts * ep_count)
    capacity = base_load + max(1, base_load // 16)
    total = ep_count * tok_rows
    groups = ep_count // GROUP
    members = GROUP * tok_rows
    cap = -(-GROUP * capacity // PACK) * PACK
    routes = groups * cap
    full = width + LANES
    here = lax.axis_index("ep")
    place = jnp.stack([here, lax.axis_index("dp"), here % GROUP, here // GROUP]).astype(jnp.int32)
    bits = dp_count.bit_length() - 1
    turns = 2
    share = width // dp_count

    def shape(*dims, dtype=bf16):
        return jax.ShapeDtypeStruct(dims, dtype)

    x_own = pl.pallas_call(
        functools.partial(pack_kernel, top),
        out_shape=shape(tok_rows, full),
        compiler_params=pltpu.CompilerParams(vmem_limit_bytes=VMEM_LIMIT),
        cost_estimate=cost(0, 4 * tok_rows * width),
        name="pack",
    )(tokens, expert_ids.T, gate_weights.T)
    x_all = lax.all_gather(x_own, "ep", axis=0, tiled=True)

    def reach(p, step):
        q = p + GROUP * step if p % GROUP == 0 else p - GROUP * step
        return q if 0 <= q < ep_count else None

    def hop(value, pairs):
        return lax.ppermute(value, "ep", pairs)

    def call(kernel, name, grid, flops, nbytes, in_specs, out_specs, out_shape, scratch_shapes, prefetch=0):
        return pl.pallas_call(
            kernel,
            grid_spec=pltpu.PrefetchScalarGridSpec(
                num_scalar_prefetch=prefetch,
                grid=(grid,),
                in_specs=in_specs,
                out_specs=out_specs,
                scratch_shapes=scratch_shapes,
            ),
            out_shape=out_shape,
            compiler_params=pltpu.CompilerParams(vmem_limit_bytes=VMEM_LIMIT),
            cost_estimate=cost(flops, nbytes),
            name=name,
        )

    row_bytes = 2 * experts * hidden * width
    w_flip = call(
        flip_kernel,
        "flip",
        experts,
        0,
        2 * row_bytes,
        in_specs=[SMEM, pl.BlockSpec((1, width, hidden), lambda b: (b, 0, 0))],
        out_specs=pl.BlockSpec((1, hidden, width), lambda b: (b, 0, 0)),
        out_shape=shape(experts, hidden, width),
        scratch_shapes=[],
    )(place, w_up)

    lines = [None] + [
        [(p, reach(p, 1)) for p in range(ep_count) if None not in (reach(p, 1), reach(p, 1 - step))]
        for step in range(1, groups)
    ]
    swaps = [None] + [
        [(p, p ^ 1) for p in range(ep_count) if reach(p, -step) is not None] for step in range(1, groups)
    ]
    dy_own = [cotangent, hop(cotangent, [(p, p ^ 1) for p in range(ep_count)])]
    dy_mine = [[hop(part, lines[1]) for part in dy_own]]
    dy_mine[0][0], w_flip = lax.optimization_barrier((dy_mine[0][0], w_flip))
    for step in range(2, groups - 1):
        dy_mine.append([hop(part, lines[step]) for part in dy_mine[-1]])
    dy_mine.append([hop(part, lines[-1]) for part in dy_mine[-1]])
    dy_other = [[hop(part, swaps[1]) for part in dy_mine[0]]]

    act = shape(experts, routes, hidden)
    pick_flops = 2 * total * experts * cap * width
    main_flops = 2 * experts * routes * width * hidden
    act3 = pltpu.VMEM((experts, routes, hidden), bf16)
    pick_v = pltpu.VMEM((groups, experts * cap, members), bf16)
    most = max(experts, groups)

    def one(kernel, name, flops, nbytes, in_specs, out_specs, out_shape, scratch_shapes):
        return pl.pallas_call(
            kernel,
            in_specs=in_specs,
            out_specs=out_specs,
            out_shape=out_shape,
            scratch_shapes=scratch_shapes,
            compiler_params=pltpu.CompilerParams(vmem_limit_bytes=VMEM_LIMIT),
            cost_estimate=cost(flops, nbytes),
            name=name,
        )

    up_after = dy_other[0] + dy_mine[-2][1:]
    pick, meta, hid, scaled, slope_g = one(
        functools.partial(up_kernel, groups, width, top, cap, len(up_after)),
        "up",
        pick_flops + main_flops,
        2 * total * full + row_bytes,
        [SMEM, ANY, ANY] + [ANY] * len(up_after),
        [ANY, pl.BlockSpec(memory_space=pltpu.VMEM), ANY, ANY, ANY],
        [shape(groups, experts * cap, members), shape(total, LANES), act, act, act],
        [
            pltpu.VMEM((groups, members, full), bf16),
            pltpu.VMEM((experts, width, hidden), bf16),
            pltpu.VMEM((experts, routes, width), bf16),
            pltpu.VMEM((experts, routes, LANES), f32),
            pick_v,
            act3,
            act3,
            act3,
            pltpu.SemaphoreType.DMA((2, most)),
            pltpu.SemaphoreType.DMA((4, experts)),
        ],
    )(place, x_all, w_up, *up_after)
    for row, swap in zip(dy_mine[1:], swaps[2:]):
        dy_other.append([])
        for part in row:
            part, hid = lax.optimization_barrier((part, hid))
            dy_other[-1].append(hop(part, swap))
    blocks = [part for row in [dy_own] + dy_mine + dy_other for part in row]

    orders = []
    for g in range(turns):
        turn = [(g + t) % bits for t in range(bits)]
        orders.append(
            tuple(sum(((p >> (bits - 1 - t)) & 1) << turn[t] for t in range(bits)) for p in range(dp_count))
        )
    orders = tuple(orders)
    cut_rows = share // turns

    def down(start, count):
        outs = one(
            functools.partial(down_kernel, orders, start),
            "down",
            16 * main_flops,
            8 * row_bytes,
            [SMEM, ANY, ANY],
            [ANY] * (2 * turns),
            [shape(dp_count // 2, count, cut_rows, hidden)] * (2 * turns),
            [
                pltpu.VMEM((count, routes, width), bf16),
                pltpu.VMEM((count, routes, hidden), bf16),
                pltpu.VMEM((turns, dp_count, count, cut_rows, hidden), bf16),
                pltpu.SemaphoreType.DMA((2, count)),
                pltpu.SemaphoreType.DMA((turns, dp_count, count)),
            ],
        )(place, kept, scaled)
        return [(outs[2 * g], outs[2 * g + 1]) for g in range(turns)]

    def exchange(state, t):
        new = []
        for g, (keep, send) in enumerate(state):
            bit = 1 << ((g + t) % bits)
            got = lax.ppermute(send, "dp", [(i, i ^ bit) for i in range(dp_count)])
            both = keep.astype(f32) + got.astype(f32)
            if t < bits - 1:
                both = both.astype(bf16)
            half = both.shape[0] // 2
            new.append((both[:half], both[half:]) if half else both[0])
        return new

    token_part, kept = one(
        functools.partial(tail_kernel, groups, cap, width, top),
        "tail",
        8 * main_flops,
        4 * row_bytes,
        [SMEM] + [ANY] * (4 * groups - 2) + [ANY] * 5 + [pl.BlockSpec(memory_space=pltpu.VMEM)],
        [ANY, ANY],
        [shape(total, full), shape(experts, routes, width)],
        [
            pick_v,
            pltpu.VMEM((groups, members, width), bf16),
            pltpu.VMEM((experts, routes, width), bf16),
            pltpu.VMEM((groups, experts * cap, full), bf16),
            pltpu.VMEM((groups, members, full), bf16),
            pltpu.VMEM((experts, width, hidden), bf16),
            pltpu.VMEM((experts, hidden, width), bf16),
            act3,
            act3,
            pltpu.SemaphoreType.DMA((groups, 2)),
            pltpu.SemaphoreType.DMA((5, experts)),
            pltpu.SemaphoreType.DMA((experts,)),
            pltpu.SemaphoreType.DMA((groups,)),
        ],
    )(place, *blocks, pick, w_down, w_flip, hid, slope_g, meta)
    summed = lax.psum_scatter(token_part, "ep", scatter_dimension=0, tiled=True)
    token_grad, gate_grad = pl.pallas_call(
        functools.partial(finish_kernel, width, top),
        out_shape=[shape(tok_rows, width), shape(top, tok_rows)],
        compiler_params=pltpu.CompilerParams(vmem_limit_bytes=VMEM_LIMIT),
        cost_estimate=cost(0, 4 * tok_rows * width),
        name="finish",
    )(summed)

    counts = [experts // 2, experts - experts // 2] if experts > 1 else [experts]
    states = [down(start, count) for start, count in zip((0, counts[0]), counts)]
    for t in range(bits - 1):
        states = [exchange(state, t) for state in states]
    last = bits - 1
    states = [
        [
            (keep, lax.ppermute(send, "dp", [(i, i ^ (1 << ((g + last) % bits))) for i in range(dp_count)]))
            for g, (keep, send) in enumerate(state)
        ]
        for state in states
    ]
    keeps = [keep for keep, _ in states[-1]]
    token_grad, keeps = lax.optimization_barrier((token_grad, keeps))
    states[-1] = [(keep, got) for keep, (_, got) in zip(keeps, states[-1])]
    down_grad, start = None, 0
    for count, state in zip(counts, states):
        operands = [x for pair in state for x in pair]
        dest = [] if down_grad is None else [down_grad]

        def put(*refs, start=start, skip=len(dest), used=len(operands)):
            put_kernel(start, *refs[:used], *refs[used + skip :])

        down_grad = pl.pallas_call(
            put,
            in_specs=[VMEM] * len(operands) + [ANY] * len(dest),
            out_specs=ANY,
            out_shape=shape(experts, share, hidden, dtype=f32),
            input_output_aliases={len(operands): 0} if dest else {},
            scratch_shapes=[
                pltpu.VMEM((turns, count, cut_rows, hidden), f32),
                pltpu.SemaphoreType.DMA((turns,)),
            ],
            compiler_params=pltpu.CompilerParams(vmem_limit_bytes=VMEM_LIMIT // 2),
            cost_estimate=cost(0, 4 * experts * share * hidden),
            name="put",
        )(*operands, *dest)
        start += count
    return (token_grad, gate_grad.T, down_grad)


def solution(mesh):
    return jax.shard_map(
        shards,
        mesh=mesh,
        in_specs=(
            P(("dp", "ep"), None),
            P(("dp", "ep"), None),
            P(("dp", "ep"), None),
            P(("dp", "ep"), None),
            P("ep", None, None),
            P("ep", None, None),
        ),
        out_specs=(P(("dp", "ep"), None), P(("dp", "ep"), None), P("ep", "dp", None)),
        check_vma=False,
    )
```

```python
import functools

import jax
import jax.numpy as jnp
from jax import lax
from jax.experimental import pallas as pl
from jax.experimental.pallas import tpu as pltpu
from jax.sharding import PartitionSpec as P

LANES = 128
PACK = 16
GROUP = 2
VMEM_LIMIT = 60 * 1024 * 1024
bf16, f32 = jnp.bfloat16, jnp.float32
ANY = pl.BlockSpec(memory_space=pl.ANY)
SMEM = pl.BlockSpec(memory_space=pltpu.SMEM)
VMEM = pl.BlockSpec(memory_space=pltpu.VMEM)
FIRST = (((0,), (0,)), ((), ()))


def dot(a, b, dims=(((1,), (0,)), ((), ()))):
    return lax.dot_general(a, b, dims, preferred_element_type=f32)


def pack_kernel(top, tokens, ids, gates, x_out):
    count, width = tokens.shape
    x_out[:, pl.ds(0, width)] = tokens[...]
    info = jnp.concatenate(
        [ids[...].astype(f32), gates[...].astype(f32), jnp.zeros((LANES - 2 * top, count), f32)], axis=0
    )
    x_out[:, pl.ds(width, LANES)] = info.T.astype(bf16)


def flip_kernel(place, w, out):
    del place
    out[0] = w[0].T


def start_blocks(place, chips, own, mine, other, dst, sem):
    half = dst.shape[1] // 2

    def start(pair, slot, flip):
        for part in range(2):
            to = (part ^ flip) * half
            if not isinstance(flip, int):
                to = pl.multiple_of(to, half)
            pltpu.make_async_copy(pair[part], dst.at[slot, pl.ds(to, half), :], sem.at[slot, part]).start()

    start(own, 0, place[2])
    for slot in range(1, chips):
        for left in (True, False):
            for core in (True, False):
                pair = (mine if left == core else other)[(slot if left else chips - slot) - 1]

                @pl.when(((place[3] >= slot) == left) & ((place[2] == 0) == core))
                def _():
                    start(pair, slot, 0 if left else 1)


def copies_of(pairs, sem):
    return [pltpu.make_async_copy(src, dst, sem.at[n]) for n, (src, dst) in enumerate(pairs)]


def staged(steps, later):
    return [later[len(later) * n // steps : len(later) * (n + 1) // steps] for n in range(steps)]


def copy_all(pairs, sem):
    copies = copies_of(pairs, sem)
    for copy in copies:
        copy.start()
    return copies


def up_kernel(groups, width, top, cap, place, x_all, w_up, *refs):
    pick_out, meta, hid_out, scaled_out, slope_out, rows, w_v, held, gates, pick, hid, scaled, slope, sems, out_sem = refs
    experts, members = held.shape[0], rows.shape[1]
    arrive = copy_all([(x_all.at[pl.ds(g * members, members), :], rows.at[g]) for g in range(groups)], sems.at[0])
    weights = copies_of([(w_up.at[b], w_v.at[b]) for b in range(experts)], sems.at[1])
    stages = staged(groups, weights)
    before = lax.broadcasted_iota(jnp.int32, (members, members), 0) < lax.broadcasted_iota(
        jnp.int32, (members, members), 1
    )
    before = before.astype(bf16)
    spot = lax.broadcasted_iota(jnp.int32, (cap, members), 0).astype(f32)
    for g in range(groups):
        arrive[g].wait()
        for copy in stages[g]:
            copy.start()
        info = rows[g, :, pl.ds(width, LANES)]
        meta[pl.ds(g * members, members), :] = info
        across = info.astype(f32).T
        ids, parts = across[:top], across[top : 2 * top]
        chosen = [ids == (place[0] * experts + b).astype(f32) for b in range(experts)]
        member = [jnp.sum(jnp.where(hit, 1.0, 0.0), axis=0, keepdims=True) for hit in chosen]
        table = jnp.concatenate(member + [jnp.zeros((PACK - experts, members), f32)], axis=0)
        prior = dot(table.astype(bf16), before)
        for b in range(experts):
            rank = jnp.where(member[b] > 0.0, prior[b : b + 1], -1.0)
            one = jnp.where(spot == rank, 1.0, 0.0)
            gate = jnp.sum(jnp.where(chosen[b], parts, 0.0), axis=0, keepdims=True)
            pick[g, pl.ds(b * cap, cap), :] = one.astype(bf16)
            gates[b, pl.ds(g * cap, cap), :] = jnp.broadcast_to(
                jnp.sum(one * gate, axis=1, keepdims=True), (cap, LANES)
            )
        got = dot(pick[g], rows[g, :, pl.ds(0, width)]).astype(bf16)
        for b in range(experts):
            held[b, pl.ds(g * cap, cap), :] = got[b * cap : (b + 1) * cap]
    outs = copy_all([(pick, pick_out)], out_sem.at[3])
    for b in range(experts):
        weights[b].wait()
        pre = dot(held[b], w_v[b])
        gate = gates[b][:, :1]
        sig = 0.5 + 0.5 * jnp.tanh(0.5 * pre)
        act = pre * sig
        hid[b] = act.astype(bf16)
        scaled[b] = (gate * act).astype(bf16)
        slope[b] = (gate * (sig + act * (1.0 - sig))).astype(bf16)
        for n, (src, dst) in enumerate(((hid, hid_out), (scaled, scaled_out), (slope, slope_out))):
            copy = pltpu.make_async_copy(src.at[b], dst.at[b], out_sem.at[n, b])
            copy.start()
            outs.append(copy)
    for copy in outs:
        copy.wait()


def down_kernel(orders, start, place, kept, scaled_in, *refs):
    outs, (rows, scaled, sent, in_sem, sem) = refs[:-5], refs[-5:]
    experts = sent.shape[2]
    arrive = copy_all([(kept.at[start + b], rows.at[b]) for b in range(experts)], in_sem.at[0])
    others = copy_all([(scaled_in.at[start + b], scaled.at[b]) for b in range(experts)], in_sem.at[1])
    parts = len(orders[0])
    half = parts // 2
    share = rows.shape[2] // parts
    cut = share // len(orders)
    copies = []
    for b in range(experts):
        arrive[b].wait()
        others[b].wait()
        for q in range(parts):
            at = pl.multiple_of((place[1] ^ q) * share, LANES)
            full = dot(rows[b, :, pl.ds(at, share)], scaled[b], FIRST).astype(bf16)
            for g, order in enumerate(orders):
                sent[g, q, b] = full[g * cut : (g + 1) * cut]
                p = order.index(q)
                copy = pltpu.make_async_copy(
                    sent.at[g, q, b], outs[2 * g + p // half].at[p % half, b], sem.at[g, q, b]
                )
                copy.start()
                copies.append(copy)
    for copy in copies:
        copy.wait()


def tail_kernel(groups, cap, width, top, place, *refs):
    count = 2 * groups - 1
    halves = [(refs[2 * n], refs[2 * n + 1]) for n in range(count)]
    own, mine, other, refs = halves[0], halves[1:groups], halves[groups:], refs[2 * count :]
    pick_in, w_down, w_flip, hid_in, slope_in, meta, out_all, kept = refs[:8]
    pick, moved, held, grads, out, down_v, flip_v, hid, slope, block_sem, sems, keep_sem, out_sem = refs[8:]
    experts, members = held.shape[0], moved.shape[1]
    half = members // 2
    first_pick = copy_all([(pick_in, pick)], sems.at[0])
    start_blocks(place, groups, own, mine, other, moved, block_sem)
    loads = [
        copies_of([(src.at[b], dst.at[b]) for b in range(experts)], sems.at[n])
        for n, (src, dst) in enumerate(((w_down, down_v), (hid_in, hid), (slope_in, slope), (w_flip, flip_v)), 1)
    ]
    stages = staged(groups, [load[b] for b in range(experts) for load in loads])
    first_pick[0].wait()
    for slot in range(groups):
        for part in range(2):
            at = pl.ds(part * half, half)
            pltpu.make_async_copy(own[0], moved.at[slot, at, :], block_sem.at[slot, part]).wait()
        for copy in stages[slot]:
            copy.start()
        group = lax.rem(place[3] - slot + groups, groups)
        first = pl.multiple_of(group * cap, PACK)
        got = dot(pick[group], moved[slot]).astype(bf16)
        for b in range(experts):
            held[b, pl.ds(first, cap), :] = got[b * cap : (b + 1) * cap]
    keep = copy_all([(held.at[b], kept.at[b]) for b in range(experts)], keep_sem)
    lane = lax.broadcasted_iota(jnp.int32, (groups * cap, LANES), 1)
    for b in range(experts):
        for load in loads[:3]:
            load[b].wait()
        back = dot(held[b], down_v[b])
        gate = jnp.sum(back * hid[b].astype(f32), axis=1, keepdims=True)
        gate = jnp.where(lane == b, gate, 0.0).astype(bf16)
        grad = (back * slope[b].astype(f32)).astype(bf16)
        loads[3][b].wait()
        route = dot(grad, flip_v[b]).astype(bf16)
        for g in range(groups):
            grads[g, pl.ds(b * cap, cap), pl.ds(0, width)] = route[g * cap : (g + 1) * cap]
            grads[g, pl.ds(b * cap, cap), pl.ds(width, LANES)] = gate[g * cap : (g + 1) * cap]
    lane = lax.broadcasted_iota(jnp.int32, (members, LANES), 1)
    for g in range(groups):
        total = dot(pick[g], grads[g], FIRST)
        out[g, :, pl.ds(0, width)] = total[:, :width].astype(bf16)
        by_expert = total[:, width:]
        ids = jnp.where(lane < top, meta[pl.ds(g * members, members), :].astype(f32), -1.0)
        picked = jnp.zeros(ids.shape, f32)
        for b in range(experts):
            hit = ids == (place[0] * experts + b).astype(f32)
            picked = picked + jnp.where(hit, by_expert[:, b : b + 1], 0.0)
        out[g, :, pl.ds(width, LANES)] = picked.astype(bf16)
        copy = pltpu.make_async_copy(out.at[g], out_all.at[pl.ds(g * members, members), :], out_sem.at[g])
        copy.start()
        keep.append(copy)
    for copy in keep:
        copy.wait()


def put_kernel(start, *refs):
    *pairs, out, total, sem = refs
    count = total.shape[1]
    cut = total.shape[2]
    copies = []
    for g in range(total.shape[0]):
        keep, got = pairs[2 * g], pairs[2 * g + 1]
        total[g] = keep[0].astype(f32) + got[0].astype(f32)
        copies.append(
            pltpu.make_async_copy(
                total.at[g], out.at[pl.ds(start, count), pl.ds(g * cut, cut), :], sem.at[g]
            )
        )
        copies[-1].start()
    for copy in copies:
        copy.wait()


def finish_kernel(width, top, rows, token, gate):
    token[...] = rows[:, pl.ds(0, width)]
    gate[...] = rows[:, pl.ds(width, LANES)].astype(f32).T[:top].astype(bf16)


def cost(flops, nbytes):
    return pl.CostEstimate(flops=int(flops), bytes_accessed=int(nbytes), transcendentals=0)


def shards(tokens, cotangent, expert_ids, gate_weights, w_up, w_down):
    tok_rows, width = tokens.shape
    top = expert_ids.shape[1]
    ep_count, dp_count = lax.axis_size("ep"), lax.axis_size("dp")
    experts, _, hidden = w_up.shape
    base_load = tok_rows * top // (experts * ep_count)
    capacity = base_load + max(1, base_load // 16)
    total = ep_count * tok_rows
    groups = ep_count // GROUP
    members = GROUP * tok_rows
    cap = -(-GROUP * capacity // PACK) * PACK
    routes = groups * cap
    full = width + LANES
    here = lax.axis_index("ep")
    place = jnp.stack([here, lax.axis_index("dp"), here % GROUP, here // GROUP]).astype(jnp.int32)
    bits = dp_count.bit_length() - 1
    turns = 2
    share = width // dp_count

    def shape(*dims, dtype=bf16):
        return jax.ShapeDtypeStruct(dims, dtype)

    x_own = pl.pallas_call(
        functools.partial(pack_kernel, top),
        out_shape=shape(tok_rows, full),
        compiler_params=pltpu.CompilerParams(vmem_limit_bytes=VMEM_LIMIT),
        cost_estimate=cost(0, 4 * tok_rows * width),
        name="pack",
    )(tokens, expert_ids.T, gate_weights.T)
    x_all = lax.all_gather(x_own, "ep", axis=0, tiled=True)

    def reach(p, step):
        q = p + GROUP * step if p % GROUP == 0 else p - GROUP * step
        return q if 0 <= q < ep_count else None

    def hop(value, pairs):
        return lax.ppermute(value, "ep", pairs)

    def call(kernel, name, grid, flops, nbytes, in_specs, out_specs, out_shape, scratch_shapes, prefetch=0):
        return pl.pallas_call(
            kernel,
            grid_spec=pltpu.PrefetchScalarGridSpec(
                num_scalar_prefetch=prefetch,
                grid=(grid,),
                in_specs=in_specs,
                out_specs=out_specs,
                scratch_shapes=scratch_shapes,
            ),
            out_shape=out_shape,
            compiler_params=pltpu.CompilerParams(vmem_limit_bytes=VMEM_LIMIT),
            cost_estimate=cost(flops, nbytes),
            name=name,
        )

    row_bytes = 2 * experts * hidden * width
    w_flip = call(
        flip_kernel,
        "flip",
        experts,
        0,
        2 * row_bytes,
        in_specs=[SMEM, pl.BlockSpec((1, width, hidden), lambda b: (b, 0, 0))],
        out_specs=pl.BlockSpec((1, hidden, width), lambda b: (b, 0, 0)),
        out_shape=shape(experts, hidden, width),
        scratch_shapes=[],
    )(place, w_up)

    lines = [None] + [
        [(p, reach(p, 1)) for p in range(ep_count) if None not in (reach(p, 1), reach(p, 1 - step))]
        for step in range(1, groups)
    ]
    swaps = [None] + [
        [(p, p ^ 1) for p in range(ep_count) if reach(p, -step) is not None] for step in range(1, groups)
    ]
    dy_own = [cotangent, hop(cotangent, [(p, p ^ 1) for p in range(ep_count)])]
    dy_mine = [[hop(part, lines[1]) for part in dy_own]]
    dy_mine[0][0], w_flip = lax.optimization_barrier((dy_mine[0][0], w_flip))
    for step in range(2, groups - 1):
        dy_mine.append([hop(part, lines[step]) for part in dy_mine[-1]])
    dy_other = [[hop(part, swaps[1]) for part in dy_mine[0]]]
    dy_mine[1][0], dy_other[0] = lax.optimization_barrier((dy_mine[1][0], dy_other[0]))
    early_swap = hop(dy_mine[1][0], swaps[2])
    own_last, other_last = dy_mine[-1]
    other_last, early_swap = lax.optimization_barrier((other_last, early_swap))
    dy_mine.append([hop(own_last, lines[-1]), hop(other_last, lines[-1])])

    act = shape(experts, routes, hidden)
    pick_flops = 2 * total * experts * cap * width
    main_flops = 2 * experts * routes * width * hidden
    act3 = pltpu.VMEM((experts, routes, hidden), bf16)
    pick_v = pltpu.VMEM((groups, experts * cap, members), bf16)
    most = max(experts, groups)

    def one(kernel, name, flops, nbytes, in_specs, out_specs, out_shape, scratch_shapes):
        return pl.pallas_call(
            kernel,
            in_specs=in_specs,
            out_specs=out_specs,
            out_shape=out_shape,
            scratch_shapes=scratch_shapes,
            compiler_params=pltpu.CompilerParams(vmem_limit_bytes=VMEM_LIMIT),
            cost_estimate=cost(flops, nbytes),
            name=name,
        )

    x_all, other_last = lax.optimization_barrier((x_all, other_last))
    pick, meta, hid, scaled, slope_g = one(
        functools.partial(up_kernel, groups, width, top, cap),
        "up",
        pick_flops + main_flops,
        2 * total * full + row_bytes,
        [SMEM, ANY, ANY],
        [ANY, pl.BlockSpec(memory_space=pltpu.VMEM), ANY, ANY, ANY],
        [shape(groups, experts * cap, members), shape(total, LANES), act, act, act],
        [
            pltpu.VMEM((groups, members, full), bf16),
            pltpu.VMEM((experts, width, hidden), bf16),
            pltpu.VMEM((experts, routes, width), bf16),
            pltpu.VMEM((experts, routes, LANES), f32),
            pick_v,
            act3,
            act3,
            act3,
            pltpu.SemaphoreType.DMA((2, most)),
            pltpu.SemaphoreType.DMA((4, experts)),
        ],
    )(place, x_all, w_up)
    for row, swap in zip(dy_mine[1:], swaps[2:]):
        dy_other.append([])
        for n, part in enumerate(row):
            if len(dy_other) == 2 and n == 0:
                dy_other[-1].append(early_swap)
                continue
            part, hid = lax.optimization_barrier((part, hid))
            dy_other[-1].append(hop(part, swap))
    blocks = [part for row in [dy_own] + dy_mine + dy_other for part in row]

    orders = []
    for g in range(turns):
        turn = [(g + t) % bits for t in range(bits)]
        orders.append(
            tuple(sum(((p >> (bits - 1 - t)) & 1) << turn[t] for t in range(bits)) for p in range(dp_count))
        )
    orders = tuple(orders)
    cut_rows = share // turns

    def down(start, count):
        outs = one(
            functools.partial(down_kernel, orders, start),
            "down",
            16 * main_flops,
            8 * row_bytes,
            [SMEM, ANY, ANY],
            [ANY] * (2 * turns),
            [shape(dp_count // 2, count, cut_rows, hidden)] * (2 * turns),
            [
                pltpu.VMEM((count, routes, width), bf16),
                pltpu.VMEM((count, routes, hidden), bf16),
                pltpu.VMEM((turns, dp_count, count, cut_rows, hidden), bf16),
                pltpu.SemaphoreType.DMA((2, count)),
                pltpu.SemaphoreType.DMA((turns, dp_count, count)),
            ],
        )(place, kept, scaled)
        return [(outs[2 * g], outs[2 * g + 1]) for g in range(turns)]

    def exchange(state, t):
        new = []
        for g, (keep, send) in enumerate(state):
            bit = 1 << ((g + t) % bits)
            got = lax.ppermute(send, "dp", [(i, i ^ bit) for i in range(dp_count)])
            both = keep.astype(f32) + got.astype(f32)
            if t < bits - 1:
                both = both.astype(bf16)
            half = both.shape[0] // 2
            new.append((both[:half], both[half:]) if half else both[0])
        return new

    token_part, kept = one(
        functools.partial(tail_kernel, groups, cap, width, top),
        "tail",
        8 * main_flops,
        4 * row_bytes,
        [SMEM] + [ANY] * (4 * groups - 2) + [ANY] * 5 + [pl.BlockSpec(memory_space=pltpu.VMEM)],
        [ANY, ANY],
        [shape(total, full), shape(experts, routes, width)],
        [
            pick_v,
            pltpu.VMEM((groups, members, width), bf16),
            pltpu.VMEM((experts, routes, width), bf16),
            pltpu.VMEM((groups, experts * cap, full), bf16),
            pltpu.VMEM((groups, members, full), bf16),
            pltpu.VMEM((experts, width, hidden), bf16),
            pltpu.VMEM((experts, hidden, width), bf16),
            act3,
            act3,
            pltpu.SemaphoreType.DMA((groups, 2)),
            pltpu.SemaphoreType.DMA((5, experts)),
            pltpu.SemaphoreType.DMA((experts,)),
            pltpu.SemaphoreType.DMA((groups,)),
        ],
    )(place, *blocks, pick, w_down, w_flip, hid, slope_g, meta)
    summed = lax.psum_scatter(token_part, "ep", scatter_dimension=0, tiled=True)
    token_grad, gate_grad = pl.pallas_call(
        functools.partial(finish_kernel, width, top),
        out_shape=[shape(tok_rows, width), shape(top, tok_rows)],
        compiler_params=pltpu.CompilerParams(vmem_limit_bytes=VMEM_LIMIT),
        cost_estimate=cost(0, 4 * tok_rows * width),
        name="finish",
    )(summed)

    counts = [experts // 2, experts - experts // 2] if experts > 1 else [experts]
    states = [down(start, count) for start, count in zip((0, counts[0]), counts)]
    for t in range(bits - 1):
        states = [exchange(state, t) for state in states]
    last = bits - 1
    states = [
        [
            (keep, lax.ppermute(send, "dp", [(i, i ^ (1 << ((g + last) % bits))) for i in range(dp_count)]))
            for g, (keep, send) in enumerate(state)
        ]
        for state in states
    ]
    keeps = [keep for keep, _ in states[-1]]
    token_grad, keeps = lax.optimization_barrier((token_grad, keeps))
    states[-1] = [(keep, got) for keep, (_, got) in zip(keeps, states[-1])]
    down_grad, start = None, 0
    for count, state in zip(counts, states):
        operands = [x for pair in state for x in pair]
        dest = [] if down_grad is None else [down_grad]

        def put(*refs, start=start, skip=len(dest), used=len(operands)):
            put_kernel(start, *refs[:used], *refs[used + skip :])

        down_grad = pl.pallas_call(
            put,
            in_specs=[VMEM] * len(operands) + [ANY] * len(dest),
            out_specs=ANY,
            out_shape=shape(experts, share, hidden, dtype=f32),
            input_output_aliases={len(operands): 0} if dest else {},
            scratch_shapes=[
                pltpu.VMEM((turns, count, cut_rows, hidden), f32),
                pltpu.SemaphoreType.DMA((turns,)),
            ],
            compiler_params=pltpu.CompilerParams(vmem_limit_bytes=VMEM_LIMIT // 2),
            cost_estimate=cost(0, 4 * experts * share * hidden),
            name="put",
        )(*operands, *dest)
        start += count
    return (token_grad, gate_grad.T, down_grad)


def solution(mesh):
    return jax.shard_map(
        shards,
        mesh=mesh,
        in_specs=(
            P(("dp", "ep"), None),
            P(("dp", "ep"), None),
            P(("dp", "ep"), None),
            P(("dp", "ep"), None),
            P("ep", None, None),
            P("ep", None, None),
        ),
        out_specs=(P(("dp", "ep"), None), P(("dp", "ep"), None), P("ep", "dp", None)),
        check_vma=False,
    )
```

```python
import functools

import jax
import jax.numpy as jnp
from jax import lax
from jax.experimental import pallas as pl
from jax.experimental.pallas import tpu as pltpu
from jax.sharding import PartitionSpec as P

LANES = 128
PACK = 16
GROUP = 2
VMEM_LIMIT = 60 * 1024 * 1024
bf16, f32 = jnp.bfloat16, jnp.float32
ANY = pl.BlockSpec(memory_space=pl.ANY)
SMEM = pl.BlockSpec(memory_space=pltpu.SMEM)
VMEM = pl.BlockSpec(memory_space=pltpu.VMEM)
FIRST = (((0,), (0,)), ((), ()))


def dot(a, b, dims=(((1,), (0,)), ((), ()))):
    return lax.dot_general(a, b, dims, preferred_element_type=f32)


def pack_kernel(top, tokens, ids, gates, x_out, extra, sem):
    count, width = tokens.shape
    rows = pltpu.make_async_copy(tokens, x_out.at[:, pl.ds(0, width)], sem.at[0])
    rows.start()
    info = jnp.concatenate(
        [ids[...].astype(f32), gates[...].astype(f32), jnp.zeros((LANES - 2 * top, count), f32)], axis=0
    )
    extra[...] = info.T.astype(bf16)
    columns = pltpu.make_async_copy(extra, x_out.at[:, pl.ds(width, LANES)], sem.at[1])
    columns.start()
    rows.wait()
    columns.wait()


def flip_kernel(place, w, out):
    del place
    out[0] = w[0].T


def start_blocks(place, chips, own, mine, other, dst, sem):
    half = dst.shape[1] // 2

    def start(pair, slot, flip):
        for part in range(2):
            to = (part ^ flip) * half
            if not isinstance(flip, int):
                to = pl.multiple_of(to, half)
            pltpu.make_async_copy(pair[part], dst.at[slot, pl.ds(to, half), :], sem.at[slot, part]).start()

    start(own, 0, place[2])
    for slot in range(1, chips):
        for left in (True, False):
            for core in (True, False):
                pair = (mine if left == core else other)[(slot if left else chips - slot) - 1]

                @pl.when(((place[3] >= slot) == left) & ((place[2] == 0) == core))
                def _():
                    start(pair, slot, 0 if left else 1)


def copies_of(pairs, sem):
    return [pltpu.make_async_copy(src, dst, sem.at[n]) for n, (src, dst) in enumerate(pairs)]


def staged(steps, later):
    return [later[len(later) * n // steps : len(later) * (n + 1) // steps] for n in range(steps)]


def copy_all(pairs, sem):
    copies = copies_of(pairs, sem)
    for copy in copies:
        copy.start()
    return copies


def up_kernel(groups, width, top, cap, place, x_all, w_up, *refs):
    pick_out, meta, hid_out, scaled_out, slope_out, rows, w_v, held, gates, pick, hid, scaled, slope, sems, out_sem = refs
    experts, members = held.shape[0], rows.shape[1]
    arrive = copy_all([(x_all.at[pl.ds(g * members, members), :], rows.at[g]) for g in range(groups)], sems.at[0])
    weights = copies_of([(w_up.at[b], w_v.at[b]) for b in range(experts)], sems.at[1])
    stages = staged(groups, weights)
    before = lax.broadcasted_iota(jnp.int32, (members, members), 0) < lax.broadcasted_iota(
        jnp.int32, (members, members), 1
    )
    before = before.astype(bf16)
    spot = lax.broadcasted_iota(jnp.int32, (cap, members), 0).astype(f32)
    for g in range(groups):
        arrive[g].wait()
        for copy in stages[g]:
            copy.start()
        info = rows[g, :, pl.ds(width, LANES)]
        meta[pl.ds(g * members, members), :] = info
        across = info.astype(f32).T
        ids, parts = across[:top], across[top : 2 * top]
        chosen = [ids == (place[0] * experts + b).astype(f32) for b in range(experts)]
        member = [jnp.sum(jnp.where(hit, 1.0, 0.0), axis=0, keepdims=True) for hit in chosen]
        table = jnp.concatenate(member + [jnp.zeros((PACK - experts, members), f32)], axis=0)
        prior = dot(table.astype(bf16), before)
        for b in range(experts):
            rank = jnp.where(member[b] > 0.0, prior[b : b + 1], -1.0)
            one = jnp.where(spot == rank, 1.0, 0.0)
            gate = jnp.sum(jnp.where(chosen[b], parts, 0.0), axis=0, keepdims=True)
            pick[g, pl.ds(b * cap, cap), :] = one.astype(bf16)
            gates[b, pl.ds(g * cap, cap), :] = jnp.broadcast_to(
                jnp.sum(one * gate, axis=1, keepdims=True), (cap, LANES)
            )
        got = dot(pick[g], rows[g, :, pl.ds(0, width)]).astype(bf16)
        for b in range(experts):
            held[b, pl.ds(g * cap, cap), :] = got[b * cap : (b + 1) * cap]
    outs = copy_all([(pick, pick_out)], out_sem.at[3])
    for b in range(experts):
        weights[b].wait()
        pre = dot(held[b], w_v[b])
        gate = gates[b][:, :1]
        sig = 0.5 + 0.5 * jnp.tanh(0.5 * pre)
        act = pre * sig
        hid[b] = act.astype(bf16)
        scaled[b] = (gate * act).astype(bf16)
        slope[b] = (gate * (sig + act * (1.0 - sig))).astype(bf16)
        for n, (src, dst) in enumerate(((hid, hid_out), (scaled, scaled_out), (slope, slope_out))):
            copy = pltpu.make_async_copy(src.at[b], dst.at[b], out_sem.at[n, b])
            copy.start()
            outs.append(copy)
    for copy in outs:
        copy.wait()


def down_kernel(orders, start, place, kept, scaled_in, *refs):
    outs, (rows, scaled, sent, in_sem, sem) = refs[:-5], refs[-5:]
    experts = sent.shape[2]
    arrive = copy_all([(kept.at[start + b], rows.at[b]) for b in range(experts)], in_sem.at[0])
    others = copy_all([(scaled_in.at[start + b], scaled.at[b]) for b in range(experts)], in_sem.at[1])
    parts = len(orders[0])
    half = parts // 2
    share = rows.shape[2] // parts
    cut = share // len(orders)
    copies = []
    for b in range(experts):
        arrive[b].wait()
        others[b].wait()
        for q in range(parts):
            at = pl.multiple_of((place[1] ^ q) * share, LANES)
            full = dot(rows[b, :, pl.ds(at, share)], scaled[b], FIRST).astype(bf16)
            for g, order in enumerate(orders):
                sent[g, q, b] = full[g * cut : (g + 1) * cut]
                p = order.index(q)
                copy = pltpu.make_async_copy(
                    sent.at[g, q, b], outs[2 * g + p // half].at[p % half, b], sem.at[g, q, b]
                )
                copy.start()
                copies.append(copy)
    for copy in copies:
        copy.wait()


def tail_kernel(groups, cap, width, top, place, *refs):
    count = 2 * groups - 1
    halves = [(refs[2 * n], refs[2 * n + 1]) for n in range(count)]
    own, mine, other, refs = halves[0], halves[1:groups], halves[groups:], refs[2 * count :]
    pick_in, w_down, w_flip, hid_in, slope_in, meta, out_all, kept = refs[:8]
    pick, moved, held, grads, out, down_v, flip_v, hid, slope, block_sem, sems, keep_sem, out_sem = refs[8:]
    experts, members = held.shape[0], moved.shape[1]
    half = members // 2
    first_pick = copy_all([(pick_in, pick)], sems.at[0])
    start_blocks(place, groups, own, mine, other, moved, block_sem)
    loads = [
        copies_of([(src.at[b], dst.at[b]) for b in range(experts)], sems.at[n])
        for n, (src, dst) in enumerate(((w_down, down_v), (hid_in, hid), (slope_in, slope), (w_flip, flip_v)), 1)
    ]
    stages = staged(groups, [load[b] for b in range(experts) for load in loads])
    first_pick[0].wait()
    for slot in range(groups):
        for part in range(2):
            at = pl.ds(part * half, half)
            pltpu.make_async_copy(own[0], moved.at[slot, at, :], block_sem.at[slot, part]).wait()
        for copy in stages[slot]:
            copy.start()
        group = lax.rem(place[3] - slot + groups, groups)
        first = pl.multiple_of(group * cap, PACK)
        got = dot(pick[group], moved[slot]).astype(bf16)
        for b in range(experts):
            held[b, pl.ds(first, cap), :] = got[b * cap : (b + 1) * cap]
    lane = lax.broadcasted_iota(jnp.int32, (groups * cap, LANES), 1)
    for b in range(experts):
        for load in loads[:3]:
            load[b].wait()
        back = dot(held[b], down_v[b])
        gate = jnp.sum(back * hid[b].astype(f32), axis=1, keepdims=True)
        gate = jnp.where(lane == b, gate, 0.0).astype(bf16)
        grad = (back * slope[b].astype(f32)).astype(bf16)
        loads[3][b].wait()
        route = dot(grad, flip_v[b]).astype(bf16)
        for g in range(groups):
            grads[g, pl.ds(b * cap, cap), pl.ds(0, width)] = route[g * cap : (g + 1) * cap]
            grads[g, pl.ds(b * cap, cap), pl.ds(width, LANES)] = gate[g * cap : (g + 1) * cap]
    keep = copy_all([(held.at[b], kept.at[b]) for b in range(experts)], keep_sem)
    lane = lax.broadcasted_iota(jnp.int32, (members, LANES), 1)
    for g in range(groups):
        total = dot(pick[g], grads[g], FIRST)
        out[g, :, pl.ds(0, width)] = total[:, :width].astype(bf16)
        by_expert = total[:, width:]
        ids = jnp.where(lane < top, meta[pl.ds(g * members, members), :].astype(f32), -1.0)
        picked = jnp.zeros(ids.shape, f32)
        for b in range(experts):
            hit = ids == (place[0] * experts + b).astype(f32)
            picked = picked + jnp.where(hit, by_expert[:, b : b + 1], 0.0)
        out[g, :, pl.ds(width, LANES)] = picked.astype(bf16)
        copy = pltpu.make_async_copy(out.at[g], out_all.at[pl.ds(g * members, members), :], out_sem.at[g])
        copy.start()
        keep.append(copy)
    for copy in keep:
        copy.wait()


def put_kernel(start, *refs):
    *pairs, out, total, sem = refs
    count = total.shape[1]
    cut = total.shape[2]
    copies = []
    for g in range(total.shape[0]):
        keep, got = pairs[2 * g], pairs[2 * g + 1]
        total[g] = keep[0].astype(f32) + got[0].astype(f32)
        copies.append(
            pltpu.make_async_copy(
                total.at[g], out.at[pl.ds(start, count), pl.ds(g * cut, cut), :], sem.at[g]
            )
        )
        copies[-1].start()
    for copy in copies:
        copy.wait()


def finish_kernel(width, top, rows, token, gate):
    token[...] = rows[:, pl.ds(0, width)]
    gate[...] = rows[:, pl.ds(width, LANES)].astype(f32).T[:top].astype(bf16)


def cost(flops, nbytes):
    return pl.CostEstimate(flops=int(flops), bytes_accessed=int(nbytes), transcendentals=0)


def shards(tokens, cotangent, expert_ids, gate_weights, w_up, w_down):
    tok_rows, width = tokens.shape
    top = expert_ids.shape[1]
    ep_count, dp_count = lax.axis_size("ep"), lax.axis_size("dp")
    experts, _, hidden = w_up.shape
    base_load = tok_rows * top // (experts * ep_count)
    capacity = base_load + max(1, base_load // 16)
    total = ep_count * tok_rows
    groups = ep_count // GROUP
    members = GROUP * tok_rows
    cap = -(-GROUP * capacity // PACK) * PACK
    routes = groups * cap
    full = width + LANES
    here = lax.axis_index("ep")
    place = jnp.stack([here, lax.axis_index("dp"), here % GROUP, here // GROUP]).astype(jnp.int32)
    bits = dp_count.bit_length() - 1
    turns = 2
    share = width // dp_count

    def shape(*dims, dtype=bf16):
        return jax.ShapeDtypeStruct(dims, dtype)

    x_own = pl.pallas_call(
        functools.partial(pack_kernel, top),
        in_specs=[ANY, VMEM, VMEM],
        out_specs=ANY,
        out_shape=shape(tok_rows, full),
        scratch_shapes=[pltpu.VMEM((tok_rows, LANES), bf16), pltpu.SemaphoreType.DMA((2,))],
        compiler_params=pltpu.CompilerParams(vmem_limit_bytes=VMEM_LIMIT),
        cost_estimate=cost(0, 4 * tok_rows * width),
        name="pack",
    )(tokens, expert_ids.T, gate_weights.T)
    x_all = lax.all_gather(x_own, "ep", axis=0, tiled=True)

    def reach(p, step):
        q = p + GROUP * step if p % GROUP == 0 else p - GROUP * step
        return q if 0 <= q < ep_count else None

    def hop(value, pairs):
        return lax.ppermute(value, "ep", pairs)

    def call(kernel, name, grid, flops, nbytes, in_specs, out_specs, out_shape, scratch_shapes, prefetch=0):
        return pl.pallas_call(
            kernel,
            grid_spec=pltpu.PrefetchScalarGridSpec(
                num_scalar_prefetch=prefetch,
                grid=(grid,),
                in_specs=in_specs,
                out_specs=out_specs,
                scratch_shapes=scratch_shapes,
            ),
            out_shape=out_shape,
            compiler_params=pltpu.CompilerParams(vmem_limit_bytes=VMEM_LIMIT),
            cost_estimate=cost(flops, nbytes),
            name=name,
        )

    row_bytes = 2 * experts * hidden * width
    w_flip = call(
        flip_kernel,
        "flip",
        experts,
        0,
        2 * row_bytes,
        in_specs=[SMEM, pl.BlockSpec((1, width, hidden), lambda b: (b, 0, 0))],
        out_specs=pl.BlockSpec((1, hidden, width), lambda b: (b, 0, 0)),
        out_shape=shape(experts, hidden, width),
        scratch_shapes=[],
    )(place, w_up)

    lines = [None] + [
        [(p, reach(p, 1)) for p in range(ep_count) if None not in (reach(p, 1), reach(p, 1 - step))]
        for step in range(1, groups)
    ]
    swaps = [None] + [
        [(p, p ^ 1) for p in range(ep_count) if reach(p, -step) is not None] for step in range(1, groups)
    ]
    dy_own = [cotangent, hop(cotangent, [(p, p ^ 1) for p in range(ep_count)])]
    dy_mine = [[hop(part, lines[1]) for part in dy_own]]
    dy_mine[0][0], w_flip = lax.optimization_barrier((dy_mine[0][0], w_flip))
    for step in range(2, groups - 1):
        dy_mine.append([hop(part, lines[step]) for part in dy_mine[-1]])
    dy_other = [[hop(part, swaps[1]) for part in dy_mine[0]]]
    dy_mine[1][0], dy_other[0] = lax.optimization_barrier((dy_mine[1][0], dy_other[0]))
    early_swap = hop(dy_mine[1][0], swaps[2])
    own_last, other_last = dy_mine[-1]
    other_last, early_swap = lax.optimization_barrier((other_last, early_swap))
    dy_mine.append([hop(own_last, lines[-1]), hop(other_last, lines[-1])])

    act = shape(experts, routes, hidden)
    pick_flops = 2 * total * experts * cap * width
    main_flops = 2 * experts * routes * width * hidden
    act3 = pltpu.VMEM((experts, routes, hidden), bf16)
    pick_v = pltpu.VMEM((groups, experts * cap, members), bf16)
    most = max(experts, groups)

    def one(kernel, name, flops, nbytes, in_specs, out_specs, out_shape, scratch_shapes):
        return pl.pallas_call(
            kernel,
            in_specs=in_specs,
            out_specs=out_specs,
            out_shape=out_shape,
            scratch_shapes=scratch_shapes,
            compiler_params=pltpu.CompilerParams(vmem_limit_bytes=VMEM_LIMIT),
            cost_estimate=cost(flops, nbytes),
            name=name,
        )

    x_all, other_last = lax.optimization_barrier((x_all, other_last))
    pick, meta, hid, scaled, slope_g = one(
        functools.partial(up_kernel, groups, width, top, cap),
        "up",
        pick_flops + main_flops,
        2 * total * full + row_bytes,
        [SMEM, ANY, ANY],
        [ANY, pl.BlockSpec(memory_space=pltpu.VMEM), ANY, ANY, ANY],
        [shape(groups, experts * cap, members), shape(total, LANES), act, act, act],
        [
            pltpu.VMEM((groups, members, full), bf16),
            pltpu.VMEM((experts, width, hidden), bf16),
            pltpu.VMEM((experts, routes, width), bf16),
            pltpu.VMEM((experts, routes, LANES), f32),
            pick_v,
            act3,
            act3,
            act3,
            pltpu.SemaphoreType.DMA((2, most)),
            pltpu.SemaphoreType.DMA((4, experts)),
        ],
    )(place, x_all, w_up)
    for row, swap in zip(dy_mine[1:], swaps[2:]):
        dy_other.append([])
        for n, part in enumerate(row):
            if len(dy_other) == 2 and n == 0:
                dy_other[-1].append(early_swap)
                continue
            part, hid = lax.optimization_barrier((part, hid))
            dy_other[-1].append(hop(part, swap))
    blocks = [part for row in [dy_own] + dy_mine + dy_other for part in row]

    orders = []
    for g in range(turns):
        turn = [(g + t) % bits for t in range(bits)]
        orders.append(
            tuple(sum(((p >> (bits - 1 - t)) & 1) << turn[t] for t in range(bits)) for p in range(dp_count))
        )
    orders = tuple(orders)
    cut_rows = share // turns

    def down(start, count):
        outs = one(
            functools.partial(down_kernel, orders, start),
            "down",
            16 * main_flops,
            8 * row_bytes,
            [SMEM, ANY, ANY],
            [ANY] * (2 * turns),
            [shape(dp_count // 2, count, cut_rows, hidden)] * (2 * turns),
            [
                pltpu.VMEM((count, routes, width), bf16),
                pltpu.VMEM((count, routes, hidden), bf16),
                pltpu.VMEM((turns, dp_count, count, cut_rows, hidden), bf16),
                pltpu.SemaphoreType.DMA((2, count)),
                pltpu.SemaphoreType.DMA((turns, dp_count, count)),
            ],
        )(place, kept, scaled)
        return [(outs[2 * g], outs[2 * g + 1]) for g in range(turns)]

    def exchange(state, t):
        new = []
        for g, (keep, send) in enumerate(state):
            bit = 1 << ((g + t) % bits)
            got = lax.ppermute(send, "dp", [(i, i ^ bit) for i in range(dp_count)])
            both = keep.astype(f32) + got.astype(f32)
            if t < bits - 1:
                both = both.astype(bf16)
            half = both.shape[0] // 2
            new.append((both[:half], both[half:]) if half else both[0])
        return new

    token_part, kept = one(
        functools.partial(tail_kernel, groups, cap, width, top),
        "tail",
        8 * main_flops,
        4 * row_bytes,
        [SMEM] + [ANY] * (4 * groups - 2) + [ANY] * 5 + [pl.BlockSpec(memory_space=pltpu.VMEM)],
        [ANY, ANY],
        [shape(total, full), shape(experts, routes, width)],
        [
            pick_v,
            pltpu.VMEM((groups, members, width), bf16),
            pltpu.VMEM((experts, routes, width), bf16),
            pltpu.VMEM((groups, experts * cap, full), bf16),
            pltpu.VMEM((groups, members, full), bf16),
            pltpu.VMEM((experts, width, hidden), bf16),
            pltpu.VMEM((experts, hidden, width), bf16),
            act3,
            act3,
            pltpu.SemaphoreType.DMA((groups, 2)),
            pltpu.SemaphoreType.DMA((5, experts)),
            pltpu.SemaphoreType.DMA((experts,)),
            pltpu.SemaphoreType.DMA((groups,)),
        ],
    )(place, *blocks, pick, w_down, w_flip, hid, slope_g, meta)
    summed = lax.psum_scatter(token_part, "ep", scatter_dimension=0, tiled=True)
    token_grad, gate_grad = pl.pallas_call(
        functools.partial(finish_kernel, width, top),
        out_shape=[shape(tok_rows, width), shape(top, tok_rows)],
        compiler_params=pltpu.CompilerParams(vmem_limit_bytes=VMEM_LIMIT),
        cost_estimate=cost(0, 4 * tok_rows * width),
        name="finish",
    )(summed)

    counts = [experts // 2, experts - experts // 2] if experts > 1 else [experts]
    states = [down(start, count) for start, count in zip((0, counts[0]), counts)]
    for t in range(bits - 1):
        states = [exchange(state, t) for state in states]
    last = bits - 1
    states = [
        [
            (keep, lax.ppermute(send, "dp", [(i, i ^ (1 << ((g + last) % bits))) for i in range(dp_count)]))
            for g, (keep, send) in enumerate(state)
        ]
        for state in states
    ]
    keeps = [keep for keep, _ in states[-1]]
    token_grad, keeps = lax.optimization_barrier((token_grad, keeps))
    states[-1] = [(keep, got) for keep, (_, got) in zip(keeps, states[-1])]
    down_grad, start = None, 0
    for count, state in zip(counts, states):
        operands = [x for pair in state for x in pair]
        dest = [] if down_grad is None else [down_grad]

        def put(*refs, start=start, skip=len(dest), used=len(operands)):
            put_kernel(start, *refs[:used], *refs[used + skip :])

        down_grad = pl.pallas_call(
            put,
            in_specs=[VMEM] * len(operands) + [ANY] * len(dest),
            out_specs=ANY,
            out_shape=shape(experts, share, hidden, dtype=f32),
            input_output_aliases={len(operands): 0} if dest else {},
            scratch_shapes=[
                pltpu.VMEM((turns, count, cut_rows, hidden), f32),
                pltpu.SemaphoreType.DMA((turns,)),
            ],
            compiler_params=pltpu.CompilerParams(vmem_limit_bytes=VMEM_LIMIT // 2),
            cost_estimate=cost(0, 4 * experts * share * hidden),
            name="put",
        )(*operands, *dest)
        start += count
    return (token_grad, gate_grad.T, down_grad)


def solution(mesh):
    return jax.shard_map(
        shards,
        mesh=mesh,
        in_specs=(
            P(("dp", "ep"), None),
            P(("dp", "ep"), None),
            P(("dp", "ep"), None),
            P(("dp", "ep"), None),
            P("ep", None, None),
            P("ep", None, None),
        ),
        out_specs=(P(("dp", "ep"), None), P(("dp", "ep"), None), P("ep", "dp", None)),
        check_vma=False,
    )
```

```python
import functools

import jax
import jax.numpy as jnp
from jax import lax
from jax.experimental import pallas as pl
from jax.experimental.pallas import tpu as pltpu
from jax.sharding import PartitionSpec as P

LANES = 128
PACK = 16
GROUP = 2
VMEM_LIMIT = 60 * 1024 * 1024
bf16, f32 = jnp.bfloat16, jnp.float32
ANY = pl.BlockSpec(memory_space=pl.ANY)
SMEM = pl.BlockSpec(memory_space=pltpu.SMEM)
VMEM = pl.BlockSpec(memory_space=pltpu.VMEM)
FIRST = (((0,), (0,)), ((), ()))


def dot(a, b, dims=(((1,), (0,)), ((), ()))):
    return lax.dot_general(a, b, dims, preferred_element_type=f32)


def pack_kernel(top, tokens, ids, gates, x_out):
    count, width = tokens.shape
    x_out[:, pl.ds(0, width)] = tokens[...]
    info = jnp.concatenate(
        [ids[...].astype(f32), gates[...].astype(f32), jnp.zeros((LANES - 2 * top, count), f32)], axis=0
    )
    x_out[:, pl.ds(width, LANES)] = info.T.astype(bf16)


def flip_kernel(place, w, out):
    del place
    out[0] = w[0].T


def start_blocks(place, chips, own, mine, other, dst, sem):
    half = dst.shape[1] // 2

    def start(pair, slot, flip):
        for part in range(2):
            to = (part ^ flip) * half
            if not isinstance(flip, int):
                to = pl.multiple_of(to, half)
            pltpu.make_async_copy(pair[part], dst.at[slot, pl.ds(to, half), :], sem.at[slot, part]).start()

    start(own, 0, place[2])
    for slot in range(1, chips):
        for left in (True, False):
            for core in (True, False):
                pair = (mine if left == core else other)[(slot if left else chips - slot) - 1]

                @pl.when(((place[3] >= slot) == left) & ((place[2] == 0) == core))
                def _():
                    start(pair, slot, 0 if left else 1)


def copies_of(pairs, sem):
    return [pltpu.make_async_copy(src, dst, sem.at[n]) for n, (src, dst) in enumerate(pairs)]


def staged(steps, later):
    return [later[len(later) * n // steps : len(later) * (n + 1) // steps] for n in range(steps)]


def copy_all(pairs, sem):
    copies = copies_of(pairs, sem)
    for copy in copies:
        copy.start()
    return copies


def up_kernel(groups, width, top, cap, place, x_all, w_up, *refs):
    pick_out, meta, hid_out, scaled_out, slope_out, rows, w_v, held, gates, pick, hid, scaled, slope, sems, out_sem = refs
    experts, members = held.shape[0], rows.shape[1]
    arrive = copy_all([(x_all.at[pl.ds(g * members, members), :], rows.at[g]) for g in range(groups)], sems.at[0])
    weights = copies_of([(w_up.at[b], w_v.at[b]) for b in range(experts)], sems.at[1])
    stages = staged(groups, weights)
    before = lax.broadcasted_iota(jnp.int32, (members, members), 0) < lax.broadcasted_iota(
        jnp.int32, (members, members), 1
    )
    before = before.astype(bf16)
    spot = lax.broadcasted_iota(jnp.int32, (cap, members), 0).astype(f32)
    for g in range(groups):
        arrive[g].wait()
        for copy in stages[g]:
            copy.start()
        info = rows[g, :, pl.ds(width, LANES)]
        meta[pl.ds(g * members, members), :] = info
        across = info.astype(f32).T
        ids, parts = across[:top], across[top : 2 * top]
        chosen = [ids == (place[0] * experts + b).astype(f32) for b in range(experts)]
        member = [jnp.sum(jnp.where(hit, 1.0, 0.0), axis=0, keepdims=True) for hit in chosen]
        table = jnp.concatenate(member + [jnp.zeros((PACK - experts, members), f32)], axis=0)
        prior = dot(table.astype(bf16), before)
        for b in range(experts):
            rank = jnp.where(member[b] > 0.0, prior[b : b + 1], -1.0)
            one = jnp.where(spot == rank, 1.0, 0.0)
            gate = jnp.sum(jnp.where(chosen[b], parts, 0.0), axis=0, keepdims=True)
            pick[g, pl.ds(b * cap, cap), :] = one.astype(bf16)
            gates[b, pl.ds(g * cap, cap), :] = jnp.broadcast_to(
                jnp.sum(one * gate, axis=1, keepdims=True), (cap, LANES)
            )
        got = dot(pick[g], rows[g, :, pl.ds(0, width)]).astype(bf16)
        for b in range(experts):
            held[b, pl.ds(g * cap, cap), :] = got[b * cap : (b + 1) * cap]
    outs = copy_all([(pick, pick_out)], out_sem.at[3])
    for b in range(experts):
        weights[b].wait()
        pre = dot(held[b], w_v[b])
        gate = gates[b][:, :1]
        sig = 0.5 + 0.5 * jnp.tanh(0.5 * pre)
        act = pre * sig
        hid[b] = act.astype(bf16)
        scaled[b] = (gate * act).astype(bf16)
        slope[b] = (gate * (sig + act * (1.0 - sig))).astype(bf16)
        for n, (src, dst) in enumerate(((hid, hid_out), (scaled, scaled_out), (slope, slope_out))):
            copy = pltpu.make_async_copy(src.at[b], dst.at[b], out_sem.at[n, b])
            copy.start()
            outs.append(copy)
    for copy in outs:
        copy.wait()


def down_kernel(orders, start, place, kept, scaled_in, *refs):
    outs, (rows, scaled, sent, in_sem, sem) = refs[:-5], refs[-5:]
    experts = sent.shape[2]
    arrive = copy_all([(kept.at[start + b], rows.at[b]) for b in range(experts)], in_sem.at[0])
    others = copy_all([(scaled_in.at[start + b], scaled.at[b]) for b in range(experts)], in_sem.at[1])
    parts = len(orders[0])
    half = parts // 2
    share = rows.shape[2] // parts
    cut = share // len(orders)
    copies = []
    for b in range(experts):
        arrive[b].wait()
        others[b].wait()
        for q in range(parts):
            at = pl.multiple_of((place[1] ^ q) * share, LANES)
            full = dot(rows[b, :, pl.ds(at, share)], scaled[b], FIRST).astype(bf16)
            for g, order in enumerate(orders):
                sent[g, q, b] = full[g * cut : (g + 1) * cut]
                p = order.index(q)
                copy = pltpu.make_async_copy(
                    sent.at[g, q, b], outs[2 * g + p // half].at[p % half, b], sem.at[g, q, b]
                )
                copy.start()
                copies.append(copy)
    for copy in copies:
        copy.wait()


def tail_kernel(groups, cap, width, top, place, *refs):
    count = 2 * groups - 1
    halves = [(refs[2 * n], refs[2 * n + 1]) for n in range(count)]
    own, mine, other, refs = halves[0], halves[1:groups], halves[groups:], refs[2 * count :]
    pick_in, w_down, w_flip, hid_in, slope_in, meta, out_all, kept = refs[:8]
    pick, moved, held, grads, out, down_v, flip_v, hid, slope, block_sem, sems, keep_sem, out_sem = refs[8:]
    experts, members = held.shape[0], moved.shape[1]
    half = members // 2
    first_pick = copy_all([(pick_in, pick)], sems.at[0])
    start_blocks(place, groups, own, mine, other, moved, block_sem)
    loads = [
        copies_of([(src.at[b], dst.at[b]) for b in range(experts)], sems.at[n])
        for n, (src, dst) in enumerate(((w_down, down_v), (hid_in, hid), (slope_in, slope), (w_flip, flip_v)), 1)
    ]
    stages = staged(groups, [load[b] for b in range(experts) for load in loads])
    first_pick[0].wait()
    for slot in range(groups):
        for part in range(2):
            at = pl.ds(part * half, half)
            pltpu.make_async_copy(own[0], moved.at[slot, at, :], block_sem.at[slot, part]).wait()
        for copy in stages[slot]:
            copy.start()
        group = lax.rem(place[3] - slot + groups, groups)
        first = pl.multiple_of(group * cap, PACK)
        got = dot(pick[group], moved[slot]).astype(bf16)
        for b in range(experts):
            held[b, pl.ds(first, cap), :] = got[b * cap : (b + 1) * cap]
    keep = copy_all([(held.at[b], kept.at[b]) for b in range(experts)], keep_sem)
    lane = lax.broadcasted_iota(jnp.int32, (groups * cap, LANES), 1)
    for b in range(experts):
        for load in loads[:3]:
            load[b].wait()
        back = dot(held[b], down_v[b])
        gate = jnp.sum(back * hid[b].astype(f32), axis=1, keepdims=True)
        gate = jnp.where(lane == b, gate, 0.0).astype(bf16)
        grad = (back * slope[b].astype(f32)).astype(bf16)
        loads[3][b].wait()
        route = dot(grad, flip_v[b]).astype(bf16)
        for g in range(groups):
            grads[g, pl.ds(b * cap, cap), pl.ds(0, width)] = route[g * cap : (g + 1) * cap]
            grads[g, pl.ds(b * cap, cap), pl.ds(width, LANES)] = gate[g * cap : (g + 1) * cap]
    lane = lax.broadcasted_iota(jnp.int32, (members, LANES), 1)
    for g in range(groups):
        total = dot(pick[g], grads[g], FIRST)
        out[g, :, pl.ds(0, width)] = total[:, :width].astype(bf16)
        by_expert = total[:, width:]
        ids = jnp.where(lane < top, meta[pl.ds(g * members, members), :].astype(f32), -1.0)
        picked = jnp.zeros(ids.shape, f32)
        for b in range(experts):
            hit = ids == (place[0] * experts + b).astype(f32)
            picked = picked + jnp.where(hit, by_expert[:, b : b + 1], 0.0)
        out[g, :, pl.ds(width, LANES)] = picked.astype(bf16)
        copy = pltpu.make_async_copy(out.at[g], out_all.at[pl.ds(g * members, members), :], out_sem.at[g])
        copy.start()
        keep.append(copy)
    for copy in keep:
        copy.wait()


def put_kernel(start, *refs):
    *pairs, out, total, sem = refs
    count = total.shape[1]
    cut = total.shape[2]
    copies = []
    for g in range(total.shape[0]):
        keep, got = pairs[2 * g], pairs[2 * g + 1]
        total[g] = keep[0].astype(f32) + got[0].astype(f32)
        copies.append(
            pltpu.make_async_copy(
                total.at[g], out.at[pl.ds(start, count), pl.ds(g * cut, cut), :], sem.at[g]
            )
        )
        copies[-1].start()
    for copy in copies:
        copy.wait()


def finish_kernel(width, top, rows, token, gate):
    token[...] = rows[:, pl.ds(0, width)]
    gate[...] = rows[:, pl.ds(width, LANES)].astype(f32).T[:top].astype(bf16)


def cost(flops, nbytes):
    return pl.CostEstimate(flops=int(flops), bytes_accessed=int(nbytes), transcendentals=0)


def shards(tokens, cotangent, expert_ids, gate_weights, w_up, w_down):
    tok_rows, width = tokens.shape
    top = expert_ids.shape[1]
    ep_count, dp_count = lax.axis_size("ep"), lax.axis_size("dp")
    experts, _, hidden = w_up.shape
    base_load = tok_rows * top // (experts * ep_count)
    capacity = base_load + max(1, base_load // 16)
    total = ep_count * tok_rows
    groups = ep_count // GROUP
    members = GROUP * tok_rows
    cap = -(-GROUP * capacity // PACK) * PACK
    routes = groups * cap
    full = width + LANES
    here = lax.axis_index("ep")
    place = jnp.stack([here, lax.axis_index("dp"), here % GROUP, here // GROUP]).astype(jnp.int32)
    bits = dp_count.bit_length() - 1
    turns = 2
    share = width // dp_count

    def shape(*dims, dtype=bf16):
        return jax.ShapeDtypeStruct(dims, dtype)

    x_own = pl.pallas_call(
        functools.partial(pack_kernel, top),
        out_shape=shape(tok_rows, full),
        compiler_params=pltpu.CompilerParams(vmem_limit_bytes=VMEM_LIMIT),
        cost_estimate=cost(0, 4 * tok_rows * width),
        name="pack",
    )(tokens, expert_ids.T, gate_weights.T)
    x_all = lax.all_gather(x_own, "ep", axis=0, tiled=True)

    def reach(p, step):
        q = p + GROUP * step if p % GROUP == 0 else p - GROUP * step
        return q if 0 <= q < ep_count else None

    def hop(value, pairs):
        return lax.ppermute(value, "ep", pairs)

    def call(kernel, name, grid, flops, nbytes, in_specs, out_specs, out_shape, scratch_shapes, prefetch=0):
        return pl.pallas_call(
            kernel,
            grid_spec=pltpu.PrefetchScalarGridSpec(
                num_scalar_prefetch=prefetch,
                grid=(grid,),
                in_specs=in_specs,
                out_specs=out_specs,
                scratch_shapes=scratch_shapes,
            ),
            out_shape=out_shape,
            compiler_params=pltpu.CompilerParams(vmem_limit_bytes=VMEM_LIMIT),
            cost_estimate=cost(flops, nbytes),
            name=name,
        )

    row_bytes = 2 * experts * hidden * width
    w_flip = call(
        flip_kernel,
        "flip",
        experts,
        0,
        2 * row_bytes,
        in_specs=[SMEM, pl.BlockSpec((1, width, hidden), lambda b: (b, 0, 0))],
        out_specs=pl.BlockSpec((1, hidden, width), lambda b: (b, 0, 0)),
        out_shape=shape(experts, hidden, width),
        scratch_shapes=[],
    )(place, w_up)

    lines = [None] + [
        [(p, reach(p, 1)) for p in range(ep_count) if None not in (reach(p, 1), reach(p, 1 - step))]
        for step in range(1, groups)
    ]
    swaps = [None] + [
        [(p, p ^ 1) for p in range(ep_count) if reach(p, -step) is not None] for step in range(1, groups)
    ]
    dy_own = [cotangent, hop(cotangent, [(p, p ^ 1) for p in range(ep_count)])]
    dy_mine = [[hop(part, lines[1]) for part in dy_own]]
    dy_mine[0][0], w_flip = lax.optimization_barrier((dy_mine[0][0], w_flip))
    for step in range(2, groups - 1):
        dy_mine.append([hop(part, lines[step]) for part in dy_mine[-1]])
    dy_other = [[hop(part, swaps[1]) for part in dy_mine[0]]]
    dy_mine[1][0], dy_other[0] = lax.optimization_barrier((dy_mine[1][0], dy_other[0]))
    early_swap = hop(dy_mine[1][0], swaps[2])
    own_last, other_last = dy_mine[-1]
    other_last, early_swap = lax.optimization_barrier((other_last, early_swap))
    dy_mine.append([hop(own_last, lines[-1]), hop(other_last, lines[-1])])

    act = shape(experts, routes, hidden)
    pick_flops = 2 * total * experts * cap * width
    main_flops = 2 * experts * routes * width * hidden
    act3 = pltpu.VMEM((experts, routes, hidden), bf16)
    pick_v = pltpu.VMEM((groups, experts * cap, members), bf16)
    most = max(experts, groups)

    def one(kernel, name, flops, nbytes, in_specs, out_specs, out_shape, scratch_shapes):
        return pl.pallas_call(
            kernel,
            in_specs=in_specs,
            out_specs=out_specs,
            out_shape=out_shape,
            scratch_shapes=scratch_shapes,
            compiler_params=pltpu.CompilerParams(vmem_limit_bytes=VMEM_LIMIT),
            cost_estimate=cost(flops, nbytes),
            name=name,
        )

    x_all, other_last = lax.optimization_barrier((x_all, other_last))
    pick, meta, hid, scaled, slope_g = one(
        functools.partial(up_kernel, groups, width, top, cap),
        "up",
        pick_flops + main_flops,
        2 * total * full + row_bytes,
        [SMEM, ANY, ANY],
        [ANY, pl.BlockSpec(memory_space=pltpu.VMEM), ANY, ANY, ANY],
        [shape(groups, experts * cap, members), shape(total, LANES), act, act, act],
        [
            pltpu.VMEM((groups, members, full), bf16),
            pltpu.VMEM((experts, width, hidden), bf16),
            pltpu.VMEM((experts, routes, width), bf16),
            pltpu.VMEM((experts, routes, LANES), f32),
            pick_v,
            act3,
            act3,
            act3,
            pltpu.SemaphoreType.DMA((2, most)),
            pltpu.SemaphoreType.DMA((4, experts)),
        ],
    )(place, x_all, w_up)
    for row, swap in zip(dy_mine[1:], swaps[2:]):
        dy_other.append([])
        for n, part in enumerate(row):
            if len(dy_other) == 2 and n == 0:
                dy_other[-1].append(early_swap)
                continue
            part, hid = lax.optimization_barrier((part, hid))
            dy_other[-1].append(hop(part, swap))
    blocks = [part for row in [dy_own] + dy_mine + dy_other for part in row]

    orders = []
    for g in range(turns):
        turn = [(g + t) % bits for t in range(bits)]
        orders.append(
            tuple(sum(((p >> (bits - 1 - t)) & 1) << turn[t] for t in range(bits)) for p in range(dp_count))
        )
    orders = tuple(orders)
    cut_rows = share // turns

    def down(start, count):
        outs = one(
            functools.partial(down_kernel, orders, start),
            "down",
            16 * main_flops,
            8 * row_bytes,
            [SMEM, ANY, ANY],
            [ANY] * (2 * turns),
            [shape(dp_count // 2, count, cut_rows, hidden)] * (2 * turns),
            [
                pltpu.VMEM((count, routes, width), bf16),
                pltpu.VMEM((count, routes, hidden), bf16),
                pltpu.VMEM((turns, dp_count, count, cut_rows, hidden), bf16),
                pltpu.SemaphoreType.DMA((2, count)),
                pltpu.SemaphoreType.DMA((turns, dp_count, count)),
            ],
        )(place, kept, scaled)
        return [(outs[2 * g], outs[2 * g + 1]) for g in range(turns)]

    def exchange(state, t):
        new = []
        for g, (keep, send) in enumerate(state):
            bit = 1 << ((g + t) % bits)
            got = lax.ppermute(send, "dp", [(i, i ^ bit) for i in range(dp_count)])
            both = keep.astype(f32) + got.astype(f32)
            if t < bits - 1:
                both = both.astype(bf16)
            half = both.shape[0] // 2
            new.append((both[:half], both[half:]) if half else both[0])
        return new

    token_part, kept = one(
        functools.partial(tail_kernel, groups, cap, width, top),
        "tail",
        8 * main_flops,
        4 * row_bytes,
        [SMEM] + [ANY] * (4 * groups - 2) + [ANY] * 5 + [pl.BlockSpec(memory_space=pltpu.VMEM)],
        [ANY, ANY],
        [shape(total, full), shape(experts, routes, width)],
        [
            pick_v,
            pltpu.VMEM((groups, members, width), bf16),
            pltpu.VMEM((experts, routes, width), bf16),
            pltpu.VMEM((groups, experts * cap, full), bf16),
            pltpu.VMEM((groups, members, full), bf16),
            pltpu.VMEM((experts, width, hidden), bf16),
            pltpu.VMEM((experts, hidden, width), bf16),
            act3,
            act3,
            pltpu.SemaphoreType.DMA((groups, 2)),
            pltpu.SemaphoreType.DMA((5, experts)),
            pltpu.SemaphoreType.DMA((experts,)),
            pltpu.SemaphoreType.DMA((groups,)),
        ],
    )(place, *blocks, pick, w_down, w_flip, hid, slope_g, meta)
    summed = lax.psum_scatter(token_part, "ep", scatter_dimension=0, tiled=True)
    token_grad, gate_grad = pl.pallas_call(
        functools.partial(finish_kernel, width, top),
        out_shape=[shape(tok_rows, width), shape(top, tok_rows)],
        compiler_params=pltpu.CompilerParams(vmem_limit_bytes=VMEM_LIMIT),
        cost_estimate=cost(0, 4 * tok_rows * width),
        name="finish",
    )(summed)

    counts = [experts - 1, 1] if experts > 1 else [experts]
    states = [down(start, count) for start, count in zip((0, counts[0]), counts)]
    for t in range(bits - 1):
        states = [exchange(state, t) for state in states]
    last = bits - 1
    states = [
        [
            (keep, lax.ppermute(send, "dp", [(i, i ^ (1 << ((g + last) % bits))) for i in range(dp_count)]))
            for g, (keep, send) in enumerate(state)
        ]
        for state in states
    ]
    keeps = [keep for keep, _ in states[-1]]
    token_grad, keeps = lax.optimization_barrier((token_grad, keeps))
    states[-1] = [(keep, got) for keep, (_, got) in zip(keeps, states[-1])]
    down_grad, start = None, 0
    for count, state in zip(counts, states):
        operands = [x for pair in state for x in pair]
        dest = [] if down_grad is None else [down_grad]

        def put(*refs, start=start, skip=len(dest), used=len(operands)):
            put_kernel(start, *refs[:used], *refs[used + skip :])

        down_grad = pl.pallas_call(
            put,
            in_specs=[VMEM] * len(operands) + [ANY] * len(dest),
            out_specs=ANY,
            out_shape=shape(experts, share, hidden, dtype=f32),
            input_output_aliases={len(operands): 0} if dest else {},
            scratch_shapes=[
                pltpu.VMEM((turns, count, cut_rows, hidden), f32),
                pltpu.SemaphoreType.DMA((turns,)),
            ],
            compiler_params=pltpu.CompilerParams(vmem_limit_bytes=VMEM_LIMIT // 2),
            cost_estimate=cost(0, 4 * experts * share * hidden),
            name="put",
        )(*operands, *dest)
        start += count
    return (token_grad, gate_grad.T, down_grad)


def solution(mesh):
    return jax.shard_map(
        shards,
        mesh=mesh,
        in_specs=(
            P(("dp", "ep"), None),
            P(("dp", "ep"), None),
            P(("dp", "ep"), None),
            P(("dp", "ep"), None),
            P("ep", None, None),
            P("ep", None, None),
        ),
        out_specs=(P(("dp", "ep"), None), P(("dp", "ep"), None), P("ep", "dp", None)),
        check_vma=False,
    )
```
